32 devices in a mesh: dp: 8 (over z, x), fsdp: 4 (over y, core).
Axes of the slice: x: 2, y: 2, z: 4, core: 2. Of those that a mesh axis runs over, the one named last changes fastest.
Arguments:
- tokens: bfloat16 [64, 320, 1024], P(('dp', 'fsdp')), may hold values from -6 to 6
- condition: float32 [3, 1024], replicated, may hold values from -6 to 6
- clip_frames: int32 [3], replicated, may hold values from 2 to 9, as said below
- ada_weight: bfloat16 [1024, 6144], P('fsdp', 'dp'), may hold values from -0.1875 to 0.1875
- ada_bias: bfloat16 [6144], P('dp'), may hold values from -1.796875 to 1.796875
- qkv_weight: bfloat16 [1024, 3072], P('fsdp', 'dp'), may hold values from -0.1875 to 0.1875
- out_weight: bfloat16 [1024, 1024], P('fsdp', 'dp'), may hold values from -0.75 to 0.75
- up_weight: bfloat16 [1024, 4096], P('fsdp', 'dp'), may hold values from -0.1875 to 0.1875
- down_weight: bfloat16 [4096, 1024], P('fsdp', 'dp'), may hold values from -0.09375 to 0.09375
- rel_table: bfloat16 [16, 2025], P('dp'), may hold values from -3 to 3
- cotangent: bfloat16 [64, 320, 1024], P(('dp', 'fsdp')), may hold values from -6 to 6
Outputs:
- output: bfloat16 [64, 320, 1024], P(('dp', 'fsdp'))
- grad_tokens: float32 [64, 320, 1024], P(('dp', 'fsdp'))
- grad_condition: float32 [3, 1024], replicated
- grad_ada_weight: float32 [1024, 6144], P('fsdp', 'dp')
- grad_ada_bias: float32 [6144], P('dp')
- grad_qkv: float32 [1024, 3072], P('fsdp', 'dp')
- grad_out: float32 [1024, 1024], P('fsdp', 'dp')
- grad_up: float32 [1024, 4096], P('fsdp', 'dp')
- grad_down: float32 [4096, 1024], P('fsdp', 'dp')
- grad_table: float32 [16, 2025], P('dp')
The draws below stay inside these ranges and needn't reach their ends.
Inputs may be any that keep to these rules, and one draw needn't show every extreme that they name: `clip_frames`: A third of the 3 clips, at places drawn from the seed, have 5 + 1 to 9 frames and span two slabs; the others have 2 to 5 frames. Some clip has 2 frames and some 2*5 - 1.
All inputs are finite; a program needn't handle non-finite values.
Results may differ from the reference program's by a relative error of at most 0.018.
The reference program's roundings to bfloat16 on the way count: a program that leaves them out, or rounds other values in their place, can miss the bound.
Values may be sent and summed in bfloat16 or wider, within the bound.
A program may use at most 320 MiB of HBM per device.

```python
import jax
import jax.numpy as jnp
from jax import lax

D = 1024
H = 16
HD = 64
FF = 4096
WT = 5
WSIDE = 8
WIN = 320
SPW = 16
REL = 2025
WINDOWS = 64
CLIPS = 3


def draw_clip_frames(key, part):
    key = jax.random.fold_in(key, 7)
    order = jax.random.permutation(jax.random.fold_in(key, 11), CLIPS)
    longer_count = CLIPS // 3
    longer = order < longer_count
    long_frames = jax.random.randint(jax.random.fold_in(key, 12), (CLIPS,), WT + 1, 2 * WT)
    short_frames = jax.random.randint(jax.random.fold_in(key, 13), (CLIPS,), 2, WT + 1)
    frames_drawn = jnp.where(longer, long_frames, short_frames)
    frames_drawn = jnp.where(order == 0, 2 * WT - 1, frames_drawn)
    frames_drawn = jnp.where(order == longer_count, 2, frames_drawn)
    return frames_drawn.astype(jnp.int32)


def levels(own_key, dims, cuts, smallest, top_value):
    level = 1.0
    for dim, shards_of in cuts:
        heights = jax.random.uniform(jax.random.fold_in(jax.random.fold_in(own_key, 6), dim), (shards_of,), jnp.float32, smallest / len(cuts), top_value / len(cuts))
        level = level * jnp.repeat(jnp.exp(heights), dims[dim] // shards_of).reshape((-1,) + (1,) * (len(dims) - 1 - dim))
    return level


def noise(stream_key, dims, deviation, limit, cuts=(), held_as=jnp.bfloat16):
    values = jax.random.normal(stream_key, dims, jnp.float32) * deviation
    if len(cuts) > 0:
        values = levels(stream_key, dims, cuts, -0.22, 0.18) * values
    return jnp.clip(values, min=-limit, max=limit).astype(held_as)


def setup_inputs(seed: int = 0) -> dict:
    keys = jax.random.split(jax.random.key(seed), 12)
    tokens = noise(keys[0], (WINDOWS, WIN, D), 1.0, 6.0, ((0, 32),))
    condition = noise(keys[1], (CLIPS, D), 1.0, 6.0, (), jnp.float32)
    clip_frames = draw_clip_frames(jax.random.fold_in(keys[11], 71), 0)
    ada_weight = noise(keys[3], (D, 6 * D), D ** -0.5, 0.1875, ((0, 4), (1, 8)))
    ada_bias = noise(keys[4], (6 * D,), 0.3, 1.796875, ((0, 8),))
    qkv_weight = noise(keys[5], (D, 3 * D), D ** -0.5, 0.1875, ((0, 4), (1, 8)))
    out_weight = noise(keys[6], (D, D), (D // 16) ** -0.5, 0.75, ((0, 4), (1, 8)))
    up_weight = noise(keys[7], (D, FF), D ** -0.5, 0.1875, ((0, 4), (1, 8)))
    down_weight = noise(keys[8], (FF, D), FF ** -0.5, 0.09375, ((0, 4), (1, 8)))
    rel_table = noise(keys[9], (H, REL), 0.5, 3.0, ((0, 8),))
    cotangent = noise(keys[10], (WINDOWS, WIN, D), 1.0, 6.0, ((0, 32),))
    return dict(tokens=tokens, condition=condition, clip_frames=clip_frames, ada_weight=ada_weight, ada_bias=ada_bias, qkv_weight=qkv_weight, out_weight=out_weight, up_weight=up_weight, down_weight=down_weight, rel_table=rel_table, cotangent=cotangent)


@jax.custom_vjp
def low(v):
    return lax.optimization_barrier(v.astype(jnp.bfloat16)).astype(jnp.float32)

@jax.custom_vjp
def low_back(v):
    return v

def low_keep(v):
    return (low(v), None)

def low_pass(kept, grad):
    return (grad,)

def back_keep(v):
    return (v, None)

def back_low(kept, grad):
    return (low(grad),)
low.defvjp(low_keep, low_pass)
low_back.defvjp(back_keep, back_low)
EPSILON = 1e-06
NEGATIVE = -1000000000.0
HIGHEST = lax.Precision.HIGHEST

def matmul_high(left, right):
    return jnp.dot(left, right, precision=HIGHEST, preferred_element_type=jnp.float32)

def normalize(values):
    center = values - lax.optimization_barrier(jnp.mean(values, axis=-1, keepdims=True))
    spread = lax.optimization_barrier(jnp.mean(center * center, axis=-1, keepdims=True))
    return center * lax.rsqrt(spread + EPSILON)

def gelu_tanh(values):
    return 0.5 * values * (1.0 + jnp.tanh(0.7978845608028654 * (values + 0.044715 * values * values * values)))

def relative_index():
    places = jnp.arange(WIN, dtype=jnp.int32)
    frame_pos = places // (WSIDE * WSIDE)
    row_pos = places // WSIDE % WSIDE
    col_pos = places % WSIDE
    side_span = 2 * WSIDE - 1
    frame_diff = frame_pos[:, None] - frame_pos[None, :] + (WT - 1)
    row_diff = row_pos[:, None] - row_pos[None, :] + (WSIDE - 1)
    col_diff = col_pos[:, None] - col_pos[None, :] + (WSIDE - 1)
    return ((frame_diff * side_span + row_diff) * side_span + col_diff).astype(jnp.int32)

def window_layout(clip_frames, first_window, window_count):
    slab_count = 1 + (clip_frames > WT).astype(jnp.int32)
    starts = (jnp.cumsum(slab_count, dtype=jnp.int32) - slab_count).astype(jnp.int32)
    global_window = first_window + jnp.arange(window_count, dtype=jnp.int32)
    slab_of = (global_window // SPW).astype(jnp.int32)
    owners = (lax.optimization_barrier(jnp.sum((starts[None, :] <= slab_of[:, None]).astype(jnp.int32), axis=1)) - 1).astype(jnp.int32)
    clip_ids = jnp.arange(clip_frames.shape[0], dtype=jnp.int32)
    member = (owners[:, None] == clip_ids[None, :]).astype(jnp.int32)
    clip_start = lax.optimization_barrier(jnp.sum(member * starts[None, :], axis=1)).astype(jnp.int32)
    own_frames = lax.optimization_barrier(jnp.sum(member * clip_frames[None, :], axis=1)).astype(jnp.int32)
    inner_slab = slab_of - clip_start
    return (jnp.minimum(own_frames - WT * inner_slab, WT).astype(jnp.int32), member)

def window_group(inputs, modulation, live_frames, rel_bias, qkv_matrix, out_matrix, up_matrix, down_matrix):
    window_count = inputs.shape[0]
    shift_one, scale_one, gate_one, shift_two, scale_two, gate_two = jnp.split(modulation[:, None, :], 6, axis=-1)
    frame_pos = jnp.arange(WIN, dtype=jnp.int32) // (WSIDE * WSIDE)
    live_mask = frame_pos[None, :] < live_frames[:, None]
    normed = low(normalize(inputs) * (1.0 + scale_one) + shift_one)
    packed = low_back(low(matmul_high(normed.reshape(window_count * WIN, D), qkv_matrix)))
    packed = packed.reshape(window_count, WIN, 3, H, HD)
    scores = jnp.einsum('wqhe,wkhe->whqk', packed[:, :, 0], packed[:, :, 1], precision=HIGHEST) * HD ** (-0.5) + rel_bias[None]
    scores = low_back(scores)
    scores = jnp.where(live_mask[:, None, None, :], scores, NEGATIVE)
    shifted = jnp.exp(scores - lax.optimization_barrier(jnp.max(scores, axis=-1, keepdims=True)))
    attention = shifted / lax.optimization_barrier(jnp.sum(shifted, axis=-1, keepdims=True))
    mixed_heads = jnp.einsum('whqk,wkhe->wqhe', low(attention), packed[:, :, 2], precision=HIGHEST)
    mixed_heads = low_back(low(mixed_heads.reshape(window_count * WIN, D)))
    attended = low_back(matmul_high(mixed_heads, out_matrix)).reshape(window_count, WIN, D)
    middle = inputs + gate_one * attended
    normed_two = low(normalize(middle) * (1.0 + scale_two) + shift_two)
    hidden = low_back(matmul_high(normed_two.reshape(window_count * WIN, D), up_matrix))
    activated = low(gelu_tanh(hidden))
    mlp_out = low_back(matmul_high(activated, down_matrix)).reshape(window_count, WIN, D)
    result = middle + gate_two * mlp_out
    return jnp.where(live_mask[:, :, None], result, 0.0)

def reference(tokens, condition, clip_frames, ada_weight, ada_bias, qkv_weight, out_weight, up_weight, down_weight, rel_table, cotangent):
    total_windows = tokens.shape[0]
    live_frames, member_int = window_layout(clip_frames, jnp.int32(0), total_windows)
    member = member_int.astype(jnp.float32)
    index_table = relative_index()
    group_count = total_windows // 8

    def forward(inputs, cond_in, ada_matrix, ada_vector, qkv_matrix, out_matrix, up_matrix, down_matrix, table_in):
        clip_mod = low_back(matmul_high(low(jax.nn.silu(cond_in)), ada_matrix) + ada_vector[None, :])
        window_mod = matmul_high(member, clip_mod)
        rel_bias = table_in[:, index_table]

        def run_group(pieces):
            return window_group(pieces[0], pieces[1], pieces[2], rel_bias, qkv_matrix, out_matrix, up_matrix, down_matrix)
        results = lax.map(jax.checkpoint(run_group), (inputs.reshape(group_count, 8, WIN, D), window_mod.reshape(group_count, 8, 6 * D), live_frames.reshape(group_count, 8)))
        return results.reshape(total_windows, WIN, D)
    primals = (tokens.astype(jnp.float32), condition.astype(jnp.float32), ada_weight.astype(jnp.float32), ada_bias.astype(jnp.float32), qkv_weight.astype(jnp.float32), out_weight.astype(jnp.float32), up_weight.astype(jnp.float32), down_weight.astype(jnp.float32), rel_table.astype(jnp.float32))
    output, pullback = jax.vjp(forward, *primals)
    grads = pullback(cotangent.astype(jnp.float32))
    return (output.astype(jnp.bfloat16), grads[0], grads[1], grads[2], grads[3], grads[4], grads[5], grads[6], grads[7], grads[8])
```

```python
import functools

import jax
import jax.numpy as jnp
from jax import lax
from jax.experimental import pallas as pl
from jax.experimental.pallas import tpu as pltpu
from jax.sharding import PartitionSpec as P

D = 1024
H = 16
HD = 64
WT = 5
WSIDE = 8
WIN = 320
SPW = 16
CELLS = WSIDE * WSIDE
FRAMES = 2 * WT - 1
OFFSETS = (2 * WSIDE - 1) ** 2
REL = FRAMES * OFFSETS
LANES = 128
TILE = 256

EPSILON = 1e-06
NEGATIVE = -1000000000.0
HIGHEST = lax.Precision.HIGHEST
F32 = jnp.float32
BF16 = jnp.bfloat16
MESH = pl.DeviceIdType.MESH
MIB = 2**20

QKV, OUT, UP, DOWN, UNITS = 0, 3, 4, 8, 12
SHARE = 256
HALF = 128


def window_layout(clip_frames, first_window, window_count):
    slab_count = 1 + (clip_frames > WT).astype(jnp.int32)
    starts = jnp.cumsum(slab_count, dtype=jnp.int32) - slab_count
    global_window = first_window + jnp.arange(window_count, dtype=jnp.int32)
    slab_of = global_window // SPW
    owners = jnp.sum((starts[None, :] <= slab_of[:, None]).astype(jnp.int32), axis=1) - 1
    clip_ids = jnp.arange(clip_frames.shape[0], dtype=jnp.int32)
    member = (owners[:, None] == clip_ids[None, :]).astype(jnp.int32)
    clip_start = jnp.sum(member * starts[None, :], axis=1)
    own_frames = jnp.sum(member * clip_frames[None, :], axis=1)
    inner_slab = slab_of - clip_start
    return (jnp.minimum(own_frames - WT * inner_slab, WT), member)


def pair_onehot():
    side_span = 2 * WSIDE - 1
    pair = lax.broadcasted_iota(jnp.int32, (OFFSETS, CELLS * CELLS), 1)
    offset = lax.broadcasted_iota(jnp.int32, (OFFSETS, CELLS * CELLS), 0)
    own, other = pair // CELLS, pair % CELLS
    row_diff = own // WSIDE - other // WSIDE + (WSIDE - 1)
    col_diff = own % WSIDE - other % WSIDE + (WSIDE - 1)
    return (row_diff * side_span + col_diff == offset).astype(BF16)


def bias_strips(table):
    heads = table.shape[0]
    by_frame = table.reshape(heads, FRAMES, OFFSETS)[:, ::-1].reshape(heads * FRAMES, OFFSETS)
    strips = jnp.dot(by_frame, pair_onehot(), preferred_element_type=F32)
    strips = strips.astype(BF16).reshape(heads, FRAMES, CELLS, CELLS)
    return strips.transpose(0, 2, 1, 3).reshape(heads, CELLS, FRAMES * CELLS)


def strips_to_table(strips):
    heads = strips.shape[0]
    by_frame = strips.reshape(heads, CELLS, FRAMES, CELLS).transpose(0, 2, 1, 3)
    by_frame = by_frame.reshape(heads * FRAMES, CELLS * CELLS)
    sums = lax.dot_general(
        by_frame,
        pair_onehot().astype(F32),
        (((1,), (1,)), ((), ())),
        precision=HIGHEST,
        preferred_element_type=F32,
    )
    return sums.reshape(heads, FRAMES, OFFSETS)[:, ::-1].reshape(heads, FRAMES * OFFSETS)


def units_of(qkv, out, up, down):
    return jnp.concatenate(
        [
            qkv.reshape(D, 8, 3, LANES).transpose(2, 1, 0, 3),
            out.reshape(D, 8, 1, LANES).transpose(2, 1, 0, 3),
            up.reshape(D, 8, 4, LANES).transpose(2, 1, 0, 3),
            down.reshape(8, 4, LANES, 8, LANES).transpose(1, 3, 0, 2, 4).reshape(4, 8, D, LANES),
        ]
    )


def weights_of(units):
    def columns(part):
        return part.transpose(2, 1, 0, 3).reshape(D, -1)

    down = units[DOWN:].reshape(4, 8, 8, LANES, LANES).transpose(2, 0, 3, 1, 4)
    return (
        columns(units[QKV:OUT]),
        columns(units[OUT:UP]),
        columns(units[UP:DOWN]),
        down.reshape(4 * D, D),
    )


def own_units(qkv, out, up, down):
    def columns(part):
        return part.reshape(SHARE, -1, LANES).transpose(1, 0, 2)

    down = down.reshape(2, 4, LANES, LANES).transpose(1, 0, 2, 3).reshape(4, SHARE, LANES)
    return jnp.concatenate([columns(qkv), columns(out), columns(up), down])


def own_blocks(shares):
    def columns(part):
        return part.transpose(1, 0, 2).reshape(SHARE, -1)

    down = shares[DOWN:].reshape(4, 2, LANES, LANES).transpose(1, 0, 2, 3).reshape(4 * SHARE, LANES)
    return (columns(shares[QKV:OUT]), columns(shares[OUT:UP]), columns(shares[UP:DOWN]), down)


def dot(left, right):
    return jnp.dot(left, right, preferred_element_type=F32)


def dot_rows(left, right):
    return lax.dot_general(left, right, (((1,), (1,)), ((), ())), preferred_element_type=F32)


def dot_tokens(left, right):
    return lax.dot_general(left, right, (((0,), (0,)), ((), ())), preferred_element_type=F32)


def tile(index):
    return pl.ds(pl.multiple_of(index * TILE, TILE), TILE)


def two_columns(unit, index):
    return jnp.concatenate([unit[2 * index], unit[2 * index + 1]], axis=1)


def some_rows(unit, index):
    return jnp.concatenate([unit[block, tile(index), :] for block in range(8)], axis=1)


def loop(count, body):
    def step(index, carry):
        body(index)
        return carry

    lax.fori_loop(0, count, step, 0)


def centered(values):
    center = values - jnp.mean(values, axis=-1, keepdims=True)
    spread = jnp.mean(center * center, axis=-1, keepdims=True)
    root = lax.rsqrt(spread + EPSILON)
    return center * root, root


def enter_kernel(tokens_ref, mod_ref, held_ref, normed_ref, packed_ref, unit_ref, sems):
    rows = 32

    def fetch(j):
        return pltpu.make_async_copy(held_ref.at[QKV + j], unit_ref.at[j % 2], sems.at[j % 2])

    fetch(0).start()
    for window in range(mod_ref.shape[0]):
        shift, scale = mod_ref[window, 0:1, :], mod_ref[window, 1:2, :]

        def step(index, window=window, shift=shift, scale=scale):
            at = pl.ds(pl.multiple_of(window * WIN + index * rows, rows), rows)
            normal, _ = centered(tokens_ref[at, :].astype(F32))
            normed_ref[at, :] = (normal * (1.0 + scale) + shift).astype(BF16)

        loop(WIN // rows, step)
    for j in range(3):
        fetch(j).wait()
        if j < 2:
            fetch(j + 1).start()

        def project(index, j=j):
            packed_ref[j, :, tile(index)] = dot(
                normed_ref[...], two_columns(unit_ref.at[j % 2], index)
            ).astype(BF16)

        loop(4, project)


def vmem():
    return pl.BlockSpec(memory_space=pltpu.VMEM)


def enter(tokens, mod, held):
    rows = tokens.shape[0]
    return pl.pallas_call(
        enter_kernel,
        in_specs=[vmem(), vmem(), pl.BlockSpec(memory_space=pl.ANY)],
        out_specs=[vmem(), vmem()],
        out_shape=[
            jax.ShapeDtypeStruct((rows, D), BF16),
            jax.ShapeDtypeStruct((3, rows, D), BF16),
        ],
        scratch_shapes=[pltpu.VMEM((2, 8, D, LANES), BF16), pltpu.SemaphoreType.DMA((2,))],
        compiler_params=pltpu.CompilerParams(vmem_limit_bytes=50 * MIB),
        name="enter",
    )(tokens, mod, held)


def attend_kernel(live_ref, query_ref, key_ref, value_ref, strip_ref, mixed_ref, probs_ref):
    live = live_ref[pl.program_id(1)] * CELLS
    key_live = lax.broadcasted_iota(jnp.int32, (1, WIN), 1) < live
    for head in range(2):
        lanes = slice(head * HD, (head + 1) * HD)
        query = query_ref[:, lanes] * BF16(HD ** (-0.5))
        keys = key_ref[:, lanes]
        values = value_ref[:, lanes]
        for frame in range(WT):
            rows = slice(frame * CELLS, (frame + 1) * CELLS)
            first = (WT - 1 - frame) * CELLS
            scores = dot_rows(query[rows], keys)
            scores = scores + strip_ref[head, :, first : first + WIN].astype(F32)
            scores = jnp.where(key_live, scores, NEGATIVE)
            shifted = jnp.exp(scores - jnp.max(scores, axis=-1, keepdims=True))
            totals = jnp.sum(shifted, axis=-1, keepdims=True)
            probs = (shifted * (1.0 / totals)).astype(BF16)
            probs_ref[head, rows] = probs
            mixed_ref[rows, lanes] = dot(probs, values).astype(BF16)


def packed_block(part):
    pairs = H // 2
    return pl.BlockSpec(
        (None, WIN, LANES),
        lambda pair, window, *_: (
            lax.rem(part * pairs + pair, 3),
            window,
            lax.div(part * pairs + pair, 3),
        ),
    )


def attend(packed, strips, live_frames):
    window_count = live_frames.shape[0]
    pairs = H // 2
    return pl.pallas_call(
        attend_kernel,
        grid_spec=pltpu.PrefetchScalarGridSpec(
            num_scalar_prefetch=1,
            grid=(pairs, window_count),
            in_specs=[
                packed_block(0),
                packed_block(1),
                packed_block(2),
                pl.BlockSpec((2, *strips.shape[1:]), lambda p, w, live: (p, 0, 0)),
            ],
            out_specs=[
                pl.BlockSpec((WIN, LANES), lambda p, w, live: (w, p)),
                pl.BlockSpec((None, 2, WIN, WIN), lambda p, w, live: (w, p, 0, 0)),
            ],
        ),
        out_shape=[
            jax.ShapeDtypeStruct((window_count * WIN, D), BF16),
            jax.ShapeDtypeStruct((window_count, H, WIN, WIN), BF16),
        ],
        name="attend",
    )(live_frames, packed, packed, packed, strips)


def attend_back_kernel(
    query_ref, key_ref, value_ref, probs_ref, grad_ref, gq_ref, gk_ref, gv_ref, strip_ref
):
    @pl.when(pl.program_id(1) == 0)
    def _():
        strip_ref[...] = jnp.zeros_like(strip_ref)

    for head in range(2):
        lanes = slice(head * HD, (head + 1) * HD)
        scale = BF16(HD ** (-0.5))
        query = query_ref[:, lanes] * scale
        keys = key_ref[:, lanes] * scale
        values = value_ref[:, lanes]
        grad = grad_ref[:, lanes]
        probs = probs_ref[head]
        gv_ref[:, lanes] = dot_tokens(grad, probs).T.astype(BF16)
        pieces = []
        for frame in range(WT):
            rows = slice(frame * CELLS, (frame + 1) * CELLS)
            first = (WT - 1 - frame) * CELLS
            grad_probs = dot_rows(grad[rows], values)
            weight = probs[rows].astype(F32)
            product = weight * grad_probs
            total = jnp.sum(product, axis=-1, keepdims=True)
            grad_scores = (product - weight * total).astype(BF16)
            strip_ref[head, :, first : first + WIN] += grad_scores.astype(F32)
            gq_ref[rows, lanes] = dot(grad_scores, keys).astype(BF16)
            pieces.append(grad_scores)
        gk_ref[:, lanes] = dot_tokens(query, jnp.concatenate(pieces, axis=0)).T.astype(BF16)


def attend_back(packed, probs, grad_mixed):
    window_count = probs.shape[0]
    rows = window_count * WIN
    pairs = H // 2

    def block():
        return pl.BlockSpec((WIN, LANES), lambda p, w: (w, p))

    return pl.pallas_call(
        attend_back_kernel,
        grid=(pairs, window_count),
        in_specs=[
            packed_block(0),
            packed_block(1),
            packed_block(2),
            pl.BlockSpec((None, 2, WIN, WIN), lambda p, w: (w, p, 0, 0)),
            block(),
        ],
        out_specs=[
            block(),
            block(),
            block(),
            pl.BlockSpec((2, CELLS, FRAMES * CELLS), lambda p, w: (p, 0, 0)),
        ],
        out_shape=[jax.ShapeDtypeStruct((rows, D), BF16)] * 3
        + [jax.ShapeDtypeStruct((H, CELLS, FRAMES * CELLS), F32)],
        name="attend_back",
    )(packed, packed, packed, probs, grad_mixed)


def each_rows(mod_ref, live_ref, body, rows=16):
    for window in range(mod_ref.shape[0]):
        live = live_ref[window] * CELLS

        def step(index, window=window, live=live):
            at = pl.ds(pl.multiple_of(window * WIN + index * rows, rows), rows)
            mods = [mod_ref[window, k : k + 1, :] for k in range(6)]
            slot = index * rows + lax.broadcasted_iota(jnp.int32, (rows, 1), 0)
            body(window, at, mods, slot < live)

        loop(WIN // rows, step)


def add_sums(sums_ref, window, which, values):
    sums_ref[window, which : which + 1, :] += jnp.sum(values, axis=0, keepdims=True)


def norm_back(grad_normed, normal, root, scale):
    grad = grad_normed * (1.0 + scale)
    mean = jnp.mean(grad, axis=-1, keepdims=True)
    along = jnp.mean(grad * normal, axis=-1, keepdims=True)
    return root * (grad - mean - normal * along)


def middle_kernel(
    live_ref,
    tokens_ref,
    cotangent_ref,
    mixed_ref,
    mod_ref,
    held_ref,
    output_ref,
    grad_middle_ref,
    grad_mixed_ref,
    sums_ref,
    part_ref,
    unit_ref,
    attended_ref,
    normed_ref,
    grad_low_ref,
    mlp_ref,
    grad_normed_ref,
    activated_ref,
    grad_hidden_ref,
    made_ref,
    fetch_sem,
    made_sem,
):
    order = [OUT] + [unit for j in range(4) for unit in (UP + j, DOWN + j)] + [OUT]

    def fetch(step):
        return pltpu.make_async_copy(
            held_ref.at[order[step]], unit_ref.at[step % 4], fetch_sem.at[step % 4]
        )

    def put(slot, unit):
        return pltpu.make_async_copy(made_ref.at[slot], part_ref.at[unit], made_sem.at[slot])

    for step in range(3):
        fetch(step).start()
    sums_ref[...] = jnp.zeros_like(sums_ref)
    mlp_ref[...] = jnp.zeros_like(mlp_ref)
    grad_normed_ref[...] = jnp.zeros_like(grad_normed_ref)
    fetch(0).wait()

    def project(index):
        attended_ref[:, tile(index)] = dot(mixed_ref[...], two_columns(unit_ref.at[0], index))

    loop(4, project)

    def modulate(window, at, mods, live):
        middle = tokens_ref[at, :].astype(F32) + mods[2] * attended_ref[at, :]
        normal, _ = centered(middle)
        normed_ref[at, :] = (normal * (1.0 + mods[4]) + mods[3]).astype(BF16)
        grad = jnp.where(live, cotangent_ref[at, :].astype(F32), 0.0)
        grad_low_ref[at, :] = (mods[5] * grad).astype(BF16)

    each_rows(mod_ref, live_ref, modulate)
    for j in range(4):
        step = 1 + 2 * j
        up, down = unit_ref.at[step % 4], unit_ref.at[(step + 1) % 4]
        fetch(step).wait()
        fetch(step + 1).wait()
        fetch(step + 2).start()
        if j < 3:
            fetch(step + 3).start()

        def hide(index, up=up, down=down):
            hidden = dot(normed_ref[...], two_columns(up, index))
            bend = jnp.tanh(0.7978845608028654 * (hidden + 0.044715 * hidden * hidden * hidden))
            activated_ref[:, tile(index)] = (0.5 * hidden * (1.0 + bend)).astype(BF16)
            slope = 0.5 * (1.0 + bend) + 0.5 * hidden * (1.0 - bend * bend) * (
                0.7978845608028654 * (1.0 + 3.0 * 0.044715 * hidden * hidden)
            )
            grad_activated = dot_rows(grad_low_ref[...], some_rows(down, index))
            grad_hidden_ref[:, tile(index)] = (grad_activated * slope).astype(BF16)

        loop(4, hide)
        if j > 0:
            put(0, DOWN + j - 1).wait()

        def down_gradient(index):
            made = dot_tokens(activated_ref[:, tile(index)], grad_low_ref[...]).astype(BF16)
            for block in range(8):
                made_ref[0, block, tile(index), :] = made[:, block * LANES : (block + 1) * LANES]

        loop(4, down_gradient)
        put(0, DOWN + j).start()
        if j > 0:
            put(1, UP + j - 1).wait()

        def up_gradient(index):
            made = dot_tokens(normed_ref[...], grad_hidden_ref[:, tile(index)]).astype(BF16)
            made_ref[1, 2 * index] = made[:, :LANES]
            made_ref[1, 2 * index + 1] = made[:, LANES:]

        loop(4, up_gradient)
        put(1, UP + j).start()

        def out_of_mlp(index, up=up, down=down):
            mlp_ref[:, tile(index)] += dot(activated_ref[...], two_columns(down, index))
            grad_normed_ref[:, tile(index)] += dot_rows(grad_hidden_ref[...], some_rows(up, index))

        loop(4, out_of_mlp)

    def join(window, at, mods, live):
        attended = attended_ref[at, :]
        middle = tokens_ref[at, :].astype(F32) + mods[2] * attended
        normal, root = centered(middle)
        mlp = mlp_ref[at, :]
        output_ref[at, :] = jnp.where(live, middle + mods[5] * mlp, 0.0).astype(BF16)
        grad_result = jnp.where(live, cotangent_ref[at, :].astype(F32), 0.0)
        grad_normed = grad_normed_ref[at, :]
        grad_middle = grad_result + norm_back(grad_normed, normal, root, mods[4])
        grad_middle_ref[at, :] = grad_middle
        grad_low_ref[at, :] = (mods[2] * grad_middle).astype(BF16)
        add_sums(sums_ref, window, 2, grad_middle * attended)
        add_sums(sums_ref, window, 3, grad_normed)
        add_sums(sums_ref, window, 4, grad_normed * normal)
        add_sums(sums_ref, window, 5, grad_result * mlp)

    each_rows(mod_ref, live_ref, join)
    fetch(9).wait()
    put(0, DOWN + 3).wait()

    def back(index):
        made = dot_tokens(mixed_ref[...], grad_low_ref[:, tile(index)]).astype(BF16)
        made_ref[0, 2 * index] = made[:, :LANES]
        made_ref[0, 2 * index + 1] = made[:, LANES:]
        grad_mixed_ref[:, tile(index)] = dot_rows(
            grad_low_ref[...], some_rows(unit_ref.at[1], index)
        ).astype(BF16)

    loop(4, back)
    put(0, OUT).start()
    put(1, UP + 3).wait()
    put(0, OUT).wait()


def middle(live_frames, tokens, cotangent, mixed, mod, held):
    rows = tokens.shape[0]
    unit = (8, D, LANES)
    return pl.pallas_call(
        middle_kernel,
        in_specs=[
            pl.BlockSpec(memory_space=pltpu.SMEM),
            vmem(),
            vmem(),
            vmem(),
            vmem(),
            pl.BlockSpec(memory_space=pl.ANY),
        ],
        out_specs=[vmem(), vmem(), vmem(), vmem(), pl.BlockSpec(memory_space=pl.ANY)],
        out_shape=[
            jax.ShapeDtypeStruct((rows, D), BF16),
            jax.ShapeDtypeStruct((rows, D), F32),
            jax.ShapeDtypeStruct((rows, D), BF16),
            jax.ShapeDtypeStruct((mod.shape[0], 8, D), F32),
            jax.ShapeDtypeStruct((UNITS, *unit), BF16),
        ],
        scratch_shapes=[
            pltpu.VMEM((4, *unit), BF16),
            pltpu.VMEM((rows, D), F32),
            pltpu.VMEM((rows, D), BF16),
            pltpu.VMEM((rows, D), BF16),
            pltpu.VMEM((rows, D), F32),
            pltpu.VMEM((rows, D), F32),
            pltpu.VMEM((rows, D), BF16),
            pltpu.VMEM((rows, D), BF16),
            pltpu.VMEM((2, *unit), BF16),
            pltpu.SemaphoreType.DMA((4,)),
            pltpu.SemaphoreType.DMA((2,)),
        ],
        compiler_params=pltpu.CompilerParams(vmem_limit_bytes=56 * MIB),
        name="middle",
    )(live_frames, tokens, cotangent, mixed, mod, held)


def leave_kernel(
    live_ref,
    tokens_ref,
    mod_ref,
    normed_ref,
    grad_middle_ref,
    gq_ref,
    gk_ref,
    gv_ref,
    held_ref,
    part_in_ref,
    grad_tokens_ref,
    sums_ref,
    part_ref,
    unit_ref,
    packed_ref,
    grad_normed_ref,
    made_ref,
    fetch_sem,
    made_sem,
):
    sources = (gq_ref, gk_ref, gv_ref)

    def fetch(j):
        return pltpu.make_async_copy(held_ref.at[QKV + j], unit_ref.at[j % 2], fetch_sem.at[j % 2])

    def put(j):
        return pltpu.make_async_copy(made_ref.at[j % 2], part_ref.at[QKV + j], made_sem.at[j % 2])

    fetch(0).start()
    sums_ref[...] = jnp.zeros_like(sums_ref)
    grad_normed_ref[...] = jnp.zeros_like(grad_normed_ref)
    for j in range(3):
        for block in range(8):
            part, column = divmod(3 * block + j, 8)
            packed_ref[:, block * LANES : (block + 1) * LANES] = sources[part][
                :, column * LANES : (column + 1) * LANES
            ]
        if j >= 2:
            put(j - 2).wait()

        def weight(index, j=j):
            made = dot_tokens(normed_ref[...], packed_ref[:, tile(index)]).astype(BF16)
            made_ref[j % 2, 2 * index] = made[:, :LANES]
            made_ref[j % 2, 2 * index + 1] = made[:, LANES:]

        loop(4, weight)
        put(j).start()
        fetch(j).wait()
        if j < 2:
            fetch(j + 1).start()

        def back(index, j=j):
            grad_normed_ref[:, tile(index)] += dot_rows(
                packed_ref[...], some_rows(unit_ref.at[j % 2], index)
            )

        loop(4, back)

    def join(window, at, mods, live):
        normal, root = centered(tokens_ref[at, :].astype(F32))
        grad_normed = grad_normed_ref[at, :]
        grad_tokens_ref[at, :] = grad_middle_ref[at, :] + norm_back(
            grad_normed, normal, root, mods[1]
        )
        add_sums(sums_ref, window, 0, grad_normed)
        add_sums(sums_ref, window, 1, grad_normed * normal)

    each_rows(mod_ref, live_ref, join)
    put(1).wait()
    put(2).wait()


def leave(live_frames, tokens, mod, normed, grad_middle, gq, gk, gv, held, part):
    rows = tokens.shape[0]
    unit = (8, D, LANES)
    anywhere = pl.BlockSpec(memory_space=pl.ANY)
    return pl.pallas_call(
        leave_kernel,
        in_specs=[pl.BlockSpec(memory_space=pltpu.SMEM)] + [vmem()] * 7 + [anywhere] * 2,
        out_specs=[vmem(), vmem(), anywhere],
        out_shape=[
            jax.ShapeDtypeStruct((rows, D), F32),
            jax.ShapeDtypeStruct((mod.shape[0], 8, D), F32),
            jax.ShapeDtypeStruct(part.shape, BF16),
        ],
        scratch_shapes=[
            pltpu.VMEM((2, *unit), BF16),
            pltpu.VMEM((rows, D), BF16),
            pltpu.VMEM((rows, D), F32),
            pltpu.VMEM((2, *unit), BF16),
            pltpu.SemaphoreType.DMA((2,)),
            pltpu.SemaphoreType.DMA((2,)),
        ],
        input_output_aliases={9: 2},
        compiler_params=pltpu.CompilerParams(vmem_limit_bytes=56 * MIB),
        name="leave",
    )(live_frames, tokens, mod, normed, grad_middle, gq, gk, gv, held, part)


class Place:
    def __init__(self):
        column, row = lax.axis_index("dp"), lax.axis_index("fsdp")
        self.z, self.x, self.y, self.c = column // 2, column % 2, row // 2, row % 2

    def at(self, z=None, x=None, y=None, c=None):
        z = self.z if z is None else z
        x = self.x if x is None else x
        y = self.y if y is None else y
        c = self.c if c is None else c
        return (z * 2 + x, y * 2 + c)

    def far(self, k):
        return lax.rem(self.z + k, 4)

    def greet(self):
        peers = [self.at(z=self.far(k)) for k in (1, 2, 3)]
        peers += [self.at(x=1 - self.x), self.at(y=1 - self.y), self.at(c=1 - self.c)]
        barrier = pltpu.get_barrier_semaphore()
        for peer in peers:
            pl.semaphore_signal(barrier, inc=1, device_id=peer, device_id_type=MESH)
        pl.semaphore_wait(barrier, len(peers))


class Gather:
    def __init__(self, place, held, send, recv, first):
        self.place, self.held, self.send, self.recv, self.first = place, held, send, recv, first

    def copies(self, unit, stage):
        p, held, index = self.place, self.held, unit - self.first

        def copy(slot, ref, device):
            return pltpu.make_async_remote_copy(
                src_ref=ref,
                dst_ref=ref,
                send_sem=self.send.at[index, slot],
                recv_sem=self.recv.at[index, slot],
                device_id=device,
                device_id_type=MESH,
            )

        if stage == 1:
            own = held.at[unit, p.z, p.x, p.y, p.c]
            return [copy(k - 1, own, p.at(z=p.far(k))) for k in (1, 2, 3)]
        if stage == 2:
            return [
                copy(3, held.at[unit, :, p.x, p.y, p.c, :HALF], p.at(x=1 - p.x)),
                copy(4, held.at[unit, :, p.x, p.y, p.c, HALF:], p.at(y=1 - p.y)),
            ]
        if stage == 3:
            return [
                copy(5, held.at[unit, :, :, p.y, p.c, :HALF], p.at(y=1 - p.y)),
                copy(6, held.at[unit, :, p.x, :, p.c, HALF:], p.at(x=1 - p.x)),
            ]
        return [copy(7, held.at[unit, :, :, :, p.c], p.at(c=1 - p.c))]

    def start(self, unit, stage):
        for copy in self.copies(unit, stage):
            copy.start()

    def arrive(self, unit, stage):
        for copy in self.copies(unit, stage):
            copy.wait_recv()

    def sent(self, unit):
        for stage in (1, 2, 3, 4):
            for copy in self.copies(unit, stage):
                copy.wait_send()


class Reduce:
    def __init__(self, place, part, total, scratch, first):
        self.place, self.part, self.total, self.first = place, part, total, first
        (self.own, self.core, self.side, self.corner, self.distant) = scratch[:5]
        self.send, self.recv, self.load = scratch[5:]

    @staticmethod
    def scratch(count):
        return [
            pltpu.VMEM((2, 4, 2, 2, SHARE, LANES), BF16),
            pltpu.VMEM((count, 4, 2, 2, SHARE, LANES), BF16),
            pltpu.VMEM((count, 2, 4, 2, HALF, LANES), BF16),
            pltpu.VMEM((count, 2, 4, HALF, LANES), BF16),
            pltpu.VMEM((count, 3, 2, HALF, LANES), BF16),
            pltpu.SemaphoreType.DMA((count, 8)),
            pltpu.SemaphoreType.DMA((count, 8)),
            pltpu.SemaphoreType.DMA((2,)),
        ]

    def own_copy(self, unit):
        slot = lax.rem(unit - self.first, 2)
        return pltpu.make_async_copy(
            self.part.at[unit, :, :, :, self.place.c], self.own.at[slot], self.load.at[slot]
        )

    def copies(self, unit, stage):
        p, index = self.place, unit - self.first

        def copy(slot, source, target, device):
            return pltpu.make_async_remote_copy(
                src_ref=source,
                dst_ref=target,
                send_sem=self.send.at[index, slot],
                recv_sem=self.recv.at[index, slot],
                device_id=device,
                device_id_type=MESH,
            )

        core, side, corner = self.core.at[index], self.side.at[index], self.corner.at[index]
        if stage == 1:
            return [copy(0, self.part.at[unit, :, :, :, 1 - p.c], core, p.at(c=1 - p.c))]
        if stage == 2:
            return [
                copy(1, core.at[:, :, 1 - p.y, :HALF], side.at[0], p.at(y=1 - p.y)),
                copy(2, core.at[:, 1 - p.x, :, HALF:], side.at[1], p.at(x=1 - p.x)),
            ]
        if stage == 3:
            return [
                copy(3, side.at[0, :, 1 - p.x], corner.at[0], p.at(x=1 - p.x)),
                copy(4, side.at[1, :, 1 - p.y], corner.at[1], p.at(y=1 - p.y)),
            ]
        return [
            copy(4 + k, corner.at[:, p.far(k)], self.distant.at[index, k - 1], p.at(z=p.far(k)))
            for k in (1, 2, 3)
        ]

    def start(self, unit, stage):
        for copy in self.copies(unit, stage):
            copy.start()
        if stage == 1:
            self.own_copy(unit).start()

    def arrive(self, unit, stage):
        for copy in self.copies(unit, stage):
            copy.wait_recv()
        if stage == 1:
            self.own_copy(unit).wait()

    def sent(self, unit):
        for stage in (1, 2, 3, 4):
            for copy in self.copies(unit, stage):
                copy.wait_send()

    def combine(self, unit, stage):
        p, index = self.place, unit - self.first
        core, side, corner = self.core.at[index], self.side.at[index], self.corner.at[index]

        def plus(left, right):
            return (left.astype(F32) + right.astype(F32)).astype(BF16)

        def from_core(step):
            z, x, y = step // 4, step // 2 % 2, step % 2
            own = self.own[lax.rem(index, 2), z, x, y]
            core[z, x, y] = plus(core[z, x, y], own)

        def from_side(step):
            z, b = step // 2, step % 2
            side[0, z, b] = plus(side[0, z, b], core[z, b, p.y, :HALF])
            side[1, z, b] = plus(side[1, z, b], core[z, p.x, b, HALF:])

        def from_corner(z):
            corner[0, z] = plus(corner[0, z], side[0, z, p.x])
            corner[1, z] = plus(corner[1, z], side[1, z, p.y])

        def from_far(half):
            total = corner[half, p.z].astype(F32)
            for k in range(3):
                total = total + self.distant[index, k, half].astype(F32)
            self.total[index, pl.ds(pl.multiple_of(half * HALF, HALF), HALF), :] = total

        count, body = {1: (16, from_core), 2: (8, from_side), 3: (4, from_corner), 4: (2, from_far)}[
            stage
        ]
        loop(count, body)

    def advance(self, unit, stage):
        self.arrive(unit, stage)
        self.combine(unit, stage)
        if stage < 4:
            self.start(unit, stage + 1)


def gather_kernel(own_ref, held_ref, local, send, recv):
    place = Place()
    place.greet()
    work = Gather(place, held_ref, send, recv, 0)

    def own_copy(unit):
        own = held_ref.at[unit, place.z, place.x, place.y, place.c]
        return pltpu.make_async_copy(own_ref.at[unit], own, local.at[unit])

    loop(UNITS, lambda unit: own_copy(unit).start())
    loop(UNITS, lambda unit: own_copy(unit).wait())
    work.start(0, 1)
    work.start(1, 1)

    def tick(step):
        @pl.when(step + 2 < UNITS)
        def _():
            work.start(step + 2, 1)

        for stage in (1, 2, 3):
            unit = step + 1 - stage

            @pl.when((unit >= 0) & (unit < UNITS))
            def _(unit=unit, stage=stage):
                work.arrive(unit, stage)
                work.start(unit, stage + 1)

    loop(UNITS + 2, tick)

    def finish(unit):
        work.arrive(unit, 4)
        work.sent(unit)

    loop(UNITS, finish)


def gather(own):
    held = pl.pallas_call(
        gather_kernel,
        in_specs=[pl.BlockSpec(memory_space=pl.ANY)],
        out_specs=pl.BlockSpec(memory_space=pl.ANY),
        out_shape=jax.ShapeDtypeStruct((UNITS, 4, 2, 2, 2, SHARE, LANES), BF16),
        scratch_shapes=[
            pltpu.SemaphoreType.DMA((UNITS,)),
            pltpu.SemaphoreType.DMA((UNITS, 8)),
            pltpu.SemaphoreType.DMA((UNITS, 8)),
        ],
        compiler_params=pltpu.CompilerParams(collective_id=0, has_side_effects=True),
        name="gather",
    )(own)
    return held.reshape(UNITS, 8, D, LANES)


def reduce_kernel(part_ref, total_ref, *scratch):
    place = Place()
    place.greet()
    work = Reduce(place, part_ref, total_ref, scratch, 0)
    work.start(0, 1)
    work.start(1, 1)

    def tick(step):
        for stage in (1, 2, 3, 4):
            unit = step + 1 - stage

            @pl.when((unit >= 0) & (unit < UNITS))
            def _(unit=unit, stage=stage):
                work.advance(unit, stage)
                if stage == 1:

                    @pl.when(unit + 2 < UNITS)
                    def _():
                        work.start(unit + 2, 1)

    loop(UNITS + 3, tick)
    loop(UNITS, work.sent)


def reduce(part):
    return pl.pallas_call(
        reduce_kernel,
        in_specs=[pl.BlockSpec(memory_space=pl.ANY)],
        out_specs=vmem(),
        out_shape=jax.ShapeDtypeStruct((UNITS, SHARE, LANES), F32),
        scratch_shapes=Reduce.scratch(UNITS),
        compiler_params=pltpu.CompilerParams(
            collective_id=1, has_side_effects=True, vmem_limit_bytes=48 * MIB
        ),
        name="reduce",
    )(part.reshape(UNITS, 4, 2, 2, 2, SHARE, LANES))


def per_device(
    special,
    tokens,
    condition,
    clip_frames,
    ada_weight,
    ada_bias,
    qkv_weight,
    out_weight,
    up_weight,
    down_weight,
    rel_table,
    cotangent,
):
    window_count = tokens.shape[0]
    clip_count = condition.shape[0]
    rows_ada, cols_ada = ada_weight.shape
    row_block = lax.axis_index("fsdp")
    col_block = lax.axis_index("dp")
    row_count = lax.axis_size("fsdp")
    first_window = lax.axis_index(("dp", "fsdp")) * window_count
    live_frames, member_int = window_layout(clip_frames, first_window, window_count)
    member = member_int.astype(F32)
    activity_low = jax.nn.silu(condition).astype(BF16)
    act_rows = lax.dynamic_slice_in_dim(activity_low, row_block * rows_ada, rows_ada, 1)

    mod_part = jnp.dot(act_rows, ada_weight, preferred_element_type=F32)
    mod_part = mod_part + jnp.where(row_block == 0, ada_bias.astype(F32), 0.0)[None, :]
    mod_size = mod_part.size
    table_size = rel_table.size
    table_part = -(-table_size // row_count)
    table_flat = jnp.pad(
        rel_table.astype(F32).reshape(-1), (0, table_part * row_count - table_size)
    )
    table_own = lax.dynamic_slice_in_dim(table_flat, row_block * table_part, table_part, 0)
    small = lax.all_gather(
        jnp.concatenate([mod_part.reshape(-1), table_own]), ("dp", "fsdp"), axis=0
    )
    small = small.reshape(-1, row_count, mod_size + table_part)
    col_count = small.shape[0]
    clip_mod = jnp.sum(small[:, :, :mod_size], axis=1)
    clip_mod = clip_mod.reshape(col_count, clip_count, cols_ada).transpose(1, 0, 2)
    clip_mod = clip_mod.reshape(clip_count, col_count * cols_ada)
    table_all = small[:, :, mod_size:].reshape(col_count, -1)[:, :table_size]
    table_all = table_all.reshape(-1, REL).astype(BF16)
    window_mod = jnp.sum(member[:, :, None] * clip_mod[None], axis=1)
    window_mod = window_mod.reshape(window_count, 6, D)
    strips = bias_strips(table_all)

    if special:
        held = gather(own_units(qkv_weight, out_weight, up_weight, down_weight))
    else:
        whole = [
            lax.all_gather(
                lax.all_gather(weight, "dp", axis=1, tiled=True), "fsdp", axis=0, tiled=True
            )
            for weight in (qkv_weight, out_weight, up_weight, down_weight)
        ]
        held = units_of(*whole)

    token_rows = tokens.reshape(window_count * WIN, D)
    cotangent_rows = cotangent.reshape(window_count * WIN, D)
    normed, packed = enter(token_rows, window_mod, held)
    mixed, probs = attend(packed, strips, live_frames)
    output, grad_middle, grad_mixed, late_sums, part = middle(
        live_frames, token_rows, cotangent_rows, mixed, window_mod, held
    )
    grad_query, grad_key, grad_value, strip_grad = attend_back(packed, probs, grad_mixed)
    grad_tokens, early_sums, part = leave(
        live_frames,
        token_rows,
        window_mod,
        normed,
        grad_middle,
        grad_query,
        grad_key,
        grad_value,
        held,
        part,
    )
    grad_window_mod = (late_sums + early_sums)[:, :6].reshape(window_count, 6 * D)
    clip_part = lax.dot_general(
        member,
        grad_window_mod,
        (((0,), (0,)), ((), ())),
        precision=HIGHEST,
        preferred_element_type=F32,
    )
    table_part = strips_to_table(strip_grad)
    grad_clip_mod, grad_table_all = lax.psum((clip_part, table_part), ("dp", "fsdp"))
    clip_low = grad_clip_mod.astype(BF16)
    clip_cols = lax.dynamic_slice_in_dim(clip_low, col_block * cols_ada, cols_ada, 1)
    grad_ada_weight = lax.dot_general(
        act_rows, clip_cols, (((0,), (0,)), ((), ())), preferred_element_type=F32
    )
    grad_ada_bias = jnp.sum(clip_cols.astype(F32), axis=0)
    cond_part = lax.dot_general(
        clip_cols, ada_weight, (((1,), (1,)), ((), ())), preferred_element_type=F32
    )
    cond_placed = lax.dynamic_update_slice_in_dim(
        jnp.zeros((clip_count, D), F32), cond_part, row_block * rows_ada, 1
    )
    cond_total = lax.psum(cond_placed, ("dp", "fsdp"))
    _, silu_back = jax.vjp(jax.nn.silu, condition)
    grad_condition = silu_back(cond_total)[0]
    heads_own = rel_table.shape[0]
    grad_table = lax.dynamic_slice_in_dim(grad_table_all, col_block * heads_own, heads_own, 0)

    if special:
        grads = own_blocks(reduce(part))
    else:
        grads = [
            lax.psum_scatter(
                lax.psum_scatter(grad, "fsdp", scatter_dimension=0, tiled=True),
                "dp",
                scatter_dimension=1,
                tiled=True,
            ).astype(F32)
            for grad in weights_of(part)
        ]
    return (
        output.reshape(tokens.shape),
        grad_tokens.reshape(tokens.shape),
        grad_condition,
        grad_ada_weight,
        grad_ada_bias,
        *grads,
        grad_table,
    )


def solution(mesh):
    special = dict(mesh.shape) == {"dp": 8, "fsdp": 4}
    both = P(("dp", "fsdp"), None, None)
    weight = P("fsdp", "dp")
    in_specs = (both, P(), P(), weight, P("dp")) + (weight,) * 4 + (P("dp", None), both)
    out_specs = (both, both, P(), weight, P("dp")) + (weight,) * 4 + (P("dp", None),)
    return jax.shard_map(
        functools.partial(per_device, special),
        mesh=mesh,
        in_specs=in_specs,
        out_specs=out_specs,
        check_vma=False,
    )
```

```python
import functools

import jax
import jax.numpy as jnp
from jax import lax
from jax.experimental import pallas as pl
from jax.experimental.pallas import tpu as pltpu
from jax.sharding import PartitionSpec as P

D = 1024
H = 16
HD = 64
WT = 5
WSIDE = 8
WIN = 320
SPW = 16
CELLS = WSIDE * WSIDE
FRAMES = 2 * WT - 1
OFFSETS = (2 * WSIDE - 1) ** 2
REL = FRAMES * OFFSETS
LANES = 128
TILE = 256
SPREAD = 80
STRIP = 640

EPSILON = 1e-06
NEGATIVE = -1000000000.0
HIGHEST = lax.Precision.HIGHEST
F32 = jnp.float32
BF16 = jnp.bfloat16
MESH = pl.DeviceIdType.MESH
MIB = 2**20

QKV, OUT, UP, DOWN, UNITS = 0, 3, 4, 8, 12
SHARE = 256
HALF = 128


def window_layout(clip_frames, first_window, window_count):
    slab_count = 1 + (clip_frames > WT).astype(jnp.int32)
    starts = jnp.cumsum(slab_count, dtype=jnp.int32) - slab_count
    global_window = first_window + jnp.arange(window_count, dtype=jnp.int32)
    slab_of = global_window // SPW
    owners = jnp.sum((starts[None, :] <= slab_of[:, None]).astype(jnp.int32), axis=1) - 1
    clip_ids = jnp.arange(clip_frames.shape[0], dtype=jnp.int32)
    member = (owners[:, None] == clip_ids[None, :]).astype(jnp.int32)
    clip_start = jnp.sum(member * starts[None, :], axis=1)
    own_frames = jnp.sum(member * clip_frames[None, :], axis=1)
    inner_slab = slab_of - clip_start
    return (jnp.minimum(own_frames - WT * inner_slab, WT), member)


def offset_spread():
    side_span = 2 * WSIDE - 1
    shape = (OFFSETS, WSIDE * LANES)
    offset = lax.broadcasted_iota(jnp.int32, shape, 0)
    place = lax.broadcasted_iota(jnp.int32, shape, 1)
    own, row, other = place // LANES, place // WSIDE % (LANES // WSIDE), place % WSIDE
    row_diff, col_diff = side_span - 1 - row, own - other + (WSIDE - 1)
    return ((row < side_span) & (row_diff * side_span + col_diff == offset)).astype(BF16)


def spread_table(table):
    heads = table.shape[0]
    by_frame = table.reshape(heads, FRAMES, OFFSETS)[:, ::-1].reshape(heads * FRAMES, OFFSETS)
    spread = jnp.dot(by_frame, offset_spread(), preferred_element_type=F32).astype(BF16)
    spread = spread.reshape(heads, FRAMES * WSIDE, LANES)
    return jnp.pad(spread, ((0, 0), (0, SPREAD - FRAMES * WSIDE), (0, 0)))


def gather_table(spread):
    heads = spread.shape[0]
    by_frame = spread[:, : FRAMES * WSIDE].reshape(heads * FRAMES, WSIDE * LANES)
    sums = lax.dot_general(
        by_frame,
        offset_spread().astype(F32),
        (((1,), (1,)), ((), ())),
        precision=HIGHEST,
        preferred_element_type=F32,
    )
    return sums.reshape(heads, FRAMES, OFFSETS)[:, ::-1].reshape(heads, FRAMES * OFFSETS)


def units_of(qkv, out, up, down):
    return jnp.concatenate(
        [
            qkv.reshape(D, 8, 3, LANES).transpose(2, 1, 0, 3),
            out.reshape(D, 8, 1, LANES).transpose(2, 1, 0, 3),
            up.reshape(D, 8, 4, LANES).transpose(2, 1, 0, 3),
            down.reshape(8, 4, LANES, 8, LANES).transpose(1, 3, 0, 2, 4).reshape(4, 8, D, LANES),
        ]
    )


def weights_of(units):
    def columns(part):
        return part.transpose(2, 1, 0, 3).reshape(D, -1)

    down = units[DOWN:].reshape(4, 8, 8, LANES, LANES).transpose(2, 0, 3, 1, 4)
    return (
        columns(units[QKV:OUT]),
        columns(units[OUT:UP]),
        columns(units[UP:DOWN]),
        down.reshape(4 * D, D),
    )


def own_blocks(shares):
    def columns(part):
        return part.transpose(1, 0, 2).reshape(SHARE, -1)

    down = shares[DOWN:].reshape(4, 2, LANES, LANES).transpose(1, 0, 2, 3).reshape(4 * SHARE, LANES)
    return (columns(shares[QKV:OUT]), columns(shares[OUT:UP]), columns(shares[UP:DOWN]), down)


def dot(left, right):
    return jnp.dot(left, right, preferred_element_type=F32)


def dot_rows(left, right):
    return lax.dot_general(left, right, (((1,), (1,)), ((), ())), preferred_element_type=F32)


def dot_tokens(left, right):
    return lax.dot_general(left, right, (((0,), (0,)), ((), ())), preferred_element_type=F32)


def tile(index):
    return pl.ds(pl.multiple_of(index * TILE, TILE), TILE)


def two_columns(unit, index):
    return jnp.concatenate([unit[index, x].reshape(D, LANES) for x in range(2)], axis=1)


def put_columns(unit, index, values):
    for x in range(2):
        unit[index, x] = values[:, x * LANES : (x + 1) * LANES].reshape(2, 2, SHARE, LANES)


def some_rows(unit, index):
    row, core = index // 2, index % 2
    blocks = [unit[block // 2, block % 2, row, core] for block in range(8)]
    return jnp.concatenate(blocks, axis=1)


def loop(count, body):
    def step(index, carry):
        body(index)
        return carry

    lax.fori_loop(0, count, step, 0)


def vmem():
    return pl.BlockSpec(memory_space=pltpu.VMEM)


def anywhere():
    return pl.BlockSpec(memory_space=pl.ANY)


def smem():
    return pl.BlockSpec(memory_space=pltpu.SMEM)


def shape(dtype, *sizes):
    return jax.ShapeDtypeStruct(sizes, dtype)


def params(collective=None, limit=58):
    if collective is None:
        return pltpu.CompilerParams(vmem_limit_bytes=limit * MIB)
    return pltpu.CompilerParams(
        vmem_limit_bytes=limit * MIB, collective_id=collective, has_side_effects=True
    )


def centered(values):
    center = values - jnp.mean(values, axis=-1, keepdims=True)
    spread = jnp.mean(center * center, axis=-1, keepdims=True)
    root = lax.rsqrt(spread + EPSILON)
    return center * root, root


def norm_back(grad_normed, normal, root, scale):
    grad = grad_normed * (1.0 + scale)
    mean = jnp.mean(grad, axis=-1, keepdims=True)
    along = jnp.mean(grad * normal, axis=-1, keepdims=True)
    return root * (grad - mean - normal * along)


def each_rows(mod_ref, live_ref, body, rows=16):
    for window in range(mod_ref.shape[0]):
        live = live_ref[window] * CELLS

        def step(index, window=window, live=live):
            at = pl.ds(pl.multiple_of(window * WIN + index * rows, rows), rows)
            mods = [mod_ref[window, k : k + 1, :] for k in range(6)]
            slot = index * rows + lax.broadcasted_iota(jnp.int32, (rows, 1), 0)
            body(window, at, mods, slot < live)

        loop(WIN // rows, step)


def add_sums(sums_ref, window, which, values):
    sums_ref[window, which : which + 1, :] += jnp.sum(values, axis=0, keepdims=True)


class Place:
    def __init__(self):
        column, row = lax.axis_index("dp"), lax.axis_index("fsdp")
        self.z, self.x, self.y, self.c = column // 2, column % 2, row // 2, row % 2

    def at(self, z=None, x=None, y=None, c=None):
        z = self.z if z is None else z
        x = self.x if x is None else x
        y = self.y if y is None else y
        c = self.c if c is None else c
        return (z * 2 + x, y * 2 + c)

    def far(self, k):
        return lax.rem(self.z + k, 4)

    def greet(self):
        peers = [self.at(z=self.far(k)) for k in (1, 2, 3)]
        peers += [self.at(x=1 - self.x), self.at(y=1 - self.y), self.at(c=1 - self.c)]
        barrier = pltpu.get_barrier_semaphore()
        for peer in peers:
            pl.semaphore_signal(barrier, inc=1, device_id=peer, device_id_type=MESH)
        pl.semaphore_wait(barrier, len(peers))


class Gather:
    def __init__(self, place, held, units, scratch):
        self.place, self.held, self.units = place, held, units
        self.send, self.recv = scratch

    @staticmethod
    def scratch(count):
        return [pltpu.SemaphoreType.DMA((count, 8))] * 2

    def copies(self, index, stage):
        p, held = self.place, self.held.at[self.units[index]]

        def copy(slot, ref, device):
            return pltpu.make_async_remote_copy(
                src_ref=ref,
                dst_ref=ref,
                send_sem=self.send.at[index, slot],
                recv_sem=self.recv.at[index, slot],
                device_id=device,
                device_id_type=MESH,
            )

        if stage == 1:
            return [copy(k - 1, held.at[p.z, p.x, p.y, p.c], p.at(z=p.far(k))) for k in (1, 2, 3)]
        if stage == 2:
            return [
                copy(3, held.at[:, p.x, p.y, p.c, :HALF], p.at(x=1 - p.x)),
                copy(4, held.at[:, p.x, p.y, p.c, HALF:], p.at(y=1 - p.y)),
            ]
        if stage == 3:
            return [
                copy(5, held.at[:, :, p.y, p.c, :HALF], p.at(y=1 - p.y)),
                copy(6, held.at[:, p.x, :, p.c, HALF:], p.at(x=1 - p.x)),
            ]
        return [copy(7, held.at[:, :, :, p.c], p.at(c=1 - p.c))]

    def start(self, index, stage):
        for copy in self.copies(index, stage):
            copy.start()

    def arrive(self, index, stage):
        for copy in self.copies(index, stage):
            copy.wait_recv()

    def sent(self):
        for index in range(len(self.units)):
            for stage in (1, 2, 3, 4):
                for copy in self.copies(index, stage):
                    copy.wait_send()

    def actions(self):
        count = len(self.units)

        def begin():
            for index in range(min(2, count)):
                self.start(index, 1)

        def tick(step):
            if step + 2 < count:
                self.start(step + 2, 1)
            for stage in (1, 2, 3):
                index = step + 1 - stage
                if 0 <= index < count:
                    self.arrive(index, stage)
                    self.start(index, stage + 1)

        return [begin] + [functools.partial(tick, step) for step in range(count + 2)]


class Reduce:
    def __init__(self, place, part, total, units, scratch):
        self.place, self.part, self.total, self.units = place, part, total, units
        self.own, self.core, self.side, self.corner, self.distant = scratch[:5]
        self.send, self.recv, self.load = scratch[5:]

    @staticmethod
    def scratch(count):
        return [
            pltpu.VMEM((2, 4, 2, 2, SHARE, LANES), BF16),
            pltpu.VMEM((count, 4, 2, 2, SHARE, LANES), BF16),
            pltpu.VMEM((count, 2, 4, 2, HALF, LANES), BF16),
            pltpu.VMEM((count, 2, 4, HALF, LANES), BF16),
            pltpu.VMEM((count, 3, 2, HALF, LANES), BF16),
            pltpu.SemaphoreType.DMA((count, 8)),
            pltpu.SemaphoreType.DMA((count, 8)),
            pltpu.SemaphoreType.DMA((2,)),
        ]

    def own_copy(self, index):
        slot = index % 2
        return pltpu.make_async_copy(
            self.part.at[self.units[index], :, :, :, self.place.c],
            self.own.at[slot],
            self.load.at[slot],
        )

    def copies(self, index, stage):
        p, part = self.place, self.part.at[self.units[index]]

        def copy(slot, source, target, device):
            return pltpu.make_async_remote_copy(
                src_ref=source,
                dst_ref=target,
                send_sem=self.send.at[index, slot],
                recv_sem=self.recv.at[index, slot],
                device_id=device,
                device_id_type=MESH,
            )

        core, side, corner = self.core.at[index], self.side.at[index], self.corner.at[index]
        if stage == 1:
            return [copy(0, part.at[:, :, :, 1 - p.c], core, p.at(c=1 - p.c))]
        if stage == 2:
            return [
                copy(1, core.at[:, :, 1 - p.y, :HALF], side.at[0], p.at(y=1 - p.y)),
                copy(2, core.at[:, 1 - p.x, :, HALF:], side.at[1], p.at(x=1 - p.x)),
            ]
        if stage == 3:
            return [
                copy(3, side.at[0, :, 1 - p.x], corner.at[0], p.at(x=1 - p.x)),
                copy(4, side.at[1, :, 1 - p.y], corner.at[1], p.at(y=1 - p.y)),
            ]
        return [
            copy(4 + k, corner.at[:, p.far(k)], self.distant.at[index, k - 1], p.at(z=p.far(k)))
            for k in (1, 2, 3)
        ]

    def start(self, index, stage):
        for copy in self.copies(index, stage):
            copy.start()
        if stage == 1:
            self.own_copy(index).start()

    def sent(self):
        for index in range(len(self.units)):
            for stage in (1, 2, 3, 4):
                for copy in self.copies(index, stage):
                    copy.wait_send()

    def combine(self, index, stage):
        p = self.place
        core, side, corner = self.core.at[index], self.side.at[index], self.corner.at[index]

        def plus(left, right):
            return (left.astype(F32) + right.astype(F32)).astype(BF16)

        def from_core(step):
            z, x, y = step // 4, step // 2 % 2, step % 2
            core[z, x, y] = plus(core[z, x, y], self.own[index % 2, z, x, y])

        def from_side(step):
            z, b = step // 2, step % 2
            side[0, z, b] = plus(side[0, z, b], core[z, b, p.y, :HALF])
            side[1, z, b] = plus(side[1, z, b], core[z, p.x, b, HALF:])

        def from_corner(z):
            corner[0, z] = plus(corner[0, z], side[0, z, p.x])
            corner[1, z] = plus(corner[1, z], side[1, z, p.y])

        def from_far(half):
            total = corner[half, p.z].astype(F32)
            for k in range(3):
                total = total + self.distant[index, k, half].astype(F32)
            self.total[index, pl.ds(pl.multiple_of(half * HALF, HALF), HALF), :] = total

        steps = {1: (16, from_core), 2: (8, from_side), 3: (4, from_corner), 4: (2, from_far)}
        loop(*steps[stage])

    def advance(self, index, stage):
        for copy in self.copies(index, stage):
            copy.wait_recv()
        if stage == 1:
            self.own_copy(index).wait()
        self.combine(index, stage)
        if stage < 4:
            self.start(index, stage + 1)

    def actions(self):
        count = len(self.units)

        def begin():
            for index in range(min(2, count)):
                self.start(index, 1)

        def tick(step):
            for stage in (1, 2, 3, 4):
                index = step + 1 - stage
                if 0 <= index < count:
                    self.advance(index, stage)
                    if stage == 1 and index + 2 < count:
                        self.start(index + 2, 1)

        return [begin] + [functools.partial(tick, step) for step in range(count + 3)]


class Small:
    def __init__(self, place, values, scratch):
        self.place, self.values = place, values
        self.from_core, self.from_x, self.from_y, self.from_z, self.send, self.recv = scratch

    @staticmethod
    def scratch(rows):
        return [
            pltpu.VMEM((4, 2, rows, LANES), F32),
            pltpu.VMEM((4, rows, LANES), F32),
            pltpu.VMEM((4, rows, LANES), F32),
            pltpu.VMEM((3, rows, LANES), F32),
            pltpu.SemaphoreType.DMA((6,)),
            pltpu.SemaphoreType.DMA((6,)),
        ]

    def copies(self, stage):
        p, values = self.place, self.values

        def copy(slot, source, target, device):
            return pltpu.make_async_remote_copy(
                src_ref=source,
                dst_ref=target,
                send_sem=self.send.at[slot],
                recv_sem=self.recv.at[slot],
                device_id=device,
                device_id_type=MESH,
            )

        if stage == 1:
            return [copy(0, values, self.from_core, p.at(c=1 - p.c))]
        if stage == 2:
            return [copy(1, values.at[:, 1 - p.x], self.from_x, p.at(x=1 - p.x))]
        if stage == 3:
            return [copy(2, values.at[:, p.x], self.from_y, p.at(y=1 - p.y))]
        return [
            copy(2 + k, values.at[p.far(k), p.x], self.from_z.at[k - 1], p.at(z=p.far(k)))
            for k in (1, 2, 3)
        ]

    def start(self, stage):
        for copy in self.copies(stage):
            copy.start()

    def advance(self, stage):
        p, values = self.place, self.values
        for copy in self.copies(stage):
            copy.wait()
        if stage == 1:
            values[...] += self.from_core[...]
        elif stage == 2:
            values[:, p.x] += self.from_x[...]
        elif stage == 3:
            values[:, p.x] += self.from_y[...]
        else:
            return values[p.z, p.x] + self.from_z[0] + self.from_z[1] + self.from_z[2]
        self.start(stage + 1)
        return None


class Copies:
    def __init__(self, send, recv):
        self.send, self.recv, self.count = send, recv, 0

    def __call__(self, source, target, device):
        slot = self.count
        self.count += 1
        copy = pltpu.make_async_remote_copy(
            src_ref=source,
            dst_ref=target,
            send_sem=self.send.at[slot],
            recv_sem=self.recv.at[slot],
            device_id=device,
            device_id_type=MESH,
        )
        copy.start()
        return copy


def spread_actions(plan, points):
    spread = [[] for _ in range(points)]
    for index, action in enumerate(plan):
        spread[min(points - 1, index * points // len(plan))].append(action)
    return spread


class Refs:
    pass


def call(kernel, name, inputs, outputs, scratch, aliases=(), collective=None, grid=None, limit=58):
    names = list(inputs) + list(outputs)
    flat = []
    for value in scratch.values():
        flat += value if isinstance(value, list) else [value]

    def body(*refs):
        held = Refs()
        rest = list(refs)
        for key in names:
            setattr(held, key, rest.pop(0))
        for key, value in scratch.items():
            if isinstance(value, list):
                setattr(held, key, [rest.pop(0) for _ in value])
            else:
                setattr(held, key, rest.pop(0))
        kernel(held)

    extra = {} if grid is None else {"grid": grid}
    result = pl.pallas_call(
        body,
        in_specs=[spec for _, spec in inputs.values()],
        out_specs=[spec for _, spec in outputs.values()],
        out_shape=[out for out, _ in outputs.values()],
        scratch_shapes=flat,
        input_output_aliases={
            list(inputs).index(one): list(outputs).index(other) for one, other in aliases
        },
        compiler_params=params(collective, limit),
        name=name,
        **extra,
    )(*[array for array, _ in inputs.values()])
    out = Refs()
    for key, value in zip(outputs, result, strict=True):
        setattr(out, key, value)
    return out


SPLIT = (4, 2, 2, 2, SHARE, LANES)
MOD_ROWS = 48
FIRST = (QKV, QKV + 1, QKV + 2)
SECOND = (OUT, UP, DOWN, UP + 1, DOWN + 1, UP + 2, DOWN + 2)
THIRD = (UP + 3, DOWN + 3)
EARLY = (DOWN, UP, DOWN + 1, UP + 1, DOWN + 2)
LATE = (UP + 2, DOWN + 3, UP + 3, OUT)


def enter_norm(refs):
    rows = 32
    for window in range(refs.mod.shape[0]):
        shift, scale = refs.mod[window, 0:1, :], refs.mod[window, 1:2, :]

        def step(index, window=window, shift=shift, scale=scale):
            at = pl.ds(pl.multiple_of(window * WIN + index * rows, rows), rows)
            normal, _ = centered(refs.tokens[at, :].astype(F32))
            refs.normed[at, :] = (normal * (1.0 + scale) + shift).astype(BF16)

        loop(WIN // rows, step)


def enter_unit(refs, j, held):
    fetch = pltpu.make_async_copy(held, refs.unit, refs.fetch)
    fetch.start()
    fetch.wait()

    def project(index):
        refs.packed[j, :, tile(index)] = dot(
            refs.normed[...], two_columns(refs.unit, index)
        ).astype(BF16)

    loop(4, project)


def enter_plain_kernel(refs):
    enter_norm(refs)
    for j in range(3):
        enter_unit(refs, j, refs.held.at[QKV + j])


def enter_kernel(refs):
    place = Place()
    place.greet()
    z, x, y, c = place.z, place.x, place.y, place.c

    own = []
    blocks = [(refs.qkv, j) for j in range(3)] + [(refs.out, 0)] + [(refs.up, j) for j in range(4)]
    for unit, (source, j) in enumerate(blocks):
        own.append((source.at[:, j * LANES : (j + 1) * LANES], refs.held.at[unit, z, x, y, c]))
    for j in range(4):
        for half in range(2):
            first = half * 512 + j * LANES
            own.append(
                (
                    refs.down.at[first : first + LANES],
                    refs.held.at[DOWN + j, z, x, y, c, half * HALF : (half + 1) * HALF],
                )
            )
    own = [
        pltpu.make_async_copy(source, target, refs.own_sem.at[index])
        for index, (source, target) in enumerate(own)
    ]
    for copy in own:
        copy.start()
    work = Gather(place, refs.held, FIRST, refs.gather)
    ticks = work.actions()
    small = Copies(*refs.small)
    copy = small(refs.mod_part, refs.from_core, place.at(c=1 - c))
    refs.table[z, x, c] = refs.table_own[c]
    for one in own:
        one.wait()
    ticks[0]()
    copy.wait()
    refs.mod_sum[...] = refs.mod_part[...] + refs.from_core[...]
    copy = small(refs.mod_sum, refs.from_y, place.at(y=1 - y))
    ticks[1]()
    copy.wait()
    refs.mods[z, x] = refs.mod_sum[...] + refs.from_y[...]
    copies = [
        small(refs.mods.at[z, x], refs.mods.at[z, x], place.at(x=1 - x)),
        small(refs.table.at[z, x, c], refs.table.at[z, x, c], place.at(x=1 - x)),
    ]
    for copy in copies:
        copy.wait()
    mods = [
        small(refs.mods.at[z], refs.mods.at[z], place.at(z=place.far(k))) for k in (1, 2, 3)
    ]
    tables = [
        small(refs.table.at[z, :, c], refs.table.at[z, :, c], place.at(z=place.far(k)))
        for k in (1, 2, 3)
    ]
    ticks[2]()
    for copy in mods:
        copy.wait()
    for window in range(refs.mod.shape[0]):
        for block in range(48):
            which, column = divmod(block, 8)
            part = refs.mods[block // 12, block // 6 % 2, block % 6 * 8 : block % 6 * 8 + 8, :]
            refs.mod[window, which : which + 1, column * LANES : (column + 1) * LANES] = jnp.sum(
                part * refs.member[window], axis=0, keepdims=True
            )
    enter_norm(refs)
    ticks[3]()
    for copy in tables:
        copy.wait()
    last = small(refs.table.at[:, :, c], refs.table.at[:, :, c], place.at(c=1 - c))
    for j in range(3):
        if j > 0:
            ticks[3 + j]()
        work.arrive(j, 4)
        enter_unit(refs, j, refs.held.at[QKV + j])
    last.wait()
    work.sent()


def attend_kernel(refs):
    work = None
    step = pl.program_id(0) * 2 + pl.program_id(1)
    if hasattr(refs, "gather"):
        place = Place()
        work = Gather(place, refs.held, SECOND, refs.gather)
        steps = spread_actions(work.actions(), 16)
        steps[0].insert(0, place.greet)
        for index, actions in enumerate(steps):
            if actions:

                @pl.when(step == index)
                def _(actions=actions):
                    for action in actions:
                        action()

    @pl.when(pl.program_id(1) == 0)
    def _():
        for head in range(2):
            spread = refs.table[head].astype(F32)
            for frame in range(FRAMES):
                block = spread[frame * WSIDE : (frame + 1) * WSIDE]
                for row in range(WSIDE):
                    first = (WSIDE - 1 - row) * WSIDE
                    refs.strip[
                        head, row * WSIDE : (row + 1) * WSIDE, frame * CELLS : (frame + 1) * CELLS
                    ] = block[:, first : first + CELLS]

    live = refs.live[pl.program_id(1)] * CELLS
    key_live = lax.broadcasted_iota(jnp.int32, (1, WIN), 1) < live
    for head in range(2):
        lanes = slice(head * HD, (head + 1) * HD)
        query = refs.query[:, lanes] * BF16(HD ** (-0.5))
        keys = refs.key[:, lanes]
        values = refs.value[:, lanes]
        for frame in range(WT):
            rows = slice(frame * CELLS, (frame + 1) * CELLS)
            first = (WT - 1 - frame) * CELLS
            scores = dot_rows(query[rows], keys) + refs.strip[head, :, first : first + WIN]
            scores = jnp.where(key_live, scores, NEGATIVE)
            shifted = jnp.exp(scores - jnp.max(scores, axis=-1, keepdims=True))
            totals = jnp.sum(shifted, axis=-1, keepdims=True)
            probs = (shifted * (1.0 / totals)).astype(BF16)
            refs.probs[head, rows] = probs
            refs.mixed[rows, lanes] = dot(probs, values).astype(BF16)

    if work is not None:

        @pl.when(step == 15)
        def _():
            for index in range(len(SECOND)):
                work.arrive(index, 4)
            work.sent()


def packed_block(part):
    pairs = H // 2
    return pl.BlockSpec(
        (None, WIN, LANES),
        lambda pair, window: (
            lax.rem(part * pairs + pair, 3),
            window,
            lax.div(part * pairs + pair, 3),
        ),
    )


def attend_back_kernel(refs):
    work = None
    step = pl.program_id(0) * 2 + pl.program_id(1)
    if hasattr(refs, "reduce"):
        place = Place()
        work = Reduce(place, refs.part, refs.total, LATE, refs.reduce)
        steps = spread_actions(work.actions(), 15)
        steps[0].insert(0, place.greet)
        for index, actions in enumerate(steps):
            if actions:

                @pl.when(step == index)
                def _(actions=actions):
                    for action in actions:
                        action()

    @pl.when(pl.program_id(1) == 0)
    def _():
        refs.strip[...] = jnp.zeros_like(refs.strip)

    for head in range(2):
        lanes = slice(head * HD, (head + 1) * HD)
        scale = BF16(HD ** (-0.5))
        query = refs.query[:, lanes] * scale
        keys = refs.key[:, lanes] * scale
        values = refs.value[:, lanes]
        grad = refs.grad[:, lanes]
        probs = refs.probs[head]
        refs.gv[:, lanes] = dot_tokens(grad, probs).T.astype(BF16)
        pieces = []
        for frame in range(WT):
            rows = slice(frame * CELLS, (frame + 1) * CELLS)
            first = (WT - 1 - frame) * CELLS
            grad_probs = dot_rows(grad[rows], values)
            weight = probs[rows].astype(F32)
            product = weight * grad_probs
            total = jnp.sum(product, axis=-1, keepdims=True)
            grad_scores = (product - weight * total).astype(BF16)
            refs.strip[head, :, first : first + WIN] += grad_scores.astype(F32)
            refs.gq[rows, lanes] = dot(grad_scores, keys).astype(BF16)
            pieces.append(grad_scores)
        refs.gk[:, lanes] = dot_tokens(query, jnp.concatenate(pieces, axis=0)).T.astype(BF16)

    @pl.when(pl.program_id(1) == pl.num_programs(1) - 1)
    def _():
        refs.table[...] = jnp.zeros_like(refs.table)
        for head in range(2):
            for frame in range(FRAMES):
                for row in range(WSIDE):
                    first = (WSIDE - 1 - row) * WSIDE
                    refs.table[
                        head, frame * WSIDE : (frame + 1) * WSIDE, first : first + CELLS
                    ] += refs.strip[
                        head, row * WSIDE : (row + 1) * WSIDE, frame * CELLS : (frame + 1) * CELLS
                    ]

    if work is not None:

        @pl.when(step == 15)
        def _():
            work.sent()


def middle_kernel(refs):
    order = [OUT] + [unit for j in range(4) for unit in (UP + j, DOWN + j)] + [OUT]
    gathering = reducing = None
    points = {}
    if hasattr(refs, "gather"):
        place = Place()
        place.greet()
        gathering = Gather(place, refs.held_out, THIRD, refs.gather)
        reducing = Reduce(place, refs.part, refs.total, EARLY, refs.reduce)
        for index, action in enumerate(gathering.actions()):
            points.setdefault((0, 1, 3, 5, 6)[index], []).append(action)
        ready = {DOWN: 4, UP: 5, DOWN + 1: 8, UP + 1: 9, DOWN + 2: 12}
        begun = -2
        for index, unit in enumerate(EARLY):
            begun = max(begun + 2, ready[unit])
            points.setdefault(begun, []).append(functools.partial(reducing.start, index, 1))
            for stage in (1, 2, 3, 4):
                points.setdefault(begun + 2 * stage - 1, []).append(
                    functools.partial(reducing.advance, index, stage)
                )

    held = refs.held_out if gathering is not None else refs.held
    count = [0]

    def pump():
        for action in points.pop(count[0], []):
            action()
        count[0] += 1

    def fetch(step):
        return pltpu.make_async_copy(
            held.at[order[step]], refs.unit.at[step % 4], refs.fetch.at[step % 4]
        )

    def start_fetch(step):
        if gathering is not None and order[step] in THIRD:
            gathering.arrive(THIRD.index(order[step]), 4)
        fetch(step).start()

    def put(slot, unit):
        return pltpu.make_async_copy(refs.made.at[slot], refs.part.at[unit], refs.made_sem.at[slot])

    for step in range(3):
        start_fetch(step)
    pump()
    refs.sums[...] = jnp.zeros_like(refs.sums)
    refs.mlp[...] = jnp.zeros_like(refs.mlp)
    refs.grad_normed[...] = jnp.zeros_like(refs.grad_normed)
    fetch(0).wait()

    def project(index):
        refs.attended[:, tile(index)] = dot(refs.mixed[...], two_columns(refs.unit.at[0], index))

    loop(4, project)
    pump()

    def modulate(window, at, mods, live):
        middle = refs.tokens[at, :].astype(F32) + mods[2] * refs.attended[at, :]
        normal, _ = centered(middle)
        refs.normed[at, :] = (normal * (1.0 + mods[4]) + mods[3]).astype(BF16)
        grad = jnp.where(live, refs.cotangent[at, :].astype(F32), 0.0)
        refs.grad_low[at, :] = (mods[5] * grad).astype(BF16)

    each_rows(refs.mod, refs.live, modulate)
    pump()
    for j in range(4):
        step = 1 + 2 * j
        up, down = refs.unit.at[step % 4], refs.unit.at[(step + 1) % 4]
        fetch(step).wait()
        fetch(step + 1).wait()
        start_fetch(step + 2)
        if j < 3:
            start_fetch(step + 3)

        def hide(index, up=up, down=down):
            hidden = dot(refs.normed[...], two_columns(up, index))
            bend = jnp.tanh(0.7978845608028654 * (hidden + 0.044715 * hidden * hidden * hidden))
            refs.activated[:, tile(index)] = (0.5 * hidden * (1.0 + bend)).astype(BF16)
            slope = 0.5 * (1.0 + bend) + 0.5 * hidden * (1.0 - bend * bend) * (
                0.7978845608028654 * (1.0 + 3.0 * 0.044715 * hidden * hidden)
            )
            grad_activated = dot_rows(refs.grad_low[...], some_rows(down, index))
            refs.grad_hidden[:, tile(index)] = (grad_activated * slope).astype(BF16)

        loop(4, hide)
        pump()

        def down_gradient(index):
            made = dot_tokens(refs.activated[:, tile(index)], refs.grad_low[...]).astype(BF16)
            for block in range(8):
                refs.made[0, block // 2, block % 2, index // 2, index % 2] = made[
                    :, block * LANES : (block + 1) * LANES
                ]

        loop(4, down_gradient)
        put(0, DOWN + j).start()
        put(0, DOWN + j).wait()
        pump()

        def up_gradient(index):
            made = dot_tokens(refs.normed[...], refs.grad_hidden[:, tile(index)]).astype(BF16)
            put_columns(refs.made.at[1], index, made)

        loop(4, up_gradient)
        put(1, UP + j).start()
        put(1, UP + j).wait()
        pump()

        def out_of_mlp(index, up=up, down=down):
            refs.mlp[:, tile(index)] += dot(refs.activated[...], two_columns(down, index))
            refs.grad_normed[:, tile(index)] += dot_rows(
                refs.grad_hidden[...], some_rows(up, index)
            )

        loop(4, out_of_mlp)
        pump()

    def join(window, at, mods, live):
        attended = refs.attended[at, :]
        middle = refs.tokens[at, :].astype(F32) + mods[2] * attended
        normal, root = centered(middle)
        mlp = refs.mlp[at, :]
        refs.output[at, :] = jnp.where(live, middle + mods[5] * mlp, 0.0).astype(BF16)
        grad_result = jnp.where(live, refs.cotangent[at, :].astype(F32), 0.0)
        grad_normed = refs.grad_normed[at, :]
        grad_middle = grad_result + norm_back(grad_normed, normal, root, mods[4])
        refs.grad_middle[at, :] = grad_middle
        refs.grad_low[at, :] = (mods[2] * grad_middle).astype(BF16)
        add_sums(refs.sums, window, 2, grad_middle * attended)
        add_sums(refs.sums, window, 3, grad_normed)
        add_sums(refs.sums, window, 4, grad_normed * normal)
        add_sums(refs.sums, window, 5, grad_result * mlp)

    each_rows(refs.mod, refs.live, join)
    pump()
    fetch(9).wait()

    def back(index):
        made = dot_tokens(refs.mixed[...], refs.grad_low[:, tile(index)]).astype(BF16)
        put_columns(refs.made.at[0], index, made)
        refs.grad_mixed[:, tile(index)] = dot_rows(
            refs.grad_low[...], some_rows(refs.unit.at[1], index)
        ).astype(BF16)

    loop(4, back)
    put(0, OUT).start()
    put(0, OUT).wait()
    while points:
        pump()
    if gathering is not None:
        gathering.sent()
        reducing.sent()


def leave_unit(refs, j, held, made):
    sources = (refs.gq, refs.gk, refs.gv)
    fetch = pltpu.make_async_copy(held, refs.unit, refs.fetch)
    fetch.start()
    for block in range(8):
        part, column = divmod(3 * block + j, 8)
        refs.packed[:, block * LANES : (block + 1) * LANES] = sources[part][
            :, column * LANES : (column + 1) * LANES
        ]

    def weight(index):
        grad = dot_tokens(refs.normed[...], refs.packed[:, tile(index)]).astype(BF16)
        put_columns(made, index, grad)

    loop(4, weight)
    fetch.wait()


def leave_back(refs):
    def back(index):
        refs.grad_normed[:, tile(index)] += dot_rows(refs.packed[...], some_rows(refs.unit, index))

    loop(4, back)


def leave_norm(refs):
    def join(window, at, mods, live):
        normal, root = centered(refs.tokens[at, :].astype(F32))
        grad_normed = refs.grad_normed[at, :]
        refs.grad_tokens[at, :] = refs.grad_middle[at, :] + norm_back(
            grad_normed, normal, root, mods[1]
        )
        add_sums(refs.sums, window, 0, grad_normed)
        add_sums(refs.sums, window, 1, grad_normed * normal)

    each_rows(refs.mod, refs.live, join)


def leave_plain_kernel(refs):
    refs.sums[...] = jnp.zeros_like(refs.sums)
    refs.grad_normed[...] = jnp.zeros_like(refs.grad_normed)
    for j in range(3):
        leave_unit(refs, j, refs.held.at[QKV + j], refs.made)
        put = pltpu.make_async_copy(refs.made, refs.part.at[j], refs.made_sem)
        put.start()
        leave_back(refs)
        put.wait()
    leave_norm(refs)


def leave_kernel(refs):
    place = Place()
    place.greet()
    z, x, y, c = place.z, place.x, place.y, place.c
    work = Reduce(place, refs.made, refs.total, (0, 1, 2), refs.reduce)
    refs.table[...] = refs.table_part[...]
    table = Small(place, refs.table, refs.table_small)
    clip = Small(place, refs.clip, refs.clip_small)
    table.start(1)
    refs.sums[...] = refs.late_sums[...]
    refs.grad_normed[...] = jnp.zeros_like(refs.grad_normed)
    leave_unit(refs, 0, refs.held.at[QKV], refs.made.at[0])
    work.start(0, 1)
    table.advance(1)
    leave_back(refs)
    work.advance(0, 1)
    leave_unit(refs, 1, refs.held.at[QKV + 1], refs.made.at[1])
    work.start(1, 1)
    table.advance(2)
    leave_back(refs)
    work.advance(1, 1)
    work.advance(0, 2)
    leave_unit(refs, 2, refs.held.at[QKV + 2], refs.made.at[2])
    work.start(2, 1)
    table.advance(3)
    leave_back(refs)
    work.advance(2, 1)
    work.advance(1, 2)
    work.advance(0, 3)
    leave_norm(refs)
    for block in range(48):
        which, column = divmod(block, 8)
        part = jnp.zeros((8, LANES), F32)
        for window in range(refs.mod.shape[0]):
            sums = refs.sums[window, which : which + 1, column * LANES : (column + 1) * LANES]
            part = part + refs.member[window] * sums
        refs.clip[block // 12, block // 6 % 2, block % 6 * 8 : block % 6 * 8 + 8, :] = part
    clip.start(1)
    work.advance(2, 2)
    work.advance(1, 3)
    clip.advance(1)
    work.advance(0, 4)
    refs.table_total[...] = table.advance(4)
    clip.advance(2)
    clip.advance(3)
    work.advance(2, 3)
    work.advance(1, 4)
    total = clip.advance(4)
    refs.clip_total[...] = total
    low = total.astype(BF16)
    cond = jnp.zeros((8, SHARE), F32)
    for block in range(6):
        cond = cond + dot_rows(
            low[block * 8 : block * 8 + 8], refs.ada[:, block * LANES : (block + 1) * LANES]
        )
    small = Copies(*refs.cond_small)
    refs.cond[y, c] = cond
    small(refs.cond.at[y, c], refs.cond.at[y, c], place.at(c=1 - c)).wait()
    small(refs.cond.at[y], refs.cond.at[y], place.at(y=1 - y)).wait()
    small(refs.cond, refs.cond_x, place.at(x=1 - x)).wait()
    refs.cond_z[z] = refs.cond[...] + refs.cond_x[...]
    copies = [
        small(refs.cond_z.at[z], refs.cond_z.at[z], place.at(z=place.far(k))) for k in (1, 2, 3)
    ]
    work.advance(2, 4)
    for copy in copies:
        copy.wait()
    refs.cond_total[...] = refs.cond_z[0] + refs.cond_z[1] + refs.cond_z[2] + refs.cond_z[3]
    work.sent()


def enter(special, tokens, held, mod, own, mod_part, member, table):
    rows = tokens.shape[0]
    inputs = {"tokens": (tokens, vmem())}
    outputs = {
        "normed": (shape(BF16, rows, D), vmem()),
        "packed": (shape(BF16, 3, rows, D), vmem()),
    }
    scratch = {"unit": pltpu.VMEM(SPLIT, BF16), "fetch": pltpu.SemaphoreType.DMA}
    if not special:
        inputs |= {"held": (held, anywhere()), "mod": (mod, vmem())}
        out = call(enter_plain_kernel, "enter_plain", inputs, outputs, scratch)
        out.mod, out.held = mod, held
        return out
    for name, block in zip(("qkv", "out", "up", "down"), own, strict=True):
        inputs[name] = (block, anywhere())
    inputs |= {
        "mod_part": (mod_part, vmem()),
        "member": (member, vmem()),
        "table_own": (table, vmem()),
    }
    outputs |= {
        "held": (shape(BF16, UNITS, *SPLIT), anywhere()),
        "mod": (shape(F32, member.shape[0], 8, D), vmem()),
        "table": (shape(BF16, 4, 2, *table.shape), vmem()),
    }
    rows_small = mod_part.shape[0]
    scratch |= {
        "own_sem": pltpu.SemaphoreType.DMA((16,)),
        "gather": Gather.scratch(len(FIRST)),
        "small": [pltpu.SemaphoreType.DMA((16,))] * 2,
        "from_core": pltpu.VMEM((rows_small, LANES), F32),
        "from_y": pltpu.VMEM((rows_small, LANES), F32),
        "mod_sum": pltpu.VMEM((rows_small, LANES), F32),
        "mods": pltpu.VMEM((4, 2, rows_small, LANES), F32),
    }
    return call(enter_kernel, "enter", inputs, outputs, scratch, collective=0)


def attend(special, packed, table, live_frames, held):
    window_count = live_frames.shape[0]
    rows = window_count * WIN
    inputs = {
        "live": (live_frames, smem()),
        "query": (packed, packed_block(0)),
        "key": (packed, packed_block(1)),
        "value": (packed, packed_block(2)),
        "table": (table, pl.BlockSpec((2, SPREAD, LANES), lambda p, w: (p, 0, 0))),
    }
    outputs = {
        "mixed": (shape(BF16, rows, D), pl.BlockSpec((WIN, LANES), lambda p, w: (w, p))),
        "probs": (
            shape(BF16, window_count, H, WIN, WIN),
            pl.BlockSpec((None, 2, WIN, WIN), lambda p, w: (w, p, 0, 0)),
        ),
    }
    scratch = {"strip": pltpu.VMEM((2, CELLS, STRIP), F32)}
    aliases, collective = (), None
    if special:
        inputs["held_in"] = (held, anywhere())
        outputs["held"] = (shape(BF16, UNITS, *SPLIT), anywhere())
        scratch["gather"] = Gather.scratch(len(SECOND))
        aliases, collective = (("held_in", "held"),), 1
    out = call(
        attend_kernel,
        "attend",
        inputs,
        outputs,
        scratch,
        aliases,
        collective,
        grid=(H // 2, window_count),
        limit=32,
    )
    if not special:
        out.held = held
    return out


def middle(special, live_frames, tokens, cotangent, mixed, mod, held):
    rows = tokens.shape[0]
    inputs = {
        "live": (live_frames, smem()),
        "tokens": (tokens, vmem()),
        "cotangent": (cotangent, vmem()),
        "mixed": (mixed, vmem()),
        "mod": (mod, vmem()),
        "held": (held, anywhere()),
    }
    outputs = {
        "output": (shape(BF16, rows, D), vmem()),
        "grad_middle": (shape(F32, rows, D), vmem()),
        "grad_mixed": (shape(BF16, rows, D), vmem()),
        "sums": (shape(F32, mod.shape[0], 8, D), vmem()),
        "part": (shape(BF16, UNITS, *SPLIT), anywhere()),
    }
    scratch = {
        "unit": pltpu.VMEM((4, *SPLIT), BF16),
        "attended": pltpu.VMEM((rows, D), F32),
        "normed": pltpu.VMEM((rows, D), BF16),
        "grad_low": pltpu.VMEM((rows, D), BF16),
        "mlp": pltpu.VMEM((rows, D), F32),
        "grad_normed": pltpu.VMEM((rows, D), F32),
        "activated": pltpu.VMEM((rows, D), BF16),
        "grad_hidden": pltpu.VMEM((rows, D), BF16),
        "made": pltpu.VMEM((2, *SPLIT), BF16),
        "fetch": pltpu.SemaphoreType.DMA((4,)),
        "made_sem": pltpu.SemaphoreType.DMA((2,)),
    }
    aliases, collective = (), None
    if special:
        outputs["held_out"] = (shape(BF16, UNITS, *SPLIT), anywhere())
        outputs["total"] = (shape(F32, len(EARLY), SHARE, LANES), vmem())
        scratch["gather"] = Gather.scratch(len(THIRD))
        scratch["reduce"] = Reduce.scratch(len(EARLY))
        aliases, collective = (("held", "held_out"),), 2
    return call(middle_kernel, "middle", inputs, outputs, scratch, aliases, collective, limit=60)


def attend_back(special, packed, probs, grad_mixed, part):
    window_count = probs.shape[0]
    rows = window_count * WIN

    def block():
        return pl.BlockSpec((WIN, LANES), lambda p, w: (w, p))

    inputs = {
        "query": (packed, packed_block(0)),
        "key": (packed, packed_block(1)),
        "value": (packed, packed_block(2)),
        "probs": (probs, pl.BlockSpec((None, 2, WIN, WIN), lambda p, w: (w, p, 0, 0))),
        "grad": (grad_mixed, block()),
    }
    outputs = {name: (shape(BF16, rows, D), block()) for name in ("gq", "gk", "gv")}
    outputs["table"] = (
        shape(F32, H, SPREAD, LANES),
        pl.BlockSpec((2, SPREAD, LANES), lambda p, w: (p, 0, 0)),
    )
    scratch = {"strip": pltpu.VMEM((2, CELLS, STRIP), F32)}
    collective = None
    if special:
        inputs["part"] = (part, anywhere())
        outputs["total"] = (
            shape(F32, len(LATE), SHARE, LANES),
            pl.BlockSpec((len(LATE), SHARE, LANES), lambda p, w: (0, 0, 0)),
        )
        scratch["reduce"] = Reduce.scratch(len(LATE))
        collective = 3
    return call(
        attend_back_kernel,
        "attend_back",
        inputs,
        outputs,
        scratch,
        collective=collective,
        grid=(H // 2, window_count),
        limit=40,
    )


def leave(special, live_frames, tokens, mod, normed, grad_middle, back, held, late_sums, ada, member):
    rows = tokens.shape[0]
    inputs = {
        "live": (live_frames, smem()),
        "tokens": (tokens, vmem()),
        "mod": (mod, vmem()),
        "normed": (normed, vmem()),
        "grad_middle": (grad_middle, vmem()),
        "gq": (back.gq, vmem()),
        "gk": (back.gk, vmem()),
        "gv": (back.gv, vmem()),
        "held": (held, anywhere()),
    }
    outputs = {"grad_tokens": (shape(F32, rows, D), vmem())}
    scratch = {
        "unit": pltpu.VMEM(SPLIT, BF16),
        "packed": pltpu.VMEM((rows, D), BF16),
        "grad_normed": pltpu.VMEM((rows, D), F32),
        "fetch": pltpu.SemaphoreType.DMA,
    }
    if not special:
        outputs["sums"] = (shape(F32, mod.shape[0], 8, D), vmem())
        outputs["part"] = (shape(BF16, 3, *SPLIT), anywhere())
        scratch["made"] = pltpu.VMEM(SPLIT, BF16)
        scratch["made_sem"] = pltpu.SemaphoreType.DMA
        return call(leave_plain_kernel, "leave_plain", inputs, outputs, scratch)
    inputs |= {
        "late_sums": (late_sums, vmem()),
        "table_part": (back.table.reshape(4, 2, 2 * SPREAD, LANES), vmem()),
        "ada": (ada, vmem()),
        "member": (member, vmem()),
    }
    outputs |= {
        "total": (shape(F32, 3, SHARE, LANES), vmem()),
        "clip_total": (shape(F32, MOD_ROWS, LANES), vmem()),
        "table_total": (shape(F32, 2 * SPREAD, LANES), vmem()),
        "cond_total": (shape(F32, 2, 2, 8, SHARE), vmem()),
    }
    scratch |= {
        "made": pltpu.VMEM((3, *SPLIT), BF16),
        "sums": pltpu.VMEM((mod.shape[0], 8, D), F32),
        "reduce": Reduce.scratch(3),
        "table": pltpu.VMEM((4, 2, 2 * SPREAD, LANES), F32),
        "table_small": Small.scratch(2 * SPREAD),
        "clip": pltpu.VMEM((4, 2, MOD_ROWS, LANES), F32),
        "clip_small": Small.scratch(MOD_ROWS),
        "cond": pltpu.VMEM((2, 2, 8, SHARE), F32),
        "cond_x": pltpu.VMEM((2, 2, 8, SHARE), F32),
        "cond_z": pltpu.VMEM((4, 2, 2, 8, SHARE), F32),
        "cond_small": [pltpu.SemaphoreType.DMA((8,))] * 2,
    }
    return call(leave_kernel, "leave", inputs, outputs, scratch, collective=4)


def per_device(
    special,
    tokens,
    condition,
    clip_frames,
    ada_weight,
    ada_bias,
    qkv_weight,
    out_weight,
    up_weight,
    down_weight,
    rel_table,
    cotangent,
):
    window_count = tokens.shape[0]
    clip_count = condition.shape[0]
    rows_ada, cols_ada = ada_weight.shape
    row_block = lax.axis_index("fsdp")
    col_block = lax.axis_index("dp")
    first_window = lax.axis_index(("dp", "fsdp")) * window_count
    live_frames, member_int = window_layout(clip_frames, first_window, window_count)
    member = member_int.astype(F32)
    activity_low = jax.nn.silu(condition).astype(BF16)
    act_rows = lax.dynamic_slice_in_dim(activity_low, row_block * rows_ada, rows_ada, 1)

    mod_part = jnp.dot(act_rows, ada_weight, preferred_element_type=F32)
    mod_part = mod_part + jnp.where(row_block == 0, ada_bias.astype(F32), 0.0)[None, :]
    token_rows = tokens.reshape(window_count * WIN, D)
    cotangent_rows = cotangent.reshape(window_count * WIN, D)
    own = (qkv_weight, out_weight, up_weight, down_weight)
    if special:
        clips = jnp.pad(mod_part, ((0, 8 - clip_count), (0, 0)))
        clips = clips.reshape(8, 6, LANES).transpose(1, 0, 2).reshape(MOD_ROWS, LANES)
        member_wide = jnp.pad(member, ((0, 0), (0, 8 - clip_count)))[:, :, None]
        member_wide = jnp.broadcast_to(member_wide, (window_count, 8, LANES))
        start = enter(
            True, token_rows, None, None, own, clips, member_wide, spread_table(rel_table)
        )
        table = start.table.reshape(H, SPREAD, LANES)
    else:
        member_wide = None
        clip_mod = lax.all_gather(lax.psum(mod_part, "fsdp"), "dp", axis=1, tiled=True)
        window_mod = jnp.sum(member[:, :, None] * clip_mod[None], axis=1)
        window_mod = jnp.pad(window_mod.reshape(window_count, 6, D), ((0, 0), (0, 2), (0, 0)))
        whole = [
            lax.all_gather(
                lax.all_gather(weight, "dp", axis=1, tiled=True), "fsdp", axis=0, tiled=True
            )
            for weight in own
        ]
        held = units_of(*whole).reshape(UNITS, *SPLIT)
        start = enter(False, token_rows, held, window_mod, None, None, None, None)
        table = spread_table(lax.all_gather(rel_table, "dp", axis=0, tiled=True))
    mod = start.mod
    across = attend(special, start.packed, table, live_frames, start.held)
    mid = middle(
        special, live_frames, token_rows, cotangent_rows, across.mixed, mod, across.held
    )
    back = attend_back(special, start.packed, across.probs, mid.grad_mixed, mid.part)
    held = mid.held_out if special else across.held
    end = leave(
        special,
        live_frames,
        token_rows,
        mod,
        start.normed,
        mid.grad_middle,
        back,
        held,
        mid.sums,
        ada_weight,
        member_wide,
    )
    if special:
        shares = [None] * UNITS
        for units, totals in ((EARLY, mid.total), (LATE, back.total), (FIRST, end.total)):
            for index, unit in enumerate(units):
                shares[unit] = totals[index]
        grads = own_blocks(jnp.stack(shares))
        clip_cols = end.clip_total.reshape(6, 8, LANES).transpose(1, 0, 2).reshape(8, cols_ada)
        clip_cols = clip_cols[:clip_count].astype(BF16)
        cond_total = end.cond_total.transpose(2, 0, 1, 3).reshape(8, D)[:clip_count]
        table_grad = gather_table(end.table_total.reshape(2, SPREAD, LANES))
    else:
        part = jnp.concatenate([end.part, mid.part[OUT:]])
        grads = [
            lax.psum_scatter(
                lax.psum_scatter(grad, "fsdp", scatter_dimension=0, tiled=True),
                "dp",
                scatter_dimension=1,
                tiled=True,
            ).astype(F32)
            for grad in weights_of(part.reshape(UNITS, 8, D, LANES))
        ]
        grad_mod = (mid.sums + end.sums)[:, :6].reshape(window_count, 6 * D)
        clip_part = lax.dot_general(
            member,
            grad_mod,
            (((0,), (0,)), ((), ())),
            precision=HIGHEST,
            preferred_element_type=F32,
        )
        clip_sum, table_sum = lax.psum((clip_part, gather_table(back.table)), ("dp", "fsdp"))
        clip_cols = lax.dynamic_slice_in_dim(
            clip_sum.astype(BF16), col_block * cols_ada, cols_ada, 1
        )
        heads_own = rel_table.shape[0]
        table_grad = lax.dynamic_slice_in_dim(table_sum, col_block * heads_own, heads_own, 0)
        cond_part = lax.dot_general(
            clip_cols, ada_weight, (((1,), (1,)), ((), ())), preferred_element_type=F32
        )
        cond_total = lax.all_gather(lax.psum(cond_part, "dp"), "fsdp", axis=1, tiled=True)
    grad_ada_weight = lax.dot_general(
        act_rows, clip_cols, (((0,), (0,)), ((), ())), preferred_element_type=F32
    )
    grad_ada_bias = jnp.sum(clip_cols.astype(F32), axis=0)
    _, silu_back = jax.vjp(jax.nn.silu, condition)
    return (
        mid.output.reshape(tokens.shape),
        end.grad_tokens.reshape(tokens.shape),
        silu_back(cond_total)[0],
        grad_ada_weight,
        grad_ada_bias,
        *grads,
        table_grad,
    )


def solution(mesh):
    special = dict(mesh.shape) == {"dp": 8, "fsdp": 4}
    both = P(("dp", "fsdp"), None, None)
    weight = P("fsdp", "dp")
    in_specs = (both, P(), P(), weight, P("dp")) + (weight,) * 4 + (P("dp", None), both)
    out_specs = (both, both, P(), weight, P("dp")) + (weight,) * 4 + (P("dp", None),)
    return jax.shard_map(
        functools.partial(per_device, special),
        mesh=mesh,
        in_specs=in_specs,
        out_specs=out_specs,
        check_vma=False,
    )
```

```python
import functools

import jax
import jax.numpy as jnp
from jax import lax
from jax.experimental import pallas as pl
from jax.experimental.pallas import tpu as pltpu
from jax.sharding import PartitionSpec as P

D = 1024
H = 16
HD = 64
WT = 5
WSIDE = 8
WIN = 320
SPW = 16
CELLS = WSIDE * WSIDE
FRAMES = 2 * WT - 1
OFFSETS = (2 * WSIDE - 1) ** 2
REL = FRAMES * OFFSETS
LANES = 128
TILE = 256
SPREAD = 80
STRIP = 640

EPSILON = 1e-06
NEGATIVE = -1000000000.0
HIGHEST = lax.Precision.HIGHEST
F32 = jnp.float32
BF16 = jnp.bfloat16
MESH = pl.DeviceIdType.MESH
MIB = 2**20

QKV, OUT, UP, DOWN, UNITS = 0, 3, 4, 8, 12
SHARE = 256
HALF = 128


def window_layout(clip_frames, first_window, window_count):
    slab_count = 1 + (clip_frames > WT).astype(jnp.int32)
    starts = jnp.cumsum(slab_count, dtype=jnp.int32) - slab_count
    global_window = first_window + jnp.arange(window_count, dtype=jnp.int32)
    slab_of = global_window // SPW
    owners = jnp.sum((starts[None, :] <= slab_of[:, None]).astype(jnp.int32), axis=1) - 1
    clip_ids = jnp.arange(clip_frames.shape[0], dtype=jnp.int32)
    member = (owners[:, None] == clip_ids[None, :]).astype(jnp.int32)
    clip_start = jnp.sum(member * starts[None, :], axis=1)
    own_frames = jnp.sum(member * clip_frames[None, :], axis=1)
    inner_slab = slab_of - clip_start
    return (jnp.minimum(own_frames - WT * inner_slab, WT), member)


def offset_spread():
    side_span = 2 * WSIDE - 1
    shape = (OFFSETS, WSIDE * LANES)
    offset = lax.broadcasted_iota(jnp.int32, shape, 0)
    place = lax.broadcasted_iota(jnp.int32, shape, 1)
    own, row, other = place // LANES, place // WSIDE % (LANES // WSIDE), place % WSIDE
    row_diff, col_diff = side_span - 1 - row, own - other + (WSIDE - 1)
    return ((row < side_span) & (row_diff * side_span + col_diff == offset)).astype(BF16)


def spread_table(table):
    heads = table.shape[0]
    by_frame = table.reshape(heads, FRAMES, OFFSETS)[:, ::-1].reshape(heads * FRAMES, OFFSETS)
    spread = jnp.dot(by_frame, offset_spread(), preferred_element_type=F32).astype(BF16)
    spread = spread.reshape(heads, FRAMES * WSIDE, LANES)
    return jnp.pad(spread, ((0, 0), (0, SPREAD - FRAMES * WSIDE), (0, 0)))


def gather_table(spread):
    heads = spread.shape[0]
    by_frame = spread[:, : FRAMES * WSIDE].reshape(heads * FRAMES, WSIDE * LANES)
    sums = lax.dot_general(
        by_frame,
        offset_spread().astype(F32),
        (((1,), (1,)), ((), ())),
        precision=HIGHEST,
        preferred_element_type=F32,
    )
    return sums.reshape(heads, FRAMES, OFFSETS)[:, ::-1].reshape(heads, FRAMES * OFFSETS)


def units_of(qkv, out, up, down):
    return jnp.concatenate(
        [
            qkv.reshape(D, 8, 3, LANES).transpose(2, 1, 0, 3),
            out.reshape(D, 8, 1, LANES).transpose(2, 1, 0, 3),
            up.reshape(D, 8, 4, LANES).transpose(2, 1, 0, 3),
            down.reshape(8, 4, LANES, 8, LANES).transpose(1, 3, 0, 2, 4).reshape(4, 8, D, LANES),
        ]
    )


def weights_of(units):
    def columns(part):
        return part.transpose(2, 1, 0, 3).reshape(D, -1)

    down = units[DOWN:].reshape(4, 8, 8, LANES, LANES).transpose(2, 0, 3, 1, 4)
    return (
        columns(units[QKV:OUT]),
        columns(units[OUT:UP]),
        columns(units[UP:DOWN]),
        down.reshape(4 * D, D),
    )


def own_blocks(shares):
    def columns(part):
        return part.transpose(1, 0, 2).reshape(SHARE, -1)

    down = shares[DOWN:].reshape(4, 2, LANES, LANES).transpose(1, 0, 2, 3).reshape(4 * SHARE, LANES)
    return (columns(shares[QKV:OUT]), columns(shares[OUT:UP]), columns(shares[UP:DOWN]), down)


def dot(left, right):
    return jnp.dot(left, right, preferred_element_type=F32)


def dot_rows(left, right):
    return lax.dot_general(left, right, (((1,), (1,)), ((), ())), preferred_element_type=F32)


def dot_tokens(left, right):
    return lax.dot_general(left, right, (((0,), (0,)), ((), ())), preferred_element_type=F32)


def half(index):
    return pl.ds(pl.multiple_of(index * 512, 512), 512)


def four_columns(unit, index):
    blocks = [unit[2 * index + x // 2, x % 2].reshape(D, LANES) for x in range(4)]
    return jnp.concatenate(blocks, axis=1)


def half_rows(unit, index):
    blocks = [unit[block // 2, block % 2, index].reshape(512, LANES) for block in range(8)]
    return jnp.concatenate(blocks, axis=1)


def put_columns(unit, index, values):
    for x in range(4):
        unit[2 * index + x // 2, x % 2] = values[:, x * LANES : (x + 1) * LANES].reshape(2, 2, SHARE, LANES)


def loop(count, body):
    def step(index, carry):
        body(index)
        return carry

    lax.fori_loop(0, count, step, 0)


def vmem():
    return pl.BlockSpec(memory_space=pltpu.VMEM)


def anywhere():
    return pl.BlockSpec(memory_space=pl.ANY)


def smem():
    return pl.BlockSpec(memory_space=pltpu.SMEM)


def shape(dtype, *sizes):
    return jax.ShapeDtypeStruct(sizes, dtype)


def params(collective=None, limit=58):
    if collective is None:
        return pltpu.CompilerParams(vmem_limit_bytes=limit * MIB)
    return pltpu.CompilerParams(
        vmem_limit_bytes=limit * MIB, collective_id=collective, has_side_effects=True
    )


def centered(values):
    center = values - jnp.mean(values, axis=-1, keepdims=True)
    spread = jnp.mean(center * center, axis=-1, keepdims=True)
    root = lax.rsqrt(spread + EPSILON)
    return center * root, root


def norm_back(grad_normed, normal, root, scale):
    grad = grad_normed * (1.0 + scale)
    mean = jnp.mean(grad, axis=-1, keepdims=True)
    along = jnp.mean(grad * normal, axis=-1, keepdims=True)
    return root * (grad - mean - normal * along)


def each_rows(mod_ref, live_ref, body, rows=32):
    for window in range(mod_ref.shape[0]):
        live = live_ref[window] * CELLS

        def step(index, window=window, live=live):
            at = pl.ds(pl.multiple_of(window * WIN + index * rows, rows), rows)
            mods = [mod_ref[window, k : k + 1, :] for k in range(6)]
            slot = index * rows + lax.broadcasted_iota(jnp.int32, (rows, 1), 0)
            body(window, at, mods, slot < live)

        loop(WIN // rows, step)


def add_sums(sums_ref, window, which, values):
    sums_ref[window, which : which + 1, :] += jnp.sum(values, axis=0, keepdims=True)


class Place:
    def __init__(self):
        column, row = lax.axis_index("dp"), lax.axis_index("fsdp")
        self.z, self.x, self.y, self.c = column // 2, column % 2, row // 2, row % 2

    def at(self, z=None, x=None, y=None, c=None):
        z = self.z if z is None else z
        x = self.x if x is None else x
        y = self.y if y is None else y
        c = self.c if c is None else c
        return (z * 2 + x, y * 2 + c)

    def far(self, k):
        return lax.rem(self.z + k, 4)

    def greet(self):
        peers = [self.at(z=self.far(k)) for k in (1, 2, 3)]
        peers += [self.at(x=1 - self.x), self.at(y=1 - self.y), self.at(c=1 - self.c)]
        barrier = pltpu.get_barrier_semaphore()
        for peer in peers:
            pl.semaphore_signal(barrier, inc=1, device_id=peer, device_id_type=MESH)
        pl.semaphore_wait(barrier, len(peers))


class Moves:
    def __init__(self, place, stages, scratch):
        self.place = place
        self.send, self.recv = scratch
        self.first, count = {}, 0
        for unit, stage in stages:
            self.first[unit, stage] = count
            count += self.counts[unit in SIDEWAYS][stage - 1]
        self.flying = []

    @classmethod
    def semaphores(cls, stages):
        count = sum(cls.counts[unit in SIDEWAYS][stage - 1] for unit, stage in stages)
        return [pltpu.SemaphoreType.DMA((count,))] * 2

    def made(self, unit, stage, moves):
        copies = []
        for index, (source, target, device) in enumerate(moves):
            slot = self.first[unit, stage] + index
            copies.append(
                pltpu.make_async_remote_copy(
                    src_ref=source,
                    dst_ref=target,
                    send_sem=self.send.at[slot],
                    recv_sem=self.recv.at[slot],
                    device_id=device,
                    device_id_type=MESH,
                )
            )
        return copies

    def begin(self, unit, stage):
        for copy in self.copies(unit, stage):
            copy.start()
        self.flying.append((unit, stage))

    def arrive(self, unit, stage):
        if (unit, stage) in self.flying:
            self.flying.remove((unit, stage))
            for copy in self.copies(unit, stage):
                copy.wait_recv()

    def sent(self):
        for unit, stage in self.first:
            for copy in self.copies(unit, stage):
                copy.wait_send()


class Gather(Moves):
    counts = ((3, 2, 2, 1), (2, 6, 2, 1))

    def __init__(self, place, held, stages, scratch):
        super().__init__(place, stages, scratch)
        self.held = held

    def copies(self, unit, stage):
        p, held = self.place, self.held.at[unit]
        at_x, at_y, at_core = p.at(x=1 - p.x), p.at(y=1 - p.y), p.at(c=1 - p.c)
        own = held.at[p.z, p.x, p.y, p.c]
        if stage == 4:
            refs = [(held.at[:, :, :, p.c], at_core)]
        elif stage == 3:
            refs = [
                (held.at[:, :, p.y, p.c, :HALF], at_y),
                (held.at[:, p.x, :, p.c, HALF:], at_x),
            ]
        elif unit in SIDEWAYS and stage == 1:
            refs = [(own.at[:HALF], at_x), (own.at[HALF:], at_y)]
        elif unit in SIDEWAYS:
            refs = []
            for k in (1, 2, 3):
                refs.append((held.at[p.z, :, p.y, p.c, :HALF], p.at(z=p.far(k))))
                refs.append((held.at[p.z, p.x, :, p.c, HALF:], p.at(z=p.far(k))))
        elif stage == 1:
            refs = [(own, p.at(z=p.far(k))) for k in (1, 2, 3)]
        else:
            refs = [
                (held.at[:, p.x, p.y, p.c, :HALF], at_x),
                (held.at[:, p.x, p.y, p.c, HALF:], at_y),
            ]
        return self.made(unit, stage, [(ref, ref, device) for ref, device in refs])

    def advance(self, unit, stage):
        self.arrive(unit, stage - 1)
        self.begin(unit, stage)

    def finish(self):
        for unit, stage in list(self.flying):
            self.arrive(unit, stage)
        self.sent()


class Reduce(Moves):
    counts = ((1, 2, 2, 3), (1, 2, 6, 2))

    def __init__(self, place, part, total, units, scratch):
        stages = [(unit, stage) for unit in units for stage in (1, 2, 3, 4)]
        super().__init__(place, stages, scratch[6:])
        self.part, self.total, self.units = part, total, units
        self.own, self.core, self.side, self.corner, self.distant, self.load = scratch[:6]

    @classmethod
    def scratch(cls, units):
        count = len(units)
        return [
            pltpu.VMEM((OWN_SLOTS, 4, 2, 2, SHARE, LANES), BF16),
            pltpu.VMEM((count, 4, 2, 2, SHARE, LANES), BF16),
            pltpu.VMEM((count, 2, 4, 2, HALF, LANES), BF16),
            pltpu.VMEM((count, 2, 4, HALF, LANES), BF16),
            pltpu.VMEM((count, 3, 2, 2, HALF, LANES), BF16),
            pltpu.SemaphoreType.DMA((OWN_SLOTS,)),
        ] + cls.semaphores([(unit, stage) for unit in units for stage in (1, 2, 3, 4)])

    def own_copy(self, unit):
        slot = self.units.index(unit) % OWN_SLOTS
        return pltpu.make_async_copy(
            self.part(unit).at[:, :, :, self.place.c], self.own.at[slot], self.load.at[slot]
        )

    def copies(self, unit, stage):
        p, index = self.place, self.units.index(unit)
        at_x, at_y, at_core = p.at(x=1 - p.x), p.at(y=1 - p.y), p.at(c=1 - p.c)
        core, side, corner = self.core.at[index], self.side.at[index], self.corner.at[index]
        distant = self.distant.at[index]
        if stage == 1:
            moves = [(self.part(unit).at[:, :, :, 1 - p.c], core, at_core)]
        elif stage == 2:
            moves = [
                (core.at[:, :, 1 - p.y, :HALF], side.at[0], at_y),
                (core.at[:, 1 - p.x, :, HALF:], side.at[1], at_x),
            ]
        elif unit in SIDEWAYS and stage == 3:
            moves = []
            for k in (1, 2, 3):
                for half in range(2):
                    source = side.at[half, p.far(k)]
                    moves.append((source, distant.at[k - 1, half], p.at(z=p.far(k))))
        elif unit in SIDEWAYS:
            moves = [
                (corner.at[0, 1 - p.x], corner.at[0, 2], at_x),
                (corner.at[1, 1 - p.y], corner.at[1, 2], at_y),
            ]
        elif stage == 3:
            moves = [
                (side.at[0, :, 1 - p.x], corner.at[0], at_x),
                (side.at[1, :, 1 - p.y], corner.at[1], at_y),
            ]
        else:
            moves = [
                (corner.at[:, p.far(k)], distant.at[k - 1, 0], p.at(z=p.far(k)))
                for k in (1, 2, 3)
            ]
        return self.made(unit, stage, moves)

    def begin(self, unit, stage):
        super().begin(unit, stage)
        if stage == 1:
            self.own_copy(unit).start()

    def combine(self, unit, stage):
        p, index = self.place, self.units.index(unit)
        core, side, corner = self.core.at[index], self.side.at[index], self.corner.at[index]
        distant = self.distant.at[index]

        def plus(left, right):
            return (left.astype(F32) + right.astype(F32)).astype(BF16)

        def from_core(step):
            z, x, y = step // 4, step // 2 % 2, step % 2
            core[z, x, y] = plus(core[z, x, y], self.own[index % OWN_SLOTS, z, x, y])

        def from_side(step):
            z, b = step // 2, step % 2
            side[0, z, b] = plus(side[0, z, b], core[z, b, p.y, :HALF])
            side[1, z, b] = plus(side[1, z, b], core[z, p.x, b, HALF:])

        def from_corner(z):
            corner[0, z] = plus(corner[0, z], side[0, z, p.x])
            corner[1, z] = plus(corner[1, z], side[1, z, p.y])

        def from_far(half):
            total = corner[half, p.z].astype(F32)
            for k in range(3):
                total = total + distant[k, 0, half].astype(F32)
            self.total[index, pl.ds(pl.multiple_of(half * HALF, HALF), HALF), :] = total

        def sideways_far(half):
            for b in range(2):
                total = side[half, p.z, b].astype(F32)
                for k in range(3):
                    total = total + distant[k, half, b].astype(F32)
                corner[half, b] = total.astype(BF16)

        def sideways_last():
            self.total[index, :HALF, :] = corner[0, p.x].astype(F32) + corner[0, 2].astype(F32)
            self.total[index, HALF:, :] = corner[1, p.y].astype(F32) + corner[1, 2].astype(F32)

        if unit in SIDEWAYS and stage == 3:
            loop(2, sideways_far)
        elif unit in SIDEWAYS and stage == 4:
            sideways_last()
        else:
            steps = {1: (16, from_core), 2: (8, from_side), 3: (4, from_corner), 4: (2, from_far)}
            loop(*steps[stage])

    def advance(self, unit, stage):
        self.arrive(unit, stage)
        if stage == 1:
            self.own_copy(unit).wait()
        self.combine(unit, stage)
        if stage < 4:
            self.begin(unit, stage + 1)


class Small:
    def __init__(self, place, values, scratch):
        self.place, self.values = place, values
        self.from_core, self.from_x, self.from_y, self.from_z, self.send, self.recv = scratch

    @staticmethod
    def scratch(rows):
        return [
            pltpu.VMEM((4, 2, rows, LANES), F32),
            pltpu.VMEM((4, rows, LANES), F32),
            pltpu.VMEM((4, rows, LANES), F32),
            pltpu.VMEM((3, rows, LANES), F32),
            pltpu.SemaphoreType.DMA((6,)),
            pltpu.SemaphoreType.DMA((6,)),
        ]

    def copies(self, stage):
        p, values = self.place, self.values

        def copy(slot, source, target, device):
            return pltpu.make_async_remote_copy(
                src_ref=source,
                dst_ref=target,
                send_sem=self.send.at[slot],
                recv_sem=self.recv.at[slot],
                device_id=device,
                device_id_type=MESH,
            )

        if stage == 1:
            return [copy(0, values, self.from_core, p.at(c=1 - p.c))]
        if stage == 2:
            return [copy(1, values.at[:, 1 - p.x], self.from_x, p.at(x=1 - p.x))]
        if stage == 3:
            return [copy(2, values.at[:, p.x], self.from_y, p.at(y=1 - p.y))]
        return [
            copy(2 + k, values.at[p.far(k), p.x], self.from_z.at[k - 1], p.at(z=p.far(k)))
            for k in (1, 2, 3)
        ]

    def start(self, stage):
        for copy in self.copies(stage):
            copy.start()

    def advance(self, stage):
        p, values = self.place, self.values
        for copy in self.copies(stage):
            copy.wait()
        if stage == 1:
            values[...] += self.from_core[...]
        elif stage == 2:
            values[:, p.x] += self.from_x[...]
        elif stage == 3:
            values[:, p.x] += self.from_y[...]
        else:
            return values[p.z, p.x] + self.from_z[0] + self.from_z[1] + self.from_z[2]
        self.start(stage + 1)
        return None


class Copies:
    def __init__(self, send, recv):
        self.send, self.recv, self.count = send, recv, 0

    def __call__(self, source, target, device):
        slot = self.count
        self.count += 1
        copy = pltpu.make_async_remote_copy(
            src_ref=source,
            dst_ref=target,
            send_sem=self.send.at[slot],
            recv_sem=self.recv.at[slot],
            device_id=device,
            device_id_type=MESH,
        )
        copy.start()
        return copy


class Refs:
    pass


def call(kernel, name, inputs, outputs, scratch, aliases=(), collective=None, grid=None, limit=58):
    names = list(inputs) + list(outputs)
    flat = []
    for value in scratch.values():
        flat += value if isinstance(value, list) else [value]

    def body(*refs):
        held = Refs()
        rest = list(refs)
        for key in names:
            setattr(held, key, rest.pop(0))
        for key, value in scratch.items():
            if isinstance(value, list):
                setattr(held, key, [rest.pop(0) for _ in value])
            else:
                setattr(held, key, rest.pop(0))
        kernel(held)

    extra = {} if grid is None else {"grid": grid}
    result = pl.pallas_call(
        body,
        in_specs=[spec for _, spec in inputs.values()],
        out_specs=[spec for _, spec in outputs.values()],
        out_shape=[out for out, _ in outputs.values()],
        scratch_shapes=flat,
        input_output_aliases={
            list(inputs).index(one): list(outputs).index(other) for one, other in aliases
        },
        compiler_params=params(collective, limit),
        name=name,
        **extra,
    )(*[array for array, _ in inputs.values()])
    out = Refs()
    for key, value in zip(outputs, result, strict=True):
        setattr(out, key, value)
    return out


SPLIT = (4, 2, 2, 2, SHARE, LANES)
MOD_ROWS = 48
OWN_SLOTS = 4
ORDER = (0, 1, 2, 3, 4, 8, 5, 9, 6, 10, 7, 11)
SIDEWAYS = ()
ENTER = (
    ((0, 1),),
    ((1, 1), (0, 2)),
    ((2, 1), (1, 2), (0, 3)),
    ((3, 1), (2, 2), (1, 3), (0, 4)),
    ((4, 1), (3, 2), (2, 3), (1, 4)),
    ((5, 1), (4, 2), (3, 3), (2, 4)),
)
ATTEND = {
    0: ((6, 1), (5, 2), (4, 3), (3, 4)),
    3: ((7, 1), (6, 2), (5, 3), (4, 4)),
    6: ((8, 1), (7, 2), (6, 3), (5, 4)),
}
MIDDLE = {
    0: ((9, 1), (8, 2), (7, 3), (6, 4)),
    2: ((10, 1), (9, 2), (8, 3), (7, 4)),
    5: ((11, 1), (10, 2), (9, 3), (8, 4)),
    7: ((11, 2), (10, 3), (9, 4)),
    9: ((11, 3), (10, 4)),
    11: ((11, 4),),
}
EARLY = (DOWN, UP, DOWN + 1)
LATE = (UP + 1, DOWN + 2, UP + 2, DOWN + 3, UP + 3, OUT, QKV, QKV + 1, QKV + 2)


def gather_stages(points):
    return [(ORDER[index], stage) for point in points for index, stage in point]


def enter_norm(refs):
    rows = 32
    for window in range(refs.mod.shape[0]):
        shift, scale = refs.mod[window, 0:1, :], refs.mod[window, 1:2, :]

        def step(index, window=window, shift=shift, scale=scale):
            at = pl.ds(pl.multiple_of(window * WIN + index * rows, rows), rows)
            normal, _ = centered(refs.tokens[at, :].astype(F32))
            refs.normed[at, :] = (normal * (1.0 + scale) + shift).astype(BF16)

        loop(WIN // rows, step)


def enter_unit(refs, j, held):
    fetch = pltpu.make_async_copy(held, refs.unit, refs.fetch)
    fetch.start()
    fetch.wait()

    def project(index):
        refs.packed[j, :, half(index)] = dot(
            refs.normed[...], four_columns(refs.unit, index)
        ).astype(BF16)

    loop(2, project)


def enter_plain_kernel(refs):
    enter_norm(refs)
    for j in range(3):
        enter_unit(refs, j, refs.held.at[QKV + j])


def enter_kernel(refs):
    place = Place()
    place.greet()
    z, x, y, c = place.z, place.x, place.y, place.c

    own = []
    for unit in range(UNITS):
        if unit >= DOWN:
            first = (unit - DOWN) * LANES
            for half in range(2):
                at = slice(half * 512 + first, half * 512 + first + LANES)
                refs.own[unit, half * HALF : (half + 1) * HALF] = refs.down[at, :]
        else:
            source, start = (
                (refs.qkv, QKV) if unit < OUT else (refs.out, OUT) if unit < UP else (refs.up, UP)
            )
            first = (unit - start) * LANES
            refs.own[unit] = source[:, first : first + LANES]
        own.append(
            pltpu.make_async_copy(
                refs.own.at[unit], refs.held.at[unit, z, x, y, c], refs.own_sem.at[unit]
            )
        )
        own[-1].start()
    work = Gather(place, refs.held, gather_stages(ENTER), refs.gather)
    points = list(ENTER)

    def tick():
        for index, stage in points.pop(0):
            work.advance(ORDER[index], stage)

    small = Copies(*refs.small)
    copy = small(refs.mod_part, refs.from_core, place.at(c=1 - c))
    for one in own:
        one.wait()
    tick()
    refs.table[z, x, c] = refs.table_own[c]
    copy.wait()
    refs.mod_sum[...] = refs.mod_part[...] + refs.from_core[...]
    copy = small(refs.mod_sum, refs.from_y, place.at(y=1 - y))
    copy.wait()
    refs.mods[z, x] = refs.mod_sum[...] + refs.from_y[...]
    copies = [
        small(refs.mods.at[z, x], refs.mods.at[z, x], place.at(x=1 - x)),
        small(refs.table.at[z, x, c], refs.table.at[z, x, c], place.at(x=1 - x)),
    ]
    copies[0].wait()
    mods = [
        small(refs.mods.at[z], refs.mods.at[z], place.at(z=place.far(k))) for k in (1, 2, 3)
    ]
    tick()
    copies[1].wait()
    tick()
    for copy in mods:
        copy.wait()
    for window in range(refs.mod.shape[0]):
        for block in range(48):
            which, column = divmod(block, 8)
            part = refs.mods[block // 12, block // 6 % 2, block % 6 * 8 : block % 6 * 8 + 8, :]
            refs.mod[window, which : which + 1, column * LANES : (column + 1) * LANES] = jnp.sum(
                part * refs.member[window], axis=0, keepdims=True
            )
    enter_norm(refs)
    tick()
    tables = [
        small(refs.table.at[z, :, c], refs.table.at[z, :, c], place.at(z=place.far(k)))
        for k in (1, 2, 3)
    ]
    work.arrive(QKV, 4)
    enter_unit(refs, 0, refs.held.at[QKV])
    tick()
    work.arrive(QKV + 1, 4)
    enter_unit(refs, 1, refs.held.at[QKV + 1])
    tick()
    for copy in tables:
        copy.wait()
    last = small(refs.table.at[:, :, c], refs.table.at[:, :, c], place.at(c=1 - c))
    work.arrive(QKV + 2, 4)
    enter_unit(refs, 2, refs.held.at[QKV + 2])
    last.wait()
    work.finish()


def attend_kernel(refs):
    work = None
    step = pl.program_id(0)
    if hasattr(refs, "gather"):
        place = Place()
        work = Gather(place, refs.held, gather_stages(ATTEND.values()), refs.gather)
        for at, stages in ATTEND.items():

            @pl.when(step == at)
            def _(at=at, stages=stages):
                if at == 0:
                    place.greet()
                for index, stage in stages:
                    work.advance(ORDER[index], stage)

    for head in range(2):
        spread = refs.table[head].astype(F32)
        for frame in range(FRAMES):
            block = spread[frame * WSIDE : (frame + 1) * WSIDE]
            for row in range(WSIDE):
                first = (WSIDE - 1 - row) * WSIDE
                refs.strip[
                    head, row * WSIDE : (row + 1) * WSIDE, frame * CELLS : (frame + 1) * CELLS
                ] = block[:, first : first + CELLS]
        for frame in range(WT):
            first = (WT - 1 - frame) * CELLS
            refs.bias[head, frame * CELLS : (frame + 1) * CELLS, :] = refs.strip[
                head, :, first : first + WIN
            ]

    for window in range(refs.live.shape[0]):
        rows = slice(window * WIN, (window + 1) * WIN)
        live = refs.live[window] * CELLS
        key_live = lax.broadcasted_iota(jnp.int32, (1, WIN), 1) < live
        for head in range(2):
            lanes = slice(head * HD, (head + 1) * HD)
            query = refs.query[rows, lanes] * BF16(HD ** (-0.5))
            scores = dot_rows(query, refs.key[rows, lanes]) + refs.bias[head]
            scores = jnp.where(key_live, scores, NEGATIVE)
            shifted = jnp.exp(scores - jnp.max(scores, axis=-1, keepdims=True))
            totals = jnp.sum(shifted, axis=-1, keepdims=True)
            probs = (shifted * (1.0 / totals)).astype(BF16)
            refs.probs[window, head] = probs
            refs.mixed[rows, lanes] = dot(probs, refs.value[rows, lanes]).astype(BF16)

    if work is not None:

        @pl.when(step == 7)
        def _():
            work.finish()


def packed_block(part, rows):
    pairs = H // 2
    return pl.BlockSpec(
        (None, rows, LANES),
        lambda pair: (
            lax.rem(part * pairs + pair, 3),
            0,
            lax.div(part * pairs + pair, 3),
        ),
    )


def attend_back_pair(refs, pair):
    scale = BF16(HD ** (-0.5))
    refs.spread[...] = jnp.zeros_like(refs.spread)
    refs.strip[...] = jnp.zeros_like(refs.strip)
    windows = refs.probs.shape[0]
    results = [[[None] * windows for _ in range(2)] for _ in range(3)]
    for head in range(2):
        lanes = slice(head * HD, (head + 1) * HD)
        bias = None
        for window in range(windows):
            rows = slice(window * WIN, (window + 1) * WIN)
            grad = refs.grad[rows, lanes]
            probs = refs.probs[window, head]
            results[2][head][window] = dot_tokens(grad, probs).T.astype(BF16)
            grad_probs = dot_rows(grad, refs.value[rows, lanes])
            weight = probs.astype(F32)
            product = weight * grad_probs
            total = jnp.sum(product, axis=-1, keepdims=True)
            grad_scores = (product - weight * total).astype(BF16)
            wide = grad_scores.astype(F32)
            bias = wide if bias is None else bias + wide
            results[0][head][window] = dot(grad_scores, refs.key[rows, lanes] * scale).astype(BF16)
            query = refs.query[rows, lanes] * scale
            results[1][head][window] = dot_tokens(query, grad_scores).T.astype(BF16)
        for frame in range(WT):
            first = (WT - 1 - frame) * CELLS
            refs.strip[head, :, first : first + WIN] += bias[frame * CELLS : (frame + 1) * CELLS]
        for frame in range(FRAMES):
            for row in range(WSIDE):
                first = (WSIDE - 1 - row) * WSIDE
                refs.spread[
                    head, frame * WSIDE : (frame + 1) * WSIDE, first : first + CELLS
                ] += refs.strip[
                    head, row * WSIDE : (row + 1) * WSIDE, frame * CELLS : (frame + 1) * CELLS
                ]
    for part in range(3):
        block = part * (H // 2) + pair
        lanes = pl.ds(pl.multiple_of(lax.div(block, 3) * LANES, LANES), LANES)
        for window in range(windows):
            rows = slice(window * WIN, (window + 1) * WIN)
            both = [results[part][head][window] for head in range(2)]
            refs.grad_packed[lax.rem(block, 3), rows, lanes] = jnp.concatenate(both, axis=1)


def middle_kernel(refs):
    order = [OUT] + [unit for j in range(4) for unit in (UP + j, DOWN + j)] + [OUT]
    gathering = reducing = None
    points = {}
    waiting = set()
    if hasattr(refs, "gather"):
        place = Place()
        place.greet()
        gathering = Gather(place, refs.held_out, gather_stages(MIDDLE.values()), refs.gather)
        reducing = Reduce(place, lambda unit: refs.part.at[unit], refs.total, EARLY, refs.reduce)
        for stages in MIDDLE.values():
            waiting |= {ORDER[index] for index, stage in stages if stage == 4}
        for unit, times in zip(
            EARLY, ((7, 9, 13, 16, 19), (9, 11, 15, 18, 20), (11, 13, 17, 20, 21)), strict=True
        ):
            points.setdefault(times[0], []).append(functools.partial(reducing.begin, unit, 1))
            for stage in (1, 2, 3, 4):
                points.setdefault(times[stage], []).append(
                    functools.partial(reducing.advance, unit, stage)
                )

    held = refs.held_out if gathering is not None else refs.held
    count = [0]

    def pump():
        for index, stage in MIDDLE.get(count[0], ()) if gathering is not None else ():
            gathering.advance(ORDER[index], stage)
            if stage == 4:
                waiting.discard(ORDER[index])
        for action in points.pop(count[0], []):
            action()
        count[0] += 1

    def fetch(step):
        return pltpu.make_async_copy(
            held.at[order[step]], refs.unit.at[step % 4], refs.fetch.at[step % 4]
        )

    def start_fetch(step):
        if gathering is not None:
            assert order[step] not in waiting
            gathering.arrive(order[step], 4)
        fetch(step).start()

    def put(slot, unit):
        return pltpu.make_async_copy(refs.made.at[slot], refs.part.at[unit], refs.made_sem.at[slot])

    for step in range(3):
        start_fetch(step)
    pump()
    refs.sums[...] = jnp.zeros_like(refs.sums)
    refs.mlp[...] = jnp.zeros_like(refs.mlp)
    refs.grad_normed[...] = jnp.zeros_like(refs.grad_normed)
    fetch(0).wait()

    def project(index):
        refs.attended[:, half(index)] = dot(refs.mixed[...], four_columns(refs.unit.at[0], index))

    loop(2, project)
    pump()

    def modulate(window, at, mods, live):
        middle = refs.tokens[at, :].astype(F32) + mods[2] * refs.attended[at, :]
        normal, _ = centered(middle)
        refs.normed[at, :] = (normal * (1.0 + mods[4]) + mods[3]).astype(BF16)
        grad = jnp.where(live, refs.cotangent[at, :].astype(F32), 0.0)
        refs.grad_low[at, :] = (mods[5] * grad).astype(BF16)

    each_rows(refs.mod, refs.live, modulate)
    pump()
    for j in range(4):
        step = 1 + 2 * j
        up, down = refs.unit.at[step % 4], refs.unit.at[(step + 1) % 4]
        fetch(step).wait()
        fetch(step + 1).wait()
        start_fetch(step + 2)

        def hide(index, up=up, down=down):
            hidden = dot(refs.normed[...], four_columns(up, index))
            bend = jnp.tanh(0.7978845608028654 * (hidden + 0.044715 * hidden * hidden * hidden))
            refs.activated[:, half(index)] = (0.5 * hidden * (1.0 + bend)).astype(BF16)
            slope = 0.5 * (1.0 + bend) + 0.5 * hidden * (1.0 - bend * bend) * (
                0.7978845608028654 * (1.0 + 3.0 * 0.044715 * hidden * hidden)
            )
            grad_activated = dot_rows(refs.grad_low[...], half_rows(down, index))
            refs.grad_hidden[:, half(index)] = (grad_activated * slope).astype(BF16)

        loop(2, hide)
        if j > 0:
            put(1, UP + j - 1).wait()
        pump()

        def down_gradient(index):
            made = dot_tokens(refs.activated[:, half(index)], refs.grad_low[...]).astype(BF16)
            for block in range(8):
                refs.made[0, block // 2, block % 2, index] = made[
                    :, block * LANES : (block + 1) * LANES
                ].reshape(2, SHARE, LANES)

        loop(2, down_gradient)
        put(0, DOWN + j).start()
        pump()

        def up_gradient(index):
            made = dot_tokens(refs.normed[...], refs.grad_hidden[:, half(index)]).astype(BF16)
            put_columns(refs.made.at[1], index, made)

        loop(2, up_gradient)
        put(0, DOWN + j).wait()
        put(1, UP + j).start()
        pump()
        if j < 3:
            start_fetch(step + 3)

        def out_of_mlp(index, up=up, down=down):
            refs.mlp[:, half(index)] += dot(refs.activated[...], four_columns(down, index))
            refs.grad_normed[:, half(index)] += dot_rows(
                refs.grad_hidden[...], half_rows(up, index)
            )

        loop(2, out_of_mlp)
        pump()

    put(1, UP + 3).wait()

    def join(window, at, mods, live):
        attended = refs.attended[at, :]
        middle = refs.tokens[at, :].astype(F32) + mods[2] * attended
        normal, root = centered(middle)
        mlp = refs.mlp[at, :]
        refs.output[at, :] = jnp.where(live, middle + mods[5] * mlp, 0.0).astype(BF16)
        grad_result = jnp.where(live, refs.cotangent[at, :].astype(F32), 0.0)
        grad_normed = refs.grad_normed[at, :]
        grad_middle = grad_result + norm_back(grad_normed, normal, root, mods[4])
        refs.grad_middle[at, :] = grad_middle
        refs.grad_low[at, :] = (mods[2] * grad_middle).astype(BF16)
        add_sums(refs.sums, window, 2, grad_middle * attended)
        add_sums(refs.sums, window, 3, grad_normed)
        add_sums(refs.sums, window, 4, grad_normed * normal)
        add_sums(refs.sums, window, 5, grad_result * mlp)

    each_rows(refs.mod, refs.live, join)
    pump()
    fetch(9).wait()

    def back(index):
        made = dot_tokens(refs.mixed[...], refs.grad_low[:, half(index)]).astype(BF16)
        put_columns(refs.made.at[0], index, made)
        refs.grad_mixed[:, half(index)] = dot_rows(
            refs.grad_low[...], half_rows(refs.unit.at[1], index)
        ).astype(BF16)

    loop(2, back)
    put(0, OUT).start()
    put(0, OUT).wait()
    while points:
        pump()
    if gathering is not None:
        gathering.finish()
        reducing.sent()


def leave_weight(refs, j, made):
    def weight(index):
        grad = dot_tokens(refs.normed[...], refs.grad_packed[j, :, half(index)]).astype(BF16)
        put_columns(made, index, grad)

    loop(2, weight)


def leave_back(refs, j):
    def back(index):
        refs.grad_normed[:, half(index)] += dot_rows(
            refs.grad_packed[j], half_rows(refs.unit, index)
        )

    loop(2, back)


def leave_norm(refs):
    def join(window, at, mods, live):
        normal, root = centered(refs.tokens[at, :].astype(F32))
        grad_normed = refs.grad_normed[at, :]
        refs.grad_tokens[at, :] = refs.grad_middle[at, :] + norm_back(
            grad_normed, normal, root, mods[1]
        )
        add_sums(refs.sums, window, 0, grad_normed)
        add_sums(refs.sums, window, 1, grad_normed * normal)

    each_rows(refs.mod, refs.live, join)


def back_plain_kernel(refs):
    step = pl.program_id(0)

    @pl.when(step < H // 2)
    def _():
        attend_back_pair(refs, jnp.minimum(step, H // 2 - 1))

    @pl.when(step == H // 2)
    def _():
        refs.sums[...] = jnp.zeros_like(refs.sums)
        refs.grad_normed[...] = jnp.zeros_like(refs.grad_normed)
        for j in range(3):
            fetch = pltpu.make_async_copy(refs.held.at[QKV + j], refs.unit, refs.fetch)
            fetch.start()
            leave_weight(refs, j, refs.made)
            put = pltpu.make_async_copy(refs.made, refs.part.at[j], refs.made_sem)
            put.start()
            fetch.wait()
            leave_back(refs, j)
            put.wait()
        leave_norm(refs)


def back_kernel(refs):
    place = Place()
    z, x, y, c = place.z, place.x, place.y, place.c
    step = pl.program_id(0)
    work = Reduce(
        place,
        lambda unit: refs.made.at[unit] if unit < OUT else refs.part.at[unit],
        refs.total,
        LATE,
        refs.reduce,
    )
    table = Small(place, refs.table, refs.table_small)
    clip = Small(place, refs.clip, refs.clip_small)

    events = []
    for index, unit in enumerate(LATE):
        start = max(0, 2 * index - 2) if unit >= OUT else 9 + unit
        events.append((start, 0, functools.partial(work.begin, unit, 1)))
        for stage in (1, 2, 3, 4):
            time = max(1 + 2 * index, start + 1) + 3 * (stage - 1)
            events.append((time, stage, functools.partial(work.advance, unit, stage)))
    events.sort(key=lambda event: event[:2])

    def run(until):
        while events and events[0][0] < until:
            events.pop(0)[2]()

    for number in range(H // 2):

        @pl.when(step == number)
        def _(number=number):
            if number == 0:
                place.greet()
            run(number + 1)

    @pl.when(step < H // 2)
    def _():
        pair = jnp.minimum(step, H // 2 - 1)
        attend_back_pair(refs, pair)
        refs.table[lax.div(pair, 2), lax.rem(pair, 2)] = refs.spread[...].reshape(
            2 * SPREAD, LANES
        )

    @pl.when(step == H // 2)
    def _():
        table.start(1)
        refs.sums[...] = refs.late_sums[...]
        refs.grad_normed[...] = jnp.zeros_like(refs.grad_normed)

        def fetch(j):
            return pltpu.make_async_copy(refs.held.at[QKV + j], refs.unit, refs.fetch)

        fetch(0).start()
        run(9)
        leave_weight(refs, 0, refs.made.at[0])
        run(10)
        leave_weight(refs, 1, refs.made.at[1])
        run(11)
        table.advance(1)
        leave_weight(refs, 2, refs.made.at[2])
        run(12)
        fetch(0).wait()
        leave_back(refs, 0)
        fetch(1).start()
        run(13)
        table.advance(2)
        fetch(1).wait()
        leave_back(refs, 1)
        fetch(2).start()
        run(14)
        table.advance(3)
        fetch(2).wait()
        leave_back(refs, 2)
        run(15)
        leave_norm(refs)
        for block in range(48):
            which, column = divmod(block, 8)
            part = jnp.zeros((8, LANES), F32)
            for window in range(refs.mod.shape[0]):
                sums = refs.sums[window, which : which + 1, column * LANES : (column + 1) * LANES]
                part = part + refs.member[window] * sums
            refs.clip[block // 12, block // 6 % 2, block % 6 * 8 : block % 6 * 8 + 8, :] = part
        clip.start(1)
        run(17)
        clip.advance(1)
        refs.table_total[...] = table.advance(4)
        run(18)
        clip.advance(2)
        run(19)
        clip.advance(3)
        run(20)
        total = clip.advance(4)
        refs.clip_total[...] = total
        low = total.astype(BF16)
        cond = jnp.zeros((8, SHARE), F32)
        for block in range(6):
            cond = cond + dot_rows(
                low[block * 8 : block * 8 + 8], refs.ada[:, block * LANES : (block + 1) * LANES]
            )
        small = Copies(*refs.cond_small)
        refs.cond[y, c] = cond
        copy = small(refs.cond.at[y, c], refs.cond.at[y, c], place.at(c=1 - c))
        run(21)
        copy.wait()
        copy = small(refs.cond.at[y], refs.cond.at[y], place.at(y=1 - y))
        run(22)
        copy.wait()
        copy = small(refs.cond, refs.cond_x, place.at(x=1 - x))
        run(23)
        copy.wait()
        refs.cond_z[z] = refs.cond[...] + refs.cond_x[...]
        copies = [
            small(refs.cond_z.at[z], refs.cond_z.at[z], place.at(z=place.far(k)))
            for k in (1, 2, 3)
        ]
        run(100)
        for copy in copies:
            copy.wait()
        refs.cond_total[...] = refs.cond_z[0] + refs.cond_z[1] + refs.cond_z[2] + refs.cond_z[3]
        work.sent()


def enter(special, tokens, held, mod, own, mod_part, member, table):
    rows = tokens.shape[0]
    inputs = {"tokens": (tokens, vmem())}
    outputs = {
        "normed": (shape(BF16, rows, D), vmem()),
        "packed": (shape(BF16, 3, rows, D), vmem()),
    }
    scratch = {"unit": pltpu.VMEM(SPLIT, BF16), "fetch": pltpu.SemaphoreType.DMA}
    if not special:
        inputs |= {"held": (held, anywhere()), "mod": (mod, vmem())}
        out = call(enter_plain_kernel, "enter_plain", inputs, outputs, scratch)
        out.mod, out.held = mod, held
        return out
    for name, block in zip(("qkv", "out", "up", "down"), own, strict=True):
        inputs[name] = (block, vmem())
    inputs |= {
        "mod_part": (mod_part, vmem()),
        "member": (member, vmem()),
        "table_own": (table, vmem()),
    }
    outputs |= {
        "held": (shape(BF16, UNITS, *SPLIT), anywhere()),
        "mod": (shape(F32, member.shape[0], 8, D), vmem()),
        "table": (shape(BF16, 4, 2, *table.shape), vmem()),
    }
    rows_small = mod_part.shape[0]
    scratch |= {
        "own": pltpu.VMEM((UNITS, SHARE, LANES), BF16),
        "own_sem": pltpu.SemaphoreType.DMA((UNITS,)),
        "gather": Gather.semaphores(gather_stages(ENTER)),
        "small": [pltpu.SemaphoreType.DMA((16,))] * 2,
        "from_core": pltpu.VMEM((rows_small, LANES), F32),
        "from_y": pltpu.VMEM((rows_small, LANES), F32),
        "mod_sum": pltpu.VMEM((rows_small, LANES), F32),
        "mods": pltpu.VMEM((4, 2, rows_small, LANES), F32),
    }
    return call(enter_kernel, "enter", inputs, outputs, scratch, collective=0)


def attend(special, packed, table, live_frames, held):
    window_count = live_frames.shape[0]
    rows = window_count * WIN
    inputs = {
        "live": (live_frames, smem()),
        "query": (packed, packed_block(0, rows)),
        "key": (packed, packed_block(1, rows)),
        "value": (packed, packed_block(2, rows)),
        "table": (table, pl.BlockSpec((2, SPREAD, LANES), lambda p: (p, 0, 0))),
    }
    outputs = {
        "mixed": (shape(BF16, rows, D), pl.BlockSpec((rows, LANES), lambda p: (0, p))),
        "probs": (
            shape(BF16, window_count, H, WIN, WIN),
            pl.BlockSpec((window_count, 2, WIN, WIN), lambda p: (0, p, 0, 0)),
        ),
    }
    scratch = {
        "strip": pltpu.VMEM((2, CELLS, STRIP), F32),
        "bias": pltpu.VMEM((2, WIN, WIN), F32),
    }
    aliases, collective = (), None
    if special:
        inputs["held_in"] = (held, anywhere())
        outputs["held"] = (shape(BF16, UNITS, *SPLIT), anywhere())
        scratch["gather"] = Gather.semaphores(gather_stages(ATTEND.values()))
        aliases, collective = (("held_in", "held"),), 1
    out = call(
        attend_kernel,
        "attend",
        inputs,
        outputs,
        scratch,
        aliases,
        collective,
        grid=(H // 2,),
        limit=32,
    )
    if not special:
        out.held = held
    return out


def middle(special, live_frames, tokens, cotangent, mixed, mod, held):
    rows = tokens.shape[0]
    inputs = {
        "live": (live_frames, smem()),
        "tokens": (tokens, vmem()),
        "cotangent": (cotangent, vmem()),
        "mixed": (mixed, vmem()),
        "mod": (mod, vmem()),
        "held": (held, anywhere()),
    }
    outputs = {
        "output": (shape(BF16, rows, D), vmem()),
        "grad_middle": (shape(F32, rows, D), vmem()),
        "grad_mixed": (shape(BF16, rows, D), vmem()),
        "sums": (shape(F32, mod.shape[0], 8, D), vmem()),
        "part": (shape(BF16, UNITS, *SPLIT), anywhere()),
    }
    scratch = {
        "unit": pltpu.VMEM((4, *SPLIT), BF16),
        "attended": pltpu.VMEM((rows, D), F32),
        "normed": pltpu.VMEM((rows, D), BF16),
        "grad_low": pltpu.VMEM((rows, D), BF16),
        "mlp": pltpu.VMEM((rows, D), F32),
        "grad_normed": pltpu.VMEM((rows, D), F32),
        "activated": pltpu.VMEM((rows, D), BF16),
        "grad_hidden": pltpu.VMEM((rows, D), BF16),
        "made": pltpu.VMEM((2, *SPLIT), BF16),
        "fetch": pltpu.SemaphoreType.DMA((4,)),
        "made_sem": pltpu.SemaphoreType.DMA((2,)),
    }
    aliases, collective = (), None
    if special:
        outputs["held_out"] = (shape(BF16, UNITS, *SPLIT), anywhere())
        outputs["total"] = (shape(F32, len(EARLY), SHARE, LANES), vmem())
        scratch["gather"] = Gather.semaphores(gather_stages(MIDDLE.values()))
        scratch["reduce"] = Reduce.scratch(EARLY)
        aliases, collective = (("held", "held_out"),), 2
    return call(middle_kernel, "middle", inputs, outputs, scratch, aliases, collective, limit=60)


def back(
    special, live_frames, tokens, mod, start, probs, mid, held, ada, member
):
    window_count = probs.shape[0]
    rows = window_count * WIN
    pairs = H // 2

    def last(pair):
        return jnp.minimum(pair, pairs - 1)

    def whole(array):
        return pl.BlockSpec(array.shape, lambda p: (0,) * len(array.shape), pipeline_mode=pl.Buffered(1))

    def packed_pair(part):
        block = packed_block(part, rows)
        return pl.BlockSpec(block.block_shape, lambda p: block.index_map(last(p)))

    inputs = {
        "live": (live_frames, smem()),
        "query": (start.packed, packed_pair(0)),
        "key": (start.packed, packed_pair(1)),
        "value": (start.packed, packed_pair(2)),
        "probs": (
            probs,
            pl.BlockSpec((window_count, 2, WIN, WIN), lambda p: (0, last(p), 0, 0)),
        ),
        "grad": (mid.grad_mixed, pl.BlockSpec((rows, LANES), lambda p: (0, last(p)))),
        "held": (held, anywhere()),
    }
    for name, array in (
        ("tokens", tokens),
        ("mod", mod),
        ("normed", start.normed),
        ("grad_middle", mid.grad_middle),
    ):
        inputs[name] = (array, whole(array))

    def result(*sizes):
        made = shape(F32, *sizes)
        return made, whole(made)

    outputs = {"grad_tokens": result(rows, D)}
    scratch = {
        "strip": pltpu.VMEM((2, CELLS, STRIP), F32),
        "grad_packed": pltpu.VMEM((3, rows, D), BF16),
        "unit": pltpu.VMEM(SPLIT, BF16),
        "grad_normed": pltpu.VMEM((rows, D), F32),
        "fetch": pltpu.SemaphoreType.DMA,
    }
    if not special:
        outputs["sums"] = result(window_count, 8, D)
        outputs["part"] = (shape(BF16, 3, *SPLIT), anywhere())
        outputs["spread"] = (
            shape(F32, H, SPREAD, LANES),
            pl.BlockSpec((2, SPREAD, LANES), lambda p: (last(p), 0, 0)),
        )
        scratch["made"] = pltpu.VMEM(SPLIT, BF16)
        scratch["made_sem"] = pltpu.SemaphoreType.DMA
        return call(
            back_plain_kernel, "back_plain", inputs, outputs, scratch, grid=(pairs + 1,)
        )
    inputs |= {
        "late_sums": (mid.sums, whole(mid.sums)),
        "ada": (ada, whole(ada)),
        "member": (member, whole(member)),
        "part": (mid.part, anywhere()),
    }
    outputs |= {
        "total": result(len(LATE), SHARE, LANES),
        "clip_total": result(MOD_ROWS, LANES),
        "table_total": result(2 * SPREAD, LANES),
        "cond_total": result(2, 2, 8, SHARE),
    }
    scratch |= {
        "spread": pltpu.VMEM((2, SPREAD, LANES), F32),
        "made": pltpu.VMEM((3, *SPLIT), BF16),
        "sums": pltpu.VMEM((window_count, 8, D), F32),
        "reduce": Reduce.scratch(LATE),
        "table": pltpu.VMEM((4, 2, 2 * SPREAD, LANES), F32),
        "table_small": Small.scratch(2 * SPREAD),
        "clip": pltpu.VMEM((4, 2, MOD_ROWS, LANES), F32),
        "clip_small": Small.scratch(MOD_ROWS),
        "cond": pltpu.VMEM((2, 2, 8, SHARE), F32),
        "cond_x": pltpu.VMEM((2, 2, 8, SHARE), F32),
        "cond_z": pltpu.VMEM((4, 2, 2, 8, SHARE), F32),
        "cond_small": [pltpu.SemaphoreType.DMA((8,))] * 2,
    }
    return call(
        back_kernel,
        "back",
        inputs,
        outputs,
        scratch,
        collective=3,
        grid=(pairs + 1,),
        limit=62,
    )


def per_device(
    special,
    tokens,
    condition,
    clip_frames,
    ada_weight,
    ada_bias,
    qkv_weight,
    out_weight,
    up_weight,
    down_weight,
    rel_table,
    cotangent,
):
    window_count = tokens.shape[0]
    clip_count = condition.shape[0]
    rows_ada, cols_ada = ada_weight.shape
    row_block = lax.axis_index("fsdp")
    col_block = lax.axis_index("dp")
    first_window = lax.axis_index(("dp", "fsdp")) * window_count
    live_frames, member_int = window_layout(clip_frames, first_window, window_count)
    member = member_int.astype(F32)
    activity_low = jax.nn.silu(condition).astype(BF16)
    act_rows = lax.dynamic_slice_in_dim(activity_low, row_block * rows_ada, rows_ada, 1)

    mod_part = jnp.dot(act_rows, ada_weight, preferred_element_type=F32)
    mod_part = mod_part + jnp.where(row_block == 0, ada_bias.astype(F32), 0.0)[None, :]
    token_rows = tokens.reshape(window_count * WIN, D)
    cotangent_rows = cotangent.reshape(window_count * WIN, D)
    own = (qkv_weight, out_weight, up_weight, down_weight)
    if special:
        clips = jnp.pad(mod_part, ((0, 8 - clip_count), (0, 0)))
        clips = clips.reshape(8, 6, LANES).transpose(1, 0, 2).reshape(MOD_ROWS, LANES)
        member_wide = jnp.pad(member, ((0, 0), (0, 8 - clip_count)))[:, :, None]
        member_wide = jnp.broadcast_to(member_wide, (window_count, 8, LANES))
        start = enter(
            True, token_rows, None, None, own, clips, member_wide, spread_table(rel_table)
        )
        table = start.table.reshape(H, SPREAD, LANES)
    else:
        member_wide = None
        clip_mod = lax.all_gather(lax.psum(mod_part, "fsdp"), "dp", axis=1, tiled=True)
        window_mod = jnp.sum(member[:, :, None] * clip_mod[None], axis=1)
        window_mod = jnp.pad(window_mod.reshape(window_count, 6, D), ((0, 0), (0, 2), (0, 0)))
        whole = [
            lax.all_gather(
                lax.all_gather(weight, "dp", axis=1, tiled=True), "fsdp", axis=0, tiled=True
            )
            for weight in own
        ]
        held = units_of(*whole).reshape(UNITS, *SPLIT)
        start = enter(False, token_rows, held, window_mod, None, None, None, None)
        table = spread_table(lax.all_gather(rel_table, "dp", axis=0, tiled=True))
    mod = start.mod
    across = attend(special, start.packed, table, live_frames, start.held)
    mid = middle(
        special, live_frames, token_rows, cotangent_rows, across.mixed, mod, across.held
    )
    held = mid.held_out if special else across.held
    end = back(
        special,
        live_frames,
        token_rows,
        mod,
        start,
        across.probs,
        mid,
        held,
        ada_weight,
        member_wide,
    )
    if special:
        shares = [None] * UNITS
        for units, totals in ((EARLY, mid.total), (LATE, end.total)):
            for index, unit in enumerate(units):
                shares[unit] = totals[index]
        grads = own_blocks(jnp.stack(shares))
        clip_cols = end.clip_total.reshape(6, 8, LANES).transpose(1, 0, 2).reshape(8, cols_ada)
        clip_cols = clip_cols[:clip_count].astype(BF16)
        cond_total = end.cond_total.transpose(2, 0, 1, 3).reshape(8, D)[:clip_count]
        table_grad = gather_table(end.table_total.reshape(2, SPREAD, LANES))
    else:
        part = jnp.concatenate([end.part, mid.part[OUT:]])
        grads = [
            lax.psum_scatter(
                lax.psum_scatter(grad, "fsdp", scatter_dimension=0, tiled=True),
                "dp",
                scatter_dimension=1,
                tiled=True,
            ).astype(F32)
            for grad in weights_of(part.reshape(UNITS, 8, D, LANES))
        ]
        grad_mod = (mid.sums + end.sums)[:, :6].reshape(window_count, 6 * D)
        clip_part = lax.dot_general(
            member,
            grad_mod,
            (((0,), (0,)), ((), ())),
            precision=HIGHEST,
            preferred_element_type=F32,
        )
        clip_sum, table_sum = lax.psum((clip_part, gather_table(end.spread)), ("dp", "fsdp"))
        clip_cols = lax.dynamic_slice_in_dim(
            clip_sum.astype(BF16), col_block * cols_ada, cols_ada, 1
        )
        heads_own = rel_table.shape[0]
        table_grad = lax.dynamic_slice_in_dim(table_sum, col_block * heads_own, heads_own, 0)
        cond_part = lax.dot_general(
            clip_cols, ada_weight, (((1,), (1,)), ((), ())), preferred_element_type=F32
        )
        cond_total = lax.all_gather(lax.psum(cond_part, "dp"), "fsdp", axis=1, tiled=True)
    grad_ada_weight = lax.dot_general(
        act_rows, clip_cols, (((0,), (0,)), ((), ())), preferred_element_type=F32
    )
    grad_ada_bias = jnp.sum(clip_cols.astype(F32), axis=0)
    _, silu_back = jax.vjp(jax.nn.silu, condition)
    return (
        mid.output.reshape(tokens.shape),
        end.grad_tokens.reshape(tokens.shape),
        silu_back(cond_total)[0],
        grad_ada_weight,
        grad_ada_bias,
        *grads,
        table_grad,
    )


def solution(mesh):
    special = dict(mesh.shape) == {"dp": 8, "fsdp": 4}
    both = P(("dp", "fsdp"), None, None)
    weight = P("fsdp", "dp")
    in_specs = (both, P(), P(), weight, P("dp")) + (weight,) * 4 + (P("dp", None), both)
    out_specs = (both, both, P(), weight, P("dp")) + (weight,) * 4 + (P("dp", None),)
    return jax.shard_map(
        functools.partial(per_device, special),
        mesh=mesh,
        in_specs=in_specs,
        out_specs=out_specs,
        check_vma=False,
    )
```

```python
import functools

import jax
import jax.numpy as jnp
from jax import lax
from jax.experimental import pallas as pl
from jax.experimental.pallas import tpu as pltpu
from jax.sharding import PartitionSpec as P

D = 1024
H = 16
HD = 64
WT = 5
WSIDE = 8
WIN = 320
SPW = 16
CELLS = WSIDE * WSIDE
FRAMES = 2 * WT - 1
OFFSETS = (2 * WSIDE - 1) ** 2
REL = FRAMES * OFFSETS
LANES = 128
TILE = 256
SPREAD = 80
WIDE = 96
STRIP = 640

EPSILON = 1e-06
NEGATIVE = -1000000000.0
HIGHEST = lax.Precision.HIGHEST
F32 = jnp.float32
BF16 = jnp.bfloat16
MESH = pl.DeviceIdType.MESH
MIB = 2**20

QKV, OUT, UP, DOWN, UNITS = 0, 3, 4, 8, 12
SHARE = 256
HALF = 128


SPLIT = (4, 2, 2, 2, SHARE, LANES)
CLIP_ROWS = 4
MOD_ROWS = 6 * CLIP_ROWS
OWN_SLOTS = 4
ORDER = (0, 1, 2, 3, 4, 8, 5, 9, 6, 10, 7, 11)
GATHER_ASIDE = (UP + 3, DOWN + 3)
REDUCE_ASIDE = (DOWN, UP + 2)
ENTER = (
    ((0, 1),),
    ((1, 1), (0, 2)),
    ((2, 1), (1, 2), (0, 3)),
    ((3, 1), (2, 2), (1, 3), (0, 4)),
    ((4, 1), (3, 2), (2, 3), (1, 4), (10, 1), (11, 1)),
    ((5, 1), (6, 1), (4, 2), (3, 3), (2, 4), (10, 2), (11, 2)),
)
ATTEND = {
    0: ((7, 1), (5, 2), (4, 3), (3, 4), (10, 3)),
    3: ((8, 1), (6, 2), (5, 3), (4, 4)),
    6: ((7, 2), (6, 3), (5, 4)),
}
MIDDLE = {
    0: ((9, 1), (8, 2), (7, 3), (6, 4), (10, 4)),
    2: ((9, 2), (8, 3), (7, 4), (11, 3)),
    5: ((9, 3), (8, 4)),
    7: ((9, 4),),
    12: ((11, 4),),
}
EARLY = (DOWN, UP, DOWN + 1, UP + 1, DOWN + 2)
DONE = EARLY[:4]
EARLY_POINTS = {
    6: ((DOWN, 0),),
    8: ((UP, 0), (DOWN, 1)),
    9: ((UP, 1),),
    10: ((DOWN + 1, 0),),
    11: ((DOWN + 1, 1),),
    12: ((UP + 1, 0), (UP, 2)),
    13: ((UP + 1, 1),),
    14: ((DOWN + 2, 0), (DOWN + 1, 2), (UP, 3)),
    15: ((DOWN + 2, 1),),
    16: ((DOWN + 1, 3), (UP + 1, 2)),
    17: ((DOWN, 2), (UP, 4)),
    18: ((UP + 1, 3), (DOWN + 2, 2)),
    19: ((DOWN, 3), (DOWN + 1, 4)),
    20: ((DOWN, 4), (UP + 1, 4)),
}
LATE = (UP + 2, DOWN + 3, UP + 3, OUT, QKV, QKV + 1, QKV + 2)
LATE_POINTS = {
    0: ((DOWN + 2, -3), (UP + 2, 0), (DOWN + 3, 0), (UP + 3, 0)),
    1: ((UP + 2, 1), (DOWN + 3, 1)),
    2: ((UP + 3, 1), (OUT, 0)),
    3: ((DOWN + 2, 3),),
    4: ((OUT, 1), (DOWN + 3, 2)),
    6: ((UP + 3, 2),),
    7: ((DOWN + 3, 3),),
    9: ((QKV, 0), (OUT, 2), (UP + 3, 3), (UP + 2, 2)),
    10: ((QKV + 1, 0), (QKV, 1)),
    11: ((QKV + 2, 0), (QKV + 1, 1), (OUT, 3), (DOWN + 2, 4)),
    12: ((QKV + 2, 1), (DOWN + 3, 4)),
    13: ((QKV, 2), (UP + 2, 3)),
    14: ((UP + 3, 4),),
    16: ((QKV + 1, 2), (QKV, 3)),
    17: ((UP + 2, 4), (OUT, 4)),
    18: ((QKV + 2, 2),),
    20: ((QKV + 1, 3),),
    22: ((QKV + 2, 3), (QKV, 4)),
    24: ((QKV + 1, 4), (QKV + 2, 4)),
}


def reduce_stages(points):
    moves = [move for at in sorted(points) for move in points[at]]
    started = [(unit, 3 if stage == -3 else stage + 1) for unit, stage in moves if stage < 4]
    return [(unit, stage) for unit, stage in started if stage > 3 or (unit, stage) in moves or stage < 3]


def gather_stages(points):
    return [(ORDER[index], stage) for point in points for index, stage in point]


def window_layout(clip_frames, first_window, window_count):
    slab_count = 1 + (clip_frames > WT).astype(jnp.int32)
    starts = jnp.cumsum(slab_count, dtype=jnp.int32) - slab_count
    global_window = first_window + jnp.arange(window_count, dtype=jnp.int32)
    slab_of = global_window // SPW
    owners = jnp.sum((starts[None, :] <= slab_of[:, None]).astype(jnp.int32), axis=1) - 1
    clip_ids = jnp.arange(clip_frames.shape[0], dtype=jnp.int32)
    member = (owners[:, None] == clip_ids[None, :]).astype(jnp.int32)
    clip_start = jnp.sum(member * starts[None, :], axis=1)
    own_frames = jnp.sum(member * clip_frames[None, :], axis=1)
    inner_slab = slab_of - clip_start
    return (jnp.minimum(own_frames - WT * inner_slab, WT), member)


def offset_spread():
    side_span = 2 * WSIDE - 1
    shape = (OFFSETS, WSIDE * LANES)
    offset = lax.broadcasted_iota(jnp.int32, shape, 0)
    place = lax.broadcasted_iota(jnp.int32, shape, 1)
    own, row, other = place // LANES, place // WSIDE % (LANES // WSIDE), place % WSIDE
    row_diff, col_diff = side_span - 1 - row, own - other + (WSIDE - 1)
    return ((row < side_span) & (row_diff * side_span + col_diff == offset)).astype(BF16)


def spread_table(table):
    heads = table.shape[0]
    by_frame = table.reshape(heads, FRAMES, OFFSETS)[:, ::-1].reshape(heads * FRAMES, OFFSETS)
    spread = jnp.dot(by_frame, offset_spread(), preferred_element_type=F32).astype(BF16)
    spread = spread.reshape(heads, FRAMES * WSIDE, LANES)
    return jnp.pad(spread, ((0, 0), (0, SPREAD - FRAMES * WSIDE), (0, 0)))


def gather_table(spread):
    heads = spread.shape[0]
    by_frame = spread[:, : FRAMES * WSIDE].reshape(heads * FRAMES, WSIDE * LANES)
    sums = lax.dot_general(
        by_frame,
        offset_spread().astype(F32),
        (((1,), (1,)), ((), ())),
        precision=HIGHEST,
        preferred_element_type=F32,
    )
    return sums.reshape(heads, FRAMES, OFFSETS)[:, ::-1].reshape(heads, FRAMES * OFFSETS)


def units_of(qkv, out, up, down):
    return jnp.concatenate(
        [
            qkv.reshape(D, 8, 3, LANES).transpose(2, 1, 0, 3),
            out.reshape(D, 8, 1, LANES).transpose(2, 1, 0, 3),
            up.reshape(D, 8, 4, LANES).transpose(2, 1, 0, 3),
            down.reshape(8, 4, LANES, 8, LANES).transpose(1, 3, 0, 2, 4).reshape(4, 8, D, LANES),
        ]
    )


def weights_of(units):
    def columns(part):
        return part.transpose(2, 1, 0, 3).reshape(D, -1)

    down = units[DOWN:].reshape(4, 8, 8, LANES, LANES).transpose(2, 0, 3, 1, 4)
    return (
        columns(units[QKV:OUT]),
        columns(units[OUT:UP]),
        columns(units[UP:DOWN]),
        down.reshape(4 * D, D),
    )


def dot(left, right):
    return jnp.dot(left, right, preferred_element_type=F32)


def dot_rows(left, right):
    return lax.dot_general(left, right, (((1,), (1,)), ((), ())), preferred_element_type=F32)


def dot_tokens(left, right):
    return lax.dot_general(left, right, (((0,), (0,)), ((), ())), preferred_element_type=F32)


def half(index):
    return pl.ds(pl.multiple_of(index * 512, 512), 512)


def four_columns(unit, index):
    blocks = [unit[2 * index + x // 2, x % 2].reshape(D, LANES) for x in range(4)]
    return jnp.concatenate(blocks, axis=1)


def half_rows(unit, index):
    blocks = [unit[block // 2, block % 2, index].reshape(512, LANES) for block in range(8)]
    return jnp.concatenate(blocks, axis=1)


def put_columns(unit, index, values):
    for x in range(4):
        unit[2 * index + x // 2, x % 2] = values[:, x * LANES : (x + 1) * LANES].reshape(2, 2, SHARE, LANES)


def loop(count, body):
    def step(index, carry):
        body(index)
        return carry

    lax.fori_loop(0, count, step, 0)


def vmem():
    return pl.BlockSpec(memory_space=pltpu.VMEM)


def anywhere():
    return pl.BlockSpec(memory_space=pl.ANY)


def smem():
    return pl.BlockSpec(memory_space=pltpu.SMEM)


def shape(dtype, *sizes):
    return jax.ShapeDtypeStruct(sizes, dtype)


def params(collective=None, limit=58):
    if collective is None:
        return pltpu.CompilerParams(vmem_limit_bytes=limit * MIB)
    return pltpu.CompilerParams(
        vmem_limit_bytes=limit * MIB, collective_id=collective, has_side_effects=True
    )


def centered(values):
    center = values - jnp.mean(values, axis=-1, keepdims=True)
    spread = jnp.mean(center * center, axis=-1, keepdims=True)
    root = lax.rsqrt(spread + EPSILON)
    return center * root, root


def norm_back(grad_normed, normal, root, scale):
    grad = grad_normed * (1.0 + scale)
    mean = jnp.mean(grad, axis=-1, keepdims=True)
    along = jnp.mean(grad * normal, axis=-1, keepdims=True)
    return root * (grad - mean - normal * along)


def each_rows(mod_ref, live_ref, body, rows=32, pump=lambda window: None):
    for window in range(mod_ref.shape[0]):
        live = live_ref[window] * CELLS

        def step(index, window=window, live=live):
            at = pl.ds(pl.multiple_of(window * WIN + index * rows, rows), rows)
            mods = [mod_ref[window, k : k + 1, :] for k in range(6)]
            slot = index * rows + lax.broadcasted_iota(jnp.int32, (rows, 1), 0)
            body(window, at, mods, slot < live)

        loop(WIN // rows, step)
        pump(window)


def add_sums(sums_ref, window, which, values):
    sums_ref[window, which : which + 1, :] += jnp.sum(values, axis=0, keepdims=True)


class Place:
    def __init__(self):
        column, row = lax.axis_index("dp"), lax.axis_index("fsdp")
        self.z, self.x, self.y, self.c = column // 2, column % 2, row // 2, row % 2

    def at(self, z=None, x=None, y=None, c=None):
        z = self.z if z is None else z
        x = self.x if x is None else x
        y = self.y if y is None else y
        c = self.c if c is None else c
        return (z * 2 + x, y * 2 + c)

    def far(self, k):
        return lax.rem(self.z + k, 4)

    def shifted(self, dz, dx, dy, dc):
        def other(index, change):
            return 1 - index if change else index

        return self.at(self.far(dz), other(self.x, dx), other(self.y, dy), other(self.c, dc))

    def greet(self, far_ones=()):
        near = [(1, 0, 0, 0), (2, 0, 0, 0), (3, 0, 0, 0), (0, 1, 0, 0), (0, 0, 1, 0), (0, 0, 0, 1)]
        peers = near + [change for change in far_ones if change not in near]
        barrier = pltpu.get_barrier_semaphore()
        for change in peers:
            pl.semaphore_signal(
                barrier, inc=1, device_id=self.shifted(*change), device_id_type=MESH
            )
        pl.semaphore_wait(barrier, len(peers))


EVERYONE = [
    (dz, dx, dy, dc)
    for dz in range(4)
    for dx in range(2)
    for dy in range(2)
    for dc in range(2)
    if (dz, dx, dy, dc) != (0, 0, 0, 0)
]
ALONG_ZX = [change for change in EVERYONE if change[2:] == (0, 0)]
ALONG_YC = [change for change in EVERYONE if change[:2] == (0, 0)]


class Moves:
    def __init__(self, place, stages, scratch):
        self.place = place
        self.send, self.recv = scratch
        self.first, count = {}, 0
        for unit, stage in stages:
            self.first[unit, stage] = count
            count += self.counts[unit in self.aside][stage - 1]
        self.flying = []

    @classmethod
    def semaphores(cls, stages):
        count = sum(cls.counts[unit in cls.aside][stage - 1] for unit, stage in stages)
        return [pltpu.SemaphoreType.DMA((count,))] * 2

    def made(self, unit, stage, moves):
        copies = []
        for index, (source, target, device) in enumerate(moves):
            slot = self.first[unit, stage] + index
            copies.append(
                pltpu.make_async_remote_copy(
                    src_ref=source,
                    dst_ref=target,
                    send_sem=self.send.at[slot],
                    recv_sem=self.recv.at[slot],
                    device_id=device,
                    device_id_type=MESH,
                )
            )
        return copies

    def begin(self, unit, stage):
        for copy in self.copies(unit, stage):
            copy.start()
        self.flying.append((unit, stage))

    def arrive(self, unit, stage):
        if (unit, stage) in self.flying:
            self.flying.remove((unit, stage))
            for copy in self.copies(unit, stage):
                copy.wait_recv()

    def sent(self):
        for unit, stage in self.first:
            for copy in self.copies(unit, stage):
                copy.wait_send()


class Gather(Moves):
    counts = ((3, 2, 2, 1), (2, 2, 3, 1))
    aside = GATHER_ASIDE

    def __init__(self, place, held, stages, scratch):
        super().__init__(place, stages, scratch)
        self.held = held

    def copies(self, unit, stage):
        p, held = self.place, self.held.at[unit]
        at_x, at_y, at_core = p.at(x=1 - p.x), p.at(y=1 - p.y), p.at(c=1 - p.c)
        own = held.at[p.z, p.x, p.y, p.c]
        if stage == 4:
            refs = [(held.at[:, :, :, p.c], at_core)]
        elif unit in self.aside and stage == 1:
            refs = [(own.at[:HALF], at_x), (own.at[HALF:], at_y)]
        elif unit in self.aside and stage == 2:
            refs = [
                (held.at[p.z, :, p.y, p.c, :HALF], at_y),
                (held.at[p.z, p.x, :, p.c, HALF:], at_x),
            ]
        elif unit in self.aside:
            refs = [(held.at[p.z, :, :, p.c], p.at(z=p.far(k))) for k in (1, 2, 3)]
        elif stage == 1:
            refs = [(own, p.at(z=p.far(k))) for k in (1, 2, 3)]
        elif stage == 2:
            refs = [
                (held.at[:, p.x, p.y, p.c, :HALF], at_x),
                (held.at[:, p.x, p.y, p.c, HALF:], at_y),
            ]
        else:
            refs = [
                (held.at[:, :, p.y, p.c, :HALF], at_y),
                (held.at[:, p.x, :, p.c, HALF:], at_x),
            ]
        return self.made(unit, stage, [(ref, ref, device) for ref, device in refs])

    def advance(self, unit, stage):
        self.arrive(unit, stage - 1)
        self.begin(unit, stage)

    def finish(self):
        for unit, stage in list(self.flying):
            self.arrive(unit, stage)
        self.sent()


class Reduce(Moves):
    counts = ((1, 2, 2, 3), (1, 3, 2, 2))
    aside = REDUCE_ASIDE

    def __init__(self, place, part, points, store, buffers, scratch):
        super().__init__(place, reduce_stages(points), scratch[2:])
        self.part, self.store, self.buffers = part, store, buffers
        self.own, self.load = scratch[:2]
        self.slots, self.loaded = {}, []

    @classmethod
    def scratch(cls, points):
        return [
            pltpu.VMEM((OWN_SLOTS, 4, 2, 2, SHARE, LANES), BF16),
            pltpu.SemaphoreType.DMA((OWN_SLOTS,)),
        ] + cls.semaphores(reduce_stages(points))

    @staticmethod
    def core_shape(count):
        return (count, 4, 2, 2, SHARE, LANES)

    @staticmethod
    def side_shape(count):
        return (count, 2, 4, 2, HALF, LANES)

    @staticmethod
    def corner_shape(count):
        return (count, 2, 4, HALF, LANES)

    @staticmethod
    def distant_shape(count):
        return (count, 3, 2, HALF, LANES)

    @staticmethod
    def aside_shape(count):
        return (count, 3, 2, 2, SHARE, LANES)

    def own_copy(self, unit):
        slot = self.slots.setdefault(unit, len(self.slots) % OWN_SLOTS)
        return pltpu.make_async_copy(
            self.part(unit).at[:, :, :, self.place.c], self.own.at[slot], self.load.at[slot]
        )

    def copies(self, unit, stage):
        p = self.place
        at_x, at_y, at_core = p.at(x=1 - p.x), p.at(y=1 - p.y), p.at(c=1 - p.c)
        core, side, corner, distant = self.buffers(unit)
        if unit in self.aside and stage == 2:
            moves = [
                (core.at[p.far(k)], distant.at[k - 1], p.at(z=p.far(k))) for k in (1, 2, 3)
            ]
        elif unit in self.aside and stage == 3:
            moves = [
                (core.at[p.z, :, 1 - p.y, :HALF], side.at[0, 0], at_y),
                (core.at[p.z, 1 - p.x, :, HALF:], side.at[1, 0], at_x),
            ]
        elif unit in self.aside and stage == 4:
            moves = [
                (side.at[0, 0, 1 - p.x], side.at[0, 1, 0], at_x),
                (side.at[1, 0, 1 - p.y], side.at[1, 1, 0], at_y),
            ]
        elif stage == 1:
            moves = [(self.part(unit).at[:, :, :, 1 - p.c], core, at_core)]
        elif stage == 2:
            moves = [
                (core.at[:, :, 1 - p.y, :HALF], side.at[0], at_y),
                (core.at[:, 1 - p.x, :, HALF:], side.at[1], at_x),
            ]
        elif stage == 3:
            moves = [
                (side.at[0, :, 1 - p.x], corner.at[0], at_x),
                (side.at[1, :, 1 - p.y], corner.at[1], at_y),
            ]
        else:
            moves = [
                (corner.at[:, p.far(k)], distant.at[k - 1], p.at(z=p.far(k))) for k in (1, 2, 3)
            ]
        return self.made(unit, stage, moves)

    def begin(self, unit, stage):
        super().begin(unit, stage)
        if stage == 1:
            self.own_copy(unit).start()
            assert self.slots[unit] not in self.loaded
            self.loaded.append(self.slots[unit])

    def combine(self, unit, stage):
        p = self.place
        core, side, corner, distant = self.buffers(unit)

        def plus(left, right):
            return (left.astype(F32) + right.astype(F32)).astype(BF16)

        def from_core(step):
            z, x, y = step // 4, step // 2 % 2, step % 2
            core[z, x, y] = plus(core[z, x, y], self.own[self.slots[unit], z, x, y])

        def from_side(step):
            z, b = step // 2, step % 2
            side[0, z, b] = plus(side[0, z, b], core[z, b, p.y, :HALF])
            side[1, z, b] = plus(side[1, z, b], core[z, p.x, b, HALF:])

        def from_corner(z):
            corner[0, z] = plus(corner[0, z], side[0, z, p.x])
            corner[1, z] = plus(corner[1, z], side[1, z, p.y])

        def from_far(half):
            total = corner[half, p.z].astype(F32)
            for k in range(3):
                total = total + distant[k, half].astype(F32)
            self.store(unit, half, total)

        def aside_far(step):
            x, y = step // 2, step % 2
            total = core[p.z, x, y].astype(F32)
            for k in range(3):
                total = total + distant[k, x, y].astype(F32)
            core[p.z, x, y] = total.astype(BF16)

        def aside_side(b):
            side[0, 0, b] = plus(side[0, 0, b], core[p.z, b, p.y, :HALF])
            side[1, 0, b] = plus(side[1, 0, b], core[p.z, p.x, b, HALF:])

        if unit in self.aside and stage == 4:
            for part, own in enumerate((p.x, p.y)):
                total = side[part, 0, own].astype(F32) + side[part, 1, 0].astype(F32)
                self.store(unit, part, total)
            return
        steps = {1: (16, from_core), 2: (8, from_side), 3: (4, from_corner), 4: (2, from_far)}
        if unit in self.aside:
            steps |= {2: (4, aside_far), 3: (2, aside_side)}
        loop(*steps[stage])

    def step(self, unit, stage):
        if stage <= 0:
            self.begin(unit, max(1, -stage))
            return
        self.arrive(unit, stage)
        if stage == 1:
            self.own_copy(unit).wait()
        self.combine(unit, stage)
        if stage == 1:
            self.loaded.remove(self.slots[unit])
        if (unit, stage + 1) in self.first:
            self.begin(unit, stage + 1)


class Copies:
    def __init__(self, send, recv):
        self.send, self.recv, self.count = send, recv, 0

    def __call__(self, source, target, device):
        slot = self.count
        self.count += 1
        copy = pltpu.make_async_remote_copy(
            src_ref=source,
            dst_ref=target,
            send_sem=self.send.at[slot],
            recv_sem=self.recv.at[slot],
            device_id=device,
            device_id_type=MESH,
        )
        copy.start()
        return copy


class Refs:
    pass


def call(kernel, name, inputs, outputs, scratch, aliases=(), collective=None, grid=None, limit=58):
    names = list(inputs) + list(outputs)
    flat = []
    for value in scratch.values():
        flat += value if isinstance(value, list) else [value]

    def body(*refs):
        held = Refs()
        rest = list(refs)
        for key in names:
            setattr(held, key, rest.pop(0))
        for key, value in scratch.items():
            if isinstance(value, list):
                setattr(held, key, [rest.pop(0) for _ in value])
            else:
                setattr(held, key, rest.pop(0))
        kernel(held)

    extra = {} if grid is None else {"grid": grid}
    result = pl.pallas_call(
        body,
        in_specs=[spec for _, spec in inputs.values()],
        out_specs=[spec for _, spec in outputs.values()],
        out_shape=[out for out, _ in outputs.values()],
        scratch_shapes=flat,
        input_output_aliases={
            list(inputs).index(one): list(outputs).index(other) for one, other in aliases
        },
        compiler_params=params(collective, limit),
        name=name,
        **extra,
    )(*[array for array, _ in inputs.values()])
    out = Refs()
    for key, value in zip(outputs, result, strict=True):
        setattr(out, key, value)
    return out


def enter_norm(refs):
    rows = 32
    for window in range(refs.mod.shape[0]):
        shift, scale = refs.mod[window, 0:1, :], refs.mod[window, 1:2, :]

        def step(index, window=window, shift=shift, scale=scale):
            at = pl.ds(pl.multiple_of(window * WIN + index * rows, rows), rows)
            normal, _ = centered(refs.tokens[at, :].astype(F32))
            refs.normed[at, :] = (normal * (1.0 + scale) + shift).astype(BF16)

        loop(WIN // rows, step)


def enter_unit(refs, j, held):
    fetch = pltpu.make_async_copy(held, refs.unit, refs.fetch)
    fetch.start()
    fetch.wait()

    def project(index):
        refs.packed[j, :, half(index)] = dot(
            refs.normed[...], four_columns(refs.unit, index)
        ).astype(BF16)

    loop(2, project)


def enter_plain_kernel(refs):
    enter_norm(refs)
    for j in range(3):
        enter_unit(refs, j, refs.held.at[QKV + j])


def act_rows(refs, place):
    first = (place.y * 2 + place.c) * SHARE
    value = refs.condition[:, pl.ds(pl.multiple_of(first, SHARE), SHARE)]
    act = value / (1.0 + jnp.exp(-value))
    return jnp.concatenate([act, jnp.zeros((8 - value.shape[0], SHARE), F32)], axis=0).astype(BF16)


def enter_layout(refs):
    windows, clips = refs.member.shape[0], refs.condition.shape[0]
    frames = [refs.frames[clip] for clip in range(clips)]
    starts = [0]
    for count in frames:
        starts.append(starts[-1] + 1 + jnp.where(count > WT, 1, 0))
    device = lax.axis_index("dp") * lax.axis_size("fsdp") + lax.axis_index("fsdp")
    refs.member[...] = jnp.zeros_like(refs.member)
    for window in range(windows):
        slab = (device * windows + window) // SPW
        live = 0
        for clip in range(clips):
            mine = starts[clip] <= slab
            if clip < clips - 1:
                mine = mine & (slab < starts[clip + 1])
            inner = frames[clip] - WT * (slab - starts[clip])
            live = live + jnp.where(mine, jnp.minimum(inner, WT), 0)
            refs.member[window, clip : clip + 1, :] = jnp.full(
                (1, LANES), jnp.where(mine, 1.0, 0.0), F32
            )
        refs.live[window] = live


def enter_table(refs):
    refs.rows[...] = jnp.zeros_like(refs.rows)
    table = refs.rel_table[...].astype(F32)
    for head in range(2):
        for frame in range(FRAMES):
            first = (FRAMES - 1 - frame) * OFFSETS
            row = head * (SPREAD // WSIDE) + frame
            refs.rows[row : row + 1, :OFFSETS] = table[head : head + 1, first : first + OFFSETS]
    shape_of = (TILE, WSIDE * LANES)
    offset = lax.broadcasted_iota(jnp.int32, shape_of, 0)
    place = lax.broadcasted_iota(jnp.int32, shape_of, 1)
    own, row, other = place // LANES, place // WSIDE % (LANES // WSIDE), place % WSIDE
    side_span = 2 * WSIDE - 1
    row_diff, col_diff = side_span - 1 - row, own - other + (WSIDE - 1)
    same = (row < side_span) & (row_diff * side_span + col_diff == offset)
    spread = dot(refs.rows[...].astype(BF16), jnp.where(same, 1.0, 0.0).astype(BF16))
    count = 2 * SPREAD // WSIDE
    for own in range(WSIDE):
        refs.spread[pl.ds(own, count, stride=WSIDE), :] = spread[
            :count, own * LANES : (own + 1) * LANES
        ]
    for head in range(2):
        refs.table_own[head] = refs.spread[head * SPREAD : (head + 1) * SPREAD, :].astype(BF16)


def enter_kernel(refs):
    place = Place()
    place.greet(ALONG_ZX + ALONG_YC)
    z, x, y, c = place.z, place.x, place.y, place.c
    small = Copies(*refs.small)
    mods = dot(act_rows(refs, place), refs.ada[...])
    mods = mods + jnp.where((y == 0) & (c == 0), 1.0, 0.0) * refs.bias[...].astype(F32)
    for block in range(6):
        refs.mod_part[block * CLIP_ROWS : (block + 1) * CLIP_ROWS, :] = mods[
            :CLIP_ROWS, block * LANES : (block + 1) * LANES
        ]
    refs.mod_parts[y, c] = refs.mod_part[...]
    parts = [
        small(refs.mod_part, refs.mod_parts.at[y, c], place.shifted(*change)) for change in ALONG_YC
    ]
    own = []
    for unit in range(UNITS):
        if unit >= DOWN:
            first = (unit - DOWN) * LANES
            for half in range(2):
                at = slice(half * 512 + first, half * 512 + first + LANES)
                refs.own[unit, half * HALF : (half + 1) * HALF] = refs.down[at, :]
        else:
            source, start = (
                (refs.qkv, QKV) if unit < OUT else (refs.out, OUT) if unit < UP else (refs.up, UP)
            )
            first = (unit - start) * LANES
            refs.own[unit] = source[:, first : first + LANES]
        own.append(
            pltpu.make_async_copy(
                refs.own.at[unit], refs.held.at[unit, z, x, y, c], refs.own_sem.at[unit]
            )
        )
        own[-1].start()
    work = Gather(place, refs.held, gather_stages(ENTER), refs.gather)
    points = list(ENTER)

    def tick():
        for index, stage in points.pop(0):
            work.advance(ORDER[index], stage)

    own[0].wait()
    tick()
    enter_layout(refs)
    enter_table(refs)
    refs.table[z, x, c] = refs.table_own[c]
    for copy in parts:
        copy.wait()
    refs.mods[z, x] = (
        refs.mod_parts[0, 0] + refs.mod_parts[0, 1] + refs.mod_parts[1, 0] + refs.mod_parts[1, 1]
    )
    mods = [
        small(refs.mods.at[z, x], refs.mods.at[z, x], place.shifted(*change))
        for change in ALONG_ZX
    ]
    for one in own[1:]:
        one.wait()
    tick()
    tick()
    for copy in mods:
        copy.wait()
    for window in range(refs.mod.shape[0]):
        for block in range(48):
            which, column = divmod(block, 8)
            first = block % 6 * CLIP_ROWS
            part = refs.mods[block // 12, block // 6 % 2, first : first + CLIP_ROWS, :]
            refs.mod[window, which : which + 1, column * LANES : (column + 1) * LANES] = jnp.sum(
                part * refs.member[window], axis=0, keepdims=True
            )
    enter_norm(refs)
    tick()
    tables = [
        small(refs.table.at[z, x, c], refs.table.at[z, x, c], place.shifted(*change))
        for change in ALONG_ZX
    ]
    work.arrive(QKV, 4)
    enter_unit(refs, 0, refs.held.at[QKV])
    tick()
    work.arrive(QKV + 1, 4)
    enter_unit(refs, 1, refs.held.at[QKV + 1])
    tick()
    for copy in tables:
        copy.wait()
    last = small(refs.table.at[:, :, c], refs.table.at[:, :, c], place.at(c=1 - c))
    work.arrive(QKV + 2, 4)
    enter_unit(refs, 2, refs.held.at[QKV + 2])
    last.wait()
    work.finish()


def attend_kernel(refs):
    work = None
    step = pl.program_id(0)
    if hasattr(refs, "gather"):
        place = Place()
        work = Gather(place, refs.held, gather_stages(ATTEND.values()), refs.gather)
        for at, stages in ATTEND.items():

            @pl.when(step == at)
            def _(at=at, stages=stages):
                if at == 0:
                    place.greet()
                for index, stage in stages:
                    work.advance(ORDER[index], stage)

    for head in range(2):
        spread = refs.table[head].astype(F32)
        for frame in range(FRAMES):
            block = spread[frame * WSIDE : (frame + 1) * WSIDE]
            for row in range(WSIDE):
                first = (WSIDE - 1 - row) * WSIDE
                refs.strip[
                    head, row * WSIDE : (row + 1) * WSIDE, frame * CELLS : (frame + 1) * CELLS
                ] = block[:, first : first + CELLS]
        for frame in range(WT):
            first = (WT - 1 - frame) * CELLS
            refs.bias[head, frame * CELLS : (frame + 1) * CELLS, :] = refs.strip[
                head, :, first : first + WIN
            ]

    for window in range(refs.live.shape[0]):
        rows = slice(window * WIN, (window + 1) * WIN)
        live = refs.live[window] * CELLS
        key_live = lax.broadcasted_iota(jnp.int32, (1, WIN), 1) < live
        for head in range(2):
            lanes = slice(head * HD, (head + 1) * HD)
            query = refs.query[rows, lanes] * BF16(HD ** (-0.5))
            scores = dot_rows(query, refs.key[rows, lanes]) + refs.bias[head]
            scores = jnp.where(key_live, scores, NEGATIVE)
            shifted = jnp.exp(scores - jnp.max(scores, axis=-1, keepdims=True))
            totals = jnp.sum(shifted, axis=-1, keepdims=True)
            probs = (shifted * (1.0 / totals)).astype(BF16)
            refs.probs[window, head] = probs
            refs.mixed[rows, lanes] = dot(probs, refs.value[rows, lanes]).astype(BF16)

    if work is not None:

        @pl.when(step == 7)
        def _():
            work.finish()


def packed_block(part, rows):
    pairs = H // 2
    return pl.BlockSpec(
        (None, rows, LANES),
        lambda pair: (
            lax.rem(part * pairs + pair, 3),
            0,
            lax.div(part * pairs + pair, 3),
        ),
    )


def attend_back_pair(refs, pair):
    scale = BF16(HD ** (-0.5))
    refs.spread[...] = jnp.zeros_like(refs.spread)
    refs.strip[...] = jnp.zeros_like(refs.strip)
    windows = refs.probs.shape[0]
    results = [[[None] * windows for _ in range(2)] for _ in range(3)]
    for head in range(2):
        lanes = slice(head * HD, (head + 1) * HD)
        bias = None
        for window in range(windows):
            rows = slice(window * WIN, (window + 1) * WIN)
            grad = refs.grad[rows, lanes]
            probs = refs.probs[window, head]
            results[2][head][window] = dot_tokens(grad, probs).T.astype(BF16)
            grad_probs = dot_rows(grad, refs.value[rows, lanes])
            weight = probs.astype(F32)
            product = weight * grad_probs
            total = jnp.sum(product, axis=-1, keepdims=True)
            grad_scores = (product - weight * total).astype(BF16)
            wide = grad_scores.astype(F32)
            bias = wide if bias is None else bias + wide
            results[0][head][window] = dot(grad_scores, refs.key[rows, lanes] * scale).astype(BF16)
            query = refs.query[rows, lanes] * scale
            results[1][head][window] = dot_tokens(query, grad_scores).T.astype(BF16)
        for frame in range(WT):
            first = (WT - 1 - frame) * CELLS
            refs.strip[head, :, first : first + WIN] += bias[frame * CELLS : (frame + 1) * CELLS]
        for frame in range(FRAMES):
            for row in range(WSIDE):
                first = (WSIDE - 1 - row) * WSIDE
                refs.spread[
                    head, frame * WSIDE : (frame + 1) * WSIDE, first : first + CELLS
                ] += refs.strip[
                    head, row * WSIDE : (row + 1) * WSIDE, frame * CELLS : (frame + 1) * CELLS
                ]
    for part in range(3):
        block = part * (H // 2) + pair
        lanes = pl.ds(pl.multiple_of(lax.div(block, 3) * LANES, LANES), LANES)
        for window in range(windows):
            rows = slice(window * WIN, (window + 1) * WIN)
            both = [results[part][head][window] for head in range(2)]
            refs.grad_packed[lax.rem(block, 3), rows, lanes] = jnp.concatenate(both, axis=1)


def middle_kernel(refs):
    order = [OUT] + [unit for j in range(4) for unit in (UP + j, DOWN + j)] + [OUT]
    gathering = reducing = None
    points = {}
    waiting = set()
    if hasattr(refs, "gather"):
        place = Place()
        place.greet()
        gathering = Gather(place, refs.held_out, gather_stages(MIDDLE.values()), refs.gather)

        def buffers(unit):
            index = EARLY.index(unit)
            core, side = refs.core.at[index], refs.side.at[index]
            if unit in REDUCE_ASIDE:
                return core, side, None, refs.aside.at[0]
            if unit not in DONE:
                return core, side, None, None
            return core, side, refs.corner.at[index], refs.distant.at[index]

        def store(unit, part, values):
            at = pl.ds(pl.multiple_of(part * HALF, HALF), HALF)
            refs.total[DONE.index(unit), at, :] = values

        reducing = Reduce(
            place, lambda unit: refs.part.at[unit], EARLY_POINTS, store, buffers, refs.reduce
        )
        for stages in MIDDLE.values():
            waiting |= {ORDER[index] for index, stage in stages if stage == 4}
        points = {at: list(moves) for at, moves in EARLY_POINTS.items()}

    held = refs.held_out if gathering is not None else refs.held
    count = [0]

    def pump():
        for index, stage in MIDDLE.get(count[0], ()) if gathering is not None else ():
            gathering.advance(ORDER[index], stage)
            if stage == 4:
                waiting.discard(ORDER[index])
        for unit, stage in points.pop(count[0], ()):
            reducing.step(unit, stage)
        count[0] += 1

    def fetch(step):
        return pltpu.make_async_copy(
            held.at[order[step]], refs.unit.at[step % 4], refs.fetch.at[step % 4]
        )

    def start_fetch(step):
        if gathering is not None:
            assert order[step] not in waiting
            gathering.arrive(order[step], 4)
        fetch(step).start()

    def put(slot, unit):
        return pltpu.make_async_copy(refs.made.at[slot], refs.part.at[unit], refs.made_sem.at[slot])

    for step in range(3):
        start_fetch(step)
    pump()
    refs.sums[...] = jnp.zeros_like(refs.sums)
    refs.mlp[...] = jnp.zeros_like(refs.mlp)
    refs.grad_normed[...] = jnp.zeros_like(refs.grad_normed)
    fetch(0).wait()

    def project(index):
        refs.attended[:, half(index)] = dot(refs.mixed[...], four_columns(refs.unit.at[0], index))

    loop(2, project)
    pump()

    def modulate(window, at, mods, live):
        middle = refs.tokens[at, :].astype(F32) + mods[2] * refs.attended[at, :]
        normal, _ = centered(middle)
        refs.normed[at, :] = (normal * (1.0 + mods[4]) + mods[3]).astype(BF16)
        grad = jnp.where(live, refs.cotangent[at, :].astype(F32), 0.0)
        refs.grad_low[at, :] = (mods[5] * grad).astype(BF16)

    each_rows(refs.mod, refs.live, modulate)
    pump()
    for j in range(4):
        step = 1 + 2 * j
        up, down = refs.unit.at[step % 4], refs.unit.at[(step + 1) % 4]
        fetch(step).wait()
        fetch(step + 1).wait()
        start_fetch(step + 2)

        def hide(index, up=up, down=down):
            hidden = dot(refs.normed[...], four_columns(up, index))
            bend = jnp.tanh(0.7978845608028654 * (hidden + 0.044715 * hidden * hidden * hidden))
            refs.activated[:, half(index)] = (0.5 * hidden * (1.0 + bend)).astype(BF16)
            slope = 0.5 * (1.0 + bend) + 0.5 * hidden * (1.0 - bend * bend) * (
                0.7978845608028654 * (1.0 + 3.0 * 0.044715 * hidden * hidden)
            )
            grad_activated = dot_rows(refs.grad_low[...], half_rows(down, index))
            refs.grad_hidden[:, half(index)] = (grad_activated * slope).astype(BF16)

        loop(2, hide)
        if j > 0:
            put(1, UP + j - 1).wait()
        pump()

        def down_gradient(index):
            made = dot_tokens(refs.activated[:, half(index)], refs.grad_low[...]).astype(BF16)
            for block in range(8):
                refs.made[0, block // 2, block % 2, index] = made[
                    :, block * LANES : (block + 1) * LANES
                ].reshape(2, SHARE, LANES)

        loop(2, down_gradient)
        put(0, DOWN + j).start()
        pump()

        def up_gradient(index):
            made = dot_tokens(refs.normed[...], refs.grad_hidden[:, half(index)]).astype(BF16)
            put_columns(refs.made.at[1], index, made)

        loop(2, up_gradient)
        put(0, DOWN + j).wait()
        put(1, UP + j).start()
        pump()
        if j < 3:
            start_fetch(step + 3)

        def out_of_mlp(index, up=up, down=down):
            refs.mlp[:, half(index)] += dot(refs.activated[...], four_columns(down, index))
            refs.grad_normed[:, half(index)] += dot_rows(
                refs.grad_hidden[...], half_rows(up, index)
            )

        loop(2, out_of_mlp)
        pump()

    put(1, UP + 3).wait()

    def join(window, at, mods, live):
        attended = refs.attended[at, :]
        middle = refs.tokens[at, :].astype(F32) + mods[2] * attended
        normal, root = centered(middle)
        mlp = refs.mlp[at, :]
        refs.output[at, :] = jnp.where(live, middle + mods[5] * mlp, 0.0).astype(BF16)
        grad_result = jnp.where(live, refs.cotangent[at, :].astype(F32), 0.0)
        grad_normed = refs.grad_normed[at, :]
        grad_middle = grad_result + norm_back(grad_normed, normal, root, mods[4])
        refs.grad_middle[at, :] = grad_middle
        refs.grad_low[at, :] = (mods[2] * grad_middle).astype(BF16)
        add_sums(refs.sums, window, 2, grad_middle * attended)
        add_sums(refs.sums, window, 3, grad_normed)
        add_sums(refs.sums, window, 4, grad_normed * normal)
        add_sums(refs.sums, window, 5, grad_result * mlp)

    each_rows(refs.mod, refs.live, join)
    pump()
    fetch(9).wait()

    def back(index):
        made = dot_tokens(refs.mixed[...], refs.grad_low[:, half(index)]).astype(BF16)
        put_columns(refs.made.at[0], index, made)
        refs.grad_mixed[:, half(index)] = dot_rows(
            refs.grad_low[...], half_rows(refs.unit.at[1], index)
        ).astype(BF16)

    loop(2, back)
    put(0, OUT).start()
    put(0, OUT).wait()
    while points:
        pump()
    if gathering is not None:
        gathering.finish()
        reducing.sent()


def leave_weight(refs, j, made):
    def weight(index):
        grad = dot_tokens(refs.normed[...], refs.grad_packed[j, :, half(index)]).astype(BF16)
        put_columns(made, index, grad)

    loop(2, weight)


def leave_back(refs, j):
    def back(index):
        refs.grad_normed[:, half(index)] += dot_rows(
            refs.grad_packed[j], half_rows(refs.unit, index)
        )

    loop(2, back)


def leave_norm(refs, pump=lambda window: None):
    def join(window, at, mods, live):
        normal, root = centered(refs.tokens[at, :].astype(F32))
        grad_normed = refs.grad_normed[at, :]
        refs.grad_tokens[at, :] = refs.grad_middle[at, :] + norm_back(
            grad_normed, normal, root, mods[1]
        )
        add_sums(refs.sums, window, 0, grad_normed)
        add_sums(refs.sums, window, 1, grad_normed * normal)

    each_rows(refs.mod, refs.live, join, pump=pump)


def back_plain_kernel(refs):
    step = pl.program_id(0)

    @pl.when(step < H // 2)
    def _():
        attend_back_pair(refs, jnp.minimum(step, H // 2 - 1))

    @pl.when(step == H // 2)
    def _():
        refs.sums[...] = jnp.zeros_like(refs.sums)
        refs.grad_normed[...] = jnp.zeros_like(refs.grad_normed)
        for j in range(3):
            fetch = pltpu.make_async_copy(refs.held.at[QKV + j], refs.unit, refs.fetch)
            fetch.start()
            leave_weight(refs, j, refs.made)
            put = pltpu.make_async_copy(refs.made, refs.part.at[j], refs.made_sem)
            put.start()
            fetch.wait()
            leave_back(refs, j)
            put.wait()
        leave_norm(refs)


def fold_spreads(refs):
    heads = H * WIDE // WSIDE
    shape_of = (WSIDE * LANES, TILE)
    place = lax.broadcasted_iota(jnp.int32, shape_of, 0)
    offset = lax.broadcasted_iota(jnp.int32, shape_of, 1)
    own, row, other = place // LANES, place // WSIDE % (LANES // WSIDE), place % WSIDE
    side_span = 2 * WSIDE - 1
    row_diff, col_diff = side_span - 1 - row, own - other + (WSIDE - 1)
    same = (row < side_span) & (row_diff * side_span + col_diff == offset)
    onto = jnp.where(same, 1.0, 0.0).astype(BF16)
    left = jnp.concatenate(
        [refs.spreads[pl.ds(own, heads, stride=WSIDE), :] for own in range(WSIDE)], axis=1
    )
    total = jnp.zeros((heads, TILE), F32)
    for _ in range(3):
        low = left.astype(BF16)
        total = total + dot(low, onto)
        left = left - low.astype(F32)
    rows = 2 * WIDE // WSIDE
    for block in range(8):
        refs.table[block // 2, block % 2] = total[block * rows : (block + 1) * rows]


def back_kernel(refs):
    place = Place()
    z, x, y, c = place.z, place.x, place.y, place.c
    step = pl.program_id(0)

    def buffers(unit):
        every = (EARLY + LATE).index(unit)
        late = every - len(EARLY)
        if late < 0:
            core, side = None, refs.side_in.at[every]
        else:
            core, side = refs.core.at[late], refs.side.at[late]
        if unit in REDUCE_ASIDE:
            return core, side, None, refs.aside.at[0]
        return core, side, refs.corner.at[every], refs.distant.at[every]

    def store(unit, part, values):
        if unit >= DOWN:
            first = part * 512 + (unit - DOWN) * LANES
            refs.grad_down[pl.ds(pl.multiple_of(first, LANES), LANES), :] = values
            return
        target, start = (
            (refs.grad_qkv, QKV)
            if unit < OUT
            else (refs.grad_out, OUT)
            if unit < UP
            else (refs.grad_up, UP)
        )
        column = (unit - start) * LANES
        target[pl.ds(pl.multiple_of(part * HALF, HALF), HALF), column : column + LANES] = values

    work = Reduce(
        place,
        lambda unit: refs.made.at[unit] if unit < OUT else refs.part.at[unit],
        LATE_POINTS,
        store,
        buffers,
        refs.reduce,
    )
    small = Copies(*refs.small)

    events = [(at, move) for at in sorted(LATE_POINTS) for move in LATE_POINTS[at]]

    def run(until):
        while events and events[0][0] < until:
            work.step(*events.pop(0)[1])

    for number in range(H // 2):

        @pl.when(step == number)
        def _(number=number):
            if number == 0:
                place.greet(EVERYONE)
            run(number + 1)

    @pl.when(step < H // 2)
    def _():
        pair = jnp.minimum(step, H // 2 - 1)
        attend_back_pair(refs, pair)
        for head in range(2):
            at = pl.ds(pl.multiple_of((pair * 2 + head) * WIDE, WIDE), WIDE)
            refs.spreads[at, :] = refs.spread[head]

    @pl.when(step == H // 2)
    def _():
        for index, unit in enumerate(DONE):
            for part in range(2):
                store(unit, part, refs.done[index, part * HALF : (part + 1) * HALF, :])
        fold_spreads(refs)
        table = []
        for dz, dx, dy, dc in ALONG_ZX:
            source = refs.table.at[place.far(dz), 1 - x if dx else x]
            table.append(small(source, refs.table_zx.at[z, x], place.shifted(dz, dx, dy, dc)))
        refs.table_zx[z, x] = refs.table[z, x]
        refs.sums[...] = refs.late_sums[...]
        refs.grad_normed[...] = jnp.zeros_like(refs.grad_normed)

        def fetch(j):
            return pltpu.make_async_copy(refs.held.at[QKV + j], refs.unit, refs.fetch)

        fetch(0).start()
        run(9)
        leave_weight(refs, 0, refs.made.at[0])
        run(10)
        leave_weight(refs, 1, refs.made.at[1])
        run(11)
        leave_weight(refs, 2, refs.made.at[2])
        run(12)
        fetch(0).wait()
        leave_back(refs, 0)
        fetch(1).start()
        run(13)
        fetch(1).wait()
        leave_back(refs, 1)
        fetch(2).start()
        run(14)
        fetch(2).wait()
        leave_back(refs, 2)
        run(15)
        leave_norm(refs, lambda window: run(17 + window))
        for copy in table:
            copy.wait()
        total = refs.table_zx[0, 0]
        for block in range(1, 8):
            total = total + refs.table_zx[block // 2, block % 2]
        refs.table_own[...] = total
        refs.table_yc[y, c] = total
        table = [
            small(refs.table_own, refs.table_yc.at[y, c], place.shifted(*change))
            for change in ALONG_YC
        ]
        for block in range(48):
            which, column = divmod(block, 8)
            part = jnp.zeros((CLIP_ROWS, LANES), F32)
            for window in range(refs.mod.shape[0]):
                sums = refs.sums[window, which : which + 1, column * LANES : (column + 1) * LANES]
                part = part + refs.member[window] * sums
            first = block % 6 * CLIP_ROWS
            refs.clip[block // 12, block // 6 % 2, first : first + CLIP_ROWS, :] = part
        copies = []
        for dz, dx, dy, dc in ALONG_ZX:
            source = refs.clip.at[place.far(dz), 1 - x if dx else x]
            copies.append(small(source, refs.clip_zx.at[z, x], place.shifted(dz, dx, dy, dc)))
        refs.clip_zx[z, x] = refs.clip[z, x]
        run(19)
        for copy in copies:
            copy.wait()
        total = refs.clip_zx[0, 0]
        for block in range(1, 8):
            total = total + refs.clip_zx[block // 2, block % 2]
        refs.clip_own[...] = total
        refs.clip_yc[y, c] = total
        copies = [
            small(refs.clip_own, refs.clip_yc.at[y, c], place.shifted(*change))
            for change in ALONG_YC
        ]
        run(21)
        for copy in copies:
            copy.wait()
        total = refs.clip_yc[0, 0] + refs.clip_yc[0, 1] + refs.clip_yc[1, 0] + refs.clip_yc[1, 1]
        total = jnp.concatenate([total, jnp.zeros((8, LANES), F32)], axis=0)
        cond = jnp.zeros((8, SHARE), F32)
        lows = []
        for block in range(6):
            lows.append(total[block * CLIP_ROWS : block * CLIP_ROWS + 8].astype(BF16))
            lanes = slice(block * LANES, (block + 1) * LANES)
            cond = cond + dot_rows(lows[-1], refs.ada[:, lanes])
        clips = refs.condition.shape[0]
        refs.cond_own[...] = jnp.zeros_like(refs.cond_own)
        for row in range(2 * clips):
            clip, side = divmod(row, 2)
            refs.cond_own[row : row + 1, :] = cond[
                clip : clip + 1, side * LANES : (side + 1) * LANES
            ]
        refs.cond_all[z, x, y, c] = refs.cond_own[...]
        copies = [
            small(refs.cond_own, refs.cond_all.at[z, x, y, c], place.shifted(*change))
            for change in EVERYONE
        ]
        for block, low in enumerate(lows):
            lanes = slice(block * LANES, (block + 1) * LANES)
            refs.grad_ada[:, lanes] = dot_tokens(act_rows(refs, place), low)
            refs.grad_bias[block : block + 1, :] = jnp.sum(
                low[:CLIP_ROWS].astype(F32), axis=0, keepdims=True
            )
        run(23)
        for copy in table:
            copy.wait()
        total = refs.table_yc[0, 0] + refs.table_yc[0, 1] + refs.table_yc[1, 0] + refs.table_yc[1, 1]
        for head in range(2):
            for frame in range(FRAMES):
                first = (FRAMES - 1 - frame) * OFFSETS
                row = head * (WIDE // WSIDE) + frame
                refs.table_total[head : head + 1, first : first + OFFSETS] = total[
                    row : row + 1, :OFFSETS
                ]
        run(100)
        for copy in copies:
            copy.wait()
        for block in range(4):
            total = refs.cond_all[0, 0, block // 2, block % 2]
            for other in range(1, 8):
                total = total + refs.cond_all[other // 2, other % 2, block // 2, block % 2]
            for row in range(2 * clips):
                clip, side = divmod(row, 2)
                first = block * SHARE + side * LANES
                value = refs.condition[clip : clip + 1, first : first + LANES]
                gate = 1.0 / (1.0 + jnp.exp(-value))
                refs.grad_condition[clip : clip + 1, first : first + LANES] = (
                    total[row : row + 1] * gate * (1.0 + value * (1.0 - gate))
                )
        work.sent()


def enter(special, tokens, held, mod, own, smalls):
    rows = tokens.shape[0]
    windows = rows // WIN
    inputs = {"tokens": (tokens, vmem())}
    outputs = {
        "normed": (shape(BF16, rows, D), vmem()),
        "packed": (shape(BF16, 3, rows, D), vmem()),
    }
    scratch = {"unit": pltpu.VMEM(SPLIT, BF16), "fetch": pltpu.SemaphoreType.DMA}
    if not special:
        inputs |= {"held": (held, anywhere()), "mod": (mod, vmem())}
        out = call(enter_plain_kernel, "enter_plain", inputs, outputs, scratch)
        out.mod, out.held = mod, held
        return out
    for name, block in zip(("qkv", "out", "up", "down"), own, strict=True):
        inputs[name] = (block, vmem())
    for name, array in zip(("condition", "ada", "bias", "rel_table"), smalls[1:], strict=True):
        inputs[name] = (array, vmem())
    inputs["frames"] = (smalls[0], smem())
    outputs |= {
        "held": (shape(BF16, UNITS, *SPLIT), anywhere()),
        "mod": (shape(F32, windows, 8, D), vmem()),
        "table": (shape(BF16, 4, 2, 2, SPREAD, LANES), vmem()),
        "member": (shape(F32, windows, CLIP_ROWS, LANES), vmem()),
        "live": (shape(jnp.int32, windows), smem()),
    }
    scratch |= {
        "own": pltpu.VMEM((UNITS, SHARE, LANES), BF16),
        "own_sem": pltpu.SemaphoreType.DMA((UNITS,)),
        "gather": Gather.semaphores(gather_stages(ENTER)),
        "small": [pltpu.SemaphoreType.DMA((18,))] * 2,
        "mod_part": pltpu.VMEM((MOD_ROWS, LANES), F32),
        "mod_parts": pltpu.VMEM((2, 2, MOD_ROWS, LANES), F32),
        "mods": pltpu.VMEM((4, 2, MOD_ROWS, LANES), F32),
        "rows": pltpu.VMEM((24, TILE), F32),
        "spread": pltpu.VMEM((2 * SPREAD, LANES), F32),
        "table_own": pltpu.VMEM((2, SPREAD, LANES), BF16),
    }
    return call(enter_kernel, "enter", inputs, outputs, scratch, collective=0)


def deliver_kernel(refs):
    names = [name for name in vars(refs) if name.startswith("from_")]
    loads, stores = [], []
    for index, name in enumerate(names):
        plain = name[len("from_") :]
        held = getattr(refs, "held_" + plain)
        loads.append(pltpu.make_async_copy(getattr(refs, name), held, refs.sems.at[0, index]))
        stores.append(pltpu.make_async_copy(held, getattr(refs, plain), refs.sems.at[1, index]))
        loads[-1].start()
    for load, store in zip(loads, stores, strict=True):
        load.wait()
        store.start()
    for store in stores:
        store.wait()


def deliver(**arrays):
    inputs = {"from_" + name: (array, anywhere()) for name, array in arrays.items()}
    outputs = {name: (shape(array.dtype, *array.shape), anywhere()) for name, array in arrays.items()}
    scratch = {"held_" + name: pltpu.VMEM(array.shape, array.dtype) for name, array in arrays.items()}
    scratch["sems"] = pltpu.SemaphoreType.DMA((2, len(arrays)))
    return call(deliver_kernel, "deliver", inputs, outputs, scratch)


def attend(special, packed, table, live_frames, held):
    window_count = live_frames.shape[0]
    rows = window_count * WIN
    inputs = {
        "live": (live_frames, smem()),
        "query": (packed, packed_block(0, rows)),
        "key": (packed, packed_block(1, rows)),
        "value": (packed, packed_block(2, rows)),
        "table": (table, pl.BlockSpec((2, SPREAD, LANES), lambda p: (p, 0, 0))),
    }
    outputs = {
        "mixed": (shape(BF16, rows, D), pl.BlockSpec((rows, LANES), lambda p: (0, p))),
        "probs": (
            shape(BF16, window_count, H, WIN, WIN),
            pl.BlockSpec((window_count, 2, WIN, WIN), lambda p: (0, p, 0, 0)),
        ),
    }
    scratch = {
        "strip": pltpu.VMEM((2, CELLS, STRIP), F32),
        "bias": pltpu.VMEM((2, WIN, WIN), F32),
    }
    aliases, collective = (), None
    if special:
        inputs["held_in"] = (held, anywhere())
        outputs["held"] = (shape(BF16, UNITS, *SPLIT), anywhere())
        scratch["gather"] = Gather.semaphores(gather_stages(ATTEND.values()))
        aliases, collective = (("held_in", "held"),), 1
    out = call(
        attend_kernel,
        "attend",
        inputs,
        outputs,
        scratch,
        aliases,
        collective,
        grid=(H // 2,),
        limit=60,
    )
    if not special:
        out.held = held
    return out


def middle(special, live_frames, tokens, cotangent, mixed, mod, held):
    rows = tokens.shape[0]
    inputs = {
        "live": (live_frames, smem()),
        "tokens": (tokens, vmem()),
        "cotangent": (cotangent, vmem()),
        "mixed": (mixed, vmem()),
        "mod": (mod, vmem()),
        "held": (held, anywhere()),
    }
    outputs = {
        "output": (shape(BF16, rows, D), vmem()),
        "grad_middle": (shape(F32, rows, D), vmem()),
        "grad_mixed": (shape(BF16, rows, D), vmem()),
        "sums": (shape(F32, mod.shape[0], 8, D), vmem()),
        "part": (shape(BF16, UNITS, *SPLIT), anywhere()),
    }
    scratch = {
        "unit": pltpu.VMEM((4, *SPLIT), BF16),
        "attended": pltpu.VMEM((rows, D), F32),
        "normed": pltpu.VMEM((rows, D), BF16),
        "grad_low": pltpu.VMEM((rows, D), BF16),
        "mlp": pltpu.VMEM((rows, D), F32),
        "grad_normed": pltpu.VMEM((rows, D), F32),
        "activated": pltpu.VMEM((rows, D), BF16),
        "grad_hidden": pltpu.VMEM((rows, D), BF16),
        "made": pltpu.VMEM((2, *SPLIT), BF16),
        "fetch": pltpu.SemaphoreType.DMA((4,)),
        "made_sem": pltpu.SemaphoreType.DMA((2,)),
    }
    aliases, collective = (), None
    if special:
        outputs["held_out"] = (shape(BF16, UNITS, *SPLIT), anywhere())
        outputs["side"] = (shape(BF16, *Reduce.side_shape(len(EARLY))), vmem())
        scratch["gather"] = Gather.semaphores(gather_stages(MIDDLE.values()))
        outputs["total"] = (shape(F32, len(DONE), SHARE, LANES), vmem())
        scratch["core"] = pltpu.VMEM(Reduce.core_shape(len(EARLY)), BF16)
        scratch["corner"] = pltpu.VMEM(Reduce.corner_shape(len(DONE)), BF16)
        scratch["distant"] = pltpu.VMEM(Reduce.distant_shape(len(DONE)), BF16)
        scratch["aside"] = pltpu.VMEM(Reduce.aside_shape(1), BF16)
        scratch["reduce"] = Reduce.scratch(EARLY_POINTS)
        aliases, collective = (("held", "held_out"),), 2
    return call(middle_kernel, "middle", inputs, outputs, scratch, aliases, collective, limit=60)


def back(
    special, live_frames, tokens, mod, start, probs, mid, held, ada, member, condition
):
    window_count = probs.shape[0]
    rows = window_count * WIN
    pairs = H // 2

    def last(pair):
        return jnp.minimum(pair, pairs - 1)

    def whole(array):
        return pl.BlockSpec(array.shape, lambda p: (0,) * len(array.shape), pipeline_mode=pl.Buffered(1))

    def packed_pair(part):
        block = packed_block(part, rows)
        return pl.BlockSpec(block.block_shape, lambda p: block.index_map(last(p)))

    inputs = {
        "live": (live_frames, smem()),
        "query": (start.packed, packed_pair(0)),
        "key": (start.packed, packed_pair(1)),
        "value": (start.packed, packed_pair(2)),
        "probs": (
            probs,
            pl.BlockSpec((window_count, 2, WIN, WIN), lambda p: (0, last(p), 0, 0)),
        ),
        "grad": (mid.grad_mixed, pl.BlockSpec((rows, LANES), lambda p: (0, last(p)))),
        "held": (held, anywhere()),
    }
    for name, array in (
        ("tokens", tokens),
        ("mod", mod),
        ("normed", start.normed),
        ("grad_middle", mid.grad_middle),
    ):
        inputs[name] = (array, whole(array))

    def result(*sizes):
        made = shape(F32, *sizes)
        return made, whole(made)

    outputs = {"grad_tokens": result(rows, D)}
    scratch = {
        "strip": pltpu.VMEM((2, CELLS, STRIP), F32),
        "grad_packed": pltpu.VMEM((3, rows, D), BF16),
        "unit": pltpu.VMEM(SPLIT, BF16),
        "grad_normed": pltpu.VMEM((rows, D), F32),
        "fetch": pltpu.SemaphoreType.DMA,
    }
    if not special:
        outputs["sums"] = result(window_count, 8, D)
        outputs["part"] = (shape(BF16, 3, *SPLIT), anywhere())
        outputs["spread"] = (
            shape(F32, H, SPREAD, LANES),
            pl.BlockSpec((2, SPREAD, LANES), lambda p: (last(p), 0, 0)),
        )
        scratch["made"] = pltpu.VMEM(SPLIT, BF16)
        scratch["made_sem"] = pltpu.SemaphoreType.DMA
        return call(
            back_plain_kernel, "back_plain", inputs, outputs, scratch, grid=(pairs + 1,)
        )
    inputs |= {
        "late_sums": (mid.sums, whole(mid.sums)),
        "ada": (ada, whole(ada)),
        "condition": (condition, whole(condition)),
        "member": (member, whole(member)),
        "side_in": (mid.side, whole(mid.side)),
        "done": (mid.total, whole(mid.total)),
        "part": (mid.part, anywhere()),
    }
    outputs |= {
        "grad_qkv": result(SHARE, 3 * LANES),
        "grad_out": result(SHARE, LANES),
        "grad_up": result(SHARE, 4 * LANES),
        "grad_down": result(4 * SHARE, LANES),
        "grad_ada": result(SHARE, 6 * LANES),
        "grad_bias": result(6, LANES),
        "grad_condition": result(*condition.shape),
        "table_total": result(2, REL),
    }
    count, late = len(EARLY + LATE), len(LATE)
    scratch |= {
        "spread": pltpu.VMEM((2, WIDE, LANES), F32),
        "spreads": pltpu.VMEM((H * WIDE, LANES), F32),
        "made": pltpu.VMEM((3, *SPLIT), BF16),
        "sums": pltpu.VMEM((window_count, 8, D), F32),
        "core": pltpu.VMEM(Reduce.core_shape(late), BF16),
        "side": pltpu.VMEM(Reduce.side_shape(late), BF16),
        "corner": pltpu.VMEM(Reduce.corner_shape(count), BF16),
        "distant": pltpu.VMEM(Reduce.distant_shape(count), BF16),
        "aside": pltpu.VMEM(Reduce.aside_shape(1), BF16),
        "reduce": Reduce.scratch(LATE_POINTS),
        "table": pltpu.VMEM((4, 2, 2 * WIDE // WSIDE, TILE), F32),
        "table_zx": pltpu.VMEM((4, 2, 2 * WIDE // WSIDE, TILE), F32),
        "table_own": pltpu.VMEM((2 * WIDE // WSIDE, TILE), F32),
        "table_yc": pltpu.VMEM((2, 2, 2 * WIDE // WSIDE, TILE), F32),
        "clip": pltpu.VMEM((4, 2, MOD_ROWS, LANES), F32),
        "clip_zx": pltpu.VMEM((4, 2, MOD_ROWS, LANES), F32),
        "clip_own": pltpu.VMEM((MOD_ROWS, LANES), F32),
        "clip_yc": pltpu.VMEM((2, 2, MOD_ROWS, LANES), F32),
        "cond_own": pltpu.VMEM((8, LANES), F32),
        "cond_all": pltpu.VMEM((4, 2, 2, 2, 8, LANES), F32),
        "small": [pltpu.SemaphoreType.DMA((51,))] * 2,
    }
    return call(
        back_kernel,
        "back",
        inputs,
        outputs,
        scratch,
        collective=3,
        grid=(pairs + 1,),
        limit=62,
    )


def per_device(
    special,
    tokens,
    condition,
    clip_frames,
    ada_weight,
    ada_bias,
    qkv_weight,
    out_weight,
    up_weight,
    down_weight,
    rel_table,
    cotangent,
):
    window_count = tokens.shape[0]
    clip_count = condition.shape[0]
    rows_ada, cols_ada = ada_weight.shape
    token_rows = tokens.reshape(window_count * WIN, D)
    cotangent_rows = cotangent.reshape(window_count * WIN, D)
    own = (qkv_weight, out_weight, up_weight, down_weight)
    if special:
        smalls = (clip_frames, condition, ada_weight, ada_bias.reshape(1, cols_ada), rel_table)
        start = enter(True, token_rows, None, None, own, smalls)
        table = start.table.reshape(H, SPREAD, LANES)
        live_frames, member_wide = start.live, start.member
    else:
        row_block = lax.axis_index("fsdp")
        col_block = lax.axis_index("dp")
        first_window = lax.axis_index(("dp", "fsdp")) * window_count
        live_frames, member_int = window_layout(clip_frames, first_window, window_count)
        member = member_int.astype(F32)
        activity_low = jax.nn.silu(condition).astype(BF16)
        rows_own = lax.dynamic_slice_in_dim(activity_low, row_block * rows_ada, rows_ada, 1)
        mod_part = jnp.dot(rows_own, ada_weight, preferred_element_type=F32)
        clip_mod = lax.all_gather(lax.psum(mod_part, "fsdp"), "dp", axis=1, tiled=True)
        bias = lax.all_gather(ada_bias, "dp", axis=0, tiled=True)
        clip_mod = clip_mod + bias.astype(F32)[None, :]
        member_wide = None
        window_mod = jnp.sum(member[:, :, None] * clip_mod[None], axis=1)
        window_mod = jnp.pad(window_mod.reshape(window_count, 6, D), ((0, 0), (0, 2), (0, 0)))
        whole = [
            lax.all_gather(
                lax.all_gather(weight, "dp", axis=1, tiled=True), "fsdp", axis=0, tiled=True
            )
            for weight in own
        ]
        held = units_of(*whole).reshape(UNITS, *SPLIT)
        start = enter(False, token_rows, held, window_mod, None, None)
        table = spread_table(lax.all_gather(rel_table, "dp", axis=0, tiled=True))
    mod = start.mod
    across = attend(special, start.packed, table, live_frames, start.held)
    mid = middle(
        special, live_frames, token_rows, cotangent_rows, across.mixed, mod, across.held
    )
    held = mid.held_out if special else across.held
    end = back(
        special,
        live_frames,
        token_rows,
        mod,
        start,
        across.probs,
        mid,
        held,
        ada_weight,
        member_wide,
        condition,
    )
    if special:
        end = deliver(
            output=mid.output,
            grad_tokens=end.grad_tokens,
            grad_condition=end.grad_condition,
            grad_ada=end.grad_ada,
            grad_bias=end.grad_bias,
            grad_qkv=end.grad_qkv,
            grad_out=end.grad_out,
            grad_up=end.grad_up,
            grad_down=end.grad_down,
            table=end.table_total,
        )
        return (
            end.output.reshape(tokens.shape),
            end.grad_tokens.reshape(tokens.shape),
            end.grad_condition,
            end.grad_ada,
            end.grad_bias.reshape(cols_ada),
            end.grad_qkv,
            end.grad_out,
            end.grad_up,
            end.grad_down,
            end.table,
        )
    part = jnp.concatenate([end.part, mid.part[OUT:]])
    grads = [
        lax.psum_scatter(
            lax.psum_scatter(grad, "fsdp", scatter_dimension=0, tiled=True),
            "dp",
            scatter_dimension=1,
            tiled=True,
        ).astype(F32)
        for grad in weights_of(part.reshape(UNITS, 8, D, LANES))
    ]
    grad_mod = (mid.sums + end.sums)[:, :6].reshape(window_count, 6 * D)
    clip_part = lax.dot_general(
        member,
        grad_mod,
        (((0,), (0,)), ((), ())),
        precision=HIGHEST,
        preferred_element_type=F32,
    )
    clip_sum, table_sum = lax.psum((clip_part, gather_table(end.spread)), ("dp", "fsdp"))
    clip_cols = lax.dynamic_slice_in_dim(
        clip_sum.astype(BF16), col_block * cols_ada, cols_ada, 1
    )
    heads_own = rel_table.shape[0]
    table_grad = lax.dynamic_slice_in_dim(table_sum, col_block * heads_own, heads_own, 0)
    cond_part = lax.dot_general(
        clip_cols, ada_weight, (((1,), (1,)), ((), ())), preferred_element_type=F32
    )
    cond_total = lax.all_gather(lax.psum(cond_part, "dp"), "fsdp", axis=1, tiled=True)
    grad_ada_weight = lax.dot_general(
        rows_own, clip_cols, (((0,), (0,)), ((), ())), preferred_element_type=F32
    )
    grad_ada_bias = jnp.sum(clip_cols.astype(F32), axis=0)
    _, silu_back = jax.vjp(jax.nn.silu, condition)
    return (
        mid.output.reshape(tokens.shape),
        end.grad_tokens.reshape(tokens.shape),
        silu_back(cond_total)[0],
        grad_ada_weight,
        grad_ada_bias,
        *grads,
        table_grad,
    )


def solution(mesh):
    special = dict(mesh.shape) == {"dp": 8, "fsdp": 4}
    both = P(("dp", "fsdp"), None, None)
    weight = P("fsdp", "dp")
    in_specs = (both, P(), P(), weight, P("dp")) + (weight,) * 4 + (P("dp", None), both)
    out_specs = (both, both, P(), weight, P("dp")) + (weight,) * 4 + (P("dp", None),)
    return jax.shard_map(
        functools.partial(per_device, special),
        mesh=mesh,
        in_specs=in_specs,
        out_specs=out_specs,
        check_vma=False,
    )
```

```python
import functools

import jax
import jax.numpy as jnp
from jax import lax
from jax.experimental import pallas as pl
from jax.experimental.pallas import tpu as pltpu
from jax.sharding import PartitionSpec as P

D = 1024
H = 16
HD = 64
WT = 5
WSIDE = 8
WIN = 320
SPW = 16
CELLS = WSIDE * WSIDE
FRAMES = 2 * WT - 1
OFFSETS = (2 * WSIDE - 1) ** 2
REL = FRAMES * OFFSETS
LANES = 128
TILE = 256
SPREAD = 80
WIDE = 96
STRIP = 640

EPSILON = 1e-06
NEGATIVE = -1000000000.0
HIGHEST = lax.Precision.HIGHEST
F32 = jnp.float32
BF16 = jnp.bfloat16
MESH = pl.DeviceIdType.MESH
MIB = 2**20

QKV, OUT, UP, DOWN, UNITS = 0, 3, 4, 8, 12
PICK = (
    (1, 2, 0),
    (1, 2, 0),
    (0, 1, 2),
    (0, 1, 2),
    (0, 1, 2),
    (2, 0, 1),
    (2, 0, 1),
    (1, 0, 2),
)
SHARE = 256
HALF = 128


SPLIT = (4, 2, 2, 2, SHARE, LANES)
CLIP_ROWS = 4
MOD_ROWS = 6 * CLIP_ROWS
OWN_SLOTS = 4
ORDER = (0, 1, 2, 3, 4, 8, 5, 9, 6, 10, 7, 11)
GATHER_ASIDE = (DOWN + 3,)
REDUCE_ASIDE = (DOWN, UP + 2)
ENTER = (((0, 1), (11, 1), (1, 1), (0, 2)), ((2, 1), (11, 2), (0, 3), (1, 2), (4, 1), (3, 1)), ((5, 1), (0, 4), (2, 2), (1, 3)), ((4, 2), (2, 3), (6, 1)), ((8, 1), (3, 2), (4, 3)))
ATTEND = {0: ((7, 1), (10, 1)), 1: ((1, 4), (5, 2), (9, 1)), 2: ((3, 3), (6, 2)), 3: ((2, 4),), 4: ((5, 3),), 5: ((4, 4), (3, 4), (7, 2), (6, 3)), 7: ((8, 2), (11, 3), (5, 4))}
MIDDLE = {0: ((7, 3), (9, 2)), 1: ((6, 4),), 2: ((8, 3),), 3: ((7, 4), (10, 2)), 4: ((9, 3),), 6: ((8, 4), (10, 3)), 7: ((9, 4),), 9: ((10, 4),), 11: ((11, 4),)}
EARLY = (DOWN, UP, DOWN + 1, UP + 1, DOWN + 2)
DONE = EARLY[:4]
EARLY_POINTS = {6: ((8, 0),), 7: ((4, 0),), 8: ((8, 1),), 9: ((4, 1), (9, 0)), 10: ((9, 1),), 11: ((5, 0), (4, 2)), 13: ((5, 1),), 14: ((10, 0), (4, 3)), 15: ((9, 2),), 16: ((8, 2), (5, 2)), 17: ((9, 3),), 18: ((8, 3), (10, 1), (5, 3)), 19: ((9, 4), (8, 4), (4, 4)), 21: ((5, 4), (10, 2))}
LATE = (UP + 2, DOWN + 3, UP + 3, OUT, QKV, QKV + 1, QKV + 2)
LATE_POINTS = {0: ((6, 0),), 1: ((6, 1), (11, 0), (10, -3), (3, 0), (7, 0)), 2: ((11, 1),), 3: ((3, 1), (0, 0), (10, 3)), 4: ((7, 1),), 5: ((3, 2),), 6: ((1, 0), (0, 1)), 7: ((3, 3), (7, 2), (11, 2)), 8: ((0, 2),), 10: ((1, 1), (7, 3), (6, 2)), 11: ((11, 3), (2, 0)), 14: ((2, 1),), 15: ((0, 3),), 16: ((1, 2),), 17: ((7, 4),), 18: ((2, 2), (1, 3), (11, 4)), 19: ((6, 3), (0, 4)), 20: ((2, 3),), 22: ((3, 4),), 23: ((1, 4), (2, 4), (6, 4), (10, 4))}
def reduce_stages(points):
    moves = [move for at in sorted(points) for move in points[at]]
    started = [(unit, 3 if stage == -3 else stage + 1) for unit, stage in moves if stage < 4]
    return [(unit, stage) for unit, stage in started if stage > 3 or (unit, stage) in moves or stage < 3]


def gather_stages(points):
    return [(ORDER[index], stage) for point in points for index, stage in point]


def forward_pair(step):
    first = (13 - step) // 8
    return first * ((step // 2 + 1) % 3 + 3 * (step % 2)) + (1 - first) * step


def backward_pair(step):
    group, place = step // 3, step % 3
    return (1 + group) % 3 + 3 * place - place // 2


def pair_unit(which, pair):
    first = (13 - pair) // 8
    sixth, seventh = ((0, 2, 0), (1, 1, 2))[0][which], ((0, 2, 0), (1, 1, 2))[1][which]
    return first * ((pair + 2) % 3) + (1 - first) * ((7 - pair) * sixth + (pair - 6) * seventh)


def pair_block(which, pair):
    return (which * (H // 2) + pair) // 3


def picked(block, j):
    return sum(jnp.where(block == index, PICK[index][j], 0) for index in range(8))


def window_layout(clip_frames, first_window, window_count):
    slab_count = 1 + (clip_frames > WT).astype(jnp.int32)
    starts = jnp.cumsum(slab_count, dtype=jnp.int32) - slab_count
    global_window = first_window + jnp.arange(window_count, dtype=jnp.int32)
    slab_of = global_window // SPW
    owners = jnp.sum((starts[None, :] <= slab_of[:, None]).astype(jnp.int32), axis=1) - 1
    clip_ids = jnp.arange(clip_frames.shape[0], dtype=jnp.int32)
    member = (owners[:, None] == clip_ids[None, :]).astype(jnp.int32)
    clip_start = jnp.sum(member * starts[None, :], axis=1)
    own_frames = jnp.sum(member * clip_frames[None, :], axis=1)
    inner_slab = slab_of - clip_start
    return (jnp.minimum(own_frames - WT * inner_slab, WT), member)


def offset_spread():
    side_span = 2 * WSIDE - 1
    shape = (OFFSETS, WSIDE * LANES)
    offset = lax.broadcasted_iota(jnp.int32, shape, 0)
    place = lax.broadcasted_iota(jnp.int32, shape, 1)
    own, row, other = place // LANES, place // WSIDE % (LANES // WSIDE), place % WSIDE
    row_diff, col_diff = side_span - 1 - row, own - other + (WSIDE - 1)
    return ((row < side_span) & (row_diff * side_span + col_diff == offset)).astype(BF16)


def spread_table(table):
    heads = table.shape[0]
    by_frame = table.reshape(heads, FRAMES, OFFSETS)[:, ::-1].reshape(heads * FRAMES, OFFSETS)
    spread = jnp.dot(by_frame, offset_spread(), preferred_element_type=F32).astype(BF16)
    spread = spread.reshape(heads, FRAMES * WSIDE, LANES)
    return jnp.pad(spread, ((0, 0), (0, SPREAD - FRAMES * WSIDE), (0, 0)))


def gather_table(spread):
    heads = spread.shape[0]
    by_frame = spread[:, : FRAMES * WSIDE].reshape(heads * FRAMES, WSIDE * LANES)
    sums = lax.dot_general(
        by_frame,
        offset_spread().astype(F32),
        (((1,), (1,)), ((), ())),
        precision=HIGHEST,
        preferred_element_type=F32,
    )
    return sums.reshape(heads, FRAMES, OFFSETS)[:, ::-1].reshape(heads, FRAMES * OFFSETS)


def units_of(qkv, out, up, down):
    return jnp.concatenate(
        [
            jnp.stack(
                [
                    jnp.stack([qkv[:, 384 * b + LANES * PICK[b][j] :][:, :LANES] for b in range(8)])
                    for j in range(3)
                ]
            ),
            out.reshape(D, 8, 1, LANES).transpose(2, 1, 0, 3),
            up.reshape(D, 8, 4, LANES).transpose(2, 1, 0, 3),
            down.reshape(8, 4, LANES, 8, LANES).transpose(1, 3, 0, 2, 4).reshape(4, 8, D, LANES),
        ]
    )


def weights_of(units):
    def columns(part):
        return part.transpose(2, 1, 0, 3).reshape(D, -1)

    down = units[DOWN:].reshape(4, 8, 8, LANES, LANES).transpose(2, 0, 3, 1, 4)
    qkv = [
        units[PICK[block].index(tile), block] for block in range(8) for tile in range(3)
    ]
    return (
        jnp.concatenate(qkv, axis=1),
        columns(units[OUT:UP]),
        columns(units[UP:DOWN]),
        down.reshape(4 * D, D),
    )


def dot(left, right):
    return jnp.dot(left, right, preferred_element_type=F32)


def dot_rows(left, right):
    return lax.dot_general(left, right, (((1,), (1,)), ((), ())), preferred_element_type=F32)


def dot_tokens(left, right):
    return lax.dot_general(left, right, (((0,), (0,)), ((), ())), preferred_element_type=F32)


def half(index):
    return pl.ds(pl.multiple_of(index * 512, 512), 512)


def four_columns(unit, index):
    blocks = [unit[2 * index + x // 2, x % 2].reshape(D, LANES) for x in range(4)]
    return jnp.concatenate(blocks, axis=1)


def half_rows(unit, index):
    blocks = [unit[block // 2, block % 2, index].reshape(512, LANES) for block in range(8)]
    return jnp.concatenate(blocks, axis=1)


def put_columns(unit, index, values):
    for x in range(4):
        unit[2 * index + x // 2, x % 2] = values[:, x * LANES : (x + 1) * LANES].reshape(2, 2, SHARE, LANES)


def loop(count, body):
    def step(index, carry):
        body(index)
        return carry

    lax.fori_loop(0, count, step, 0)


def vmem():
    return pl.BlockSpec(memory_space=pltpu.VMEM)


def anywhere():
    return pl.BlockSpec(memory_space=pl.ANY)


def smem():
    return pl.BlockSpec(memory_space=pltpu.SMEM)


def shape(dtype, *sizes):
    return jax.ShapeDtypeStruct(sizes, dtype)


def params(collective=None, limit=58):
    if collective is None:
        return pltpu.CompilerParams(vmem_limit_bytes=limit * MIB)
    return pltpu.CompilerParams(
        vmem_limit_bytes=limit * MIB, collective_id=collective, has_side_effects=True
    )


def centered(values):
    center = values - jnp.mean(values, axis=-1, keepdims=True)
    spread = jnp.mean(center * center, axis=-1, keepdims=True)
    root = lax.rsqrt(spread + EPSILON)
    return center * root, root


def norm_back(grad_normed, normal, root, scale):
    grad = grad_normed * (1.0 + scale)
    mean = jnp.mean(grad, axis=-1, keepdims=True)
    along = jnp.mean(grad * normal, axis=-1, keepdims=True)
    return root * (grad - mean - normal * along)


def each_rows(mod_ref, live_ref, body, rows=32, pump=lambda window: None):
    for window in range(mod_ref.shape[0]):
        live = live_ref[window] * CELLS

        def step(index, window=window, live=live):
            at = pl.ds(pl.multiple_of(window * WIN + index * rows, rows), rows)
            mods = [mod_ref[window, k : k + 1, :] for k in range(6)]
            slot = index * rows + lax.broadcasted_iota(jnp.int32, (rows, 1), 0)
            body(window, at, mods, slot < live)

        loop(WIN // rows, step)
        pump(window)


def add_sums(sums_ref, window, which, values):
    sums_ref[window, which : which + 1, :] += jnp.sum(values, axis=0, keepdims=True)


class Place:
    def __init__(self):
        column, row = lax.axis_index("dp"), lax.axis_index("fsdp")
        self.z, self.x, self.y, self.c = column // 2, column % 2, row // 2, row % 2

    def at(self, z=None, x=None, y=None, c=None):
        z = self.z if z is None else z
        x = self.x if x is None else x
        y = self.y if y is None else y
        c = self.c if c is None else c
        return (z * 2 + x, y * 2 + c)

    def far(self, k):
        return lax.rem(self.z + k, 4)

    def shifted(self, dz, dx, dy, dc):
        def other(index, change):
            return 1 - index if change else index

        return self.at(self.far(dz), other(self.x, dx), other(self.y, dy), other(self.c, dc))

    def greet(self, far_ones=()):
        near = [(1, 0, 0, 0), (2, 0, 0, 0), (3, 0, 0, 0), (0, 1, 0, 0), (0, 0, 1, 0), (0, 0, 0, 1)]
        peers = near + [change for change in far_ones if change not in near]
        barrier = pltpu.get_barrier_semaphore()
        for change in peers:
            pl.semaphore_signal(
                barrier, inc=1, device_id=self.shifted(*change), device_id_type=MESH
            )
        pl.semaphore_wait(barrier, len(peers))


EVERYONE = [
    (dz, dx, dy, dc)
    for dz in range(4)
    for dx in range(2)
    for dy in range(2)
    for dc in range(2)
    if (dz, dx, dy, dc) != (0, 0, 0, 0)
]
ALONG_ZX = [change for change in EVERYONE if change[2:] == (0, 0)]
ALONG_YC = [change for change in EVERYONE if change[:2] == (0, 0)]


class Moves:
    def __init__(self, place, stages, scratch):
        self.place = place
        self.send, self.recv = scratch
        self.first, count = {}, 0
        for unit, stage in stages:
            self.first[unit, stage] = count
            count += self.counts[unit in self.aside][stage - 1]
        self.flying = []

    @classmethod
    def semaphores(cls, stages):
        count = sum(cls.counts[unit in cls.aside][stage - 1] for unit, stage in stages)
        return [pltpu.SemaphoreType.DMA((count,))] * 2

    def made(self, unit, stage, moves):
        copies = []
        for index, (source, target, device) in enumerate(moves):
            slot = self.first[unit, stage] + index
            copies.append(
                pltpu.make_async_remote_copy(
                    src_ref=source,
                    dst_ref=target,
                    send_sem=self.send.at[slot],
                    recv_sem=self.recv.at[slot],
                    device_id=device,
                    device_id_type=MESH,
                )
            )
        return copies

    def begin(self, unit, stage):
        for copy in self.copies(unit, stage):
            copy.start()
        self.flying.append((unit, stage))

    def arrive(self, unit, stage):
        if (unit, stage) in self.flying:
            self.flying.remove((unit, stage))
            for copy in self.copies(unit, stage):
                copy.wait_recv()

    def sent(self):
        for unit, stage in self.first:
            for copy in self.copies(unit, stage):
                copy.wait_send()


class Gather(Moves):
    counts = ((3, 2, 2, 1), (2, 2, 3, 1))
    aside = GATHER_ASIDE

    def __init__(self, place, held, stages, scratch):
        super().__init__(place, stages, scratch)
        self.held = held

    def copies(self, unit, stage):
        p, held = self.place, self.held.at[unit]
        at_x, at_y, at_core = p.at(x=1 - p.x), p.at(y=1 - p.y), p.at(c=1 - p.c)
        own = held.at[p.z, p.x, p.y, p.c]
        if stage == 4:
            refs = [(held.at[:, :, :, p.c], at_core)]
        elif unit in self.aside and stage == 1:
            refs = [(own.at[:HALF], at_x), (own.at[HALF:], at_y)]
        elif unit in self.aside and stage == 2:
            refs = [
                (held.at[p.z, :, p.y, p.c, :HALF], at_y),
                (held.at[p.z, p.x, :, p.c, HALF:], at_x),
            ]
        elif unit in self.aside:
            refs = [(held.at[p.z, :, :, p.c], p.at(z=p.far(k))) for k in (1, 2, 3)]
        elif stage == 1:
            refs = [(own, p.at(z=p.far(k))) for k in (1, 2, 3)]
        elif stage == 2:
            refs = [
                (held.at[:, p.x, p.y, p.c, :HALF], at_x),
                (held.at[:, p.x, p.y, p.c, HALF:], at_y),
            ]
        else:
            refs = [
                (held.at[:, :, p.y, p.c, :HALF], at_y),
                (held.at[:, p.x, :, p.c, HALF:], at_x),
            ]
        return self.made(unit, stage, [(ref, ref, device) for ref, device in refs])

    def advance(self, unit, stage):
        self.arrive(unit, stage - 1)
        self.begin(unit, stage)

    def finish(self):
        for unit, stage in list(self.flying):
            self.arrive(unit, stage)
        self.sent()


class Reduce(Moves):
    counts = ((1, 2, 2, 3), (1, 3, 2, 2))
    aside = REDUCE_ASIDE

    def __init__(self, place, part, points, store, buffers, scratch):
        super().__init__(place, reduce_stages(points), scratch[2:])
        self.part, self.store, self.buffers = part, store, buffers
        self.own, self.load = scratch[:2]
        self.slots, self.loaded = {}, []

    @classmethod
    def scratch(cls, points):
        return [
            pltpu.VMEM((OWN_SLOTS, 4, 2, 2, SHARE, LANES), BF16),
            pltpu.SemaphoreType.DMA((OWN_SLOTS,)),
        ] + cls.semaphores(reduce_stages(points))

    @staticmethod
    def core_shape(count):
        return (count, 4, 2, 2, SHARE, LANES)

    @staticmethod
    def side_shape(count):
        return (count, 2, 4, 2, HALF, LANES)

    @staticmethod
    def corner_shape(count):
        return (count, 2, 4, HALF, LANES)

    @staticmethod
    def distant_shape(count):
        return (count, 3, 2, HALF, LANES)

    @staticmethod
    def aside_shape(count):
        return (count, 3, 2, 2, SHARE, LANES)

    def own_copy(self, unit):
        slot = self.slots.setdefault(unit, len(self.slots) % OWN_SLOTS)
        return pltpu.make_async_copy(
            self.part(unit).at[:, :, :, self.place.c], self.own.at[slot], self.load.at[slot]
        )

    def copies(self, unit, stage):
        p = self.place
        at_x, at_y, at_core = p.at(x=1 - p.x), p.at(y=1 - p.y), p.at(c=1 - p.c)
        core, side, corner, distant = self.buffers(unit)
        if unit in self.aside and stage == 2:
            moves = [
                (core.at[p.far(k)], distant.at[k - 1], p.at(z=p.far(k))) for k in (1, 2, 3)
            ]
        elif unit in self.aside and stage == 3:
            moves = [
                (core.at[p.z, :, 1 - p.y, :HALF], side.at[0, 0], at_y),
                (core.at[p.z, 1 - p.x, :, HALF:], side.at[1, 0], at_x),
            ]
        elif unit in self.aside and stage == 4:
            moves = [
                (side.at[0, 0, 1 - p.x], side.at[0, 1, 0], at_x),
                (side.at[1, 0, 1 - p.y], side.at[1, 1, 0], at_y),
            ]
        elif stage == 1:
            moves = [(self.part(unit).at[:, :, :, 1 - p.c], core, at_core)]
        elif stage == 2:
            moves = [
                (core.at[:, :, 1 - p.y, :HALF], side.at[0], at_y),
                (core.at[:, 1 - p.x, :, HALF:], side.at[1], at_x),
            ]
        elif stage == 3:
            moves = [
                (side.at[0, :, 1 - p.x], corner.at[0], at_x),
                (side.at[1, :, 1 - p.y], corner.at[1], at_y),
            ]
        else:
            moves = [
                (corner.at[:, p.far(k)], distant.at[k - 1], p.at(z=p.far(k))) for k in (1, 2, 3)
            ]
        return self.made(unit, stage, moves)

    def begin(self, unit, stage):
        super().begin(unit, stage)
        if stage == 1:
            self.own_copy(unit).start()
            assert self.slots[unit] not in self.loaded
            self.loaded.append(self.slots[unit])

    def combine(self, unit, stage):
        p = self.place
        core, side, corner, distant = self.buffers(unit)

        def plus(left, right):
            return (left.astype(F32) + right.astype(F32)).astype(BF16)

        def from_core(step):
            z, x, y = step // 4, step // 2 % 2, step % 2
            core[z, x, y] = plus(core[z, x, y], self.own[self.slots[unit], z, x, y])

        def from_side(step):
            z, b = step // 2, step % 2
            side[0, z, b] = plus(side[0, z, b], core[z, b, p.y, :HALF])
            side[1, z, b] = plus(side[1, z, b], core[z, p.x, b, HALF:])

        def from_corner(z):
            corner[0, z] = plus(corner[0, z], side[0, z, p.x])
            corner[1, z] = plus(corner[1, z], side[1, z, p.y])

        def from_far(half):
            total = corner[half, p.z].astype(F32)
            for k in range(3):
                total = total + distant[k, half].astype(F32)
            self.store(unit, half, total)

        def aside_far(step):
            x, y = step // 2, step % 2
            total = core[p.z, x, y].astype(F32)
            for k in range(3):
                total = total + distant[k, x, y].astype(F32)
            core[p.z, x, y] = total.astype(BF16)

        def aside_side(b):
            side[0, 0, b] = plus(side[0, 0, b], core[p.z, b, p.y, :HALF])
            side[1, 0, b] = plus(side[1, 0, b], core[p.z, p.x, b, HALF:])

        if unit in self.aside and stage == 4:
            for part, own in enumerate((p.x, p.y)):
                total = side[part, 0, own].astype(F32) + side[part, 1, 0].astype(F32)
                self.store(unit, part, total)
            return
        steps = {1: (16, from_core), 2: (8, from_side), 3: (4, from_corner), 4: (2, from_far)}
        if unit in self.aside:
            steps |= {2: (4, aside_far), 3: (2, aside_side)}
        loop(*steps[stage])

    def step(self, unit, stage):
        if stage <= 0:
            self.begin(unit, max(1, -stage))
            return
        self.arrive(unit, stage)
        if stage == 1:
            self.own_copy(unit).wait()
        self.combine(unit, stage)
        if stage == 1:
            self.loaded.remove(self.slots[unit])
        if (unit, stage + 1) in self.first:
            self.begin(unit, stage + 1)


class Copies:
    def __init__(self, send, recv):
        self.send, self.recv, self.count = send, recv, 0

    def __call__(self, source, target, device):
        slot = self.count
        self.count += 1
        copy = pltpu.make_async_remote_copy(
            src_ref=source,
            dst_ref=target,
            send_sem=self.send.at[slot],
            recv_sem=self.recv.at[slot],
            device_id=device,
            device_id_type=MESH,
        )
        copy.start()
        return copy


class Refs:
    pass


def call(kernel, name, inputs, outputs, scratch, aliases=(), collective=None, grid=None, limit=58):
    names = list(inputs) + list(outputs)
    flat = []
    for value in scratch.values():
        flat += value if isinstance(value, list) else [value]

    def body(*refs):
        held = Refs()
        rest = list(refs)
        for key in names:
            setattr(held, key, rest.pop(0))
        for key, value in scratch.items():
            if isinstance(value, list):
                setattr(held, key, [rest.pop(0) for _ in value])
            else:
                setattr(held, key, rest.pop(0))
        kernel(held)

    extra = {} if grid is None else {"grid": grid}
    made = functools.partial(
        pl.pallas_call,
        body,
        in_specs=[spec for _, spec in inputs.values()],
        out_specs=[spec for _, spec in outputs.values()],
        out_shape=[out for out, _ in outputs.values()],
        scratch_shapes=flat,
        input_output_aliases={
            list(inputs).index(one): list(outputs).index(other) for one, other in aliases
        },
        compiler_params=params(collective, limit),
        name=name,
        **extra,
    )
    arrays = [array for array, _ in inputs.values()]
    if name == "start":
        result = made()(*arrays)
    else:
        result = made()(*arrays)
    out = Refs()
    for key, value in zip(outputs, result, strict=True):
        setattr(out, key, value)
    return out


def enter_norm(refs, pump=lambda: None):
    rows = 32
    for window in range(refs.mod.shape[0]):
        shift, scale = refs.mod[window, 0:1, :], refs.mod[window, 1:2, :]

        def step(index, window=window, shift=shift, scale=scale):
            at = pl.ds(pl.multiple_of(window * WIN + index * rows, rows), rows)
            normal, _ = centered(refs.tokens[at, :].astype(F32))
            refs.normed[at, :] = (normal * (1.0 + scale) + shift).astype(BF16)

        loop(WIN // rows, step)
        pump()


def enter_unit(refs, j, held, put=False):
    unit = refs.units.at[0]
    fetch = pltpu.make_async_copy(held, unit, refs.fetches.at[0])
    fetch.start()
    fetch.wait()

    def project(index):
        refs.packed[j, :, half(index)] = dot(refs.normed[...], four_columns(unit, index)).astype(
            BF16
        )

    loop(2, project)
    if put:
        packed_copy(refs, j).start()


def packed_copy(refs, j):
    return pltpu.make_async_copy(refs.packed.at[j], refs.packed_out.at[j], refs.packed_sem.at[j])


def enter_plain_kernel(refs):
    enter_norm(refs)
    for j in range(3):
        enter_unit(refs, j, refs.held.at[QKV + j])


def act_rows(refs, place):
    first = (place.y * 2 + place.c) * SHARE
    value = refs.condition[:, pl.ds(pl.multiple_of(first, SHARE), SHARE)]
    act = value / (1.0 + jnp.exp(-value))
    return jnp.concatenate([act, jnp.zeros((8 - value.shape[0], SHARE), F32)], axis=0).astype(BF16)


def enter_layout(refs):
    windows, clips = refs.member.shape[0], refs.condition.shape[0]
    frames = [refs.frames[clip] for clip in range(clips)]
    starts = [0]
    for count in frames:
        starts.append(starts[-1] + 1 + jnp.where(count > WT, 1, 0))
    device = lax.axis_index("dp") * lax.axis_size("fsdp") + lax.axis_index("fsdp")
    refs.member[...] = jnp.zeros_like(refs.member)
    for window in range(windows):
        slab = (device * windows + window) // SPW
        live = 0
        for clip in range(clips):
            mine = starts[clip] <= slab
            if clip < clips - 1:
                mine = mine & (slab < starts[clip + 1])
            inner = frames[clip] - WT * (slab - starts[clip])
            live = live + jnp.where(mine, jnp.minimum(inner, WT), 0)
            refs.member[window, clip : clip + 1, :] = jnp.full(
                (1, LANES), jnp.where(mine, 1.0, 0.0), F32
            )
        refs.live[window] = live


def enter_table(refs):
    refs.rows[...] = jnp.zeros_like(refs.rows)
    table = refs.rel_table[...].astype(F32)
    for head in range(2):
        for frame in range(FRAMES):
            first = (FRAMES - 1 - frame) * OFFSETS
            row = head * (SPREAD // WSIDE) + frame
            refs.rows[row : row + 1, :OFFSETS] = table[head : head + 1, first : first + OFFSETS]
    shape_of = (TILE, WSIDE * LANES)
    offset = lax.broadcasted_iota(jnp.int32, shape_of, 0)
    place = lax.broadcasted_iota(jnp.int32, shape_of, 1)
    own, row, other = place // LANES, place // WSIDE % (LANES // WSIDE), place % WSIDE
    side_span = 2 * WSIDE - 1
    row_diff, col_diff = side_span - 1 - row, own - other + (WSIDE - 1)
    same = (row < side_span) & (row_diff * side_span + col_diff == offset)
    spread = dot(refs.rows[...].astype(BF16), jnp.where(same, 1.0, 0.0).astype(BF16))
    count = 2 * SPREAD // WSIDE
    for own in range(WSIDE):
        refs.spread[pl.ds(own, count, stride=WSIDE), :] = spread[
            :count, own * LANES : (own + 1) * LANES
        ]
    for head in range(2):
        refs.table_own[head] = refs.spread[head * SPREAD : (head + 1) * SPREAD, :].astype(BF16)


def enter(refs, place, work):
    place.greet(ALONG_ZX + ALONG_YC)
    z, x, y, c = place.z, place.x, place.y, place.c
    small = Copies(*refs.small)
    mods = dot(act_rows(refs, place), refs.ada[...])
    mods = mods + jnp.where((y == 0) & (c == 0), 1.0, 0.0) * refs.bias_in[...].astype(F32)
    for block in range(6):
        refs.mod_part[block * CLIP_ROWS : (block + 1) * CLIP_ROWS, :] = mods[
            :CLIP_ROWS, block * LANES : (block + 1) * LANES
        ]
    refs.mod_parts[y, c] = refs.mod_part[...]
    parts = [
        small(refs.mod_part, refs.mod_parts.at[y, c], place.shifted(*change)) for change in ALONG_YC
    ]
    own = []
    for unit in range(UNITS):
        if unit < OUT:
            first = picked(z * 2 + x, unit) * LANES
            refs.own[unit] = refs.qkv[:, pl.ds(pl.multiple_of(first, LANES), LANES)]
        elif unit >= DOWN:
            first = (unit - DOWN) * LANES
            for half in range(2):
                at = slice(half * 512 + first, half * 512 + first + LANES)
                refs.own[unit, half * HALF : (half + 1) * HALF] = refs.down[at, :]
        else:
            source, start = (refs.out, OUT) if unit < UP else (refs.up, UP)
            first = (unit - start) * LANES
            refs.own[unit] = source[:, first : first + LANES]
        own.append(
            pltpu.make_async_copy(
                refs.own.at[unit], refs.held.at[unit, z, x, y, c], refs.own_sem.at[unit]
            )
        )
        own[-1].start()
    points = list(ENTER)

    loaded = []

    def load(unit):
        if unit not in loaded:
            own[unit].wait()
            loaded.append(unit)

    def tick():
        for index, stage in points.pop(0):
            if stage == 1:
                load(ORDER[index])
            work.advance(ORDER[index], stage)

    tick()
    enter_layout(refs)
    enter_table(refs)
    refs.table[z, x, c] = refs.table_own[c]
    for copy in parts:
        copy.wait()
    refs.mods[z, x] = (
        refs.mod_parts[0, 0] + refs.mod_parts[0, 1] + refs.mod_parts[1, 0] + refs.mod_parts[1, 1]
    )
    mods = [
        small(refs.mods.at[z, x], refs.mods.at[z, x], place.shifted(*change))
        for change in ALONG_ZX
    ]
    for unit in range(UNITS):
        load(unit)
    tick()
    for copy in mods:
        copy.wait()
    tables = [
        small(refs.table.at[z, x, c], refs.table.at[z, x, c], place.shifted(*change))
        for change in ALONG_ZX
    ]
    for window in range(refs.mod.shape[0]):
        for block in range(48):
            which, column = divmod(block, 8)
            first = block % 6 * CLIP_ROWS
            part = refs.mods[block // 12, block // 6 % 2, first : first + CLIP_ROWS, :]
            refs.mod[window, which : which + 1, column * LANES : (column + 1) * LANES] = jnp.sum(
                part * refs.member[window], axis=0, keepdims=True
            )
    tick()
    enter_norm(refs, tick)
    for copy in tables:
        copy.wait()
    last = small(refs.table.at[:, :, c], refs.table.at[:, :, c], place.at(c=1 - c))
    work.arrive(QKV, 4)
    enter_unit(refs, 0, refs.held.at[QKV], put=True)
    last.wait()


def attend_pair(refs, table, part, put):
    for head in range(2):
        spread = table(head).astype(F32)
        for frame in range(FRAMES):
            block = spread[frame * WSIDE : (frame + 1) * WSIDE]
            for row in range(WSIDE):
                first = (WSIDE - 1 - row) * WSIDE
                refs.strip[
                    head, row * WSIDE : (row + 1) * WSIDE, frame * CELLS : (frame + 1) * CELLS
                ] = block[:, first : first + CELLS]
        for frame in range(WT):
            first = (WT - 1 - frame) * CELLS
            refs.bias[head, frame * CELLS : (frame + 1) * CELLS, :] = refs.strip[
                head, :, first : first + WIN
            ]
    for window in range(refs.live.shape[0]):
        rows = slice(window * WIN, (window + 1) * WIN)
        live = refs.live[window] * CELLS
        key_live = lax.broadcasted_iota(jnp.int32, (1, WIN), 1) < live
        query, key, value = (part(which, rows) for which in range(3))
        mixed = []
        for head in range(2):
            lanes = slice(head * HD, (head + 1) * HD)
            scores = dot_rows(query[:, lanes] * BF16(HD ** (-0.5)), key[:, lanes]) + refs.bias[head]
            scores = jnp.where(key_live, scores, NEGATIVE)
            shifted = jnp.exp(scores - jnp.max(scores, axis=-1, keepdims=True))
            totals = jnp.sum(shifted, axis=-1, keepdims=True)
            probs = (shifted * (1.0 / totals)).astype(BF16)
            refs.probs[window, head] = probs
            mixed.append(dot(probs, value[:, lanes]).astype(BF16))
        put(rows, jnp.concatenate(mixed, axis=1))


def attend_plain_kernel(refs):
    sources = (refs.query, refs.key, refs.value)

    def put(rows, values):
        refs.mixed[rows, :] = values

    attend_pair(
        refs, lambda head: refs.table[head], lambda which, rows: sources[which][rows, :], put
    )


def start_kernel(refs):
    step = pl.program_id(0)
    pairs = H // 2
    place = Place()
    stages = gather_stages(ENTER + tuple(ATTEND.values()) + tuple(MIDDLE.values()))
    work = Gather(place, refs.held, stages, refs.gather)

    @pl.when(step == 0)
    def _():
        enter(refs, place, work)

    for at in range(pairs):

        @pl.when(step == at + 1)
        def _(at=at):
            for index, stage in ATTEND.get(at, ()):
                work.advance(ORDER[index], stage)
            if at in (2, 4):
                work.arrive(QKV + at // 2, 4)
                enter_unit(refs, at // 2, refs.held.at[QKV + at // 2], put=True)

    @pl.when((step > 0) & (step <= pairs))
    def _():
        pair = forward_pair(jnp.clip(step - 1, 0, pairs - 1))

        def columns(block):
            return pl.ds(pl.multiple_of(block * LANES, LANES), LANES)

        def part(which, rows):
            return refs.packed[pair_unit(which, pair), rows, columns(pair_block(which, pair))]

        def table(head):
            return refs.table[pair // 2, pair % 2, head]

        def put(rows, values):
            refs.mixed[rows, columns(pair)] = values

        attend_pair(refs, table, part, put)

    @pl.when(step == pairs)
    def _():
        for j in range(3):
            packed_copy(refs, j).wait()

    @pl.when(step == pairs + 1)
    def _():
        middle(refs, place, work)


def packed_block(which, rows, pair):
    return pl.BlockSpec(
        (None, rows, LANES),
        lambda step: (pair_unit(which, pair(step)), 0, pair_block(which, pair(step))),
    )


def attend_back_pair(refs, pair):
    scale = BF16(HD ** (-0.5))
    refs.spread[...] = jnp.zeros_like(refs.spread)
    refs.strip[...] = jnp.zeros_like(refs.strip)
    windows = refs.probs.shape[0]
    results = [[[None] * windows for _ in range(2)] for _ in range(3)]
    for head in range(2):
        lanes = slice(head * HD, (head + 1) * HD)
        bias = None
        for window in range(windows):
            rows = slice(window * WIN, (window + 1) * WIN)
            grad = refs.grad[rows, lanes]
            probs = refs.probs[window, head]
            results[2][head][window] = dot_tokens(grad, probs).T.astype(BF16)
            grad_probs = dot_rows(grad, refs.value[rows, lanes])
            weight = probs.astype(F32)
            product = weight * grad_probs
            total = jnp.sum(product, axis=-1, keepdims=True)
            grad_scores = (product - weight * total).astype(BF16)
            wide = grad_scores.astype(F32)
            bias = wide if bias is None else bias + wide
            results[0][head][window] = dot(grad_scores, refs.key[rows, lanes] * scale).astype(BF16)
            query = refs.query[rows, lanes] * scale
            results[1][head][window] = dot_tokens(query, grad_scores).T.astype(BF16)
        for frame in range(WT):
            first = (WT - 1 - frame) * CELLS
            refs.strip[head, :, first : first + WIN] += bias[frame * CELLS : (frame + 1) * CELLS]
        for frame in range(FRAMES):
            for row in range(WSIDE):
                first = (WSIDE - 1 - row) * WSIDE
                refs.spread[
                    head, frame * WSIDE : (frame + 1) * WSIDE, first : first + CELLS
                ] += refs.strip[
                    head, row * WSIDE : (row + 1) * WSIDE, frame * CELLS : (frame + 1) * CELLS
                ]
    for part in range(3):
        lanes = pl.ds(pl.multiple_of(pair_block(part, pair) * LANES, LANES), LANES)
        for window in range(windows):
            rows = slice(window * WIN, (window + 1) * WIN)
            both = [results[part][head][window] for head in range(2)]
            refs.grad_packed[pair_unit(part, pair), rows, lanes] = jnp.concatenate(both, axis=1)


def middle(refs, place=None, gathering=None):
    order = [OUT] + [unit for j in range(4) for unit in (UP + j, DOWN + j)] + [OUT]
    activated, grad_hidden, grad_low = (refs.packed.at[index] for index in range(3))
    reducing = None
    points = {}
    waiting = set()
    if gathering is not None:

        def buffers(unit):
            index = EARLY.index(unit)
            core, side = refs.core.at[index], refs.side.at[index]
            if unit not in DONE:
                return core, side, None, None
            if unit in REDUCE_ASIDE:
                return core, side, None, refs.aside.at[0]
            return core, side, refs.corner.at[index], refs.distant.at[index]

        def store(unit, part, values):
            at = pl.ds(pl.multiple_of(part * HALF, HALF), HALF)
            refs.total[DONE.index(unit), at, :] = values

        reducing = Reduce(
            place, lambda unit: refs.part.at[unit], EARLY_POINTS, store, buffers, refs.reduce
        )
        for stages in MIDDLE.values():
            waiting |= {ORDER[index] for index, stage in stages if stage == 4}
        points = {at: list(moves) for at, moves in EARLY_POINTS.items()}

    count = [0]

    def pump():
        for index, stage in MIDDLE.get(count[0], ()) if gathering is not None else ():
            gathering.advance(ORDER[index], stage)
            if stage == 4:
                waiting.discard(ORDER[index])
        for unit, stage in points.pop(count[0], ()):
            reducing.step(unit, stage)
        count[0] += 1

    def fetch(step):
        return pltpu.make_async_copy(
            refs.held.at[order[step]], refs.units.at[step % 4], refs.fetches.at[step % 4]
        )

    def start_fetch(step):
        if gathering is not None:
            assert order[step] not in waiting
            gathering.arrive(order[step], 4)
        fetch(step).start()

    def put(slot, unit):
        return pltpu.make_async_copy(refs.made.at[slot], refs.part.at[unit], refs.made_sem.at[slot])

    for step in range(3):
        start_fetch(step)
    pump()
    refs.sums[...] = jnp.zeros_like(refs.sums)
    refs.mlp[...] = jnp.zeros_like(refs.mlp)
    refs.grad_normed[...] = jnp.zeros_like(refs.grad_normed)
    fetch(0).wait()

    def project(index):
        refs.attended[:, half(index)] = dot(refs.mixed[...], four_columns(refs.units.at[0], index))

    loop(2, project)
    pump()

    def modulate(window, at, mods, live):
        middle = refs.tokens[at, :].astype(F32) + mods[2] * refs.attended[at, :]
        normal, _ = centered(middle)
        refs.normed2[at, :] = (normal * (1.0 + mods[4]) + mods[3]).astype(BF16)
        grad = jnp.where(live, refs.cotangent[at, :].astype(F32), 0.0)
        grad_low[at, :] = (mods[5] * grad).astype(BF16)

    each_rows(refs.mod, refs.live, modulate)
    pump()
    for j in range(4):
        step = 1 + 2 * j
        up, down = refs.units.at[step % 4], refs.units.at[(step + 1) % 4]
        fetch(step).wait()
        fetch(step + 1).wait()
        start_fetch(step + 2)

        def hide(index, up=up, down=down):
            hidden = dot(refs.normed2[...], four_columns(up, index))
            bend = jnp.tanh(0.7978845608028654 * (hidden + 0.044715 * hidden * hidden * hidden))
            activated[:, half(index)] = (0.5 * hidden * (1.0 + bend)).astype(BF16)
            slope = 0.5 * (1.0 + bend) + 0.5 * hidden * (1.0 - bend * bend) * (
                0.7978845608028654 * (1.0 + 3.0 * 0.044715 * hidden * hidden)
            )
            grad_activated = dot_rows(grad_low[...], half_rows(down, index))
            grad_hidden[:, half(index)] = (grad_activated * slope).astype(BF16)

        loop(2, hide)
        if j > 0:
            put(1, UP + j - 1).wait()
        pump()

        def down_gradient(index):
            made = dot_tokens(activated[:, half(index)], grad_low[...]).astype(BF16)
            for block in range(8):
                refs.made[0, block // 2, block % 2, index] = made[
                    :, block * LANES : (block + 1) * LANES
                ].reshape(2, SHARE, LANES)

        loop(2, down_gradient)
        put(0, DOWN + j).start()
        pump()

        def up_gradient(index):
            made = dot_tokens(refs.normed2[...], grad_hidden[:, half(index)]).astype(BF16)
            put_columns(refs.made.at[1], index, made)

        loop(2, up_gradient)
        put(0, DOWN + j).wait()
        put(1, UP + j).start()
        pump()
        if j < 3:
            start_fetch(step + 3)

        def out_of_mlp(index, up=up, down=down):
            refs.mlp[:, half(index)] += dot(activated[...], four_columns(down, index))
            refs.grad_normed[:, half(index)] += dot_rows(
                grad_hidden[...], half_rows(up, index)
            )

        loop(2, out_of_mlp)
        pump()

    put(1, UP + 3).wait()

    def join(window, at, mods, live):
        attended = refs.attended[at, :]
        middle = refs.tokens[at, :].astype(F32) + mods[2] * attended
        normal, root = centered(middle)
        mlp = refs.mlp[at, :]
        refs.output[at, :] = jnp.where(live, middle + mods[5] * mlp, 0.0).astype(BF16)
        grad_result = jnp.where(live, refs.cotangent[at, :].astype(F32), 0.0)
        grad_normed = refs.grad_normed[at, :]
        grad_middle = grad_result + norm_back(grad_normed, normal, root, mods[4])
        refs.grad_middle[at, :] = grad_middle
        grad_low[at, :] = (mods[2] * grad_middle).astype(BF16)
        add_sums(refs.sums, window, 2, grad_middle * attended)
        add_sums(refs.sums, window, 3, grad_normed)
        add_sums(refs.sums, window, 4, grad_normed * normal)
        add_sums(refs.sums, window, 5, grad_result * mlp)

    each_rows(refs.mod, refs.live, join)
    pump()
    fetch(9).wait()

    def back(index):
        made = dot_tokens(refs.mixed[...], grad_low[:, half(index)]).astype(BF16)
        put_columns(refs.made.at[0], index, made)
        refs.grad_mixed[:, half(index)] = dot_rows(
            grad_low[...], half_rows(refs.units.at[1], index)
        ).astype(BF16)

    loop(2, back)
    put(0, OUT).start()
    put(0, OUT).wait()
    while points:
        pump()
    for index, unit in enumerate(EARLY if gathering is not None else ()):
        if unit not in DONE:

            def keep(z, index=index):
                for part in range(2):
                    refs.side_out[index - len(DONE), part, z] = refs.side[index, part, z]

            loop(4, keep)
    if gathering is not None:
        gathering.finish()
        reducing.sent()


def leave_weight(refs, j, made):
    def weight(index):
        grad = dot_tokens(refs.normed[...], refs.grad_packed[j, :, half(index)]).astype(BF16)
        put_columns(made, index, grad)

    loop(2, weight)


def leave_back(refs, j):
    def back(index):
        refs.grad_normed[:, half(index)] += dot_rows(
            refs.grad_packed[j], half_rows(refs.unit, index)
        )

    loop(2, back)


def leave_norm(refs, pump=lambda window: None):
    def join(window, at, mods, live):
        normal, root = centered(refs.tokens[at, :].astype(F32))
        grad_normed = refs.grad_normed[at, :]
        refs.grad_tokens[at, :] = refs.grad_middle[at, :] + norm_back(
            grad_normed, normal, root, mods[1]
        )
        add_sums(refs.sums, window, 0, grad_normed)
        add_sums(refs.sums, window, 1, grad_normed * normal)

    each_rows(refs.mod, refs.live, join, pump=pump)


def back_plain_kernel(refs):
    step = pl.program_id(0)

    @pl.when(step < H // 2)
    def _():
        attend_back_pair(refs, backward_pair(jnp.minimum(step, H // 2 - 1)))

    @pl.when(step == H // 2)
    def _():
        refs.sums[...] = jnp.zeros_like(refs.sums)
        refs.grad_normed[...] = jnp.zeros_like(refs.grad_normed)
        for j in range(3):
            fetch = pltpu.make_async_copy(refs.held.at[QKV + j], refs.unit, refs.fetch)
            fetch.start()
            leave_weight(refs, j, refs.made)
            put = pltpu.make_async_copy(refs.made, refs.part.at[j], refs.made_sem)
            put.start()
            fetch.wait()
            leave_back(refs, j)
            put.wait()
        leave_norm(refs)


def fold_spreads(refs):
    heads = H * WIDE // WSIDE
    shape_of = (WSIDE * LANES, TILE)
    place = lax.broadcasted_iota(jnp.int32, shape_of, 0)
    offset = lax.broadcasted_iota(jnp.int32, shape_of, 1)
    own, row, other = place // LANES, place // WSIDE % (LANES // WSIDE), place % WSIDE
    side_span = 2 * WSIDE - 1
    row_diff, col_diff = side_span - 1 - row, own - other + (WSIDE - 1)
    same = (row < side_span) & (row_diff * side_span + col_diff == offset)
    onto = jnp.where(same, 1.0, 0.0).astype(BF16)
    left = jnp.concatenate(
        [refs.spreads[pl.ds(own, heads, stride=WSIDE), :] for own in range(WSIDE)], axis=1
    )
    total = jnp.zeros((heads, TILE), F32)
    for _ in range(3):
        low = left.astype(BF16)
        total = total + dot(low, onto)
        left = left - low.astype(F32)
    rows = 2 * WIDE // WSIDE
    for block in range(8):
        refs.table[block // 2, block % 2] = total[block * rows : (block + 1) * rows]


def back_kernel(refs):
    place = Place()
    z, x, y, c = place.z, place.x, place.y, place.c
    step = pl.program_id(0)

    def buffers(unit):
        every = (EARLY + LATE).index(unit)
        late = every - len(EARLY)
        assert unit not in DONE
        if late < 0:
            core, side = None, refs.side_in.at[every - len(DONE)]
        else:
            core, side = refs.core.at[late], refs.side.at[late]
        if unit in REDUCE_ASIDE:
            return core, side, None, refs.aside.at[0]
        return core, side, refs.corner.at[every], refs.distant.at[every]

    def store(unit, part, values):
        if unit >= DOWN:
            first = part * 512 + (unit - DOWN) * LANES
            refs.grad_down[pl.ds(pl.multiple_of(first, LANES), LANES), :] = values
            return
        at = pl.ds(pl.multiple_of(part * HALF, HALF), HALF)
        if unit < OUT:
            column = picked(z * 2 + x, unit) * LANES
            refs.grad_qkv[at, pl.ds(pl.multiple_of(column, LANES), LANES)] = values
            return
        target, start = (refs.grad_out, OUT) if unit < UP else (refs.grad_up, UP)
        column = (unit - start) * LANES
        target[at, column : column + LANES] = values

    work = Reduce(
        place,
        lambda unit: refs.made.at[unit] if unit < OUT else refs.part.at[unit],
        LATE_POINTS,
        store,
        buffers,
        refs.reduce,
    )
    small = Copies(*refs.small)

    events = [(at, move) for at in sorted(LATE_POINTS) for move in LATE_POINTS[at]]

    def run(until):
        while events and events[0][0] < until:
            work.step(*events.pop(0)[1])

    for number in range(H // 2):

        @pl.when(step == number)
        def _(number=number):
            if number == 0:
                place.greet(EVERYONE)
            if number in (3, 6):
                leave_weight(refs, number // 3 - 1, refs.made.at[number // 3 - 1])
            run(number + 1)

    @pl.when(step < H // 2)
    def _():
        pair = backward_pair(jnp.minimum(step, H // 2 - 1))
        attend_back_pair(refs, pair)
        for head in range(2):
            at = pl.ds(pl.multiple_of((pair * 2 + head) * WIDE, WIDE), WIDE)
            refs.spreads[at, :] = refs.spread[head]

    @pl.when(step == H // 2)
    def _():
        for index, unit in enumerate(DONE):
            for part in range(2):
                store(unit, part, refs.done[index, part * HALF : (part + 1) * HALF, :])
        fold_spreads(refs)
        table = []
        for dz, dx, dy, dc in ALONG_ZX:
            source = refs.table.at[place.far(dz), 1 - x if dx else x]
            table.append(small(source, refs.table_zx.at[z, x], place.shifted(dz, dx, dy, dc)))
        refs.table_zx[z, x] = refs.table[z, x]
        refs.sums[...] = refs.late_sums[...]
        refs.grad_normed[...] = jnp.zeros_like(refs.grad_normed)

        def fetch(j):
            return pltpu.make_async_copy(refs.held.at[QKV + j], refs.unit, refs.fetch)

        fetch(0).start()
        leave_weight(refs, 2, refs.made.at[2])
        run(12)
        fetch(0).wait()
        leave_back(refs, 0)
        fetch(1).start()
        run(13)
        fetch(1).wait()
        leave_back(refs, 1)
        fetch(2).start()
        run(14)
        fetch(2).wait()
        leave_back(refs, 2)
        run(15)
        leave_norm(refs, lambda window: run(17 + window))
        for copy in table:
            copy.wait()
        total = refs.table_zx[0, 0]
        for block in range(1, 8):
            total = total + refs.table_zx[block // 2, block % 2]
        refs.table_own[...] = total
        refs.table_yc[y, c] = total
        table = [
            small(refs.table_own, refs.table_yc.at[y, c], place.shifted(*change))
            for change in ALONG_YC
        ]
        for block in range(48):
            which, column = divmod(block, 8)
            part = jnp.zeros((CLIP_ROWS, LANES), F32)
            for window in range(refs.mod.shape[0]):
                sums = refs.sums[window, which : which + 1, column * LANES : (column + 1) * LANES]
                part = part + refs.member[window] * sums
            first = block % 6 * CLIP_ROWS
            refs.clip[block // 12, block // 6 % 2, first : first + CLIP_ROWS, :] = part
        copies = []
        for dz, dx, dy, dc in ALONG_ZX:
            source = refs.clip.at[place.far(dz), 1 - x if dx else x]
            copies.append(small(source, refs.clip_zx.at[z, x], place.shifted(dz, dx, dy, dc)))
        refs.clip_zx[z, x] = refs.clip[z, x]
        run(19)
        for copy in copies:
            copy.wait()
        total = refs.clip_zx[0, 0]
        for block in range(1, 8):
            total = total + refs.clip_zx[block // 2, block % 2]
        refs.clip_own[...] = total
        refs.clip_yc[y, c] = total
        copies = [
            small(refs.clip_own, refs.clip_yc.at[y, c], place.shifted(*change))
            for change in ALONG_YC
        ]
        run(21)
        for copy in copies:
            copy.wait()
        total = refs.clip_yc[0, 0] + refs.clip_yc[0, 1] + refs.clip_yc[1, 0] + refs.clip_yc[1, 1]
        total = jnp.concatenate([total, jnp.zeros((8, LANES), F32)], axis=0)
        cond = jnp.zeros((8, SHARE), F32)
        lows = []
        for block in range(6):
            lows.append(total[block * CLIP_ROWS : block * CLIP_ROWS + 8].astype(BF16))
            lanes = slice(block * LANES, (block + 1) * LANES)
            cond = cond + dot_rows(lows[-1], refs.ada[:, lanes])
        clips = refs.condition.shape[0]
        refs.cond_own[...] = jnp.zeros_like(refs.cond_own)
        for row in range(2 * clips):
            clip, side = divmod(row, 2)
            refs.cond_own[row : row + 1, :] = cond[
                clip : clip + 1, side * LANES : (side + 1) * LANES
            ]
        refs.cond_all[z, x, y, c] = refs.cond_own[...]
        copies = [
            small(refs.cond_own, refs.cond_all.at[z, x, y, c], place.shifted(*change))
            for change in EVERYONE
        ]
        for block, low in enumerate(lows):
            lanes = slice(block * LANES, (block + 1) * LANES)
            refs.grad_ada[:, lanes] = dot_tokens(act_rows(refs, place), low)
            refs.grad_bias[block : block + 1, :] = jnp.sum(
                low[:CLIP_ROWS].astype(F32), axis=0, keepdims=True
            )
        run(23)
        for copy in table:
            copy.wait()
        total = refs.table_yc[0, 0] + refs.table_yc[0, 1] + refs.table_yc[1, 0] + refs.table_yc[1, 1]
        for head in range(2):
            for frame in range(FRAMES):
                first = (FRAMES - 1 - frame) * OFFSETS
                row = head * (WIDE // WSIDE) + frame
                refs.table_total[head : head + 1, first : first + OFFSETS] = total[
                    row : row + 1, :OFFSETS
                ]
        run(100)
        for copy in copies:
            copy.wait()
        for block in range(4):
            total = refs.cond_all[0, 0, block // 2, block % 2]
            for other in range(1, 8):
                total = total + refs.cond_all[other // 2, other % 2, block // 2, block % 2]
            for row in range(2 * clips):
                clip, side = divmod(row, 2)
                first = block * SHARE + side * LANES
                value = refs.condition[clip : clip + 1, first : first + LANES]
                gate = 1.0 / (1.0 + jnp.exp(-value))
                refs.grad_condition[clip : clip + 1, first : first + LANES] = (
                    total[row : row + 1] * gate * (1.0 + value * (1.0 - gate))
                )
        work.sent()


def enter_plain(tokens, held, mod):
    rows = tokens.shape[0]
    inputs = {"tokens": (tokens, vmem()), "held": (held, anywhere()), "mod": (mod, vmem())}
    outputs = {
        "normed": (shape(BF16, rows, D), vmem()),
        "packed": (shape(BF16, 3, rows, D), vmem()),
    }
    scratch = {
        "units": pltpu.VMEM((1, *SPLIT), BF16),
        "fetches": pltpu.SemaphoreType.DMA((1,)),
    }
    return call(enter_plain_kernel, "enter_plain", inputs, outputs, scratch)


def whole(array):
    return pl.BlockSpec(
        array.shape, lambda p: (0,) * len(array.shape), pipeline_mode=pl.Buffered(1)
    )


def result(dtype, *sizes):
    made = shape(dtype, *sizes)
    return made, whole(made)


def attend_probs(windows, first):
    def pair(step):
        return forward_pair(jnp.clip(step - first, 0, H // 2 - 1))

    return (
        shape(BF16, windows, H, WIN, WIN),
        pl.BlockSpec((windows, 2, WIN, WIN), lambda p: (0, pair(p), 0, 0)),
    )


def attend_scratch():
    return {"strip": pltpu.VMEM((2, CELLS, STRIP), F32), "bias": pltpu.VMEM((2, WIN, WIN), F32)}


def middle_outputs(rows):
    return {
        "output": result(BF16, rows, D),
        "grad_middle": result(F32, rows, D),
        "grad_mixed": result(BF16, rows, D),
        "sums": result(F32, rows // WIN, 8, D),
        "part": (shape(BF16, UNITS, *SPLIT), anywhere()),
    }


def middle_scratch(rows):
    return {
        "units": pltpu.VMEM((4, *SPLIT), BF16),
        "attended": pltpu.VMEM((rows, D), F32),
        "normed2": pltpu.VMEM((rows, D), BF16),
        "mlp": pltpu.VMEM((rows, D), F32),
        "grad_normed": pltpu.VMEM((rows, D), F32),
        "packed": pltpu.VMEM((3, rows, D), BF16),
        "made": pltpu.VMEM((2, *SPLIT), BF16),
        "fetches": pltpu.SemaphoreType.DMA((4,)),
        "made_sem": pltpu.SemaphoreType.DMA((2,)),
    }


def middle_plain(live_frames, tokens, cotangent, mixed, mod, held):
    rows = tokens.shape[0]
    inputs = {
        name: (array, whole(array))
        for name, array in (
            ("tokens", tokens),
            ("cotangent", cotangent),
            ("mixed", mixed),
            ("mod", mod),
        )
    }
    inputs |= {"live": (live_frames, smem()), "held": (held, anywhere())}
    return call(
        middle, "middle", inputs, middle_outputs(rows), middle_scratch(rows), grid=(1,), limit=60
    )


def begin(tokens, cotangent, own, smalls):
    rows = tokens.shape[0]
    windows = rows // WIN
    inputs = {"tokens": (tokens, whole(tokens)), "cotangent": (cotangent, whole(cotangent))}
    for name, block in zip(("qkv", "out", "up", "down"), own, strict=True):
        inputs[name] = (block, whole(block))
    for name, array in zip(("condition", "ada", "bias_in", "rel_table"), smalls[1:], strict=True):
        inputs[name] = (array, whole(array))
    inputs["frames"] = (smalls[0], smem())
    outputs = middle_outputs(rows) | {
        "probs": attend_probs(windows, 1),
        "side_out": result(BF16, *Reduce.side_shape(len(EARLY) - len(DONE))),
        "total": result(F32, len(DONE), SHARE, LANES),
        "normed": result(BF16, rows, D),
        "packed_out": (shape(BF16, 3, rows, D), anywhere()),
        "held": (shape(BF16, UNITS, *SPLIT), anywhere()),
        "mod": result(F32, windows, 8, D),
        "member": result(F32, windows, CLIP_ROWS, LANES),
        "live": (shape(jnp.int32, windows), smem()),
    }
    stages = gather_stages(ENTER + tuple(ATTEND.values()) + tuple(MIDDLE.values()))
    scratch = attend_scratch() | middle_scratch(rows)
    scratch |= {
        "mixed": pltpu.VMEM((rows, D), BF16),
        "core": pltpu.VMEM(Reduce.core_shape(len(EARLY)), BF16),
        "side": pltpu.VMEM(Reduce.side_shape(len(EARLY)), BF16),
        "corner": pltpu.VMEM(Reduce.corner_shape(len(DONE)), BF16),
        "distant": pltpu.VMEM(Reduce.distant_shape(len(DONE)), BF16),
        "aside": pltpu.VMEM(Reduce.aside_shape(1), BF16),
        "reduce": Reduce.scratch(EARLY_POINTS),
        "packed_sem": pltpu.SemaphoreType.DMA((3,)),
        "own": pltpu.VMEM((UNITS, SHARE, LANES), BF16),
        "own_sem": pltpu.SemaphoreType.DMA((UNITS,)),
        "gather": Gather.semaphores(stages),
        "small": [pltpu.SemaphoreType.DMA((18,))] * 2,
        "mod_part": pltpu.VMEM((MOD_ROWS, LANES), F32),
        "mod_parts": pltpu.VMEM((2, 2, MOD_ROWS, LANES), F32),
        "mods": pltpu.VMEM((4, 2, MOD_ROWS, LANES), F32),
        "rows": pltpu.VMEM((24, TILE), F32),
        "spread": pltpu.VMEM((2 * SPREAD, LANES), F32),
        "table_own": pltpu.VMEM((2, SPREAD, LANES), BF16),
        "table": pltpu.VMEM((4, 2, 2, SPREAD, LANES), BF16),
    }
    return call(
        start_kernel,
        "start",
        inputs,
        outputs,
        scratch,
        collective=0,
        grid=(H // 2 + 2,),
        limit=63,
    )


def deliver_kernel(refs):
    names = [name for name in vars(refs) if name.startswith("from_")]
    loads, stores = [], []
    for index, name in enumerate(names):
        plain = name[len("from_") :]
        held = getattr(refs, "held_" + plain)
        loads.append(pltpu.make_async_copy(getattr(refs, name), held, refs.sems.at[0, index]))
        stores.append(pltpu.make_async_copy(held, getattr(refs, plain), refs.sems.at[1, index]))
        loads[-1].start()
    for load, store in zip(loads, stores, strict=True):
        load.wait()
        store.start()
    for store in stores:
        store.wait()


def deliver(**arrays):
    inputs = {"from_" + name: (array, anywhere()) for name, array in arrays.items()}
    outputs = {name: (shape(array.dtype, *array.shape), anywhere()) for name, array in arrays.items()}
    scratch = {"held_" + name: pltpu.VMEM(array.shape, array.dtype) for name, array in arrays.items()}
    scratch["sems"] = pltpu.SemaphoreType.DMA((2, len(arrays)))
    return call(deliver_kernel, "deliver", inputs, outputs, scratch)


def attend_plain(packed, table, live_frames):
    windows = live_frames.shape[0]
    rows = windows * WIN
    inputs = {
        "live": (live_frames, smem()),
        "query": (packed, packed_block(0, rows, forward_pair)),
        "key": (packed, packed_block(1, rows, forward_pair)),
        "value": (packed, packed_block(2, rows, forward_pair)),
        "table": (table, pl.BlockSpec((2, SPREAD, LANES), lambda p: (forward_pair(p), 0, 0))),
    }
    return call(
        attend_plain_kernel,
        "attend_plain",
        inputs,
        {
            "mixed": (
                shape(BF16, rows, D),
                pl.BlockSpec((rows, LANES), lambda p: (0, forward_pair(p))),
            ),
            "probs": attend_probs(windows, 0),
        },
        attend_scratch(),
        grid=(H // 2,),
    )


def back(
    special, live_frames, tokens, mod, packed, normed, probs, mid, held, ada, member, condition
):
    window_count = probs.shape[0]
    rows = window_count * WIN
    pairs = H // 2

    def last(step):
        return backward_pair(jnp.minimum(step, pairs - 1))

    def packed_pair(which):
        return packed_block(which, rows, last)

    inputs = {
        "live": (live_frames, smem()),
        "query": (packed, packed_pair(0)),
        "key": (packed, packed_pair(1)),
        "value": (packed, packed_pair(2)),
        "probs": (
            probs,
            pl.BlockSpec((window_count, 2, WIN, WIN), lambda p: (0, last(p), 0, 0)),
        ),
        "grad": (mid.grad_mixed, pl.BlockSpec((rows, LANES), lambda p: (0, last(p)))),
        "held": (held, anywhere()),
    }
    for name, array in (
        ("tokens", tokens),
        ("mod", mod),
        ("normed", normed),
        ("grad_middle", mid.grad_middle),
    ):
        inputs[name] = (array, whole(array))

    outputs = {"grad_tokens": result(F32, rows, D)}
    scratch = {
        "strip": pltpu.VMEM((2, CELLS, STRIP), F32),
        "grad_packed": pltpu.VMEM((3, rows, D), BF16),
        "unit": pltpu.VMEM(SPLIT, BF16),
        "grad_normed": pltpu.VMEM((rows, D), F32),
        "fetch": pltpu.SemaphoreType.DMA,
    }
    if not special:
        outputs["sums"] = result(F32, window_count, 8, D)
        outputs["part"] = (shape(BF16, 3, *SPLIT), anywhere())
        outputs["spread"] = (
            shape(F32, H, SPREAD, LANES),
            pl.BlockSpec((2, SPREAD, LANES), lambda p: (last(p), 0, 0)),
        )
        scratch["made"] = pltpu.VMEM(SPLIT, BF16)
        scratch["made_sem"] = pltpu.SemaphoreType.DMA
        return call(
            back_plain_kernel, "back_plain", inputs, outputs, scratch, grid=(pairs + 1,)
        )
    inputs |= {
        "late_sums": (mid.sums, whole(mid.sums)),
        "ada": (ada, whole(ada)),
        "condition": (condition, whole(condition)),
        "member": (member, whole(member)),
        "side_in": (mid.side_out, whole(mid.side_out)),
        "done": (mid.total, whole(mid.total)),
        "part": (mid.part, anywhere()),
    }
    outputs |= {
        "grad_qkv": result(F32, SHARE, 3 * LANES),
        "grad_out": result(F32, SHARE, LANES),
        "grad_up": result(F32, SHARE, 4 * LANES),
        "grad_down": result(F32, 4 * SHARE, LANES),
        "grad_ada": result(F32, SHARE, 6 * LANES),
        "grad_bias": result(F32, 6, LANES),
        "grad_condition": result(F32, *condition.shape),
        "table_total": result(F32, 2, REL),
    }
    count, late = len(EARLY + LATE), len(LATE)
    scratch |= {
        "spread": pltpu.VMEM((2, WIDE, LANES), F32),
        "spreads": pltpu.VMEM((H * WIDE, LANES), F32),
        "made": pltpu.VMEM((3, *SPLIT), BF16),
        "sums": pltpu.VMEM((window_count, 8, D), F32),
        "core": pltpu.VMEM(Reduce.core_shape(late), BF16),
        "side": pltpu.VMEM(Reduce.side_shape(late), BF16),
        "corner": pltpu.VMEM(Reduce.corner_shape(count), BF16),
        "distant": pltpu.VMEM(Reduce.distant_shape(count), BF16),
        "aside": pltpu.VMEM(Reduce.aside_shape(1), BF16),
        "reduce": Reduce.scratch(LATE_POINTS),
        "table": pltpu.VMEM((4, 2, 2 * WIDE // WSIDE, TILE), F32),
        "table_zx": pltpu.VMEM((4, 2, 2 * WIDE // WSIDE, TILE), F32),
        "table_own": pltpu.VMEM((2 * WIDE // WSIDE, TILE), F32),
        "table_yc": pltpu.VMEM((2, 2, 2 * WIDE // WSIDE, TILE), F32),
        "clip": pltpu.VMEM((4, 2, MOD_ROWS, LANES), F32),
        "clip_zx": pltpu.VMEM((4, 2, MOD_ROWS, LANES), F32),
        "clip_own": pltpu.VMEM((MOD_ROWS, LANES), F32),
        "clip_yc": pltpu.VMEM((2, 2, MOD_ROWS, LANES), F32),
        "cond_own": pltpu.VMEM((8, LANES), F32),
        "cond_all": pltpu.VMEM((4, 2, 2, 2, 8, LANES), F32),
        "small": [pltpu.SemaphoreType.DMA((51,))] * 2,
    }
    return call(
        back_kernel,
        "back",
        inputs,
        outputs,
        scratch,
        collective=3,
        grid=(pairs + 1,),
        limit=62,
    )


def per_device(
    special,
    tokens,
    condition,
    clip_frames,
    ada_weight,
    ada_bias,
    qkv_weight,
    out_weight,
    up_weight,
    down_weight,
    rel_table,
    cotangent,
):
    window_count = tokens.shape[0]
    clip_count = condition.shape[0]
    rows_ada, cols_ada = ada_weight.shape
    token_rows = tokens.reshape(window_count * WIN, D)
    cotangent_rows = cotangent.reshape(window_count * WIN, D)
    own = (qkv_weight, out_weight, up_weight, down_weight)
    if special:
        smalls = (clip_frames, condition, ada_weight, ada_bias.reshape(1, cols_ada), rel_table)
        start = across = mid = begin(token_rows, cotangent_rows, own, smalls)
        live_frames, member_wide, mod = start.live, start.member, start.mod
        packed, held = start.packed_out, start.held
    else:
        row_block = lax.axis_index("fsdp")
        col_block = lax.axis_index("dp")
        first_window = lax.axis_index(("dp", "fsdp")) * window_count
        live_frames, member_int = window_layout(clip_frames, first_window, window_count)
        member = member_int.astype(F32)
        activity_low = jax.nn.silu(condition).astype(BF16)
        rows_own = lax.dynamic_slice_in_dim(activity_low, row_block * rows_ada, rows_ada, 1)
        mod_part = jnp.dot(rows_own, ada_weight, preferred_element_type=F32)
        clip_mod = lax.all_gather(lax.psum(mod_part, "fsdp"), "dp", axis=1, tiled=True)
        bias = lax.all_gather(ada_bias, "dp", axis=0, tiled=True)
        clip_mod = clip_mod + bias.astype(F32)[None, :]
        member_wide = None
        window_mod = jnp.sum(member[:, :, None] * clip_mod[None], axis=1)
        window_mod = jnp.pad(window_mod.reshape(window_count, 6, D), ((0, 0), (0, 2), (0, 0)))
        whole = [
            lax.all_gather(
                lax.all_gather(weight, "dp", axis=1, tiled=True), "fsdp", axis=0, tiled=True
            )
            for weight in own
        ]
        held = units_of(*whole).reshape(UNITS, *SPLIT)
        mod = window_mod
        start = enter_plain(token_rows, held, mod)
        packed = start.packed
        table = spread_table(lax.all_gather(rel_table, "dp", axis=0, tiled=True))
        across = attend_plain(packed, table, live_frames)
        mid = middle_plain(live_frames, token_rows, cotangent_rows, across.mixed, mod, held)
    end = back(
        special,
        live_frames,
        token_rows,
        mod,
        packed,
        start.normed,
        across.probs,
        mid,
        held,
        ada_weight,
        member_wide,
        condition,
    )
    if special:
        end = deliver(
            output=mid.output,
            grad_tokens=end.grad_tokens,
            grad_condition=end.grad_condition,
            grad_ada=end.grad_ada,
            grad_bias=end.grad_bias,
            grad_qkv=end.grad_qkv,
            grad_out=end.grad_out,
            grad_up=end.grad_up,
            grad_down=end.grad_down,
            table=end.table_total,
        )
        return (
            end.output.reshape(tokens.shape),
            end.grad_tokens.reshape(tokens.shape),
            end.grad_condition,
            end.grad_ada,
            end.grad_bias.reshape(cols_ada),
            end.grad_qkv,
            end.grad_out,
            end.grad_up,
            end.grad_down,
            end.table,
        )
    part = jnp.concatenate([end.part, mid.part[OUT:]])
    grads = [
        lax.psum_scatter(
            lax.psum_scatter(grad, "fsdp", scatter_dimension=0, tiled=True),
            "dp",
            scatter_dimension=1,
            tiled=True,
        ).astype(F32)
        for grad in weights_of(part.reshape(UNITS, 8, D, LANES))
    ]
    grad_mod = (mid.sums + end.sums)[:, :6].reshape(window_count, 6 * D)
    clip_part = lax.dot_general(
        member,
        grad_mod,
        (((0,), (0,)), ((), ())),
        precision=HIGHEST,
        preferred_element_type=F32,
    )
    clip_sum, table_sum = lax.psum((clip_part, gather_table(end.spread)), ("dp", "fsdp"))
    clip_cols = lax.dynamic_slice_in_dim(
        clip_sum.astype(BF16), col_block * cols_ada, cols_ada, 1
    )
    heads_own = rel_table.shape[0]
    table_grad = lax.dynamic_slice_in_dim(table_sum, col_block * heads_own, heads_own, 0)
    cond_part = lax.dot_general(
        clip_cols, ada_weight, (((1,), (1,)), ((), ())), preferred_element_type=F32
    )
    cond_total = lax.all_gather(lax.psum(cond_part, "dp"), "fsdp", axis=1, tiled=True)
    grad_ada_weight = lax.dot_general(
        rows_own, clip_cols, (((0,), (0,)), ((), ())), preferred_element_type=F32
    )
    grad_ada_bias = jnp.sum(clip_cols.astype(F32), axis=0)
    _, silu_back = jax.vjp(jax.nn.silu, condition)
    return (
        mid.output.reshape(tokens.shape),
        end.grad_tokens.reshape(tokens.shape),
        silu_back(cond_total)[0],
        grad_ada_weight,
        grad_ada_bias,
        *grads,
        table_grad,
    )


def solution(mesh):
    special = dict(mesh.shape) == {"dp": 8, "fsdp": 4}
    both = P(("dp", "fsdp"), None, None)
    weight = P("fsdp", "dp")
    in_specs = (both, P(), P(), weight, P("dp")) + (weight,) * 4 + (P("dp", None), both)
    out_specs = (both, both, P(), weight, P("dp")) + (weight,) * 4 + (P("dp", None),)
    return jax.shard_map(
        functools.partial(per_device, special),
        mesh=mesh,
        in_specs=in_specs,
        out_specs=out_specs,
        check_vma=False,
    )
```

```python
import functools

import jax
import jax.numpy as jnp
from jax import lax
from jax.experimental import pallas as pl
from jax.experimental.pallas import tpu as pltpu
from jax.sharding import PartitionSpec as P

D = 1024
H = 16
HD = 64
WT = 5
WSIDE = 8
WIN = 320
SPW = 16
CELLS = WSIDE * WSIDE
FRAMES = 2 * WT - 1
OFFSETS = (2 * WSIDE - 1) ** 2
REL = FRAMES * OFFSETS
LANES = 128
TILE = 256
SPREAD = 80
WIDE = 96
STRIP = 640

EPSILON = 1e-06
NEGATIVE = -1000000000.0
HIGHEST = lax.Precision.HIGHEST
F32 = jnp.float32
BF16 = jnp.bfloat16
MESH = pl.DeviceIdType.MESH
MIB = 2**20

QKV, OUT, UP, DOWN, UNITS = 0, 3, 4, 8, 12
PICK = (
    (1, 2, 0),
    (1, 2, 0),
    (0, 1, 2),
    (0, 1, 2),
    (0, 1, 2),
    (2, 0, 1),
    (2, 0, 1),
    (1, 0, 2),
)
SHARE = 256
HALF = 128


SPLIT = (4, 2, 2, 2, SHARE, LANES)
CLIP_ROWS = 4
MOD_ROWS = 6 * CLIP_ROWS
OWN_SLOTS = 4
ORDER = (0, 1, 2, 3, 4, 8, 5, 9, 6, 10, 7, 11)
GATHER_ASIDE = (DOWN + 3,)
REDUCE_ASIDE = (DOWN, UP + 2)
ENTER = (((0, 1), (1, 1), (11, 1), (0, 2)), ((2, 1), (0, 3), (5, 1)), ((1, 2), (2, 2), (0, 4), (1, 3)), ((7, 1),), ((5, 2), (3, 1)), ((1, 4), (4, 1), (11, 2), (2, 3), (6, 1)))
ATTEND = {0: ((8, 1), (5, 3)), 1: ((7, 2), (10, 1)), 3: ((3, 2), (4, 2), (2, 4)), 4: ((6, 2), (3, 3)), 5: ((5, 4), (4, 3), (9, 1), (6, 3)), 7: ((11, 3), (3, 4), (8, 2), (7, 3), (4, 4))}
MIDDLE = {1: ((6, 4),), 2: ((8, 3),), 3: ((9, 2),), 4: ((10, 2), (7, 4)), 5: ((8, 4),), 6: ((9, 3), (11, 4)), 7: ((10, 3),), 8: ((9, 4),), 10: ((10, 4),)}
EARLY = (DOWN, UP, DOWN + 1, UP + 1, DOWN + 2)
DONE = EARLY[:4]
EARLY_POINTS = {5: ((8, 0),), 7: ((8, 1), (4, 0)), 9: ((4, 1), (9, 0)), 10: ((9, 1),), 12: ((5, 0),), 13: ((4, 2), (9, 2), (5, 1)), 15: ((10, 0), (8, 2), (9, 3)), 17: ((4, 3), (5, 2), (10, 1)), 18: ((8, 3), (9, 4), (5, 3)), 19: ((10, 2),), 20: ((5, 4),), 22: ((8, 4), (4, 4))}
LATE = (UP + 2, DOWN + 3, UP + 3, OUT, QKV, QKV + 1, QKV + 2)
LATE_POINTS = {0: ((6, 0), (11, 0)), 1: ((6, 1), (3, 0), (10, -3), (11, 1)), 2: ((7, 0), (3, 1)), 3: ((10, 3), (11, 2)), 5: ((7, 1), (3, 2), (0, 0)), 6: ((11, 3), (1, 0)), 7: ((7, 2), (3, 3), (0, 1)), 11: ((1, 1), (2, 0)), 12: ((7, 3), (0, 2)), 14: ((1, 2),), 15: ((0, 3), (2, 1), (3, 4)), 16: ((6, 2), (10, 4)), 18: ((1, 3), (2, 2), (6, 3)), 19: ((2, 3),), 20: ((6, 4),), 22: ((2, 4), (1, 4)), 23: ((11, 4),), 24: ((0, 4), (7, 4))}
def reduce_stages(points):
    moves = [move for at in sorted(points) for move in points[at]]
    started = [(unit, 3 if stage == -3 else stage + 1) for unit, stage in moves if stage < 4]
    return [(unit, stage) for unit, stage in started if stage > 3 or (unit, stage) in moves or stage < 3]


def gather_stages(points):
    return [(ORDER[index], stage) for point in points for index, stage in point]


def forward_pair(step):
    first = (13 - step) // 8
    return first * ((step // 2 + 1) % 3 + 3 * (step % 2)) + (1 - first) * step


def backward_pair(step):
    group, place = step // 3, step % 3
    return (1 + group) % 3 + 3 * place - place // 2


def pair_unit(which, pair):
    first = (13 - pair) // 8
    sixth, seventh = ((0, 2, 0), (1, 1, 2))[0][which], ((0, 2, 0), (1, 1, 2))[1][which]
    return first * ((pair + 2) % 3) + (1 - first) * ((7 - pair) * sixth + (pair - 6) * seventh)


def pair_block(which, pair):
    return (which * (H // 2) + pair) // 3


def picked(block, j):
    return sum(jnp.where(block == index, PICK[index][j], 0) for index in range(8))


def window_layout(clip_frames, first_window, window_count):
    slab_count = 1 + (clip_frames > WT).astype(jnp.int32)
    starts = jnp.cumsum(slab_count, dtype=jnp.int32) - slab_count
    global_window = first_window + jnp.arange(window_count, dtype=jnp.int32)
    slab_of = global_window // SPW
    owners = jnp.sum((starts[None, :] <= slab_of[:, None]).astype(jnp.int32), axis=1) - 1
    clip_ids = jnp.arange(clip_frames.shape[0], dtype=jnp.int32)
    member = (owners[:, None] == clip_ids[None, :]).astype(jnp.int32)
    clip_start = jnp.sum(member * starts[None, :], axis=1)
    own_frames = jnp.sum(member * clip_frames[None, :], axis=1)
    inner_slab = slab_of - clip_start
    return (jnp.minimum(own_frames - WT * inner_slab, WT), member)


def offset_spread():
    side_span = 2 * WSIDE - 1
    shape = (OFFSETS, WSIDE * LANES)
    offset = lax.broadcasted_iota(jnp.int32, shape, 0)
    place = lax.broadcasted_iota(jnp.int32, shape, 1)
    own, row, other = place // LANES, place // WSIDE % (LANES // WSIDE), place % WSIDE
    row_diff, col_diff = side_span - 1 - row, own - other + (WSIDE - 1)
    return ((row < side_span) & (row_diff * side_span + col_diff == offset)).astype(BF16)


def spread_table(table):
    heads = table.shape[0]
    by_frame = table.reshape(heads, FRAMES, OFFSETS)[:, ::-1].reshape(heads * FRAMES, OFFSETS)
    spread = jnp.dot(by_frame, offset_spread(), preferred_element_type=F32).astype(BF16)
    spread = spread.reshape(heads, FRAMES * WSIDE, LANES)
    return jnp.pad(spread, ((0, 0), (0, SPREAD - FRAMES * WSIDE), (0, 0)))


def gather_table(spread):
    heads = spread.shape[0]
    by_frame = spread[:, : FRAMES * WSIDE].reshape(heads * FRAMES, WSIDE * LANES)
    sums = lax.dot_general(
        by_frame,
        offset_spread().astype(F32),
        (((1,), (1,)), ((), ())),
        precision=HIGHEST,
        preferred_element_type=F32,
    )
    return sums.reshape(heads, FRAMES, OFFSETS)[:, ::-1].reshape(heads, FRAMES * OFFSETS)


def units_of(qkv, out, up, down):
    return jnp.concatenate(
        [
            jnp.stack(
                [
                    jnp.stack([qkv[:, 384 * b + LANES * PICK[b][j] :][:, :LANES] for b in range(8)])
                    for j in range(3)
                ]
            ),
            out.reshape(D, 8, 1, LANES).transpose(2, 1, 0, 3),
            up.reshape(D, 8, 4, LANES).transpose(2, 1, 0, 3),
            down.reshape(8, 4, LANES, 8, LANES).transpose(1, 3, 0, 2, 4).reshape(4, 8, D, LANES),
        ]
    )


def weights_of(units):
    def columns(part):
        return part.transpose(2, 1, 0, 3).reshape(D, -1)

    down = units[DOWN:].reshape(4, 8, 8, LANES, LANES).transpose(2, 0, 3, 1, 4)
    qkv = [
        units[PICK[block].index(tile), block] for block in range(8) for tile in range(3)
    ]
    return (
        jnp.concatenate(qkv, axis=1),
        columns(units[OUT:UP]),
        columns(units[UP:DOWN]),
        down.reshape(4 * D, D),
    )


def dot(left, right):
    return jnp.dot(left, right, preferred_element_type=F32)


def dot_rows(left, right):
    return lax.dot_general(left, right, (((1,), (1,)), ((), ())), preferred_element_type=F32)


def dot_tokens(left, right):
    return lax.dot_general(left, right, (((0,), (0,)), ((), ())), preferred_element_type=F32)


def half(index):
    return pl.ds(pl.multiple_of(index * 512, 512), 512)


def four_columns(unit, index):
    blocks = [unit[2 * index + x // 2, x % 2].reshape(D, LANES) for x in range(4)]
    return jnp.concatenate(blocks, axis=1)


def half_rows(unit, index):
    blocks = [unit[block // 2, block % 2, index].reshape(512, LANES) for block in range(8)]
    return jnp.concatenate(blocks, axis=1)


def put_columns(unit, index, values):
    for x in range(4):
        unit[2 * index + x // 2, x % 2] = values[:, x * LANES : (x + 1) * LANES].reshape(2, 2, SHARE, LANES)


def loop(count, body):
    def step(index, carry):
        body(index)
        return carry

    lax.fori_loop(0, count, step, 0)


def vmem():
    return pl.BlockSpec(memory_space=pltpu.VMEM)


def anywhere():
    return pl.BlockSpec(memory_space=pl.ANY)


def smem():
    return pl.BlockSpec(memory_space=pltpu.SMEM)


def shape(dtype, *sizes):
    return jax.ShapeDtypeStruct(sizes, dtype)


def params(collective=None, limit=58):
    if collective is None:
        return pltpu.CompilerParams(vmem_limit_bytes=limit * MIB)
    return pltpu.CompilerParams(
        vmem_limit_bytes=limit * MIB, collective_id=collective, has_side_effects=True
    )


def centered(values):
    center = values - jnp.mean(values, axis=-1, keepdims=True)
    spread = jnp.mean(center * center, axis=-1, keepdims=True)
    root = lax.rsqrt(spread + EPSILON)
    return center * root, root


def norm_back(grad_normed, normal, root, scale):
    grad = grad_normed * (1.0 + scale)
    mean = jnp.mean(grad, axis=-1, keepdims=True)
    along = jnp.mean(grad * normal, axis=-1, keepdims=True)
    return root * (grad - mean - normal * along)


def each_rows(mod_ref, live_ref, body, rows=32, pump=lambda window: None):
    for window in range(mod_ref.shape[0]):
        live = live_ref[window] * CELLS

        def step(index, window=window, live=live):
            at = pl.ds(pl.multiple_of(window * WIN + index * rows, rows), rows)
            mods = [mod_ref[window, k : k + 1, :] for k in range(6)]
            slot = index * rows + lax.broadcasted_iota(jnp.int32, (rows, 1), 0)
            body(window, at, mods, slot < live)

        loop(WIN // rows, step)
        pump(window)


def add_sums(sums_ref, window, which, values):
    sums_ref[window, which : which + 1, :] += jnp.sum(values, axis=0, keepdims=True)


class Place:
    def __init__(self):
        column, row = lax.axis_index("dp"), lax.axis_index("fsdp")
        self.z, self.x, self.y, self.c = column // 2, column % 2, row // 2, row % 2

    def at(self, z=None, x=None, y=None, c=None):
        z = self.z if z is None else z
        x = self.x if x is None else x
        y = self.y if y is None else y
        c = self.c if c is None else c
        return (z * 2 + x, y * 2 + c)

    def far(self, k):
        return lax.rem(self.z + k, 4)

    def shifted(self, dz, dx, dy, dc):
        def other(index, change):
            return 1 - index if change else index

        return self.at(self.far(dz), other(self.x, dx), other(self.y, dy), other(self.c, dc))

    def greet(self, far_ones=()):
        near = [(1, 0, 0, 0), (2, 0, 0, 0), (3, 0, 0, 0), (0, 1, 0, 0), (0, 0, 1, 0), (0, 0, 0, 1)]
        peers = near + [change for change in far_ones if change not in near]
        barrier = pltpu.get_barrier_semaphore()
        for change in peers:
            pl.semaphore_signal(
                barrier, inc=1, device_id=self.shifted(*change), device_id_type=MESH
            )
        pl.semaphore_wait(barrier, len(peers))


EVERYONE = [
    (dz, dx, dy, dc)
    for dz in range(4)
    for dx in range(2)
    for dy in range(2)
    for dc in range(2)
    if (dz, dx, dy, dc) != (0, 0, 0, 0)
]
ALONG_ZX = [change for change in EVERYONE if change[2:] == (0, 0)]
ALONG_YC = [change for change in EVERYONE if change[:2] == (0, 0)]


class Moves:
    def __init__(self, place, stages, scratch):
        self.place = place
        self.send, self.recv = scratch
        self.first, count = {}, 0
        for unit, stage in stages:
            self.first[unit, stage] = count
            count += self.counts[unit in self.aside][stage - 1]
        self.flying = []

    @classmethod
    def semaphores(cls, stages):
        count = sum(cls.counts[unit in cls.aside][stage - 1] for unit, stage in stages)
        return [pltpu.SemaphoreType.DMA((count,))] * 2

    def made(self, unit, stage, moves):
        copies = []
        for index, (source, target, device) in enumerate(moves):
            slot = self.first[unit, stage] + index
            copies.append(
                pltpu.make_async_remote_copy(
                    src_ref=source,
                    dst_ref=target,
                    send_sem=self.send.at[slot],
                    recv_sem=self.recv.at[slot],
                    device_id=device,
                    device_id_type=MESH,
                )
            )
        return copies

    def begin(self, unit, stage):
        for copy in self.copies(unit, stage):
            copy.start()
        self.flying.append((unit, stage))

    def arrive(self, unit, stage):
        if (unit, stage) in self.flying:
            self.flying.remove((unit, stage))
            for copy in self.copies(unit, stage):
                copy.wait_recv()

    def sent(self):
        for unit, stage in self.first:
            for copy in self.copies(unit, stage):
                copy.wait_send()


class Gather(Moves):
    counts = ((3, 2, 2, 1), (2, 2, 3, 1))
    aside = GATHER_ASIDE

    def __init__(self, place, held, stages, scratch):
        super().__init__(place, stages, scratch)
        self.held = held

    def copies(self, unit, stage):
        p, held = self.place, self.held.at[unit]
        at_x, at_y, at_core = p.at(x=1 - p.x), p.at(y=1 - p.y), p.at(c=1 - p.c)
        own = held.at[p.z, p.x, p.y, p.c]
        if stage == 4:
            refs = [(held.at[:, :, :, p.c], at_core)]
        elif unit in self.aside and stage == 1:
            refs = [(own.at[:HALF], at_x), (own.at[HALF:], at_y)]
        elif unit in self.aside and stage == 2:
            refs = [
                (held.at[p.z, :, p.y, p.c, :HALF], at_y),
                (held.at[p.z, p.x, :, p.c, HALF:], at_x),
            ]
        elif unit in self.aside:
            refs = [(held.at[p.z, :, :, p.c], p.at(z=p.far(k))) for k in (1, 2, 3)]
        elif stage == 1:
            refs = [(own, p.at(z=p.far(k))) for k in (1, 2, 3)]
        elif stage == 2:
            refs = [
                (held.at[:, p.x, p.y, p.c, :HALF], at_x),
                (held.at[:, p.x, p.y, p.c, HALF:], at_y),
            ]
        else:
            refs = [
                (held.at[:, :, p.y, p.c, :HALF], at_y),
                (held.at[:, p.x, :, p.c, HALF:], at_x),
            ]
        return self.made(unit, stage, [(ref, ref, device) for ref, device in refs])

    def advance(self, unit, stage):
        self.arrive(unit, stage - 1)
        self.begin(unit, stage)

    def finish(self):
        for unit, stage in list(self.flying):
            self.arrive(unit, stage)
        self.sent()


class Reduce(Moves):
    counts = ((1, 2, 2, 3), (1, 3, 2, 2))
    aside = REDUCE_ASIDE

    def __init__(self, place, part, points, store, buffers, scratch):
        super().__init__(place, reduce_stages(points), scratch[2:])
        self.part, self.store, self.buffers = part, store, buffers
        self.own, self.load = scratch[:2]
        self.slots, self.loaded = {}, []

    @classmethod
    def scratch(cls, points):
        return [
            pltpu.VMEM((OWN_SLOTS, 4, 2, 2, SHARE, LANES), BF16),
            pltpu.SemaphoreType.DMA((OWN_SLOTS,)),
        ] + cls.semaphores(reduce_stages(points))

    @staticmethod
    def core_shape(count):
        return (count, 4, 2, 2, SHARE, LANES)

    @staticmethod
    def side_shape(count):
        return (count, 2, 4, 2, HALF, LANES)

    @staticmethod
    def corner_shape(count):
        return (count, 2, 4, HALF, LANES)

    @staticmethod
    def distant_shape(count):
        return (count, 3, 2, HALF, LANES)

    @staticmethod
    def aside_shape(count):
        return (count, 3, 2, 2, SHARE, LANES)

    def own_copy(self, unit):
        slot = self.slots.setdefault(unit, len(self.slots) % OWN_SLOTS)
        return pltpu.make_async_copy(
            self.part(unit).at[:, :, :, self.place.c], self.own.at[slot], self.load.at[slot]
        )

    def copies(self, unit, stage):
        p = self.place
        at_x, at_y, at_core = p.at(x=1 - p.x), p.at(y=1 - p.y), p.at(c=1 - p.c)
        core, side, corner, distant = self.buffers(unit)
        if unit in self.aside and stage == 2:
            moves = [
                (core.at[p.far(k)], distant.at[k - 1], p.at(z=p.far(k))) for k in (1, 2, 3)
            ]
        elif unit in self.aside and stage == 3:
            moves = [
                (core.at[p.z, :, 1 - p.y, :HALF], side.at[0, 0], at_y),
                (core.at[p.z, 1 - p.x, :, HALF:], side.at[1, 0], at_x),
            ]
        elif unit in self.aside and stage == 4:
            moves = [
                (side.at[0, 0, 1 - p.x], side.at[0, 1, 0], at_x),
                (side.at[1, 0, 1 - p.y], side.at[1, 1, 0], at_y),
            ]
        elif stage == 1:
            moves = [(self.part(unit).at[:, :, :, 1 - p.c], core, at_core)]
        elif stage == 2:
            moves = [
                (core.at[:, :, 1 - p.y, :HALF], side.at[0], at_y),
                (core.at[:, 1 - p.x, :, HALF:], side.at[1], at_x),
            ]
        elif stage == 3:
            moves = [
                (side.at[0, :, 1 - p.x], corner.at[0], at_x),
                (side.at[1, :, 1 - p.y], corner.at[1], at_y),
            ]
        else:
            moves = [
                (corner.at[:, p.far(k)], distant.at[k - 1], p.at(z=p.far(k))) for k in (1, 2, 3)
            ]
        return self.made(unit, stage, moves)

    def begin(self, unit, stage):
        super().begin(unit, stage)
        if stage == 1:
            self.own_copy(unit).start()
            assert self.slots[unit] not in self.loaded
            self.loaded.append(self.slots[unit])

    def combine(self, unit, stage):
        p = self.place
        core, side, corner, distant = self.buffers(unit)

        def plus(left, right):
            return (left.astype(F32) + right.astype(F32)).astype(BF16)

        def from_core(step):
            z, x, y = step // 4, step // 2 % 2, step % 2
            core[z, x, y] = plus(core[z, x, y], self.own[self.slots[unit], z, x, y])

        def from_side(step):
            z, b = step // 2, step % 2
            side[0, z, b] = plus(side[0, z, b], core[z, b, p.y, :HALF])
            side[1, z, b] = plus(side[1, z, b], core[z, p.x, b, HALF:])

        def from_corner(z):
            corner[0, z] = plus(corner[0, z], side[0, z, p.x])
            corner[1, z] = plus(corner[1, z], side[1, z, p.y])

        def from_far(half):
            total = corner[half, p.z].astype(F32)
            for k in range(3):
                total = total + distant[k, half].astype(F32)
            self.store(unit, half, total)

        def aside_far(step):
            x, y = step // 2, step % 2
            total = core[p.z, x, y].astype(F32)
            for k in range(3):
                total = total + distant[k, x, y].astype(F32)
            core[p.z, x, y] = total.astype(BF16)

        def aside_side(b):
            side[0, 0, b] = plus(side[0, 0, b], core[p.z, b, p.y, :HALF])
            side[1, 0, b] = plus(side[1, 0, b], core[p.z, p.x, b, HALF:])

        if unit in self.aside and stage == 4:
            for part, own in enumerate((p.x, p.y)):
                total = side[part, 0, own].astype(F32) + side[part, 1, 0].astype(F32)
                self.store(unit, part, total)
            return
        steps = {1: (16, from_core), 2: (8, from_side), 3: (4, from_corner), 4: (2, from_far)}
        if unit in self.aside:
            steps |= {2: (4, aside_far), 3: (2, aside_side)}
        loop(*steps[stage])

    def step(self, unit, stage):
        if stage <= 0:
            self.begin(unit, max(1, -stage))
            return
        self.arrive(unit, stage)
        if stage == 1:
            self.own_copy(unit).wait()
        self.combine(unit, stage)
        if stage == 1:
            self.loaded.remove(self.slots[unit])
        if (unit, stage + 1) in self.first:
            self.begin(unit, stage + 1)


class Copies:
    def __init__(self, send, recv):
        self.send, self.recv, self.count = send, recv, 0

    def __call__(self, source, target, device):
        slot = self.count
        self.count += 1
        copy = pltpu.make_async_remote_copy(
            src_ref=source,
            dst_ref=target,
            send_sem=self.send.at[slot],
            recv_sem=self.recv.at[slot],
            device_id=device,
            device_id_type=MESH,
        )
        copy.start()
        return copy


class Refs:
    pass


def call(kernel, name, inputs, outputs, scratch, aliases=(), collective=None, grid=None, limit=58):
    names = list(inputs) + list(outputs)
    flat = []
    for value in scratch.values():
        flat += value if isinstance(value, list) else [value]

    def body(*refs):
        held = Refs()
        rest = list(refs)
        for key in names:
            setattr(held, key, rest.pop(0))
        for key, value in scratch.items():
            if isinstance(value, list):
                setattr(held, key, [rest.pop(0) for _ in value])
            else:
                setattr(held, key, rest.pop(0))
        kernel(held)

    extra = {} if grid is None else {"grid": grid}
    made = functools.partial(
        pl.pallas_call,
        body,
        in_specs=[spec for _, spec in inputs.values()],
        out_specs=[spec for _, spec in outputs.values()],
        out_shape=[out for out, _ in outputs.values()],
        scratch_shapes=flat,
        input_output_aliases={
            list(inputs).index(one): list(outputs).index(other) for one, other in aliases
        },
        compiler_params=params(collective, limit),
        name=name,
        **extra,
    )
    arrays = [array for array, _ in inputs.values()]
    if name == "start":
        result = made()(*arrays)
    else:
        result = made()(*arrays)
    out = Refs()
    for key, value in zip(outputs, result, strict=True):
        setattr(out, key, value)
    return out


def enter_norm(refs, pump=lambda: None):
    rows = 32
    for window in range(refs.mod.shape[0]):
        shift, scale = refs.mod[window, 0:1, :], refs.mod[window, 1:2, :]

        def step(index, window=window, shift=shift, scale=scale):
            at = pl.ds(pl.multiple_of(window * WIN + index * rows, rows), rows)
            normal, _ = centered(refs.tokens[at, :].astype(F32))
            refs.normed[at, :] = (normal * (1.0 + scale) + shift).astype(BF16)

        loop(WIN // rows, step)
        pump()


def enter_unit(refs, j, held, put=False):
    unit = refs.units.at[0]
    fetch = pltpu.make_async_copy(held, unit, refs.fetches.at[0])
    fetch.start()
    fetch.wait()

    def project(index):
        refs.packed[j, :, half(index)] = dot(refs.normed[...], four_columns(unit, index)).astype(
            BF16
        )

    loop(2, project)
    if put:
        packed_copy(refs, j).start()


def packed_copy(refs, j):
    return pltpu.make_async_copy(refs.packed.at[j], refs.packed_out.at[j], refs.packed_sem.at[j])


def enter_plain_kernel(refs):
    enter_norm(refs)
    for j in range(3):
        enter_unit(refs, j, refs.held.at[QKV + j])


def act_rows(refs, place):
    first = (place.y * 2 + place.c) * SHARE
    value = refs.condition[:, pl.ds(pl.multiple_of(first, SHARE), SHARE)]
    act = value / (1.0 + jnp.exp(-value))
    return jnp.concatenate([act, jnp.zeros((8 - value.shape[0], SHARE), F32)], axis=0).astype(BF16)


def enter_layout(refs):
    windows, clips = refs.member.shape[0], refs.condition.shape[0]
    frames = [refs.frames[clip] for clip in range(clips)]
    starts = [0]
    for count in frames:
        starts.append(starts[-1] + 1 + jnp.where(count > WT, 1, 0))
    device = lax.axis_index("dp") * lax.axis_size("fsdp") + lax.axis_index("fsdp")
    refs.member[...] = jnp.zeros_like(refs.member)
    for window in range(windows):
        slab = (device * windows + window) // SPW
        live = 0
        for clip in range(clips):
            mine = starts[clip] <= slab
            if clip < clips - 1:
                mine = mine & (slab < starts[clip + 1])
            inner = frames[clip] - WT * (slab - starts[clip])
            live = live + jnp.where(mine, jnp.minimum(inner, WT), 0)
            refs.member[window, clip : clip + 1, :] = jnp.full(
                (1, LANES), jnp.where(mine, 1.0, 0.0), F32
            )
        refs.live[window] = live


def enter_table(refs):
    refs.rows[...] = jnp.zeros_like(refs.rows)
    table = refs.rel_table[...].astype(F32)
    for head in range(2):
        for frame in range(FRAMES):
            first = (FRAMES - 1 - frame) * OFFSETS
            row = head * (SPREAD // WSIDE) + frame
            refs.rows[row : row + 1, :OFFSETS] = table[head : head + 1, first : first + OFFSETS]
    shape_of = (TILE, WSIDE * LANES)
    offset = lax.broadcasted_iota(jnp.int32, shape_of, 0)
    place = lax.broadcasted_iota(jnp.int32, shape_of, 1)
    own, row, other = place // LANES, place // WSIDE % (LANES // WSIDE), place % WSIDE
    side_span = 2 * WSIDE - 1
    row_diff, col_diff = side_span - 1 - row, own - other + (WSIDE - 1)
    same = (row < side_span) & (row_diff * side_span + col_diff == offset)
    spread = dot(refs.rows[...].astype(BF16), jnp.where(same, 1.0, 0.0).astype(BF16))
    count = 2 * SPREAD // WSIDE
    for own in range(WSIDE):
        refs.spread[pl.ds(own, count, stride=WSIDE), :] = spread[
            :count, own * LANES : (own + 1) * LANES
        ]
    for head in range(2):
        refs.table_own[head] = refs.spread[head * SPREAD : (head + 1) * SPREAD, :].astype(BF16)


def enter(refs, place, work):
    place.greet(ALONG_ZX + ALONG_YC)
    z, x, y, c = place.z, place.x, place.y, place.c
    small = Copies(*refs.small)
    mods = dot(act_rows(refs, place), refs.ada[...])
    mods = mods + jnp.where((y == 0) & (c == 0), 1.0, 0.0) * refs.bias_in[...].astype(F32)
    for block in range(6):
        refs.mod_part[block * CLIP_ROWS : (block + 1) * CLIP_ROWS, :] = mods[
            :CLIP_ROWS, block * LANES : (block + 1) * LANES
        ]
    refs.mod_parts[y, c] = refs.mod_part[...]
    parts = [
        small(refs.mod_part, refs.mod_parts.at[y, c], place.shifted(*change)) for change in ALONG_YC
    ]
    own = []
    for unit in range(UNITS):
        if unit < OUT:
            first = picked(z * 2 + x, unit) * LANES
            refs.own[unit] = refs.qkv[:, pl.ds(pl.multiple_of(first, LANES), LANES)]
        elif unit >= DOWN:
            first = (unit - DOWN) * LANES
            for half in range(2):
                at = slice(half * 512 + first, half * 512 + first + LANES)
                refs.own[unit, half * HALF : (half + 1) * HALF] = refs.down[at, :]
        else:
            source, start = (refs.out, OUT) if unit < UP else (refs.up, UP)
            first = (unit - start) * LANES
            refs.own[unit] = source[:, first : first + LANES]
        own.append(
            pltpu.make_async_copy(
                refs.own.at[unit], refs.held.at[unit, z, x, y, c], refs.own_sem.at[unit]
            )
        )
        own[-1].start()
    points = list(ENTER)

    loaded = []

    def load(unit):
        if unit not in loaded:
            own[unit].wait()
            loaded.append(unit)

    def tick():
        for index, stage in points.pop(0):
            if stage == 1:
                load(ORDER[index])
            work.advance(ORDER[index], stage)

    tick()
    enter_layout(refs)
    enter_table(refs)
    refs.table[z, x, c] = refs.table_own[c]
    for copy in parts:
        copy.wait()
    refs.mods[z, x] = (
        refs.mod_parts[0, 0] + refs.mod_parts[0, 1] + refs.mod_parts[1, 0] + refs.mod_parts[1, 1]
    )
    mods = [
        small(refs.mods.at[z, x], refs.mods.at[z, x], place.shifted(*change))
        for change in ALONG_ZX
    ]
    for unit in range(UNITS):
        load(unit)
    tick()
    for copy in mods:
        copy.wait()
    tables = [
        small(refs.table.at[z, x, c], refs.table.at[z, x, c], place.shifted(*change))
        for change in ALONG_ZX
    ]
    for window in range(refs.mod.shape[0]):
        for block in range(48):
            which, column = divmod(block, 8)
            first = block % 6 * CLIP_ROWS
            part = refs.mods[block // 12, block // 6 % 2, first : first + CLIP_ROWS, :]
            refs.mod[window, which : which + 1, column * LANES : (column + 1) * LANES] = jnp.sum(
                part * refs.member[window], axis=0, keepdims=True
            )
    tick()
    enter_norm(refs, tick)
    for copy in tables:
        copy.wait()
    last = small(refs.table.at[:, :, c], refs.table.at[:, :, c], place.at(c=1 - c))
    work.arrive(QKV, 4)
    tick()
    enter_unit(refs, 0, refs.held.at[QKV], put=True)
    last.wait()


def attend_pair(refs, table, part, put):
    for head in range(2):
        spread = table(head).astype(F32)
        for frame in range(FRAMES):
            block = spread[frame * WSIDE : (frame + 1) * WSIDE]
            for row in range(WSIDE):
                first = (WSIDE - 1 - row) * WSIDE
                refs.strip[
                    head, row * WSIDE : (row + 1) * WSIDE, frame * CELLS : (frame + 1) * CELLS
                ] = block[:, first : first + CELLS]
        for frame in range(WT):
            first = (WT - 1 - frame) * CELLS
            refs.bias[head, frame * CELLS : (frame + 1) * CELLS, :] = refs.strip[
                head, :, first : first + WIN
            ]
    for window in range(refs.live.shape[0]):
        rows = slice(window * WIN, (window + 1) * WIN)
        live = refs.live[window] * CELLS
        key_live = lax.broadcasted_iota(jnp.int32, (1, WIN), 1) < live
        query, key, value = (part(which, rows) for which in range(3))
        mixed = []
        for head in range(2):
            lanes = slice(head * HD, (head + 1) * HD)
            scores = dot_rows(query[:, lanes] * BF16(HD ** (-0.5)), key[:, lanes]) + refs.bias[head]
            scores = jnp.where(key_live, scores, NEGATIVE)
            shifted = jnp.exp(scores - jnp.max(scores, axis=-1, keepdims=True))
            totals = jnp.sum(shifted, axis=-1, keepdims=True)
            probs = (shifted * (1.0 / totals)).astype(BF16)
            refs.probs[window, head] = probs
            mixed.append(dot(probs, value[:, lanes]).astype(BF16))
        put(rows, jnp.concatenate(mixed, axis=1))


def attend_plain_kernel(refs):
    sources = (refs.query, refs.key, refs.value)

    def put(rows, values):
        refs.mixed[rows, :] = values

    attend_pair(
        refs, lambda head: refs.table[head], lambda which, rows: sources[which][rows, :], put
    )


def start_kernel(refs):
    step = pl.program_id(0)
    pairs = H // 2
    place = Place()
    stages = gather_stages(ENTER + tuple(ATTEND.values()) + tuple(MIDDLE.values()))
    work = Gather(place, refs.held, stages, refs.gather)

    @pl.when(step == 0)
    def _():
        enter(refs, place, work)

    for at in range(pairs):

        @pl.when(step == at + 1)
        def _(at=at):
            for index, stage in ATTEND.get(at, ()):
                work.advance(ORDER[index], stage)
            if at in (2, 4):
                work.arrive(QKV + at // 2, 4)
                enter_unit(refs, at // 2, refs.held.at[QKV + at // 2], put=True)

    @pl.when((step > 0) & (step <= pairs))
    def _():
        pair = forward_pair(jnp.clip(step - 1, 0, pairs - 1))

        def columns(block):
            return pl.ds(pl.multiple_of(block * LANES, LANES), LANES)

        def part(which, rows):
            return refs.packed[pair_unit(which, pair), rows, columns(pair_block(which, pair))]

        def table(head):
            return refs.table[pair // 2, pair % 2, head]

        def put(rows, values):
            refs.mixed[rows, columns(pair)] = values

        attend_pair(refs, table, part, put)

    @pl.when(step == pairs)
    def _():
        for j in range(3):
            packed_copy(refs, j).wait()

    @pl.when(step == pairs + 1)
    def _():
        middle(refs, place, work)


def packed_block(which, rows, pair):
    return pl.BlockSpec(
        (None, rows, LANES),
        lambda step: (pair_unit(which, pair(step)), 0, pair_block(which, pair(step))),
    )


def attend_back_pair(refs, pair):
    scale = BF16(HD ** (-0.5))
    refs.spread[...] = jnp.zeros_like(refs.spread)
    refs.strip[...] = jnp.zeros_like(refs.strip)
    windows = refs.probs.shape[0]
    results = [[[None] * windows for _ in range(2)] for _ in range(3)]
    for head in range(2):
        lanes = slice(head * HD, (head + 1) * HD)
        bias = None
        for window in range(windows):
            rows = slice(window * WIN, (window + 1) * WIN)
            grad = refs.grad[rows, lanes]
            probs = refs.probs[window, head]
            results[2][head][window] = dot_tokens(grad, probs).T.astype(BF16)
            grad_probs = dot_rows(grad, refs.value[rows, lanes])
            weight = probs.astype(F32)
            product = weight * grad_probs
            total = jnp.sum(product, axis=-1, keepdims=True)
            grad_scores = (product - weight * total).astype(BF16)
            wide = grad_scores.astype(F32)
            bias = wide if bias is None else bias + wide
            results[0][head][window] = dot(grad_scores, refs.key[rows, lanes] * scale).astype(BF16)
            query = refs.query[rows, lanes] * scale
            results[1][head][window] = dot_tokens(query, grad_scores).T.astype(BF16)
        for frame in range(WT):
            first = (WT - 1 - frame) * CELLS
            refs.strip[head, :, first : first + WIN] += bias[frame * CELLS : (frame + 1) * CELLS]
        for frame in range(FRAMES):
            for row in range(WSIDE):
                first = (WSIDE - 1 - row) * WSIDE
                refs.spread[
                    head, frame * WSIDE : (frame + 1) * WSIDE, first : first + CELLS
                ] += refs.strip[
                    head, row * WSIDE : (row + 1) * WSIDE, frame * CELLS : (frame + 1) * CELLS
                ]
    for part in range(3):
        lanes = pl.ds(pl.multiple_of(pair_block(part, pair) * LANES, LANES), LANES)
        for window in range(windows):
            rows = slice(window * WIN, (window + 1) * WIN)
            both = [results[part][head][window] for head in range(2)]
            refs.grad_packed[pair_unit(part, pair), rows, lanes] = jnp.concatenate(both, axis=1)


def middle(refs, place=None, gathering=None):
    order = [OUT] + [unit for j in range(4) for unit in (UP + j, DOWN + j)] + [OUT]
    activated, grad_hidden, grad_low = (refs.packed.at[index] for index in range(3))
    reducing = None
    points = {}
    waiting = set()
    if gathering is not None:

        def buffers(unit):
            index = EARLY.index(unit)
            core, side = refs.core.at[index], refs.side.at[index]
            if unit not in DONE:
                return core, side, None, None
            if unit in REDUCE_ASIDE:
                return core, side, None, refs.aside.at[0]
            return core, side, refs.corner.at[index], refs.distant.at[index]

        def store(unit, part, values):
            at = pl.ds(pl.multiple_of(part * HALF, HALF), HALF)
            refs.total[DONE.index(unit), at, :] = values

        reducing = Reduce(
            place, lambda unit: refs.part.at[unit], EARLY_POINTS, store, buffers, refs.reduce
        )
        for stages in MIDDLE.values():
            waiting |= {ORDER[index] for index, stage in stages if stage == 4}
        points = {at: list(moves) for at, moves in EARLY_POINTS.items()}

    count = [0]

    def pump():
        for index, stage in MIDDLE.get(count[0], ()) if gathering is not None else ():
            gathering.advance(ORDER[index], stage)
            if stage == 4:
                waiting.discard(ORDER[index])
        for unit, stage in points.pop(count[0], ()):
            reducing.step(unit, stage)
        count[0] += 1

    def fetch(step):
        return pltpu.make_async_copy(
            refs.held.at[order[step]], refs.units.at[step % 4], refs.fetches.at[step % 4]
        )

    def start_fetch(step):
        if gathering is not None:
            assert order[step] not in waiting
            gathering.arrive(order[step], 4)
        fetch(step).start()

    def put(slot, unit):
        return pltpu.make_async_copy(refs.made.at[slot], refs.part.at[unit], refs.made_sem.at[slot])

    for step in range(3):
        start_fetch(step)
    pump()
    refs.sums[...] = jnp.zeros_like(refs.sums)
    refs.mlp[...] = jnp.zeros_like(refs.mlp)
    refs.grad_normed[...] = jnp.zeros_like(refs.grad_normed)
    fetch(0).wait()

    def project(index):
        refs.attended[:, half(index)] = dot(refs.mixed[...], four_columns(refs.units.at[0], index))

    loop(2, project)
    pump()

    def modulate(window, at, mods, live):
        middle = refs.tokens[at, :].astype(F32) + mods[2] * refs.attended[at, :]
        normal, _ = centered(middle)
        refs.normed2[at, :] = (normal * (1.0 + mods[4]) + mods[3]).astype(BF16)
        grad = jnp.where(live, refs.cotangent[at, :].astype(F32), 0.0)
        grad_low[at, :] = (mods[5] * grad).astype(BF16)

    each_rows(refs.mod, refs.live, modulate)
    pump()
    for j in range(4):
        step = 1 + 2 * j
        up, down = refs.units.at[step % 4], refs.units.at[(step + 1) % 4]
        fetch(step).wait()
        fetch(step + 1).wait()
        start_fetch(step + 2)

        def hide(index, up=up, down=down):
            hidden = dot(refs.normed2[...], four_columns(up, index))
            bend = jnp.tanh(0.7978845608028654 * (hidden + 0.044715 * hidden * hidden * hidden))
            activated[:, half(index)] = (0.5 * hidden * (1.0 + bend)).astype(BF16)
            slope = 0.5 * (1.0 + bend) + 0.5 * hidden * (1.0 - bend * bend) * (
                0.7978845608028654 * (1.0 + 3.0 * 0.044715 * hidden * hidden)
            )
            grad_activated = dot_rows(grad_low[...], half_rows(down, index))
            grad_hidden[:, half(index)] = (grad_activated * slope).astype(BF16)

        loop(2, hide)
        if j > 0:
            put(1, UP + j - 1).wait()
        pump()

        def down_gradient(index):
            made = dot_tokens(activated[:, half(index)], grad_low[...]).astype(BF16)
            for block in range(8):
                refs.made[0, block // 2, block % 2, index] = made[
                    :, block * LANES : (block + 1) * LANES
                ].reshape(2, SHARE, LANES)

        loop(2, down_gradient)
        put(0, DOWN + j).start()
        pump()

        def up_gradient(index):
            made = dot_tokens(refs.normed2[...], grad_hidden[:, half(index)]).astype(BF16)
            put_columns(refs.made.at[1], index, made)

        loop(2, up_gradient)
        put(0, DOWN + j).wait()
        put(1, UP + j).start()
        pump()
        if j < 3:
            start_fetch(step + 3)

        def out_of_mlp(index, up=up, down=down):
            refs.mlp[:, half(index)] += dot(activated[...], four_columns(down, index))
            refs.grad_normed[:, half(index)] += dot_rows(
                grad_hidden[...], half_rows(up, index)
            )

        loop(2, out_of_mlp)
        pump()

    put(1, UP + 3).wait()

    def join(window, at, mods, live):
        attended = refs.attended[at, :]
        middle = refs.tokens[at, :].astype(F32) + mods[2] * attended
        normal, root = centered(middle)
        mlp = refs.mlp[at, :]
        refs.output[at, :] = jnp.where(live, middle + mods[5] * mlp, 0.0).astype(BF16)
        grad_result = jnp.where(live, refs.cotangent[at, :].astype(F32), 0.0)
        grad_normed = refs.grad_normed[at, :]
        grad_middle = grad_result + norm_back(grad_normed, normal, root, mods[4])
        refs.grad_middle[at, :] = grad_middle
        grad_low[at, :] = (mods[2] * grad_middle).astype(BF16)
        add_sums(refs.sums, window, 2, grad_middle * attended)
        add_sums(refs.sums, window, 3, grad_normed)
        add_sums(refs.sums, window, 4, grad_normed * normal)
        add_sums(refs.sums, window, 5, grad_result * mlp)

    each_rows(refs.mod, refs.live, join)
    pump()
    fetch(9).wait()

    def back(index):
        made = dot_tokens(refs.mixed[...], grad_low[:, half(index)]).astype(BF16)
        put_columns(refs.made.at[0], index, made)
        refs.grad_mixed[:, half(index)] = dot_rows(
            grad_low[...], half_rows(refs.units.at[1], index)
        ).astype(BF16)

    loop(2, back)
    put(0, OUT).start()
    put(0, OUT).wait()
    while points:
        pump()
    for index, unit in enumerate(EARLY if gathering is not None else ()):
        if unit not in DONE:

            def keep(z, index=index):
                for part in range(2):
                    refs.side_out[index - len(DONE), part, z] = refs.side[index, part, z]

            loop(4, keep)
    if gathering is not None:
        gathering.finish()
        reducing.sent()


def leave_weight(refs, j, made):
    def weight(index):
        grad = dot_tokens(refs.normed[...], refs.grad_packed[j, :, half(index)]).astype(BF16)
        put_columns(made, index, grad)

    loop(2, weight)


def leave_back(refs, j):
    def back(index):
        refs.grad_normed[:, half(index)] += dot_rows(
            refs.grad_packed[j], half_rows(refs.unit, index)
        )

    loop(2, back)


def leave_norm(refs, pump=lambda window: None):
    def join(window, at, mods, live):
        normal, root = centered(refs.tokens[at, :].astype(F32))
        grad_normed = refs.grad_normed[at, :]
        refs.grad_tokens[at, :] = refs.grad_middle[at, :] + norm_back(
            grad_normed, normal, root, mods[1]
        )
        add_sums(refs.sums, window, 0, grad_normed)
        add_sums(refs.sums, window, 1, grad_normed * normal)

    each_rows(refs.mod, refs.live, join, pump=pump)


def back_plain_kernel(refs):
    step = pl.program_id(0)

    @pl.when(step < H // 2)
    def _():
        attend_back_pair(refs, backward_pair(jnp.minimum(step, H // 2 - 1)))

    @pl.when(step == H // 2)
    def _():
        refs.sums[...] = jnp.zeros_like(refs.sums)
        refs.grad_normed[...] = jnp.zeros_like(refs.grad_normed)
        for j in range(3):
            fetch = pltpu.make_async_copy(refs.held.at[QKV + j], refs.unit, refs.fetch)
            fetch.start()
            leave_weight(refs, j, refs.made)
            put = pltpu.make_async_copy(refs.made, refs.part.at[j], refs.made_sem)
            put.start()
            fetch.wait()
            leave_back(refs, j)
            put.wait()
        leave_norm(refs)


def fold_spreads(refs):
    heads = H * WIDE // WSIDE
    shape_of = (WSIDE * LANES, TILE)
    place = lax.broadcasted_iota(jnp.int32, shape_of, 0)
    offset = lax.broadcasted_iota(jnp.int32, shape_of, 1)
    own, row, other = place // LANES, place // WSIDE % (LANES // WSIDE), place % WSIDE
    side_span = 2 * WSIDE - 1
    row_diff, col_diff = side_span - 1 - row, own - other + (WSIDE - 1)
    same = (row < side_span) & (row_diff * side_span + col_diff == offset)
    onto = jnp.where(same, 1.0, 0.0).astype(BF16)
    left = jnp.concatenate(
        [refs.spreads[pl.ds(own, heads, stride=WSIDE), :] for own in range(WSIDE)], axis=1
    )
    total = jnp.zeros((heads, TILE), F32)
    for _ in range(3):
        low = left.astype(BF16)
        total = total + dot(low, onto)
        left = left - low.astype(F32)
    rows = 2 * WIDE // WSIDE
    for block in range(8):
        refs.table[block // 2, block % 2] = total[block * rows : (block + 1) * rows]


def back_kernel(refs):
    place = Place()
    z, x, y, c = place.z, place.x, place.y, place.c
    step = pl.program_id(0)

    def buffers(unit):
        every = (EARLY + LATE).index(unit)
        late = every - len(EARLY)
        assert unit not in DONE
        if late < 0:
            core, side = None, refs.side_in.at[every - len(DONE)]
        else:
            core, side = refs.core.at[late], refs.side.at[late]
        if unit in REDUCE_ASIDE:
            return core, side, None, refs.aside.at[0]
        return core, side, refs.corner.at[every], refs.distant.at[every]

    def store(unit, part, values):
        if unit >= DOWN:
            first = part * 512 + (unit - DOWN) * LANES
            refs.grad_down[pl.ds(pl.multiple_of(first, LANES), LANES), :] = values
            return
        at = pl.ds(pl.multiple_of(part * HALF, HALF), HALF)
        if unit < OUT:
            column = picked(z * 2 + x, unit) * LANES
            refs.grad_qkv[at, pl.ds(pl.multiple_of(column, LANES), LANES)] = values
            return
        target, start = (refs.grad_out, OUT) if unit < UP else (refs.grad_up, UP)
        column = (unit - start) * LANES
        target[at, column : column + LANES] = values

    work = Reduce(
        place,
        lambda unit: refs.made.at[unit] if unit < OUT else refs.part.at[unit],
        LATE_POINTS,
        store,
        buffers,
        refs.reduce,
    )
    small = Copies(*refs.small)

    events = [(at, move) for at in sorted(LATE_POINTS) for move in LATE_POINTS[at]]

    def run(until):
        while events and events[0][0] < until:
            work.step(*events.pop(0)[1])

    for number in range(H // 2):

        @pl.when(step == number)
        def _(number=number):
            if number == 0:
                place.greet(EVERYONE)
            if number in (3, 6):
                leave_weight(refs, number // 3 - 1, refs.made.at[number // 3 - 1])
            run(number + 1)

    @pl.when(step < H // 2)
    def _():
        pair = backward_pair(jnp.minimum(step, H // 2 - 1))
        attend_back_pair(refs, pair)
        for head in range(2):
            at = pl.ds(pl.multiple_of((pair * 2 + head) * WIDE, WIDE), WIDE)
            refs.spreads[at, :] = refs.spread[head]

    @pl.when(step == H // 2)
    def _():
        for index, unit in enumerate(DONE):
            for part in range(2):
                store(unit, part, refs.done[index, part * HALF : (part + 1) * HALF, :])
        fold_spreads(refs)
        table = []
        for dz, dx, dy, dc in ALONG_ZX:
            source = refs.table.at[place.far(dz), 1 - x if dx else x]
            table.append(small(source, refs.table_zx.at[z, x], place.shifted(dz, dx, dy, dc)))
        refs.table_zx[z, x] = refs.table[z, x]
        refs.sums[...] = refs.late_sums[...]
        refs.grad_normed[...] = jnp.zeros_like(refs.grad_normed)

        def fetch(j):
            return pltpu.make_async_copy(refs.held.at[QKV + j], refs.unit, refs.fetch)

        fetch(0).start()
        leave_weight(refs, 2, refs.made.at[2])
        run(12)
        fetch(0).wait()
        leave_back(refs, 0)
        fetch(1).start()
        run(13)
        fetch(1).wait()
        leave_back(refs, 1)
        fetch(2).start()
        run(14)
        fetch(2).wait()
        leave_back(refs, 2)
        run(15)
        leave_norm(refs, lambda window: run(17 + window))
        for copy in table:
            copy.wait()
        total = refs.table_zx[0, 0]
        for block in range(1, 8):
            total = total + refs.table_zx[block // 2, block % 2]
        refs.table_own[...] = total
        refs.table_yc[y, c] = total
        table = [
            small(refs.table_own, refs.table_yc.at[y, c], place.shifted(*change))
            for change in ALONG_YC
        ]
        for block in range(48):
            which, column = divmod(block, 8)
            part = jnp.zeros((CLIP_ROWS, LANES), F32)
            for window in range(refs.mod.shape[0]):
                sums = refs.sums[window, which : which + 1, column * LANES : (column + 1) * LANES]
                part = part + refs.member[window] * sums
            first = block % 6 * CLIP_ROWS
            refs.clip[block // 12, block // 6 % 2, first : first + CLIP_ROWS, :] = part
        copies = []
        for dz, dx, dy, dc in ALONG_ZX:
            source = refs.clip.at[place.far(dz), 1 - x if dx else x]
            copies.append(small(source, refs.clip_zx.at[z, x], place.shifted(dz, dx, dy, dc)))
        refs.clip_zx[z, x] = refs.clip[z, x]
        run(19)
        for copy in copies:
            copy.wait()
        total = refs.clip_zx[0, 0]
        for block in range(1, 8):
            total = total + refs.clip_zx[block // 2, block % 2]
        refs.clip_own[...] = total
        refs.clip_yc[y, c] = total
        copies = [
            small(refs.clip_own, refs.clip_yc.at[y, c], place.shifted(*change))
            for change in ALONG_YC
        ]
        run(21)
        for copy in copies:
            copy.wait()
        total = refs.clip_yc[0, 0] + refs.clip_yc[0, 1] + refs.clip_yc[1, 0] + refs.clip_yc[1, 1]
        total = jnp.concatenate([total, jnp.zeros((8, LANES), F32)], axis=0)
        cond = jnp.zeros((8, SHARE), F32)
        lows = []
        for block in range(6):
            lows.append(total[block * CLIP_ROWS : block * CLIP_ROWS + 8].astype(BF16))
            lanes = slice(block * LANES, (block + 1) * LANES)
            cond = cond + dot_rows(lows[-1], refs.ada[:, lanes])
        clips = refs.condition.shape[0]
        refs.cond_own[...] = jnp.zeros_like(refs.cond_own)
        for row in range(2 * clips):
            clip, side = divmod(row, 2)
            refs.cond_own[row : row + 1, :] = cond[
                clip : clip + 1, side * LANES : (side + 1) * LANES
            ]
        refs.cond_all[z, x, y, c] = refs.cond_own[...]
        copies = [
            small(refs.cond_own, refs.cond_all.at[z, x, y, c], place.shifted(*change))
            for change in EVERYONE
        ]
        for block, low in enumerate(lows):
            lanes = slice(block * LANES, (block + 1) * LANES)
            refs.grad_ada[:, lanes] = dot_tokens(act_rows(refs, place), low)
            refs.grad_bias[block : block + 1, :] = jnp.sum(
                low[:CLIP_ROWS].astype(F32), axis=0, keepdims=True
            )
        run(23)
        for copy in table:
            copy.wait()
        total = refs.table_yc[0, 0] + refs.table_yc[0, 1] + refs.table_yc[1, 0] + refs.table_yc[1, 1]
        for head in range(2):
            for frame in range(FRAMES):
                first = (FRAMES - 1 - frame) * OFFSETS
                row = head * (WIDE // WSIDE) + frame
                refs.table_total[head : head + 1, first : first + OFFSETS] = total[
                    row : row + 1, :OFFSETS
                ]
        run(100)
        for copy in copies:
            copy.wait()
        for block in range(4):
            total = refs.cond_all[0, 0, block // 2, block % 2]
            for other in range(1, 8):
                total = total + refs.cond_all[other // 2, other % 2, block // 2, block % 2]
            for row in range(2 * clips):
                clip, side = divmod(row, 2)
                first = block * SHARE + side * LANES
                value = refs.condition[clip : clip + 1, first : first + LANES]
                gate = 1.0 / (1.0 + jnp.exp(-value))
                refs.grad_condition[clip : clip + 1, first : first + LANES] = (
                    total[row : row + 1] * gate * (1.0 + value * (1.0 - gate))
                )
        work.sent()


def enter_plain(tokens, held, mod):
    rows = tokens.shape[0]
    inputs = {"tokens": (tokens, vmem()), "held": (held, anywhere()), "mod": (mod, vmem())}
    outputs = {
        "normed": (shape(BF16, rows, D), vmem()),
        "packed": (shape(BF16, 3, rows, D), vmem()),
    }
    scratch = {
        "units": pltpu.VMEM((1, *SPLIT), BF16),
        "fetches": pltpu.SemaphoreType.DMA((1,)),
    }
    return call(enter_plain_kernel, "enter_plain", inputs, outputs, scratch)


def whole(array):
    return pl.BlockSpec(
        array.shape, lambda p: (0,) * len(array.shape), pipeline_mode=pl.Buffered(1)
    )


def result(dtype, *sizes):
    made = shape(dtype, *sizes)
    return made, whole(made)


def attend_probs(windows, first):
    def pair(step):
        return forward_pair(jnp.clip(step - first, 0, H // 2 - 1))

    return (
        shape(BF16, windows, H, WIN, WIN),
        pl.BlockSpec((windows, 2, WIN, WIN), lambda p: (0, pair(p), 0, 0)),
    )


def attend_scratch():
    return {"strip": pltpu.VMEM((2, CELLS, STRIP), F32), "bias": pltpu.VMEM((2, WIN, WIN), F32)}


def middle_outputs(rows):
    return {
        "output": result(BF16, rows, D),
        "grad_middle": result(F32, rows, D),
        "grad_mixed": result(BF16, rows, D),
        "sums": result(F32, rows // WIN, 8, D),
        "part": (shape(BF16, UNITS, *SPLIT), anywhere()),
    }


def middle_scratch(rows):
    return {
        "units": pltpu.VMEM((4, *SPLIT), BF16),
        "attended": pltpu.VMEM((rows, D), F32),
        "normed2": pltpu.VMEM((rows, D), BF16),
        "mlp": pltpu.VMEM((rows, D), F32),
        "grad_normed": pltpu.VMEM((rows, D), F32),
        "packed": pltpu.VMEM((3, rows, D), BF16),
        "made": pltpu.VMEM((2, *SPLIT), BF16),
        "fetches": pltpu.SemaphoreType.DMA((4,)),
        "made_sem": pltpu.SemaphoreType.DMA((2,)),
    }


def middle_plain(live_frames, tokens, cotangent, mixed, mod, held):
    rows = tokens.shape[0]
    inputs = {
        name: (array, whole(array))
        for name, array in (
            ("tokens", tokens),
            ("cotangent", cotangent),
            ("mixed", mixed),
            ("mod", mod),
        )
    }
    inputs |= {"live": (live_frames, smem()), "held": (held, anywhere())}
    return call(
        middle, "middle", inputs, middle_outputs(rows), middle_scratch(rows), grid=(1,), limit=60
    )


def begin(tokens, cotangent, own, smalls):
    rows = tokens.shape[0]
    windows = rows // WIN
    inputs = {"tokens": (tokens, whole(tokens)), "cotangent": (cotangent, whole(cotangent))}
    for name, block in zip(("qkv", "out", "up", "down"), own, strict=True):
        inputs[name] = (block, whole(block))
    for name, array in zip(("condition", "ada", "bias_in", "rel_table"), smalls[1:], strict=True):
        inputs[name] = (array, whole(array))
    inputs["frames"] = (smalls[0], smem())
    outputs = middle_outputs(rows) | {
        "probs": attend_probs(windows, 1),
        "side_out": result(BF16, *Reduce.side_shape(len(EARLY) - len(DONE))),
        "total": result(F32, len(DONE), SHARE, LANES),
        "normed": result(BF16, rows, D),
        "packed_out": (shape(BF16, 3, rows, D), anywhere()),
        "held": (shape(BF16, UNITS, *SPLIT), anywhere()),
        "mod": result(F32, windows, 8, D),
        "member": result(F32, windows, CLIP_ROWS, LANES),
        "live": (shape(jnp.int32, windows), smem()),
    }
    stages = gather_stages(ENTER + tuple(ATTEND.values()) + tuple(MIDDLE.values()))
    scratch = attend_scratch() | middle_scratch(rows)
    scratch |= {
        "mixed": pltpu.VMEM((rows, D), BF16),
        "core": pltpu.VMEM(Reduce.core_shape(len(EARLY)), BF16),
        "side": pltpu.VMEM(Reduce.side_shape(len(EARLY)), BF16),
        "corner": pltpu.VMEM(Reduce.corner_shape(len(DONE)), BF16),
        "distant": pltpu.VMEM(Reduce.distant_shape(len(DONE)), BF16),
        "aside": pltpu.VMEM(Reduce.aside_shape(1), BF16),
        "reduce": Reduce.scratch(EARLY_POINTS),
        "packed_sem": pltpu.SemaphoreType.DMA((3,)),
        "own": pltpu.VMEM((UNITS, SHARE, LANES), BF16),
        "own_sem": pltpu.SemaphoreType.DMA((UNITS,)),
        "gather": Gather.semaphores(stages),
        "small": [pltpu.SemaphoreType.DMA((18,))] * 2,
        "mod_part": pltpu.VMEM((MOD_ROWS, LANES), F32),
        "mod_parts": pltpu.VMEM((2, 2, MOD_ROWS, LANES), F32),
        "mods": pltpu.VMEM((4, 2, MOD_ROWS, LANES), F32),
        "rows": pltpu.VMEM((24, TILE), F32),
        "spread": pltpu.VMEM((2 * SPREAD, LANES), F32),
        "table_own": pltpu.VMEM((2, SPREAD, LANES), BF16),
        "table": pltpu.VMEM((4, 2, 2, SPREAD, LANES), BF16),
    }
    return call(
        start_kernel,
        "start",
        inputs,
        outputs,
        scratch,
        collective=0,
        grid=(H // 2 + 2,),
        limit=60,
    )


def deliver_kernel(refs):
    names = [name for name in vars(refs) if name.startswith("from_")]
    loads, stores = [], []
    for index, name in enumerate(names):
        plain = name[len("from_") :]
        held = getattr(refs, "held_" + plain)
        loads.append(pltpu.make_async_copy(getattr(refs, name), held, refs.sems.at[0, index]))
        stores.append(pltpu.make_async_copy(held, getattr(refs, plain), refs.sems.at[1, index]))
        loads[-1].start()
    for load, store in zip(loads, stores, strict=True):
        load.wait()
        store.start()
    for store in stores:
        store.wait()


def deliver(**arrays):
    inputs = {"from_" + name: (array, anywhere()) for name, array in arrays.items()}
    outputs = {name: (shape(array.dtype, *array.shape), anywhere()) for name, array in arrays.items()}
    scratch = {"held_" + name: pltpu.VMEM(array.shape, array.dtype) for name, array in arrays.items()}
    scratch["sems"] = pltpu.SemaphoreType.DMA((2, len(arrays)))
    return call(deliver_kernel, "deliver", inputs, outputs, scratch)


def attend_plain(packed, table, live_frames):
    windows = live_frames.shape[0]
    rows = windows * WIN
    inputs = {
        "live": (live_frames, smem()),
        "query": (packed, packed_block(0, rows, forward_pair)),
        "key": (packed, packed_block(1, rows, forward_pair)),
        "value": (packed, packed_block(2, rows, forward_pair)),
        "table": (table, pl.BlockSpec((2, SPREAD, LANES), lambda p: (forward_pair(p), 0, 0))),
    }
    return call(
        attend_plain_kernel,
        "attend_plain",
        inputs,
        {
            "mixed": (
                shape(BF16, rows, D),
                pl.BlockSpec((rows, LANES), lambda p: (0, forward_pair(p))),
            ),
            "probs": attend_probs(windows, 0),
        },
        attend_scratch(),
        grid=(H // 2,),
    )


def back(
    special, live_frames, tokens, mod, packed, normed, probs, mid, held, ada, member, condition
):
    window_count = probs.shape[0]
    rows = window_count * WIN
    pairs = H // 2

    def last(step):
        return backward_pair(jnp.minimum(step, pairs - 1))

    def packed_pair(which):
        return packed_block(which, rows, last)

    inputs = {
        "live": (live_frames, smem()),
        "query": (packed, packed_pair(0)),
        "key": (packed, packed_pair(1)),
        "value": (packed, packed_pair(2)),
        "probs": (
            probs,
            pl.BlockSpec((window_count, 2, WIN, WIN), lambda p: (0, last(p), 0, 0)),
        ),
        "grad": (mid.grad_mixed, pl.BlockSpec((rows, LANES), lambda p: (0, last(p)))),
        "held": (held, anywhere()),
    }
    for name, array in (
        ("tokens", tokens),
        ("mod", mod),
        ("normed", normed),
        ("grad_middle", mid.grad_middle),
    ):
        inputs[name] = (array, whole(array))

    outputs = {"grad_tokens": result(F32, rows, D)}
    scratch = {
        "strip": pltpu.VMEM((2, CELLS, STRIP), F32),
        "grad_packed": pltpu.VMEM((3, rows, D), BF16),
        "unit": pltpu.VMEM(SPLIT, BF16),
        "grad_normed": pltpu.VMEM((rows, D), F32),
        "fetch": pltpu.SemaphoreType.DMA,
    }
    if not special:
        outputs["sums"] = result(F32, window_count, 8, D)
        outputs["part"] = (shape(BF16, 3, *SPLIT), anywhere())
        outputs["spread"] = (
            shape(F32, H, SPREAD, LANES),
            pl.BlockSpec((2, SPREAD, LANES), lambda p: (last(p), 0, 0)),
        )
        scratch["made"] = pltpu.VMEM(SPLIT, BF16)
        scratch["made_sem"] = pltpu.SemaphoreType.DMA
        return call(
            back_plain_kernel, "back_plain", inputs, outputs, scratch, grid=(pairs + 1,)
        )
    inputs |= {
        "late_sums": (mid.sums, whole(mid.sums)),
        "ada": (ada, whole(ada)),
        "condition": (condition, whole(condition)),
        "member": (member, whole(member)),
        "side_in": (mid.side_out, whole(mid.side_out)),
        "done": (mid.total, whole(mid.total)),
        "part": (mid.part, anywhere()),
    }
    outputs |= {
        "grad_qkv": result(F32, SHARE, 3 * LANES),
        "grad_out": result(F32, SHARE, LANES),
        "grad_up": result(F32, SHARE, 4 * LANES),
        "grad_down": result(F32, 4 * SHARE, LANES),
        "grad_ada": result(F32, SHARE, 6 * LANES),
        "grad_bias": result(F32, 6, LANES),
        "grad_condition": result(F32, *condition.shape),
        "table_total": result(F32, 2, REL),
    }
    count, late = len(EARLY + LATE), len(LATE)
    scratch |= {
        "spread": pltpu.VMEM((2, WIDE, LANES), F32),
        "spreads": pltpu.VMEM((H * WIDE, LANES), F32),
        "made": pltpu.VMEM((3, *SPLIT), BF16),
        "sums": pltpu.VMEM((window_count, 8, D), F32),
        "core": pltpu.VMEM(Reduce.core_shape(late), BF16),
        "side": pltpu.VMEM(Reduce.side_shape(late), BF16),
        "corner": pltpu.VMEM(Reduce.corner_shape(count), BF16),
        "distant": pltpu.VMEM(Reduce.distant_shape(count), BF16),
        "aside": pltpu.VMEM(Reduce.aside_shape(1), BF16),
        "reduce": Reduce.scratch(LATE_POINTS),
        "table": pltpu.VMEM((4, 2, 2 * WIDE // WSIDE, TILE), F32),
        "table_zx": pltpu.VMEM((4, 2, 2 * WIDE // WSIDE, TILE), F32),
        "table_own": pltpu.VMEM((2 * WIDE // WSIDE, TILE), F32),
        "table_yc": pltpu.VMEM((2, 2, 2 * WIDE // WSIDE, TILE), F32),
        "clip": pltpu.VMEM((4, 2, MOD_ROWS, LANES), F32),
        "clip_zx": pltpu.VMEM((4, 2, MOD_ROWS, LANES), F32),
        "clip_own": pltpu.VMEM((MOD_ROWS, LANES), F32),
        "clip_yc": pltpu.VMEM((2, 2, MOD_ROWS, LANES), F32),
        "cond_own": pltpu.VMEM((8, LANES), F32),
        "cond_all": pltpu.VMEM((4, 2, 2, 2, 8, LANES), F32),
        "small": [pltpu.SemaphoreType.DMA((51,))] * 2,
    }
    return call(
        back_kernel,
        "back",
        inputs,
        outputs,
        scratch,
        collective=3,
        grid=(pairs + 1,),
        limit=60,
    )


def per_device(
    special,
    tokens,
    condition,
    clip_frames,
    ada_weight,
    ada_bias,
    qkv_weight,
    out_weight,
    up_weight,
    down_weight,
    rel_table,
    cotangent,
):
    window_count = tokens.shape[0]
    clip_count = condition.shape[0]
    rows_ada, cols_ada = ada_weight.shape
    token_rows = tokens.reshape(window_count * WIN, D)
    cotangent_rows = cotangent.reshape(window_count * WIN, D)
    own = (qkv_weight, out_weight, up_weight, down_weight)
    if special:
        smalls = (clip_frames, condition, ada_weight, ada_bias.reshape(1, cols_ada), rel_table)
        start = across = mid = begin(token_rows, cotangent_rows, own, smalls)
        live_frames, member_wide, mod = start.live, start.member, start.mod
        packed, held = start.packed_out, start.held
    else:
        row_block = lax.axis_index("fsdp")
        col_block = lax.axis_index("dp")
        first_window = lax.axis_index(("dp", "fsdp")) * window_count
        live_frames, member_int = window_layout(clip_frames, first_window, window_count)
        member = member_int.astype(F32)
        activity_low = jax.nn.silu(condition).astype(BF16)
        rows_own = lax.dynamic_slice_in_dim(activity_low, row_block * rows_ada, rows_ada, 1)
        mod_part = jnp.dot(rows_own, ada_weight, preferred_element_type=F32)
        clip_mod = lax.all_gather(lax.psum(mod_part, "fsdp"), "dp", axis=1, tiled=True)
        bias = lax.all_gather(ada_bias, "dp", axis=0, tiled=True)
        clip_mod = clip_mod + bias.astype(F32)[None, :]
        member_wide = None
        window_mod = jnp.sum(member[:, :, None] * clip_mod[None], axis=1)
        window_mod = jnp.pad(window_mod.reshape(window_count, 6, D), ((0, 0), (0, 2), (0, 0)))
        whole = [
            lax.all_gather(
                lax.all_gather(weight, "dp", axis=1, tiled=True), "fsdp", axis=0, tiled=True
            )
            for weight in own
        ]
        held = units_of(*whole).reshape(UNITS, *SPLIT)
        mod = window_mod
        start = enter_plain(token_rows, held, mod)
        packed = start.packed
        table = spread_table(lax.all_gather(rel_table, "dp", axis=0, tiled=True))
        across = attend_plain(packed, table, live_frames)
        mid = middle_plain(live_frames, token_rows, cotangent_rows, across.mixed, mod, held)
    end = back(
        special,
        live_frames,
        token_rows,
        mod,
        packed,
        start.normed,
        across.probs,
        mid,
        held,
        ada_weight,
        member_wide,
        condition,
    )
    if special:
        end = deliver(
            output=mid.output,
            grad_tokens=end.grad_tokens,
            grad_condition=end.grad_condition,
            grad_ada=end.grad_ada,
            grad_bias=end.grad_bias,
            grad_qkv=end.grad_qkv,
            grad_out=end.grad_out,
            grad_up=end.grad_up,
            grad_down=end.grad_down,
            table=end.table_total,
        )
        return (
            end.output.reshape(tokens.shape),
            end.grad_tokens.reshape(tokens.shape),
            end.grad_condition,
            end.grad_ada,
            end.grad_bias.reshape(cols_ada),
            end.grad_qkv,
            end.grad_out,
            end.grad_up,
            end.grad_down,
            end.table,
        )
    part = jnp.concatenate([end.part, mid.part[OUT:]])
    grads = [
        lax.psum_scatter(
            lax.psum_scatter(grad, "fsdp", scatter_dimension=0, tiled=True),
            "dp",
            scatter_dimension=1,
            tiled=True,
        ).astype(F32)
        for grad in weights_of(part.reshape(UNITS, 8, D, LANES))
    ]
    grad_mod = (mid.sums + end.sums)[:, :6].reshape(window_count, 6 * D)
    clip_part = lax.dot_general(
        member,
        grad_mod,
        (((0,), (0,)), ((), ())),
        precision=HIGHEST,
        preferred_element_type=F32,
    )
    clip_sum, table_sum = lax.psum((clip_part, gather_table(end.spread)), ("dp", "fsdp"))
    clip_cols = lax.dynamic_slice_in_dim(
        clip_sum.astype(BF16), col_block * cols_ada, cols_ada, 1
    )
    heads_own = rel_table.shape[0]
    table_grad = lax.dynamic_slice_in_dim(table_sum, col_block * heads_own, heads_own, 0)
    cond_part = lax.dot_general(
        clip_cols, ada_weight, (((1,), (1,)), ((), ())), preferred_element_type=F32
    )
    cond_total = lax.all_gather(lax.psum(cond_part, "dp"), "fsdp", axis=1, tiled=True)
    grad_ada_weight = lax.dot_general(
        rows_own, clip_cols, (((0,), (0,)), ((), ())), preferred_element_type=F32
    )
    grad_ada_bias = jnp.sum(clip_cols.astype(F32), axis=0)
    _, silu_back = jax.vjp(jax.nn.silu, condition)
    return (
        mid.output.reshape(tokens.shape),
        end.grad_tokens.reshape(tokens.shape),
        silu_back(cond_total)[0],
        grad_ada_weight,
        grad_ada_bias,
        *grads,
        table_grad,
    )


def solution(mesh):
    special = dict(mesh.shape) == {"dp": 8, "fsdp": 4}
    both = P(("dp", "fsdp"), None, None)
    weight = P("fsdp", "dp")
    in_specs = (both, P(), P(), weight, P("dp")) + (weight,) * 4 + (P("dp", None), both)
    out_specs = (both, both, P(), weight, P("dp")) + (weight,) * 4 + (P("dp", None),)
    return jax.shard_map(
        functools.partial(per_device, special),
        mesh=mesh,
        in_specs=in_specs,
        out_specs=out_specs,
        check_vma=False,
    )
```

```python
import functools

import jax
import jax.numpy as jnp
from jax import lax
from jax.experimental import pallas as pl
from jax.experimental.pallas import tpu as pltpu
from jax.sharding import PartitionSpec as P

D = 1024
H = 16
HD = 64
WT = 5
WSIDE = 8
WIN = 320
SPW = 16
CELLS = WSIDE * WSIDE
FRAMES = 2 * WT - 1
OFFSETS = (2 * WSIDE - 1) ** 2
REL = FRAMES * OFFSETS
LANES = 128
TILE = 256
SPREAD = 80
WIDE = 96
STRIP = 640

EPSILON = 1e-06
NEGATIVE = -1000000000.0
HIGHEST = lax.Precision.HIGHEST
F32 = jnp.float32
BF16 = jnp.bfloat16
MESH = pl.DeviceIdType.MESH
MIB = 2**20

QKV, OUT, UP, DOWN, UNITS = 0, 3, 4, 8, 12
PICK = (
    (1, 2, 0),
    (1, 2, 0),
    (0, 1, 2),
    (0, 1, 2),
    (0, 1, 2),
    (2, 0, 1),
    (2, 0, 1),
    (1, 0, 2),
)
SHARE = 256
HALF = 128


SPLIT = (4, 2, 2, 2, SHARE, LANES)
CLIP_ROWS = 4
MOD_ROWS = 6 * CLIP_ROWS
OWN_SLOTS = 4
ORDER = (0, 1, 2, 3, 4, 8, 5, 9, 6, 10, 7, 11)
GATHER_ASIDE = (DOWN + 3,)
REDUCE_ASIDE = (DOWN, UP + 2)
ENTER = (((0, 1), (1, 1), (11, 1), (0, 2)), ((2, 1), (0, 3), (5, 1)), ((1, 2), (2, 2), (0, 4), (1, 3)), ((7, 1),), ((5, 2), (3, 1)), ((1, 4), (4, 1), (11, 2), (2, 3), (6, 1)))
ATTEND = {0: ((8, 1), (5, 3)), 1: ((7, 2), (10, 1)), 3: ((3, 2), (4, 2), (2, 4)), 4: ((6, 2), (3, 3)), 5: ((5, 4), (4, 3), (9, 1), (6, 3)), 7: ((11, 3), (3, 4), (8, 2), (7, 3), (4, 4))}
MIDDLE = {1: ((6, 4),), 2: ((8, 3),), 3: ((9, 2),), 4: ((10, 2), (7, 4)), 5: ((8, 4),), 6: ((9, 3), (11, 4)), 7: ((10, 3),), 8: ((9, 4),), 10: ((10, 4),)}
EARLY = (DOWN, UP, DOWN + 1, UP + 1, DOWN + 2)
DONE = EARLY[:4]
EARLY_POINTS = {5: ((8, 0),), 7: ((8, 1), (4, 0)), 9: ((4, 1), (9, 0)), 10: ((9, 1),), 12: ((5, 0),), 13: ((4, 2), (9, 2), (5, 1)), 15: ((10, 0), (8, 2), (9, 3)), 17: ((4, 3), (5, 2), (10, 1)), 18: ((8, 3), (9, 4), (5, 3)), 19: ((10, 2),), 20: ((5, 4),), 22: ((8, 4), (4, 4))}
LATE = (UP + 2, DOWN + 3, UP + 3, OUT, QKV, QKV + 1, QKV + 2)
LATE_POINTS = {0: ((6, 0), (11, 0)), 1: ((6, 1), (3, 0), (10, -3), (11, 1)), 2: ((7, 0), (3, 1)), 3: ((10, 3), (11, 2)), 5: ((7, 1), (3, 2), (0, 0)), 6: ((11, 3), (1, 0)), 7: ((7, 2), (3, 3), (0, 1)), 11: ((1, 1), (2, 0)), 12: ((7, 3), (0, 2)), 14: ((1, 2),), 15: ((0, 3), (2, 1), (3, 4)), 16: ((6, 2), (10, 4)), 18: ((1, 3), (2, 2), (6, 3)), 19: ((2, 3),), 20: ((6, 4),), 22: ((2, 4), (1, 4)), 23: ((11, 4),), 24: ((0, 4), (7, 4))}
def reduce_stages(points):
    moves = [move for at in sorted(points) for move in points[at]]
    started = [(unit, 3 if stage == -3 else stage + 1) for unit, stage in moves if stage < 4]
    return [(unit, stage) for unit, stage in started if stage > 3 or (unit, stage) in moves or stage < 3]


def gather_stages(points):
    return [(ORDER[index], stage) for point in points for index, stage in point]


def forward_pair(step):
    first = (13 - step) // 8
    return first * ((step // 2 + 1) % 3 + 3 * (step % 2)) + (1 - first) * step


def backward_pair(step):
    group, place = step // 3, step % 3
    return (1 + group) % 3 + 3 * place - place // 2


def pair_unit(which, pair):
    first = (13 - pair) // 8
    sixth, seventh = ((0, 2, 0), (1, 1, 2))[0][which], ((0, 2, 0), (1, 1, 2))[1][which]
    return first * ((pair + 2) % 3) + (1 - first) * ((7 - pair) * sixth + (pair - 6) * seventh)


def pair_block(which, pair):
    return (which * (H // 2) + pair) // 3


def picked(block, j):
    return sum(jnp.where(block == index, PICK[index][j], 0) for index in range(8))


def window_layout(clip_frames, first_window, window_count):
    slab_count = 1 + (clip_frames > WT).astype(jnp.int32)
    starts = jnp.cumsum(slab_count, dtype=jnp.int32) - slab_count
    global_window = first_window + jnp.arange(window_count, dtype=jnp.int32)
    slab_of = global_window // SPW
    owners = jnp.sum((starts[None, :] <= slab_of[:, None]).astype(jnp.int32), axis=1) - 1
    clip_ids = jnp.arange(clip_frames.shape[0], dtype=jnp.int32)
    member = (owners[:, None] == clip_ids[None, :]).astype(jnp.int32)
    clip_start = jnp.sum(member * starts[None, :], axis=1)
    own_frames = jnp.sum(member * clip_frames[None, :], axis=1)
    inner_slab = slab_of - clip_start
    return (jnp.minimum(own_frames - WT * inner_slab, WT), member)


def offset_spread():
    side_span = 2 * WSIDE - 1
    shape = (OFFSETS, WSIDE * LANES)
    offset = lax.broadcasted_iota(jnp.int32, shape, 0)
    place = lax.broadcasted_iota(jnp.int32, shape, 1)
    own, row, other = place // LANES, place // WSIDE % (LANES // WSIDE), place % WSIDE
    row_diff, col_diff = side_span - 1 - row, own - other + (WSIDE - 1)
    return ((row < side_span) & (row_diff * side_span + col_diff == offset)).astype(BF16)


def spread_table(table):
    heads = table.shape[0]
    by_frame = table.reshape(heads, FRAMES, OFFSETS)[:, ::-1].reshape(heads * FRAMES, OFFSETS)
    spread = jnp.dot(by_frame, offset_spread(), preferred_element_type=F32).astype(BF16)
    spread = spread.reshape(heads, FRAMES * WSIDE, LANES)
    return jnp.pad(spread, ((0, 0), (0, SPREAD - FRAMES * WSIDE), (0, 0)))


def gather_table(spread):
    heads = spread.shape[0]
    by_frame = spread[:, : FRAMES * WSIDE].reshape(heads * FRAMES, WSIDE * LANES)
    sums = lax.dot_general(
        by_frame,
        offset_spread().astype(F32),
        (((1,), (1,)), ((), ())),
        precision=HIGHEST,
        preferred_element_type=F32,
    )
    return sums.reshape(heads, FRAMES, OFFSETS)[:, ::-1].reshape(heads, FRAMES * OFFSETS)


def units_of(qkv, out, up, down):
    return jnp.concatenate(
        [
            jnp.stack(
                [
                    jnp.stack([qkv[:, 384 * b + LANES * PICK[b][j] :][:, :LANES] for b in range(8)])
                    for j in range(3)
                ]
            ),
            out.reshape(D, 8, 1, LANES).transpose(2, 1, 0, 3),
            up.reshape(D, 8, 4, LANES).transpose(2, 1, 0, 3),
            down.reshape(8, 4, LANES, 8, LANES).transpose(1, 3, 0, 2, 4).reshape(4, 8, D, LANES),
        ]
    )


def weights_of(units):
    def columns(part):
        return part.transpose(2, 1, 0, 3).reshape(D, -1)

    down = units[DOWN:].reshape(4, 8, 8, LANES, LANES).transpose(2, 0, 3, 1, 4)
    qkv = [
        units[PICK[block].index(tile), block] for block in range(8) for tile in range(3)
    ]
    return (
        jnp.concatenate(qkv, axis=1),
        columns(units[OUT:UP]),
        columns(units[UP:DOWN]),
        down.reshape(4 * D, D),
    )


def dot(left, right):
    return jnp.dot(left, right, preferred_element_type=F32)


def dot_rows(left, right):
    return lax.dot_general(left, right, (((1,), (1,)), ((), ())), preferred_element_type=F32)


def dot_tokens(left, right):
    return lax.dot_general(left, right, (((0,), (0,)), ((), ())), preferred_element_type=F32)


def half(index):
    return pl.ds(pl.multiple_of(index * 512, 512), 512)


def four_columns(unit, index):
    blocks = [unit[2 * index + x // 2, x % 2].reshape(D, LANES) for x in range(4)]
    return jnp.concatenate(blocks, axis=1)


def half_rows(unit, index):
    blocks = [unit[block // 2, block % 2, index].reshape(512, LANES) for block in range(8)]
    return jnp.concatenate(blocks, axis=1)


def put_columns(unit, index, values):
    for x in range(4):
        unit[2 * index + x // 2, x % 2] = values[:, x * LANES : (x + 1) * LANES].reshape(2, 2, SHARE, LANES)


def loop(count, body):
    def step(index, carry):
        body(index)
        return carry

    lax.fori_loop(0, count, step, 0)


def vmem():
    return pl.BlockSpec(memory_space=pltpu.VMEM)


def anywhere():
    return pl.BlockSpec(memory_space=pl.ANY)


def smem():
    return pl.BlockSpec(memory_space=pltpu.SMEM)


def shape(dtype, *sizes):
    return jax.ShapeDtypeStruct(sizes, dtype)


def params(collective=None, limit=58):
    if collective is None:
        return pltpu.CompilerParams(vmem_limit_bytes=limit * MIB)
    return pltpu.CompilerParams(
        vmem_limit_bytes=limit * MIB, collective_id=collective, has_side_effects=True
    )


def centered(values):
    center = values - jnp.mean(values, axis=-1, keepdims=True)
    spread = jnp.mean(center * center, axis=-1, keepdims=True)
    root = lax.rsqrt(spread + EPSILON)
    return center * root, root


def norm_back(grad_normed, normal, root, scale):
    grad = grad_normed * (1.0 + scale)
    mean = jnp.mean(grad, axis=-1, keepdims=True)
    along = jnp.mean(grad * normal, axis=-1, keepdims=True)
    return root * (grad - mean - normal * along)


def each_rows(mod_ref, live_ref, body, rows=32, pump=lambda window: None):
    for window in range(mod_ref.shape[0]):
        live = live_ref[window] * CELLS

        def step(index, window=window, live=live):
            at = pl.ds(pl.multiple_of(window * WIN + index * rows, rows), rows)
            mods = [mod_ref[window, k : k + 1, :] for k in range(6)]
            slot = index * rows + lax.broadcasted_iota(jnp.int32, (rows, 1), 0)
            body(window, at, mods, slot < live)

        loop(WIN // rows, step)
        pump(window)


def add_sums(sums_ref, window, which, values):
    sums_ref[window, which : which + 1, :] += jnp.sum(values, axis=0, keepdims=True)


class Place:
    def __init__(self):
        column, row = lax.axis_index("dp"), lax.axis_index("fsdp")
        self.z, self.x, self.y, self.c = column // 2, column % 2, row // 2, row % 2

    def at(self, z=None, x=None, y=None, c=None):
        z = self.z if z is None else z
        x = self.x if x is None else x
        y = self.y if y is None else y
        c = self.c if c is None else c
        return (z * 2 + x, y * 2 + c)

    def far(self, k):
        return lax.rem(self.z + k, 4)

    def shifted(self, dz, dx, dy, dc):
        def other(index, change):
            return 1 - index if change else index

        return self.at(self.far(dz), other(self.x, dx), other(self.y, dy), other(self.c, dc))

    def greet(self, far_ones=()):
        near = [(1, 0, 0, 0), (2, 0, 0, 0), (3, 0, 0, 0), (0, 1, 0, 0), (0, 0, 1, 0), (0, 0, 0, 1)]
        peers = near + [change for change in far_ones if change not in near]
        barrier = pltpu.get_barrier_semaphore()
        for change in peers:
            pl.semaphore_signal(
                barrier, inc=1, device_id=self.shifted(*change), device_id_type=MESH
            )
        pl.semaphore_wait(barrier, len(peers))


EVERYONE = [
    (dz, dx, dy, dc)
    for dz in range(4)
    for dx in range(2)
    for dy in range(2)
    for dc in range(2)
    if (dz, dx, dy, dc) != (0, 0, 0, 0)
]
ALONG_ZX = [change for change in EVERYONE if change[2:] == (0, 0)]
ALONG_YC = [change for change in EVERYONE if change[:2] == (0, 0)]


class Moves:
    def __init__(self, place, stages, scratch):
        self.place = place
        self.send, self.recv = scratch
        self.first, count = {}, 0
        for unit, stage in stages:
            self.first[unit, stage] = count
            count += self.counts[unit in self.aside][stage - 1]
        self.flying = []

    @classmethod
    def semaphores(cls, stages):
        count = sum(cls.counts[unit in cls.aside][stage - 1] for unit, stage in stages)
        return [pltpu.SemaphoreType.DMA((count,))] * 2

    def made(self, unit, stage, moves):
        copies = []
        for index, (source, target, device) in enumerate(moves):
            slot = self.first[unit, stage] + index
            copies.append(
                pltpu.make_async_remote_copy(
                    src_ref=source,
                    dst_ref=target,
                    send_sem=self.send.at[slot],
                    recv_sem=self.recv.at[slot],
                    device_id=device,
                    device_id_type=MESH,
                )
            )
        return copies

    def begin(self, unit, stage):
        for copy in self.copies(unit, stage):
            copy.start()
        self.flying.append((unit, stage))

    def arrive(self, unit, stage):
        if (unit, stage) in self.flying:
            self.flying.remove((unit, stage))
            for copy in self.copies(unit, stage):
                copy.wait_recv()

    def sent(self):
        for unit, stage in self.first:
            for copy in self.copies(unit, stage):
                copy.wait_send()


class Gather(Moves):
    counts = ((3, 2, 2, 1), (2, 2, 3, 1))
    aside = GATHER_ASIDE

    def __init__(self, place, held, stages, scratch):
        super().__init__(place, stages, scratch)
        self.held = held

    def copies(self, unit, stage):
        p, held = self.place, self.held.at[unit]
        at_x, at_y, at_core = p.at(x=1 - p.x), p.at(y=1 - p.y), p.at(c=1 - p.c)
        own = held.at[p.z, p.x, p.y, p.c]
        if stage == 4:
            refs = [(held.at[:, :, :, p.c], at_core)]
        elif unit in self.aside and stage == 1:
            refs = [(own.at[:HALF], at_x), (own.at[HALF:], at_y)]
        elif unit in self.aside and stage == 2:
            refs = [
                (held.at[p.z, :, p.y, p.c, :HALF], at_y),
                (held.at[p.z, p.x, :, p.c, HALF:], at_x),
            ]
        elif unit in self.aside:
            refs = [(held.at[p.z, :, :, p.c], p.at(z=p.far(k))) for k in (1, 2, 3)]
        elif stage == 1:
            refs = [(own, p.at(z=p.far(k))) for k in (1, 2, 3)]
        elif stage == 2:
            refs = [
                (held.at[:, p.x, p.y, p.c, :HALF], at_x),
                (held.at[:, p.x, p.y, p.c, HALF:], at_y),
            ]
        else:
            refs = [
                (held.at[:, :, p.y, p.c, :HALF], at_y),
                (held.at[:, p.x, :, p.c, HALF:], at_x),
            ]
        return self.made(unit, stage, [(ref, ref, device) for ref, device in refs])

    def advance(self, unit, stage):
        self.arrive(unit, stage - 1)
        self.begin(unit, stage)

    def finish(self):
        for unit, stage in list(self.flying):
            self.arrive(unit, stage)
        self.sent()


class Reduce(Moves):
    counts = ((1, 2, 2, 3), (1, 3, 2, 2))
    aside = REDUCE_ASIDE

    def __init__(self, place, part, points, store, buffers, scratch):
        super().__init__(place, reduce_stages(points), scratch[2:])
        self.part, self.store, self.buffers = part, store, buffers
        self.own, self.load = scratch[:2]
        self.slots, self.loaded = {}, []

    @classmethod
    def scratch(cls, points):
        return [
            pltpu.VMEM((OWN_SLOTS, 4, 2, 2, SHARE, LANES), BF16),
            pltpu.SemaphoreType.DMA((OWN_SLOTS,)),
        ] + cls.semaphores(reduce_stages(points))

    @staticmethod
    def core_shape(count):
        return (count, 4, 2, 2, SHARE, LANES)

    @staticmethod
    def side_shape(count):
        return (count, 2, 4, 2, HALF, LANES)

    @staticmethod
    def corner_shape(count):
        return (count, 2, 4, HALF, LANES)

    @staticmethod
    def distant_shape(count):
        return (count, 3, 2, HALF, LANES)

    @staticmethod
    def aside_shape(count):
        return (count, 3, 2, 2, SHARE, LANES)

    def own_copy(self, unit):
        slot = self.slots.setdefault(unit, len(self.slots) % OWN_SLOTS)
        return pltpu.make_async_copy(
            self.part(unit).at[:, :, :, self.place.c], self.own.at[slot], self.load.at[slot]
        )

    def copies(self, unit, stage):
        p = self.place
        at_x, at_y, at_core = p.at(x=1 - p.x), p.at(y=1 - p.y), p.at(c=1 - p.c)
        core, side, corner, distant = self.buffers(unit)
        if unit in self.aside and stage == 2:
            moves = [
                (core.at[p.far(k)], distant.at[k - 1], p.at(z=p.far(k))) for k in (1, 2, 3)
            ]
        elif unit in self.aside and stage == 3:
            moves = [
                (core.at[p.z, :, 1 - p.y, :HALF], side.at[0, 0], at_y),
                (core.at[p.z, 1 - p.x, :, HALF:], side.at[1, 0], at_x),
            ]
        elif unit in self.aside and stage == 4:
            moves = [
                (side.at[0, 0, 1 - p.x], side.at[0, 1, 0], at_x),
                (side.at[1, 0, 1 - p.y], side.at[1, 1, 0], at_y),
            ]
        elif stage == 1:
            moves = [(self.part(unit).at[:, :, :, 1 - p.c], core, at_core)]
        elif stage == 2:
            moves = [
                (core.at[:, :, 1 - p.y, :HALF], side.at[0], at_y),
                (core.at[:, 1 - p.x, :, HALF:], side.at[1], at_x),
            ]
        elif stage == 3:
            moves = [
                (side.at[0, :, 1 - p.x], corner.at[0], at_x),
                (side.at[1, :, 1 - p.y], corner.at[1], at_y),
            ]
        else:
            moves = [
                (corner.at[:, p.far(k)], distant.at[k - 1], p.at(z=p.far(k))) for k in (1, 2, 3)
            ]
        return self.made(unit, stage, moves)

    def begin(self, unit, stage):
        super().begin(unit, stage)
        if stage == 1:
            self.own_copy(unit).start()
            assert self.slots[unit] not in self.loaded
            self.loaded.append(self.slots[unit])

    def combine(self, unit, stage):
        p = self.place
        core, side, corner, distant = self.buffers(unit)

        def plus(left, right):
            return (left.astype(F32) + right.astype(F32)).astype(BF16)

        def from_core(step):
            z, x, y = step // 4, step // 2 % 2, step % 2
            core[z, x, y] = plus(core[z, x, y], self.own[self.slots[unit], z, x, y])

        def from_side(step):
            z, b = step // 2, step % 2
            side[0, z, b] = plus(side[0, z, b], core[z, b, p.y, :HALF])
            side[1, z, b] = plus(side[1, z, b], core[z, p.x, b, HALF:])

        def from_corner(z):
            corner[0, z] = plus(corner[0, z], side[0, z, p.x])
            corner[1, z] = plus(corner[1, z], side[1, z, p.y])

        def from_far(half):
            total = corner[half, p.z].astype(F32)
            for k in range(3):
                total = total + distant[k, half].astype(F32)
            self.store(unit, half, total)

        def aside_far(step):
            x, y = step // 2, step % 2
            total = core[p.z, x, y].astype(F32)
            for k in range(3):
                total = total + distant[k, x, y].astype(F32)
            core[p.z, x, y] = total.astype(BF16)

        def aside_side(b):
            side[0, 0, b] = plus(side[0, 0, b], core[p.z, b, p.y, :HALF])
            side[1, 0, b] = plus(side[1, 0, b], core[p.z, p.x, b, HALF:])

        if unit in self.aside and stage == 4:
            for part, own in enumerate((p.x, p.y)):
                total = side[part, 0, own].astype(F32) + side[part, 1, 0].astype(F32)
                self.store(unit, part, total)
            return
        steps = {1: (16, from_core), 2: (8, from_side), 3: (4, from_corner), 4: (2, from_far)}
        if unit in self.aside:
            steps |= {2: (4, aside_far), 3: (2, aside_side)}
        loop(*steps[stage])

    def step(self, unit, stage):
        if stage <= 0:
            self.begin(unit, max(1, -stage))
            return
        self.arrive(unit, stage)
        if stage == 1:
            self.own_copy(unit).wait()
        self.combine(unit, stage)
        if stage == 1:
            self.loaded.remove(self.slots[unit])
        if (unit, stage + 1) in self.first:
            self.begin(unit, stage + 1)


class Copies:
    def __init__(self, send, recv):
        self.send, self.recv, self.count = send, recv, 0

    def __call__(self, source, target, device):
        slot = self.count
        self.count += 1
        copy = pltpu.make_async_remote_copy(
            src_ref=source,
            dst_ref=target,
            send_sem=self.send.at[slot],
            recv_sem=self.recv.at[slot],
            device_id=device,
            device_id_type=MESH,
        )
        copy.start()
        return copy


class Refs:
    pass


def call(kernel, name, inputs, outputs, scratch, aliases=(), collective=None, grid=None, limit=58):
    names = list(inputs) + list(outputs)
    flat = []
    for value in scratch.values():
        flat += value if isinstance(value, list) else [value]

    def body(*refs):
        held = Refs()
        rest = list(refs)
        for key in names:
            setattr(held, key, rest.pop(0))
        for key, value in scratch.items():
            if isinstance(value, list):
                setattr(held, key, [rest.pop(0) for _ in value])
            else:
                setattr(held, key, rest.pop(0))
        kernel(held)

    extra = {} if grid is None else {"grid": grid}
    made = functools.partial(
        pl.pallas_call,
        body,
        in_specs=[spec for _, spec in inputs.values()],
        out_specs=[spec for _, spec in outputs.values()],
        out_shape=[out for out, _ in outputs.values()],
        scratch_shapes=flat,
        input_output_aliases={
            list(inputs).index(one): list(outputs).index(other) for one, other in aliases
        },
        compiler_params=params(collective, limit),
        name=name,
        **extra,
    )
    arrays = [array for array, _ in inputs.values()]
    if name == "start":
        result = made()(*arrays)
    else:
        result = made()(*arrays)
    out = Refs()
    for key, value in zip(outputs, result, strict=True):
        setattr(out, key, value)
    return out


def enter_norm(refs, pump=lambda: None):
    rows = 32
    for window in range(refs.mod.shape[0]):
        shift, scale = refs.mod[window, 0:1, :], refs.mod[window, 1:2, :]

        def step(index, window=window, shift=shift, scale=scale):
            at = pl.ds(pl.multiple_of(window * WIN + index * rows, rows), rows)
            normal, _ = centered(refs.tokens[at, :].astype(F32))
            refs.normed[at, :] = (normal * (1.0 + scale) + shift).astype(BF16)

        loop(WIN // rows, step)
        pump()


def enter_unit(refs, j, held, put=False):
    unit = refs.units.at[0]
    fetch = pltpu.make_async_copy(held, unit, refs.fetches.at[0])
    fetch.start()
    fetch.wait()

    def project(index):
        refs.packed[j, :, half(index)] = dot(refs.normed[...], four_columns(unit, index)).astype(
            BF16
        )

    loop(2, project)
    if put:
        packed_copy(refs, j).start()


def normed_copy(refs):
    return pltpu.make_async_copy(refs.normed, refs.normed_out, refs.packed_sem.at[3])


def packed_copy(refs, j):
    return pltpu.make_async_copy(refs.packed.at[j], refs.packed_out.at[j], refs.packed_sem.at[j])


def enter_plain_kernel(refs):
    enter_norm(refs)
    for j in range(3):
        enter_unit(refs, j, refs.held.at[QKV + j])


def act_rows(refs, place):
    first = (place.y * 2 + place.c) * SHARE
    value = refs.condition[:, pl.ds(pl.multiple_of(first, SHARE), SHARE)]
    act = value / (1.0 + jnp.exp(-value))
    return jnp.concatenate([act, jnp.zeros((8 - value.shape[0], SHARE), F32)], axis=0).astype(BF16)


def enter_layout(refs):
    windows, clips = refs.member.shape[0], refs.condition.shape[0]
    frames = [refs.frames[clip] for clip in range(clips)]
    starts = [0]
    for count in frames:
        starts.append(starts[-1] + 1 + jnp.where(count > WT, 1, 0))
    device = lax.axis_index("dp") * lax.axis_size("fsdp") + lax.axis_index("fsdp")
    refs.member[...] = jnp.zeros_like(refs.member)
    for window in range(windows):
        slab = (device * windows + window) // SPW
        live = 0
        for clip in range(clips):
            mine = starts[clip] <= slab
            if clip < clips - 1:
                mine = mine & (slab < starts[clip + 1])
            inner = frames[clip] - WT * (slab - starts[clip])
            live = live + jnp.where(mine, jnp.minimum(inner, WT), 0)
            refs.member[window, clip : clip + 1, :] = jnp.full(
                (1, LANES), jnp.where(mine, 1.0, 0.0), F32
            )
        refs.live[window] = live


def enter_table(refs):
    refs.rows[...] = jnp.zeros_like(refs.rows)
    table = refs.rel_table[...].astype(F32)
    for head in range(2):
        for frame in range(FRAMES):
            first = (FRAMES - 1 - frame) * OFFSETS
            row = head * (SPREAD // WSIDE) + frame
            refs.rows[row : row + 1, :OFFSETS] = table[head : head + 1, first : first + OFFSETS]
    shape_of = (TILE, WSIDE * LANES)
    offset = lax.broadcasted_iota(jnp.int32, shape_of, 0)
    place = lax.broadcasted_iota(jnp.int32, shape_of, 1)
    own, row, other = place // LANES, place // WSIDE % (LANES // WSIDE), place % WSIDE
    side_span = 2 * WSIDE - 1
    row_diff, col_diff = side_span - 1 - row, own - other + (WSIDE - 1)
    same = (row < side_span) & (row_diff * side_span + col_diff == offset)
    spread = dot(refs.rows[...].astype(BF16), jnp.where(same, 1.0, 0.0).astype(BF16))
    count = 2 * SPREAD // WSIDE
    for own in range(WSIDE):
        refs.spread[pl.ds(own, count, stride=WSIDE), :] = spread[
            :count, own * LANES : (own + 1) * LANES
        ]
    for head in range(2):
        refs.table_own[head] = refs.spread[head * SPREAD : (head + 1) * SPREAD, :].astype(BF16)


def enter(refs, place, work):
    place.greet(ALONG_ZX + ALONG_YC)
    z, x, y, c = place.z, place.x, place.y, place.c
    small = Copies(*refs.small)
    mods = dot(act_rows(refs, place), refs.ada[...])
    mods = mods + jnp.where((y == 0) & (c == 0), 1.0, 0.0) * refs.bias_in[...].astype(F32)
    for block in range(6):
        refs.mod_part[block * CLIP_ROWS : (block + 1) * CLIP_ROWS, :] = mods[
            :CLIP_ROWS, block * LANES : (block + 1) * LANES
        ]
    refs.mod_parts[y, c] = refs.mod_part[...]
    parts = [
        small(refs.mod_part, refs.mod_parts.at[y, c], place.shifted(*change)) for change in ALONG_YC
    ]
    own = []
    for unit in range(UNITS):
        if unit < OUT:
            first = picked(z * 2 + x, unit) * LANES
            refs.own[unit] = refs.qkv[:, pl.ds(pl.multiple_of(first, LANES), LANES)]
        elif unit >= DOWN:
            first = (unit - DOWN) * LANES
            for half in range(2):
                at = slice(half * 512 + first, half * 512 + first + LANES)
                refs.own[unit, half * HALF : (half + 1) * HALF] = refs.down[at, :]
        else:
            source, start = (refs.out, OUT) if unit < UP else (refs.up, UP)
            first = (unit - start) * LANES
            refs.own[unit] = source[:, first : first + LANES]
        own.append(
            pltpu.make_async_copy(
                refs.own.at[unit], refs.held.at[unit, z, x, y, c], refs.own_sem.at[unit]
            )
        )
        own[-1].start()
    points = list(ENTER)

    loaded = []

    def load(unit):
        if unit not in loaded:
            own[unit].wait()
            loaded.append(unit)

    def tick():
        for index, stage in points.pop(0):
            if stage == 1:
                load(ORDER[index])
            work.advance(ORDER[index], stage)

    tick()
    enter_layout(refs)
    enter_table(refs)
    refs.table[z, x, c] = refs.table_own[c]
    for copy in parts:
        copy.wait()
    refs.mods[z, x] = (
        refs.mod_parts[0, 0] + refs.mod_parts[0, 1] + refs.mod_parts[1, 0] + refs.mod_parts[1, 1]
    )
    mods = [
        small(refs.mods.at[z, x], refs.mods.at[z, x], place.shifted(*change))
        for change in ALONG_ZX
    ]
    for unit in range(UNITS):
        load(unit)
    tick()
    for copy in mods:
        copy.wait()
    tables = [
        small(refs.table.at[z, x, c], refs.table.at[z, x, c], place.shifted(*change))
        for change in ALONG_ZX
    ]
    for window in range(refs.mod.shape[0]):
        for block in range(48):
            which, column = divmod(block, 8)
            first = block % 6 * CLIP_ROWS
            part = refs.mods[block // 12, block // 6 % 2, first : first + CLIP_ROWS, :]
            refs.mod[window, which : which + 1, column * LANES : (column + 1) * LANES] = jnp.sum(
                part * refs.member[window], axis=0, keepdims=True
            )
    tick()
    enter_norm(refs, tick)
    normed_copy(refs).start()
    for copy in tables:
        copy.wait()
    last = small(refs.table.at[:, :, c], refs.table.at[:, :, c], place.at(c=1 - c))
    work.arrive(QKV, 4)
    tick()
    enter_unit(refs, 0, refs.held.at[QKV], put=True)
    last.wait()


def attend_pair(refs, table, part, put):
    for head in range(2):
        spread = table(head).astype(F32)
        for frame in range(FRAMES):
            block = spread[frame * WSIDE : (frame + 1) * WSIDE]
            for row in range(WSIDE):
                first = (WSIDE - 1 - row) * WSIDE
                refs.strip[
                    head, row * WSIDE : (row + 1) * WSIDE, frame * CELLS : (frame + 1) * CELLS
                ] = block[:, first : first + CELLS]
        for frame in range(WT):
            first = (WT - 1 - frame) * CELLS
            refs.bias[head, frame * CELLS : (frame + 1) * CELLS, :] = refs.strip[
                head, :, first : first + WIN
            ]
    for window in range(refs.live.shape[0]):
        rows = slice(window * WIN, (window + 1) * WIN)
        live = refs.live[window] * CELLS
        key_live = lax.broadcasted_iota(jnp.int32, (1, WIN), 1) < live
        query, key, value = (part(which, rows) for which in range(3))
        mixed = []
        for head in range(2):
            lanes = slice(head * HD, (head + 1) * HD)
            scores = dot_rows(query[:, lanes] * BF16(HD ** (-0.5)), key[:, lanes]) + refs.bias[head]
            scores = jnp.where(key_live, scores, NEGATIVE)
            shifted = jnp.exp(scores - jnp.max(scores, axis=-1, keepdims=True))
            totals = jnp.sum(shifted, axis=-1, keepdims=True)
            probs = (shifted * (1.0 / totals)).astype(BF16)
            refs.probs[window, head] = probs
            mixed.append(dot(probs, value[:, lanes]).astype(BF16))
        put(rows, jnp.concatenate(mixed, axis=1))


def attend_plain_kernel(refs):
    sources = (refs.query, refs.key, refs.value)

    def put(rows, values):
        refs.mixed[rows, :] = values

    attend_pair(
        refs, lambda head: refs.table[head], lambda which, rows: sources[which][rows, :], put
    )


def start_kernel(refs):
    step = pl.program_id(0)
    pairs = H // 2
    place = Place()
    stages = gather_stages(ENTER + tuple(ATTEND.values()) + tuple(MIDDLE.values()))
    work = Gather(place, refs.held, stages, refs.gather)

    @pl.when(step == 0)
    def _():
        enter(refs, place, work)

    for at in range(pairs):

        @pl.when(step == at + 1)
        def _(at=at):
            for index, stage in ATTEND.get(at, ()):
                work.advance(ORDER[index], stage)
            if at in (2, 4):
                work.arrive(QKV + at // 2, 4)
                enter_unit(refs, at // 2, refs.held.at[QKV + at // 2], put=True)

    @pl.when((step > 0) & (step <= pairs))
    def _():
        pair = forward_pair(jnp.clip(step - 1, 0, pairs - 1))

        def columns(block):
            return pl.ds(pl.multiple_of(block * LANES, LANES), LANES)

        def part(which, rows):
            return refs.packed[pair_unit(which, pair), rows, columns(pair_block(which, pair))]

        def table(head):
            return refs.table[pair // 2, pair % 2, head]

        def put(rows, values):
            refs.mixed[rows, columns(pair)] = values

        attend_pair(refs, table, part, put)

    @pl.when(step == pairs)
    def _():
        for j in range(3):
            packed_copy(refs, j).wait()
        normed_copy(refs).wait()

    @pl.when(step == pairs + 1)
    def _():
        middle(refs, place, work)


def packed_block(which, rows, pair):
    return pl.BlockSpec(
        (None, rows, LANES),
        lambda step: (pair_unit(which, pair(step)), 0, pair_block(which, pair(step))),
    )


def attend_back_pair(refs, pair):
    scale = BF16(HD ** (-0.5))
    refs.spread[...] = jnp.zeros_like(refs.spread)
    refs.strip[...] = jnp.zeros_like(refs.strip)
    windows = refs.probs.shape[0]
    results = [[[None] * windows for _ in range(2)] for _ in range(3)]
    for head in range(2):
        lanes = slice(head * HD, (head + 1) * HD)
        bias = None
        for window in range(windows):
            rows = slice(window * WIN, (window + 1) * WIN)
            grad = refs.grad[rows, lanes]
            probs = refs.probs[window, head]
            results[2][head][window] = dot_tokens(grad, probs).T.astype(BF16)
            grad_probs = dot_rows(grad, refs.value[rows, lanes])
            weight = probs.astype(F32)
            product = weight * grad_probs
            total = jnp.sum(product, axis=-1, keepdims=True)
            grad_scores = (product - weight * total).astype(BF16)
            wide = grad_scores.astype(F32)
            bias = wide if bias is None else bias + wide
            results[0][head][window] = dot(grad_scores, refs.key[rows, lanes] * scale).astype(BF16)
            query = refs.query[rows, lanes] * scale
            results[1][head][window] = dot_tokens(query, grad_scores).T.astype(BF16)
        for frame in range(WT):
            first = (WT - 1 - frame) * CELLS
            refs.strip[head, :, first : first + WIN] += bias[frame * CELLS : (frame + 1) * CELLS]
        for frame in range(FRAMES):
            for row in range(WSIDE):
                first = (WSIDE - 1 - row) * WSIDE
                refs.spread[
                    head, frame * WSIDE : (frame + 1) * WSIDE, first : first + CELLS
                ] += refs.strip[
                    head, row * WSIDE : (row + 1) * WSIDE, frame * CELLS : (frame + 1) * CELLS
                ]
    for part in range(3):
        lanes = pl.ds(pl.multiple_of(pair_block(part, pair) * LANES, LANES), LANES)
        for window in range(windows):
            rows = slice(window * WIN, (window + 1) * WIN)
            both = [results[part][head][window] for head in range(2)]
            refs.grad_packed[pair_unit(part, pair), rows, lanes] = jnp.concatenate(both, axis=1)


def middle(refs, place=None, gathering=None):
    order = [OUT] + [unit for j in range(4) for unit in (UP + j, DOWN + j)] + [OUT]
    activated, grad_hidden, grad_low = (refs.packed.at[index] for index in range(3))
    reducing = None
    points = {}
    waiting = set()
    if gathering is not None:

        def buffers(unit):
            index = EARLY.index(unit)
            core, side = refs.core.at[index], refs.side.at[index]
            if unit not in DONE:
                return core, side, None, None
            if unit in REDUCE_ASIDE:
                return core, side, None, refs.aside.at[0]
            return core, side, refs.corner.at[index], refs.distant.at[index]

        def store(unit, part, values):
            at = pl.ds(pl.multiple_of(part * HALF, HALF), HALF)
            refs.total[DONE.index(unit), at, :] = values

        reducing = Reduce(
            place, lambda unit: refs.part.at[unit], EARLY_POINTS, store, buffers, refs.reduce
        )
        for stages in MIDDLE.values():
            waiting |= {ORDER[index] for index, stage in stages if stage == 4}
        points = {at: list(moves) for at, moves in EARLY_POINTS.items()}

    count = [0]

    def pump():
        for index, stage in MIDDLE.get(count[0], ()) if gathering is not None else ():
            gathering.advance(ORDER[index], stage)
            if stage == 4:
                waiting.discard(ORDER[index])
        for unit, stage in points.pop(count[0], ()):
            reducing.step(unit, stage)
        count[0] += 1

    def fetch(step):
        return pltpu.make_async_copy(
            refs.held.at[order[step]], refs.units.at[step % 4], refs.fetches.at[step % 4]
        )

    def start_fetch(step):
        if gathering is not None:
            assert order[step] not in waiting
            gathering.arrive(order[step], 4)
        fetch(step).start()

    def put(slot, unit):
        return pltpu.make_async_copy(refs.made.at[slot], refs.part.at[unit], refs.made_sem.at[slot])

    for step in range(3):
        start_fetch(step)
    pump()
    refs.sums[...] = jnp.zeros_like(refs.sums)
    refs.mlp[...] = jnp.zeros_like(refs.mlp)
    refs.grad_normed[...] = jnp.zeros_like(refs.grad_normed)
    fetch(0).wait()

    def project(index):
        refs.attended[:, half(index)] = dot(refs.mixed[...], four_columns(refs.units.at[0], index))

    loop(2, project)
    pump()

    def modulate(window, at, mods, live):
        middle = refs.tokens[at, :].astype(F32) + mods[2] * refs.attended[at, :]
        normal, _ = centered(middle)
        refs.normed[at, :] = (normal * (1.0 + mods[4]) + mods[3]).astype(BF16)
        grad = jnp.where(live, refs.cotangent[at, :].astype(F32), 0.0)
        grad_low[at, :] = (mods[5] * grad).astype(BF16)

    each_rows(refs.mod, refs.live, modulate)
    pump()
    for j in range(4):
        step = 1 + 2 * j
        up, down = refs.units.at[step % 4], refs.units.at[(step + 1) % 4]
        fetch(step).wait()
        fetch(step + 1).wait()
        start_fetch(step + 2)

        def hide(index, up=up, down=down):
            hidden = dot(refs.normed[...], four_columns(up, index))
            bend = jnp.tanh(0.7978845608028654 * (hidden + 0.044715 * hidden * hidden * hidden))
            activated[:, half(index)] = (0.5 * hidden * (1.0 + bend)).astype(BF16)
            slope = 0.5 * (1.0 + bend) + 0.5 * hidden * (1.0 - bend * bend) * (
                0.7978845608028654 * (1.0 + 3.0 * 0.044715 * hidden * hidden)
            )
            grad_activated = dot_rows(grad_low[...], half_rows(down, index))
            grad_hidden[:, half(index)] = (grad_activated * slope).astype(BF16)

        loop(2, hide)
        if j > 0:
            put(1, UP + j - 1).wait()
        pump()

        def down_gradient(index):
            made = dot_tokens(activated[:, half(index)], grad_low[...]).astype(BF16)
            for block in range(8):
                refs.made[0, block // 2, block % 2, index] = made[
                    :, block * LANES : (block + 1) * LANES
                ].reshape(2, SHARE, LANES)

        loop(2, down_gradient)
        put(0, DOWN + j).start()
        pump()

        def up_gradient(index):
            made = dot_tokens(refs.normed[...], grad_hidden[:, half(index)]).astype(BF16)
            put_columns(refs.made.at[1], index, made)

        loop(2, up_gradient)
        put(0, DOWN + j).wait()
        put(1, UP + j).start()
        pump()
        if j < 3:
            start_fetch(step + 3)

        def out_of_mlp(index, up=up, down=down):
            refs.mlp[:, half(index)] += dot(activated[...], four_columns(down, index))
            refs.grad_normed[:, half(index)] += dot_rows(
                grad_hidden[...], half_rows(up, index)
            )

        loop(2, out_of_mlp)
        pump()

    put(1, UP + 3).wait()

    def join(window, at, mods, live):
        attended = refs.attended[at, :]
        middle = refs.tokens[at, :].astype(F32) + mods[2] * attended
        normal, root = centered(middle)
        mlp = refs.mlp[at, :]
        refs.normed[at, :] = jnp.where(live, middle + mods[5] * mlp, 0.0).astype(BF16)
        grad_result = jnp.where(live, refs.cotangent[at, :].astype(F32), 0.0)
        grad_normed = refs.grad_normed[at, :]
        grad_middle = grad_result + norm_back(grad_normed, normal, root, mods[4])
        refs.mlp[at, :] = grad_middle
        grad_low[at, :] = (mods[2] * grad_middle).astype(BF16)
        add_sums(refs.sums, window, 2, grad_middle * attended)
        add_sums(refs.sums, window, 3, grad_normed)
        add_sums(refs.sums, window, 4, grad_normed * normal)
        add_sums(refs.sums, window, 5, grad_result * mlp)

    each_rows(refs.mod, refs.live, join)
    results = [
        pltpu.make_async_copy(source, target, refs.result_sem.at[index])
        for index, (source, target) in enumerate(
            (
                (refs.normed, refs.output),
                (refs.mlp, refs.grad_middle),
                (activated, refs.grad_mixed),
            )
        )
    ]
    results[0].start()
    results[1].start()
    pump()
    fetch(9).wait()

    def back(index):
        made = dot_tokens(refs.mixed[...], grad_low[:, half(index)]).astype(BF16)
        put_columns(refs.made.at[0], index, made)
        activated[:, half(index)] = dot_rows(
            grad_low[...], half_rows(refs.units.at[1], index)
        ).astype(BF16)

    loop(2, back)
    results[2].start()
    put(0, OUT).start()
    put(0, OUT).wait()
    while points:
        pump()
    for index, unit in enumerate(EARLY if gathering is not None else ()):
        if unit not in DONE:

            def keep(z, index=index):
                for part in range(2):
                    refs.side_out[index - len(DONE), part, z] = refs.side[index, part, z]

            loop(4, keep)
    for copy in results:
        copy.wait()
    if gathering is not None:
        gathering.finish()
        reducing.sent()


def leave_weight(refs, j, made):
    def weight(index):
        grad = dot_tokens(refs.normed[...], refs.grad_packed[j, :, half(index)]).astype(BF16)
        put_columns(made, index, grad)

    loop(2, weight)


def leave_back(refs, j):
    def back(index):
        refs.grad_normed[:, half(index)] += dot_rows(
            refs.grad_packed[j], half_rows(refs.unit, index)
        )

    loop(2, back)


def leave_norm(refs, pump=lambda window: None):
    def join(window, at, mods, live):
        normal, root = centered(refs.tokens[at, :].astype(F32))
        grad_normed = refs.grad_normed[at, :]
        refs.grad_tokens[at, :] = refs.grad_middle[at, :] + norm_back(
            grad_normed, normal, root, mods[1]
        )
        add_sums(refs.sums, window, 0, grad_normed)
        add_sums(refs.sums, window, 1, grad_normed * normal)

    each_rows(refs.mod, refs.live, join, pump=pump)


def back_plain_kernel(refs):
    step = pl.program_id(0)

    @pl.when(step < H // 2)
    def _():
        attend_back_pair(refs, backward_pair(jnp.minimum(step, H // 2 - 1)))

    @pl.when(step == H // 2)
    def _():
        refs.sums[...] = jnp.zeros_like(refs.sums)
        refs.grad_normed[...] = jnp.zeros_like(refs.grad_normed)
        for j in range(3):
            fetch = pltpu.make_async_copy(refs.held.at[QKV + j], refs.unit, refs.fetch)
            fetch.start()
            leave_weight(refs, j, refs.made)
            put = pltpu.make_async_copy(refs.made, refs.part.at[j], refs.made_sem)
            put.start()
            fetch.wait()
            leave_back(refs, j)
            put.wait()
        leave_norm(refs)


def fold_spreads(refs):
    heads = H * WIDE // WSIDE
    shape_of = (WSIDE * LANES, TILE)
    place = lax.broadcasted_iota(jnp.int32, shape_of, 0)
    offset = lax.broadcasted_iota(jnp.int32, shape_of, 1)
    own, row, other = place // LANES, place // WSIDE % (LANES // WSIDE), place % WSIDE
    side_span = 2 * WSIDE - 1
    row_diff, col_diff = side_span - 1 - row, own - other + (WSIDE - 1)
    same = (row < side_span) & (row_diff * side_span + col_diff == offset)
    onto = jnp.where(same, 1.0, 0.0).astype(BF16)
    left = jnp.concatenate(
        [refs.spreads[pl.ds(own, heads, stride=WSIDE), :] for own in range(WSIDE)], axis=1
    )
    total = jnp.zeros((heads, TILE), F32)
    for _ in range(3):
        low = left.astype(BF16)
        total = total + dot(low, onto)
        left = left - low.astype(F32)
    rows = 2 * WIDE // WSIDE
    for block in range(8):
        refs.table[block // 2, block % 2] = total[block * rows : (block + 1) * rows]


def back_kernel(refs):
    place = Place()
    z, x, y, c = place.z, place.x, place.y, place.c
    step = pl.program_id(0)

    def buffers(unit):
        every = (EARLY + LATE).index(unit)
        late = every - len(EARLY)
        assert unit not in DONE
        if late < 0:
            core, side = None, refs.side_in.at[every - len(DONE)]
        else:
            core, side = refs.core.at[late], refs.side.at[late]
        if unit in REDUCE_ASIDE:
            return core, side, None, refs.aside.at[0]
        return core, side, refs.corner.at[every], refs.distant.at[every]

    def store(unit, part, values):
        if unit >= DOWN:
            first = part * 512 + (unit - DOWN) * LANES
            refs.grad_down[pl.ds(pl.multiple_of(first, LANES), LANES), :] = values
            return
        at = pl.ds(pl.multiple_of(part * HALF, HALF), HALF)
        if unit < OUT:
            column = picked(z * 2 + x, unit) * LANES
            refs.grad_qkv[at, pl.ds(pl.multiple_of(column, LANES), LANES)] = values
            return
        target, start = (refs.grad_out, OUT) if unit < UP else (refs.grad_up, UP)
        column = (unit - start) * LANES
        target[at, column : column + LANES] = values

    work = Reduce(
        place,
        lambda unit: refs.made.at[unit] if unit < OUT else refs.part.at[unit],
        LATE_POINTS,
        store,
        buffers,
        refs.reduce,
    )
    small = Copies(*refs.small)

    events = [(at, move) for at in sorted(LATE_POINTS) for move in LATE_POINTS[at]]

    def run(until):
        while events and events[0][0] < until:
            work.step(*events.pop(0)[1])

    for number in range(H // 2):

        @pl.when(step == number)
        def _(number=number):
            if number == 0:
                place.greet(EVERYONE)
            if number in (3, 6):
                leave_weight(refs, number // 3 - 1, refs.made.at[number // 3 - 1])
            run(number + 1)

    @pl.when(step < H // 2)
    def _():
        pair = backward_pair(jnp.minimum(step, H // 2 - 1))
        attend_back_pair(refs, pair)
        for head in range(2):
            at = pl.ds(pl.multiple_of((pair * 2 + head) * WIDE, WIDE), WIDE)
            refs.spreads[at, :] = refs.spread[head]

    @pl.when(step == H // 2)
    def _():
        for index, unit in enumerate(DONE):
            for part in range(2):
                store(unit, part, refs.done[index, part * HALF : (part + 1) * HALF, :])
        fold_spreads(refs)
        table = []
        for dz, dx, dy, dc in ALONG_ZX:
            source = refs.table.at[place.far(dz), 1 - x if dx else x]
            table.append(small(source, refs.table_zx.at[z, x], place.shifted(dz, dx, dy, dc)))
        refs.table_zx[z, x] = refs.table[z, x]
        refs.sums[...] = refs.late_sums[...]
        refs.grad_normed[...] = jnp.zeros_like(refs.grad_normed)

        def fetch(j):
            return pltpu.make_async_copy(refs.held.at[QKV + j], refs.unit, refs.fetch)

        fetch(0).start()
        leave_weight(refs, 2, refs.made.at[2])
        run(12)
        fetch(0).wait()
        leave_back(refs, 0)
        fetch(1).start()
        run(13)
        fetch(1).wait()
        leave_back(refs, 1)
        fetch(2).start()
        run(14)
        fetch(2).wait()
        leave_back(refs, 2)
        run(15)
        leave_norm(refs, lambda window: run(17 + window))
        for copy in table:
            copy.wait()
        total = refs.table_zx[0, 0]
        for block in range(1, 8):
            total = total + refs.table_zx[block // 2, block % 2]
        refs.table_own[...] = total
        refs.table_yc[y, c] = total
        table = [
            small(refs.table_own, refs.table_yc.at[y, c], place.shifted(*change))
            for change in ALONG_YC
        ]
        for block in range(48):
            which, column = divmod(block, 8)
            part = jnp.zeros((CLIP_ROWS, LANES), F32)
            for window in range(refs.mod.shape[0]):
                sums = refs.sums[window, which : which + 1, column * LANES : (column + 1) * LANES]
                part = part + refs.member[window] * sums
            first = block % 6 * CLIP_ROWS
            refs.clip[block // 12, block // 6 % 2, first : first + CLIP_ROWS, :] = part
        copies = []
        for dz, dx, dy, dc in ALONG_ZX:
            source = refs.clip.at[place.far(dz), 1 - x if dx else x]
            copies.append(small(source, refs.clip_zx.at[z, x], place.shifted(dz, dx, dy, dc)))
        refs.clip_zx[z, x] = refs.clip[z, x]
        run(19)
        for copy in copies:
            copy.wait()
        total = refs.clip_zx[0, 0]
        for block in range(1, 8):
            total = total + refs.clip_zx[block // 2, block % 2]
        refs.clip_own[...] = total
        refs.clip_yc[y, c] = total
        copies = [
            small(refs.clip_own, refs.clip_yc.at[y, c], place.shifted(*change))
            for change in ALONG_YC
        ]
        run(21)
        for copy in copies:
            copy.wait()
        total = refs.clip_yc[0, 0] + refs.clip_yc[0, 1] + refs.clip_yc[1, 0] + refs.clip_yc[1, 1]
        total = jnp.concatenate([total, jnp.zeros((8, LANES), F32)], axis=0)
        cond = jnp.zeros((8, SHARE), F32)
        lows = []
        for block in range(6):
            lows.append(total[block * CLIP_ROWS : block * CLIP_ROWS + 8].astype(BF16))
            lanes = slice(block * LANES, (block + 1) * LANES)
            cond = cond + dot_rows(lows[-1], refs.ada[:, lanes])
        clips = refs.condition.shape[0]
        refs.cond_own[...] = jnp.zeros_like(refs.cond_own)
        for row in range(2 * clips):
            clip, side = divmod(row, 2)
            refs.cond_own[row : row + 1, :] = cond[
                clip : clip + 1, side * LANES : (side + 1) * LANES
            ]
        refs.cond_all[z, x, y, c] = refs.cond_own[...]
        copies = [
            small(refs.cond_own, refs.cond_all.at[z, x, y, c], place.shifted(*change))
            for change in EVERYONE
        ]
        for block, low in enumerate(lows):
            lanes = slice(block * LANES, (block + 1) * LANES)
            refs.grad_ada[:, lanes] = dot_tokens(act_rows(refs, place), low)
            refs.grad_bias[block : block + 1, :] = jnp.sum(
                low[:CLIP_ROWS].astype(F32), axis=0, keepdims=True
            )
        run(23)
        for copy in table:
            copy.wait()
        total = refs.table_yc[0, 0] + refs.table_yc[0, 1] + refs.table_yc[1, 0] + refs.table_yc[1, 1]
        for head in range(2):
            for frame in range(FRAMES):
                first = (FRAMES - 1 - frame) * OFFSETS
                row = head * (WIDE // WSIDE) + frame
                refs.table_total[head : head + 1, first : first + OFFSETS] = total[
                    row : row + 1, :OFFSETS
                ]
        run(100)
        for copy in copies:
            copy.wait()
        for block in range(4):
            total = refs.cond_all[0, 0, block // 2, block % 2]
            for other in range(1, 8):
                total = total + refs.cond_all[other // 2, other % 2, block // 2, block % 2]
            for row in range(2 * clips):
                clip, side = divmod(row, 2)
                first = block * SHARE + side * LANES
                value = refs.condition[clip : clip + 1, first : first + LANES]
                gate = 1.0 / (1.0 + jnp.exp(-value))
                refs.grad_condition[clip : clip + 1, first : first + LANES] = (
                    total[row : row + 1] * gate * (1.0 + value * (1.0 - gate))
                )
        work.sent()


def enter_plain(tokens, held, mod):
    rows = tokens.shape[0]
    inputs = {"tokens": (tokens, vmem()), "held": (held, anywhere()), "mod": (mod, vmem())}
    outputs = {
        "normed": (shape(BF16, rows, D), vmem()),
        "packed": (shape(BF16, 3, rows, D), vmem()),
    }
    scratch = {
        "units": pltpu.VMEM((1, *SPLIT), BF16),
        "fetches": pltpu.SemaphoreType.DMA((1,)),
    }
    return call(enter_plain_kernel, "enter_plain", inputs, outputs, scratch)


def whole(array):
    return pl.BlockSpec(
        array.shape, lambda p: (0,) * len(array.shape), pipeline_mode=pl.Buffered(1)
    )


def result(dtype, *sizes):
    made = shape(dtype, *sizes)
    return made, whole(made)


def attend_probs(windows, first):
    def pair(step):
        return forward_pair(jnp.clip(step - first, 0, H // 2 - 1))

    return (
        shape(BF16, windows, H, WIN, WIN),
        pl.BlockSpec((windows, 2, WIN, WIN), lambda p: (0, pair(p), 0, 0)),
    )


def attend_scratch():
    return {"strip": pltpu.VMEM((2, CELLS, STRIP), F32), "bias": pltpu.VMEM((2, WIN, WIN), F32)}


def middle_outputs(rows):
    return {
        "output": (shape(BF16, rows, D), anywhere()),
        "grad_middle": (shape(F32, rows, D), anywhere()),
        "grad_mixed": (shape(BF16, rows, D), anywhere()),
        "sums": result(F32, rows // WIN, 8, D),
        "part": (shape(BF16, UNITS, *SPLIT), anywhere()),
    }


def middle_scratch(rows):
    return {
        "units": pltpu.VMEM((4, *SPLIT), BF16),
        "attended": pltpu.VMEM((rows, D), F32),
        "normed": pltpu.VMEM((rows, D), BF16),
        "result_sem": pltpu.SemaphoreType.DMA((3,)),
        "mlp": pltpu.VMEM((rows, D), F32),
        "grad_normed": pltpu.VMEM((rows, D), F32),
        "packed": pltpu.VMEM((3, rows, D), BF16),
        "made": pltpu.VMEM((2, *SPLIT), BF16),
        "fetches": pltpu.SemaphoreType.DMA((4,)),
        "made_sem": pltpu.SemaphoreType.DMA((2,)),
    }


def middle_plain(live_frames, tokens, cotangent, mixed, mod, held):
    rows = tokens.shape[0]
    inputs = {
        name: (array, whole(array))
        for name, array in (
            ("tokens", tokens),
            ("cotangent", cotangent),
            ("mixed", mixed),
            ("mod", mod),
        )
    }
    inputs |= {"live": (live_frames, smem()), "held": (held, anywhere())}
    return call(
        middle, "middle", inputs, middle_outputs(rows), middle_scratch(rows), grid=(1,), limit=60
    )


def begin(tokens, cotangent, own, smalls):
    rows = tokens.shape[0]
    windows = rows // WIN
    inputs = {"tokens": (tokens, whole(tokens)), "cotangent": (cotangent, whole(cotangent))}
    for name, block in zip(("qkv", "out", "up", "down"), own, strict=True):
        inputs[name] = (block, whole(block))
    for name, array in zip(("condition", "ada", "bias_in", "rel_table"), smalls[1:], strict=True):
        inputs[name] = (array, whole(array))
    inputs["frames"] = (smalls[0], smem())
    outputs = middle_outputs(rows) | {
        "probs": attend_probs(windows, 1),
        "side_out": result(BF16, *Reduce.side_shape(len(EARLY) - len(DONE))),
        "total": result(F32, len(DONE), SHARE, LANES),
        "normed_out": (shape(BF16, rows, D), anywhere()),
        "packed_out": (shape(BF16, 3, rows, D), anywhere()),
        "held": (shape(BF16, UNITS, *SPLIT), anywhere()),
        "mod": result(F32, windows, 8, D),
        "member": result(F32, windows, CLIP_ROWS, LANES),
        "live": (shape(jnp.int32, windows), smem()),
    }
    stages = gather_stages(ENTER + tuple(ATTEND.values()) + tuple(MIDDLE.values()))
    scratch = attend_scratch() | middle_scratch(rows)
    scratch |= {
        "mixed": pltpu.VMEM((rows, D), BF16),
        "core": pltpu.VMEM(Reduce.core_shape(len(EARLY)), BF16),
        "side": pltpu.VMEM(Reduce.side_shape(len(EARLY)), BF16),
        "corner": pltpu.VMEM(Reduce.corner_shape(len(DONE)), BF16),
        "distant": pltpu.VMEM(Reduce.distant_shape(len(DONE)), BF16),
        "aside": pltpu.VMEM(Reduce.aside_shape(1), BF16),
        "reduce": Reduce.scratch(EARLY_POINTS),
        "packed_sem": pltpu.SemaphoreType.DMA((4,)),
        "own": pltpu.VMEM((UNITS, SHARE, LANES), BF16),
        "own_sem": pltpu.SemaphoreType.DMA((UNITS,)),
        "gather": Gather.semaphores(stages),
        "small": [pltpu.SemaphoreType.DMA((18,))] * 2,
        "mod_part": pltpu.VMEM((MOD_ROWS, LANES), F32),
        "mod_parts": pltpu.VMEM((2, 2, MOD_ROWS, LANES), F32),
        "mods": pltpu.VMEM((4, 2, MOD_ROWS, LANES), F32),
        "rows": pltpu.VMEM((24, TILE), F32),
        "spread": pltpu.VMEM((2 * SPREAD, LANES), F32),
        "table_own": pltpu.VMEM((2, SPREAD, LANES), BF16),
        "table": pltpu.VMEM((4, 2, 2, SPREAD, LANES), BF16),
    }
    return call(
        start_kernel,
        "start",
        inputs,
        outputs,
        scratch,
        collective=0,
        grid=(H // 2 + 2,),
        limit=52,
    )


def deliver_kernel(refs):
    names = [name for name in vars(refs) if name.startswith("from_")]
    loads, stores = [], []
    for index, name in enumerate(names):
        plain = name[len("from_") :]
        held = getattr(refs, "held_" + plain)
        loads.append(pltpu.make_async_copy(getattr(refs, name), held, refs.sems.at[0, index]))
        stores.append(pltpu.make_async_copy(held, getattr(refs, plain), refs.sems.at[1, index]))
        loads[-1].start()
    for load, store in zip(loads, stores, strict=True):
        load.wait()
        store.start()
    for store in stores:
        store.wait()


def deliver(**arrays):
    inputs = {"from_" + name: (array, anywhere()) for name, array in arrays.items()}
    outputs = {name: (shape(array.dtype, *array.shape), anywhere()) for name, array in arrays.items()}
    scratch = {"held_" + name: pltpu.VMEM(array.shape, array.dtype) for name, array in arrays.items()}
    scratch["sems"] = pltpu.SemaphoreType.DMA((2, len(arrays)))
    return call(deliver_kernel, "deliver", inputs, outputs, scratch)


def attend_plain(packed, table, live_frames):
    windows = live_frames.shape[0]
    rows = windows * WIN
    inputs = {
        "live": (live_frames, smem()),
        "query": (packed, packed_block(0, rows, forward_pair)),
        "key": (packed, packed_block(1, rows, forward_pair)),
        "value": (packed, packed_block(2, rows, forward_pair)),
        "table": (table, pl.BlockSpec((2, SPREAD, LANES), lambda p: (forward_pair(p), 0, 0))),
    }
    return call(
        attend_plain_kernel,
        "attend_plain",
        inputs,
        {
            "mixed": (
                shape(BF16, rows, D),
                pl.BlockSpec((rows, LANES), lambda p: (0, forward_pair(p))),
            ),
            "probs": attend_probs(windows, 0),
        },
        attend_scratch(),
        grid=(H // 2,),
    )


def back(
    special, live_frames, tokens, mod, packed, normed, probs, mid, held, ada, member, condition
):
    window_count = probs.shape[0]
    rows = window_count * WIN
    pairs = H // 2

    def last(step):
        return backward_pair(jnp.minimum(step, pairs - 1))

    def packed_pair(which):
        return packed_block(which, rows, last)

    inputs = {
        "live": (live_frames, smem()),
        "query": (packed, packed_pair(0)),
        "key": (packed, packed_pair(1)),
        "value": (packed, packed_pair(2)),
        "probs": (
            probs,
            pl.BlockSpec((window_count, 2, WIN, WIN), lambda p: (0, last(p), 0, 0)),
        ),
        "grad": (mid.grad_mixed, pl.BlockSpec((rows, LANES), lambda p: (0, last(p)))),
        "held": (held, anywhere()),
    }
    for name, array in (
        ("tokens", tokens),
        ("mod", mod),
        ("normed", normed),
        ("grad_middle", mid.grad_middle),
    ):
        inputs[name] = (array, whole(array))

    outputs = {"grad_tokens": result(F32, rows, D)}
    scratch = {
        "strip": pltpu.VMEM((2, CELLS, STRIP), F32),
        "grad_packed": pltpu.VMEM((3, rows, D), BF16),
        "unit": pltpu.VMEM(SPLIT, BF16),
        "grad_normed": pltpu.VMEM((rows, D), F32),
        "fetch": pltpu.SemaphoreType.DMA,
    }
    if not special:
        outputs["sums"] = result(F32, window_count, 8, D)
        outputs["part"] = (shape(BF16, 3, *SPLIT), anywhere())
        outputs["spread"] = (
            shape(F32, H, SPREAD, LANES),
            pl.BlockSpec((2, SPREAD, LANES), lambda p: (last(p), 0, 0)),
        )
        scratch["made"] = pltpu.VMEM(SPLIT, BF16)
        scratch["made_sem"] = pltpu.SemaphoreType.DMA
        return call(
            back_plain_kernel, "back_plain", inputs, outputs, scratch, grid=(pairs + 1,)
        )
    inputs |= {
        "late_sums": (mid.sums, whole(mid.sums)),
        "ada": (ada, whole(ada)),
        "condition": (condition, whole(condition)),
        "member": (member, whole(member)),
        "side_in": (mid.side_out, whole(mid.side_out)),
        "done": (mid.total, whole(mid.total)),
        "part": (mid.part, anywhere()),
    }
    outputs |= {
        "grad_qkv": result(F32, SHARE, 3 * LANES),
        "grad_out": result(F32, SHARE, LANES),
        "grad_up": result(F32, SHARE, 4 * LANES),
        "grad_down": result(F32, 4 * SHARE, LANES),
        "grad_ada": result(F32, SHARE, 6 * LANES),
        "grad_bias": result(F32, 6, LANES),
        "grad_condition": result(F32, *condition.shape),
        "table_total": result(F32, 2, REL),
    }
    count, late = len(EARLY + LATE), len(LATE)
    scratch |= {
        "spread": pltpu.VMEM((2, WIDE, LANES), F32),
        "spreads": pltpu.VMEM((H * WIDE, LANES), F32),
        "made": pltpu.VMEM((3, *SPLIT), BF16),
        "sums": pltpu.VMEM((window_count, 8, D), F32),
        "core": pltpu.VMEM(Reduce.core_shape(late), BF16),
        "side": pltpu.VMEM(Reduce.side_shape(late), BF16),
        "corner": pltpu.VMEM(Reduce.corner_shape(count), BF16),
        "distant": pltpu.VMEM(Reduce.distant_shape(count), BF16),
        "aside": pltpu.VMEM(Reduce.aside_shape(1), BF16),
        "reduce": Reduce.scratch(LATE_POINTS),
        "table": pltpu.VMEM((4, 2, 2 * WIDE // WSIDE, TILE), F32),
        "table_zx": pltpu.VMEM((4, 2, 2 * WIDE // WSIDE, TILE), F32),
        "table_own": pltpu.VMEM((2 * WIDE // WSIDE, TILE), F32),
        "table_yc": pltpu.VMEM((2, 2, 2 * WIDE // WSIDE, TILE), F32),
        "clip": pltpu.VMEM((4, 2, MOD_ROWS, LANES), F32),
        "clip_zx": pltpu.VMEM((4, 2, MOD_ROWS, LANES), F32),
        "clip_own": pltpu.VMEM((MOD_ROWS, LANES), F32),
        "clip_yc": pltpu.VMEM((2, 2, MOD_ROWS, LANES), F32),
        "cond_own": pltpu.VMEM((8, LANES), F32),
        "cond_all": pltpu.VMEM((4, 2, 2, 2, 8, LANES), F32),
        "small": [pltpu.SemaphoreType.DMA((51,))] * 2,
    }
    return call(
        back_kernel,
        "back",
        inputs,
        outputs,
        scratch,
        collective=3,
        grid=(pairs + 1,),
        limit=52,
    )


def per_device(
    special,
    tokens,
    condition,
    clip_frames,
    ada_weight,
    ada_bias,
    qkv_weight,
    out_weight,
    up_weight,
    down_weight,
    rel_table,
    cotangent,
):
    window_count = tokens.shape[0]
    clip_count = condition.shape[0]
    rows_ada, cols_ada = ada_weight.shape
    token_rows = tokens.reshape(window_count * WIN, D)
    cotangent_rows = cotangent.reshape(window_count * WIN, D)
    own = (qkv_weight, out_weight, up_weight, down_weight)
    if special:
        smalls = (clip_frames, condition, ada_weight, ada_bias.reshape(1, cols_ada), rel_table)
        start = across = mid = begin(token_rows, cotangent_rows, own, smalls)
        live_frames, member_wide, mod = start.live, start.member, start.mod
        packed, held, normed = start.packed_out, start.held, start.normed_out
    else:
        row_block = lax.axis_index("fsdp")
        col_block = lax.axis_index("dp")
        first_window = lax.axis_index(("dp", "fsdp")) * window_count
        live_frames, member_int = window_layout(clip_frames, first_window, window_count)
        member = member_int.astype(F32)
        activity_low = jax.nn.silu(condition).astype(BF16)
        rows_own = lax.dynamic_slice_in_dim(activity_low, row_block * rows_ada, rows_ada, 1)
        mod_part = jnp.dot(rows_own, ada_weight, preferred_element_type=F32)
        clip_mod = lax.all_gather(lax.psum(mod_part, "fsdp"), "dp", axis=1, tiled=True)
        bias = lax.all_gather(ada_bias, "dp", axis=0, tiled=True)
        clip_mod = clip_mod + bias.astype(F32)[None, :]
        member_wide = None
        window_mod = jnp.sum(member[:, :, None] * clip_mod[None], axis=1)
        window_mod = jnp.pad(window_mod.reshape(window_count, 6, D), ((0, 0), (0, 2), (0, 0)))
        whole = [
            lax.all_gather(
                lax.all_gather(weight, "dp", axis=1, tiled=True), "fsdp", axis=0, tiled=True
            )
            for weight in own
        ]
        held = units_of(*whole).reshape(UNITS, *SPLIT)
        mod = window_mod
        start = enter_plain(token_rows, held, mod)
        packed, normed = start.packed, start.normed
        table = spread_table(lax.all_gather(rel_table, "dp", axis=0, tiled=True))
        across = attend_plain(packed, table, live_frames)
        mid = middle_plain(live_frames, token_rows, cotangent_rows, across.mixed, mod, held)
    end = back(
        special,
        live_frames,
        token_rows,
        mod,
        packed,
        normed,
        across.probs,
        mid,
        held,
        ada_weight,
        member_wide,
        condition,
    )
    if special:
        end = deliver(
            output=mid.output,
            grad_tokens=end.grad_tokens,
            grad_condition=end.grad_condition,
            grad_ada=end.grad_ada,
            grad_bias=end.grad_bias,
            grad_qkv=end.grad_qkv,
            grad_out=end.grad_out,
            grad_up=end.grad_up,
            grad_down=end.grad_down,
            table=end.table_total,
        )
        return (
            end.output.reshape(tokens.shape),
            end.grad_tokens.reshape(tokens.shape),
            end.grad_condition,
            end.grad_ada,
            end.grad_bias.reshape(cols_ada),
            end.grad_qkv,
            end.grad_out,
            end.grad_up,
            end.grad_down,
            end.table,
        )
    part = jnp.concatenate([end.part, mid.part[OUT:]])
    grads = [
        lax.psum_scatter(
            lax.psum_scatter(grad, "fsdp", scatter_dimension=0, tiled=True),
            "dp",
            scatter_dimension=1,
            tiled=True,
        ).astype(F32)
        for grad in weights_of(part.reshape(UNITS, 8, D, LANES))
    ]
    grad_mod = (mid.sums + end.sums)[:, :6].reshape(window_count, 6 * D)
    clip_part = lax.dot_general(
        member,
        grad_mod,
        (((0,), (0,)), ((), ())),
        precision=HIGHEST,
        preferred_element_type=F32,
    )
    clip_sum, table_sum = lax.psum((clip_part, gather_table(end.spread)), ("dp", "fsdp"))
    clip_cols = lax.dynamic_slice_in_dim(
        clip_sum.astype(BF16), col_block * cols_ada, cols_ada, 1
    )
    heads_own = rel_table.shape[0]
    table_grad = lax.dynamic_slice_in_dim(table_sum, col_block * heads_own, heads_own, 0)
    cond_part = lax.dot_general(
        clip_cols, ada_weight, (((1,), (1,)), ((), ())), preferred_element_type=F32
    )
    cond_total = lax.all_gather(lax.psum(cond_part, "dp"), "fsdp", axis=1, tiled=True)
    grad_ada_weight = lax.dot_general(
        rows_own, clip_cols, (((0,), (0,)), ((), ())), preferred_element_type=F32
    )
    grad_ada_bias = jnp.sum(clip_cols.astype(F32), axis=0)
    _, silu_back = jax.vjp(jax.nn.silu, condition)
    return (
        mid.output.reshape(tokens.shape),
        end.grad_tokens.reshape(tokens.shape),
        silu_back(cond_total)[0],
        grad_ada_weight,
        grad_ada_bias,
        *grads,
        table_grad,
    )


def solution(mesh):
    special = dict(mesh.shape) == {"dp": 8, "fsdp": 4}
    both = P(("dp", "fsdp"), None, None)
    weight = P("fsdp", "dp")
    in_specs = (both, P(), P(), weight, P("dp")) + (weight,) * 4 + (P("dp", None), both)
    out_specs = (both, both, P(), weight, P("dp")) + (weight,) * 4 + (P("dp", None),)
    return jax.shard_map(
        functools.partial(per_device, special),
        mesh=mesh,
        in_specs=in_specs,
        out_specs=out_specs,
        check_vma=False,
    )
```

```python
import functools

import jax
import jax.numpy as jnp
from jax import lax
from jax.experimental import pallas as pl
from jax.experimental.pallas import tpu as pltpu
from jax.sharding import PartitionSpec as P

D = 1024
H = 16
HD = 64
WT = 5
WSIDE = 8
WIN = 320
SPW = 16
CELLS = WSIDE * WSIDE
FRAMES = 2 * WT - 1
OFFSETS = (2 * WSIDE - 1) ** 2
REL = FRAMES * OFFSETS
LANES = 128
TILE = 256
SPREAD = 80
WIDE = 96
STRIP = 640

EPSILON = 1e-06
NEGATIVE = -1000000000.0
HIGHEST = lax.Precision.HIGHEST
F32 = jnp.float32
BF16 = jnp.bfloat16
MESH = pl.DeviceIdType.MESH
MIB = 2**20

QKV, OUT, UP, DOWN, UNITS = 0, 3, 4, 8, 12
PICK = (
    (1, 2, 0),
    (1, 2, 0),
    (0, 1, 2),
    (0, 1, 2),
    (0, 1, 2),
    (2, 0, 1),
    (2, 0, 1),
    (1, 0, 2),
)
SHARE = 256
HALF = 128


SPLIT = (4, 2, 2, 2, SHARE, LANES)
CLIP_ROWS = 4
MOD_ROWS = 6 * CLIP_ROWS
OWN_SLOTS = 4
ORDER = (0, 1, 2, 3, 4, 8, 5, 9, 6, 10, 7, 11)
GATHER_ASIDE = (DOWN + 3,)
REDUCE_ASIDE = (DOWN, UP + 2)
ENTER = (((2, 1), (0, 1), (11, 1), (11, 2), (2, 2), (1, 1)), ((2, 3), (0, 2), (6, 1), (1, 2)), ((0, 3),), ((1, 3), (5, 1), (3, 1), (6, 2)), ((2, 4), (0, 4), (4, 1), (5, 2)), ((8, 1), (6, 3)))
ATTEND = {0: ((3, 2), (7, 1), (5, 3)), 1: ((1, 4),), 2: ((4, 2), (10, 1)), 3: ((3, 3), (9, 1)), 4: ((4, 3),), 5: ((5, 4),), 6: ((3, 4), (7, 2), (8, 2)), 7: ((4, 4),)}
MIDDLE = {0: ((8, 3), (7, 3), (6, 4)), 2: ((11, 3),), 3: ((10, 2), (9, 2)), 4: ((7, 4), (8, 4)), 5: ((10, 3),), 6: ((9, 3),), 8: ((10, 4),), 9: ((9, 4),), 11: ((11, 4),)}
EARLY = (DOWN, UP, DOWN + 1, UP + 1, DOWN + 2)
DONE = EARLY[:4]
EARLY_POINTS = {7: ((4, 0), (8, 0)), 8: ((4, 1),), 9: ((8, 1),), 10: ((9, 0), (4, 2)), 11: ((9, 1), (5, 0)), 12: ((4, 3),), 13: ((5, 1),), 14: ((10, 0), (9, 2)), 16: ((5, 2),), 17: ((8, 2), (9, 3), (10, 1)), 18: ((8, 3), (5, 3)), 19: ((8, 4), (4, 4)), 20: ((5, 4),), 21: ((10, 2), (9, 4))}
LATE = (UP + 2, DOWN + 3, UP + 3, OUT, QKV, QKV + 1, QKV + 2)
LATE_POINTS = {0: ((6, 0), (10, -3), (11, 0)), 1: ((6, 1), (11, 1)), 2: ((7, 0),), 3: ((3, 0), (7, 1), (11, 2)), 4: ((0, 0), (3, 1), (10, 3)), 6: ((7, 2), (1, 0), (0, 1)), 7: ((11, 3), (3, 2)), 8: ((6, 2), (10, 4), (11, 4)), 10: ((1, 1),), 11: ((7, 3), (3, 3)), 12: ((0, 2),), 13: ((2, 0),), 14: ((2, 1),), 15: ((1, 2),), 16: ((0, 3),), 18: ((1, 3), (6, 3), (2, 2)), 19: ((6, 4), (2, 3)), 20: ((1, 4),), 21: ((3, 4),), 22: ((7, 4),), 24: ((0, 4), (2, 4))}
def reduce_stages(points):
    moves = [move for at in sorted(points) for move in points[at]]
    started = [(unit, 3 if stage == -3 else stage + 1) for unit, stage in moves if stage < 4]
    return [(unit, stage) for unit, stage in started if stage > 3 or (unit, stage) in moves or stage < 3]


def gather_stages(points):
    return [(ORDER[index], stage) for point in points for index, stage in point]


def forward_pair(step):
    first = (13 - step) // 8
    return first * ((step // 2 + 1) % 3 + 3 * (step % 2)) + (1 - first) * step


def backward_pair(step):
    group, place = step // 3, step % 3
    return (1 + group) % 3 + 3 * place - place // 2


def pair_unit(which, pair):
    first = (13 - pair) // 8
    sixth, seventh = ((0, 2, 0), (1, 1, 2))[0][which], ((0, 2, 0), (1, 1, 2))[1][which]
    return first * ((pair + 2) % 3) + (1 - first) * ((7 - pair) * sixth + (pair - 6) * seventh)


def pair_block(which, pair):
    return (which * (H // 2) + pair) // 3


def picked(block, j):
    return sum(jnp.where(block == index, PICK[index][j], 0) for index in range(8))


def window_layout(clip_frames, first_window, window_count):
    slab_count = 1 + (clip_frames > WT).astype(jnp.int32)
    starts = jnp.cumsum(slab_count, dtype=jnp.int32) - slab_count
    global_window = first_window + jnp.arange(window_count, dtype=jnp.int32)
    slab_of = global_window // SPW
    owners = jnp.sum((starts[None, :] <= slab_of[:, None]).astype(jnp.int32), axis=1) - 1
    clip_ids = jnp.arange(clip_frames.shape[0], dtype=jnp.int32)
    member = (owners[:, None] == clip_ids[None, :]).astype(jnp.int32)
    clip_start = jnp.sum(member * starts[None, :], axis=1)
    own_frames = jnp.sum(member * clip_frames[None, :], axis=1)
    inner_slab = slab_of - clip_start
    return (jnp.minimum(own_frames - WT * inner_slab, WT), member)


def offset_spread():
    side_span = 2 * WSIDE - 1
    shape = (OFFSETS, WSIDE * LANES)
    offset = lax.broadcasted_iota(jnp.int32, shape, 0)
    place = lax.broadcasted_iota(jnp.int32, shape, 1)
    own, row, other = place // LANES, place // WSIDE % (LANES // WSIDE), place % WSIDE
    row_diff, col_diff = side_span - 1 - row, own - other + (WSIDE - 1)
    return ((row < side_span) & (row_diff * side_span + col_diff == offset)).astype(BF16)


def spread_table(table):
    heads = table.shape[0]
    by_frame = table.reshape(heads, FRAMES, OFFSETS)[:, ::-1].reshape(heads * FRAMES, OFFSETS)
    spread = jnp.dot(by_frame, offset_spread(), preferred_element_type=F32).astype(BF16)
    spread = spread.reshape(heads, FRAMES * WSIDE, LANES)
    return jnp.pad(spread, ((0, 0), (0, SPREAD - FRAMES * WSIDE), (0, 0)))


def gather_table(spread):
    heads = spread.shape[0]
    by_frame = spread[:, : FRAMES * WSIDE].reshape(heads * FRAMES, WSIDE * LANES)
    sums = lax.dot_general(
        by_frame,
        offset_spread().astype(F32),
        (((1,), (1,)), ((), ())),
        precision=HIGHEST,
        preferred_element_type=F32,
    )
    return sums.reshape(heads, FRAMES, OFFSETS)[:, ::-1].reshape(heads, FRAMES * OFFSETS)


def units_of(qkv, out, up, down):
    return jnp.concatenate(
        [
            jnp.stack(
                [
                    jnp.stack([qkv[:, 384 * b + LANES * PICK[b][j] :][:, :LANES] for b in range(8)])
                    for j in range(3)
                ]
            ),
            out.reshape(D, 8, 1, LANES).transpose(2, 1, 0, 3),
            up.reshape(D, 8, 4, LANES).transpose(2, 1, 0, 3),
            down.reshape(8, 4, LANES, 8, LANES).transpose(1, 3, 0, 2, 4).reshape(4, 8, D, LANES),
        ]
    )


def weights_of(units):
    def columns(part):
        return part.transpose(2, 1, 0, 3).reshape(D, -1)

    down = units[DOWN:].reshape(4, 8, 8, LANES, LANES).transpose(2, 0, 3, 1, 4)
    qkv = [
        units[PICK[block].index(tile), block] for block in range(8) for tile in range(3)
    ]
    return (
        jnp.concatenate(qkv, axis=1),
        columns(units[OUT:UP]),
        columns(units[UP:DOWN]),
        down.reshape(4 * D, D),
    )


def dot(left, right):
    return jnp.dot(left, right, preferred_element_type=F32)


def dot_rows(left, right):
    return lax.dot_general(left, right, (((1,), (1,)), ((), ())), preferred_element_type=F32)


def dot_tokens(left, right):
    return lax.dot_general(left, right, (((0,), (0,)), ((), ())), preferred_element_type=F32)


def half(index):
    return pl.ds(pl.multiple_of(index * 512, 512), 512)


def four_columns(unit, index):
    blocks = [unit[2 * index + x // 2, x % 2].reshape(D, LANES) for x in range(4)]
    return jnp.concatenate(blocks, axis=1)


def half_rows(unit, index):
    blocks = [unit[block // 2, block % 2, index].reshape(512, LANES) for block in range(8)]
    return jnp.concatenate(blocks, axis=1)


def put_columns(unit, index, values):
    for x in range(4):
        unit[2 * index + x // 2, x % 2] = values[:, x * LANES : (x + 1) * LANES].reshape(2, 2, SHARE, LANES)


def loop(count, body):
    def step(index, carry):
        body(index)
        return carry

    lax.fori_loop(0, count, step, 0)


def vmem():
    return pl.BlockSpec(memory_space=pltpu.VMEM)


def anywhere():
    return pl.BlockSpec(memory_space=pl.ANY)


def smem():
    return pl.BlockSpec(memory_space=pltpu.SMEM)


def shape(dtype, *sizes):
    return jax.ShapeDtypeStruct(sizes, dtype)


def params(collective=None, limit=58):
    if collective is None:
        return pltpu.CompilerParams(vmem_limit_bytes=limit * MIB)
    return pltpu.CompilerParams(
        vmem_limit_bytes=limit * MIB, collective_id=collective, has_side_effects=True
    )


def centered(values):
    center = values - jnp.mean(values, axis=-1, keepdims=True)
    spread = jnp.mean(center * center, axis=-1, keepdims=True)
    root = lax.rsqrt(spread + EPSILON)
    return center * root, root


def norm_back(grad_normed, normal, root, scale):
    grad = grad_normed * (1.0 + scale)
    mean = jnp.mean(grad, axis=-1, keepdims=True)
    along = jnp.mean(grad * normal, axis=-1, keepdims=True)
    return root * (grad - mean - normal * along)


def each_rows(mod_ref, live_ref, body, rows=32, pump=lambda window: None):
    for window in range(mod_ref.shape[0]):
        live = live_ref[window] * CELLS

        def step(index, window=window, live=live):
            at = pl.ds(pl.multiple_of(window * WIN + index * rows, rows), rows)
            mods = [mod_ref[window, k : k + 1, :] for k in range(6)]
            slot = index * rows + lax.broadcasted_iota(jnp.int32, (rows, 1), 0)
            body(window, at, mods, slot < live)

        loop(WIN // rows, step)
        pump(window)


def add_sums(sums_ref, window, which, values):
    sums_ref[window, which : which + 1, :] += jnp.sum(values, axis=0, keepdims=True)


class Place:
    def __init__(self):
        column, row = lax.axis_index("dp"), lax.axis_index("fsdp")
        self.z, self.x, self.y, self.c = column // 2, column % 2, row // 2, row % 2

    def at(self, z=None, x=None, y=None, c=None):
        z = self.z if z is None else z
        x = self.x if x is None else x
        y = self.y if y is None else y
        c = self.c if c is None else c
        return (z * 2 + x, y * 2 + c)

    def far(self, k):
        return lax.rem(self.z + k, 4)

    def shifted(self, dz, dx, dy, dc):
        def other(index, change):
            return 1 - index if change else index

        return self.at(self.far(dz), other(self.x, dx), other(self.y, dy), other(self.c, dc))

    def greet(self, far_ones=()):
        near = [(1, 0, 0, 0), (2, 0, 0, 0), (3, 0, 0, 0), (0, 1, 0, 0), (0, 0, 1, 0), (0, 0, 0, 1)]
        peers = near + [change for change in far_ones if change not in near]
        barrier = pltpu.get_barrier_semaphore()
        for change in peers:
            pl.semaphore_signal(
                barrier, inc=1, device_id=self.shifted(*change), device_id_type=MESH
            )
        pl.semaphore_wait(barrier, len(peers))


EVERYONE = [
    (dz, dx, dy, dc)
    for dz in range(4)
    for dx in range(2)
    for dy in range(2)
    for dc in range(2)
    if (dz, dx, dy, dc) != (0, 0, 0, 0)
]
ALONG_ZX = [change for change in EVERYONE if change[2:] == (0, 0)]
ALONG_YC = [change for change in EVERYONE if change[:2] == (0, 0)]


class Moves:
    def __init__(self, place, stages, scratch):
        self.place = place
        self.send, self.recv = scratch
        self.first, count = {}, 0
        for unit, stage in stages:
            self.first[unit, stage] = count
            count += self.counts[unit in self.aside][stage - 1]
        self.flying = []

    @classmethod
    def semaphores(cls, stages):
        count = sum(cls.counts[unit in cls.aside][stage - 1] for unit, stage in stages)
        return [pltpu.SemaphoreType.DMA((count,))] * 2

    def made(self, unit, stage, moves):
        copies = []
        for index, (source, target, device) in enumerate(moves):
            slot = self.first[unit, stage] + index
            copies.append(
                pltpu.make_async_remote_copy(
                    src_ref=source,
                    dst_ref=target,
                    send_sem=self.send.at[slot],
                    recv_sem=self.recv.at[slot],
                    device_id=device,
                    device_id_type=MESH,
                )
            )
        return copies

    def begin(self, unit, stage):
        for copy in self.copies(unit, stage):
            copy.start()
        self.flying.append((unit, stage))

    def arrive(self, unit, stage):
        if (unit, stage) in self.flying:
            self.flying.remove((unit, stage))
            for copy in self.copies(unit, stage):
                copy.wait_recv()

    def sent(self):
        for unit, stage in self.first:
            for copy in self.copies(unit, stage):
                copy.wait_send()


class Gather(Moves):
    counts = ((3, 2, 2, 1), (2, 2, 3, 1))
    aside = GATHER_ASIDE

    def __init__(self, place, held, stages, scratch):
        super().__init__(place, stages, scratch)
        self.held = held

    def copies(self, unit, stage):
        p, held = self.place, self.held.at[unit]
        at_x, at_y, at_core = p.at(x=1 - p.x), p.at(y=1 - p.y), p.at(c=1 - p.c)
        own = held.at[p.z, p.x, p.y, p.c]
        if stage == 4:
            refs = [(held.at[:, :, :, p.c], at_core)]
        elif unit in self.aside and stage == 1:
            refs = [(own.at[:HALF], at_x), (own.at[HALF:], at_y)]
        elif unit in self.aside and stage == 2:
            refs = [
                (held.at[p.z, :, p.y, p.c, :HALF], at_y),
                (held.at[p.z, p.x, :, p.c, HALF:], at_x),
            ]
        elif unit in self.aside:
            refs = [(held.at[p.z, :, :, p.c], p.at(z=p.far(k))) for k in (1, 2, 3)]
        elif stage == 1:
            refs = [(own, p.at(z=p.far(k))) for k in (1, 2, 3)]
        elif stage == 2:
            refs = [
                (held.at[:, p.x, p.y, p.c, :HALF], at_x),
                (held.at[:, p.x, p.y, p.c, HALF:], at_y),
            ]
        else:
            refs = [
                (held.at[:, :, p.y, p.c, :HALF], at_y),
                (held.at[:, p.x, :, p.c, HALF:], at_x),
            ]
        return self.made(unit, stage, [(ref, ref, device) for ref, device in refs])

    def advance(self, unit, stage):
        self.arrive(unit, stage - 1)
        self.begin(unit, stage)

    def finish(self):
        for unit, stage in list(self.flying):
            self.arrive(unit, stage)
        self.sent()


class Reduce(Moves):
    counts = ((1, 2, 2, 3), (1, 3, 2, 2))
    aside = REDUCE_ASIDE

    def __init__(self, place, part, points, store, buffers, scratch):
        super().__init__(place, reduce_stages(points), scratch[2:])
        self.part, self.store, self.buffers = part, store, buffers
        self.own, self.load = scratch[:2]
        self.slots, self.loaded = {}, []

    @classmethod
    def scratch(cls, points):
        return [
            pltpu.VMEM((OWN_SLOTS, 4, 2, 2, SHARE, LANES), BF16),
            pltpu.SemaphoreType.DMA((OWN_SLOTS,)),
        ] + cls.semaphores(reduce_stages(points))

    @staticmethod
    def core_shape(count):
        return (count, 4, 2, 2, SHARE, LANES)

    @staticmethod
    def side_shape(count):
        return (count, 2, 4, 2, HALF, LANES)

    @staticmethod
    def corner_shape(count):
        return (count, 2, 4, HALF, LANES)

    @staticmethod
    def distant_shape(count):
        return (count, 3, 2, HALF, LANES)

    @staticmethod
    def aside_shape(count):
        return (count, 3, 2, 2, SHARE, LANES)

    def own_copy(self, unit):
        slot = self.slots.setdefault(unit, len(self.slots) % OWN_SLOTS)
        return pltpu.make_async_copy(
            self.part(unit).at[:, :, :, self.place.c], self.own.at[slot], self.load.at[slot]
        )

    def copies(self, unit, stage):
        p = self.place
        at_x, at_y, at_core = p.at(x=1 - p.x), p.at(y=1 - p.y), p.at(c=1 - p.c)
        core, side, corner, distant = self.buffers(unit)
        if unit in self.aside and stage == 2:
            moves = [
                (core.at[p.far(k)], distant.at[k - 1], p.at(z=p.far(k))) for k in (1, 2, 3)
            ]
        elif unit in self.aside and stage == 3:
            moves = [
                (core.at[p.z, :, 1 - p.y, :HALF], side.at[0, 0], at_y),
                (core.at[p.z, 1 - p.x, :, HALF:], side.at[1, 0], at_x),
            ]
        elif unit in self.aside and stage == 4:
            moves = [
                (side.at[0, 0, 1 - p.x], side.at[0, 1, 0], at_x),
                (side.at[1, 0, 1 - p.y], side.at[1, 1, 0], at_y),
            ]
        elif stage == 1:
            moves = [(self.part(unit).at[:, :, :, 1 - p.c], core, at_core)]
        elif stage == 2:
            moves = [
                (core.at[:, :, 1 - p.y, :HALF], side.at[0], at_y),
                (core.at[:, 1 - p.x, :, HALF:], side.at[1], at_x),
            ]
        elif stage == 3:
            moves = [
                (side.at[0, :, 1 - p.x], corner.at[0], at_x),
                (side.at[1, :, 1 - p.y], corner.at[1], at_y),
            ]
        else:
            moves = [
                (corner.at[:, p.far(k)], distant.at[k - 1], p.at(z=p.far(k))) for k in (1, 2, 3)
            ]
        return self.made(unit, stage, moves)

    def begin(self, unit, stage):
        super().begin(unit, stage)
        if stage == 1:
            self.own_copy(unit).start()
            assert self.slots[unit] not in self.loaded
            self.loaded.append(self.slots[unit])

    def combine(self, unit, stage):
        p = self.place
        core, side, corner, distant = self.buffers(unit)

        def plus(left, right):
            return (left.astype(F32) + right.astype(F32)).astype(BF16)

        def from_core(step):
            z, x, y = step // 4, step // 2 % 2, step % 2
            core[z, x, y] = plus(core[z, x, y], self.own[self.slots[unit], z, x, y])

        def from_side(step):
            z, b = step // 2, step % 2
            side[0, z, b] = plus(side[0, z, b], core[z, b, p.y, :HALF])
            side[1, z, b] = plus(side[1, z, b], core[z, p.x, b, HALF:])

        def from_corner(z):
            corner[0, z] = plus(corner[0, z], side[0, z, p.x])
            corner[1, z] = plus(corner[1, z], side[1, z, p.y])

        def from_far(half):
            total = corner[half, p.z].astype(F32)
            for k in range(3):
                total = total + distant[k, half].astype(F32)
            self.store(unit, half, total)

        def aside_far(step):
            x, y = step // 2, step % 2
            total = core[p.z, x, y].astype(F32)
            for k in range(3):
                total = total + distant[k, x, y].astype(F32)
            core[p.z, x, y] = total.astype(BF16)

        def aside_side(b):
            side[0, 0, b] = plus(side[0, 0, b], core[p.z, b, p.y, :HALF])
            side[1, 0, b] = plus(side[1, 0, b], core[p.z, p.x, b, HALF:])

        if unit in self.aside and stage == 4:
            for part, own in enumerate((p.x, p.y)):
                total = side[part, 0, own].astype(F32) + side[part, 1, 0].astype(F32)
                self.store(unit, part, total)
            return
        steps = {1: (16, from_core), 2: (8, from_side), 3: (4, from_corner), 4: (2, from_far)}
        if unit in self.aside:
            steps |= {2: (4, aside_far), 3: (2, aside_side)}
        loop(*steps[stage])

    def step(self, unit, stage):
        if stage <= 0:
            self.begin(unit, max(1, -stage))
            return
        self.arrive(unit, stage)
        if stage == 1:
            self.own_copy(unit).wait()
        self.combine(unit, stage)
        if stage == 1:
            self.loaded.remove(self.slots[unit])
        if (unit, stage + 1) in self.first:
            self.begin(unit, stage + 1)


class Copies:
    def __init__(self, send, recv):
        self.send, self.recv, self.count = send, recv, 0

    def __call__(self, source, target, device):
        slot = self.count
        self.count += 1
        copy = pltpu.make_async_remote_copy(
            src_ref=source,
            dst_ref=target,
            send_sem=self.send.at[slot],
            recv_sem=self.recv.at[slot],
            device_id=device,
            device_id_type=MESH,
        )
        copy.start()
        return copy


class Refs:
    pass


def call(kernel, name, inputs, outputs, scratch, aliases=(), collective=None, grid=None, limit=58):
    names = list(inputs) + list(outputs)
    flat = []
    for value in scratch.values():
        flat += value if isinstance(value, list) else [value]

    def body(*refs):
        held = Refs()
        rest = list(refs)
        for key in names:
            setattr(held, key, rest.pop(0))
        for key, value in scratch.items():
            if isinstance(value, list):
                setattr(held, key, [rest.pop(0) for _ in value])
            else:
                setattr(held, key, rest.pop(0))
        kernel(held)

    extra = {} if grid is None else {"grid": grid}
    made = functools.partial(
        pl.pallas_call,
        body,
        in_specs=[spec for _, spec in inputs.values()],
        out_specs=[spec for _, spec in outputs.values()],
        out_shape=[out for out, _ in outputs.values()],
        scratch_shapes=flat,
        input_output_aliases={
            list(inputs).index(one): list(outputs).index(other) for one, other in aliases
        },
        compiler_params=params(collective, limit),
        name=name,
        **extra,
    )
    arrays = [array for array, _ in inputs.values()]
    if name == "start":
        result = made()(*arrays)
    else:
        result = made()(*arrays)
    out = Refs()
    for key, value in zip(outputs, result, strict=True):
        setattr(out, key, value)
    return out


def enter_norm(refs, pump=lambda: None):
    rows = 32
    for window in range(refs.mod.shape[0]):
        shift, scale = refs.mod[window, 0:1, :], refs.mod[window, 1:2, :]

        def step(index, window=window, shift=shift, scale=scale):
            at = pl.ds(pl.multiple_of(window * WIN + index * rows, rows), rows)
            normal, _ = centered(refs.tokens[at, :].astype(F32))
            refs.normed[at, :] = (normal * (1.0 + scale) + shift).astype(BF16)

        loop(WIN // rows, step)
        pump()


def enter_unit(refs, j, held, put=False):
    unit = refs.units.at[0]
    fetch = pltpu.make_async_copy(held, unit, refs.fetches.at[0])
    fetch.start()
    fetch.wait()

    def project(index):
        refs.packed[j, :, half(index)] = dot(refs.normed[...], four_columns(unit, index)).astype(
            BF16
        )

    loop(2, project)
    if put:
        packed_copy(refs, j).start()


def normed_copy(refs):
    return pltpu.make_async_copy(refs.normed, refs.normed_out, refs.packed_sem.at[3])


def packed_copy(refs, j):
    return pltpu.make_async_copy(refs.packed.at[j], refs.packed_out.at[j], refs.packed_sem.at[j])


def enter_plain_kernel(refs):
    enter_norm(refs)
    for j in range(3):
        enter_unit(refs, j, refs.held.at[QKV + j])


def act_rows(refs, place):
    first = (place.y * 2 + place.c) * SHARE
    value = refs.condition[:, pl.ds(pl.multiple_of(first, SHARE), SHARE)]
    act = value / (1.0 + jnp.exp(-value))
    return jnp.concatenate([act, jnp.zeros((8 - value.shape[0], SHARE), F32)], axis=0).astype(BF16)


def enter_layout(refs):
    windows, clips = refs.member.shape[0], refs.condition.shape[0]
    frames = [refs.frames[clip] for clip in range(clips)]
    starts = [0]
    for count in frames:
        starts.append(starts[-1] + 1 + jnp.where(count > WT, 1, 0))
    device = lax.axis_index("dp") * lax.axis_size("fsdp") + lax.axis_index("fsdp")
    refs.member[...] = jnp.zeros_like(refs.member)
    for window in range(windows):
        slab = (device * windows + window) // SPW
        live = 0
        for clip in range(clips):
            mine = starts[clip] <= slab
            if clip < clips - 1:
                mine = mine & (slab < starts[clip + 1])
            inner = frames[clip] - WT * (slab - starts[clip])
            live = live + jnp.where(mine, jnp.minimum(inner, WT), 0)
            refs.member[window, clip : clip + 1, :] = jnp.full(
                (1, LANES), jnp.where(mine, 1.0, 0.0), F32
            )
        refs.live[window] = live


def enter_table(refs):
    refs.rows[...] = jnp.zeros_like(refs.rows)
    table = refs.rel_table[...].astype(F32)
    for head in range(2):
        for frame in range(FRAMES):
            first = (FRAMES - 1 - frame) * OFFSETS
            row = head * (SPREAD // WSIDE) + frame
            refs.rows[row : row + 1, :OFFSETS] = table[head : head + 1, first : first + OFFSETS]
    shape_of = (TILE, WSIDE * LANES)
    offset = lax.broadcasted_iota(jnp.int32, shape_of, 0)
    place = lax.broadcasted_iota(jnp.int32, shape_of, 1)
    own, row, other = place // LANES, place // WSIDE % (LANES // WSIDE), place % WSIDE
    side_span = 2 * WSIDE - 1
    row_diff, col_diff = side_span - 1 - row, own - other + (WSIDE - 1)
    same = (row < side_span) & (row_diff * side_span + col_diff == offset)
    spread = dot(refs.rows[...].astype(BF16), jnp.where(same, 1.0, 0.0).astype(BF16))
    count = 2 * SPREAD // WSIDE
    for own in range(WSIDE):
        refs.spread[pl.ds(own, count, stride=WSIDE), :] = spread[
            :count, own * LANES : (own + 1) * LANES
        ]
    for head in range(2):
        refs.table_own[head] = refs.spread[head * SPREAD : (head + 1) * SPREAD, :].astype(BF16)


def enter(refs, place, work):
    place.greet(ALONG_ZX + ALONG_YC)
    z, x, y, c = place.z, place.x, place.y, place.c
    small = Copies(*refs.small)
    mods = dot(act_rows(refs, place), refs.ada[...])
    mods = mods + jnp.where((y == 0) & (c == 0), 1.0, 0.0) * refs.bias_in[...].astype(F32)
    for block in range(6):
        refs.mod_part[block * CLIP_ROWS : (block + 1) * CLIP_ROWS, :] = mods[
            :CLIP_ROWS, block * LANES : (block + 1) * LANES
        ]
    refs.mod_parts[y, c] = refs.mod_part[...]
    parts = [
        small(refs.mod_part, refs.mod_parts.at[y, c], place.shifted(*change)) for change in ALONG_YC
    ]
    own = []
    for unit in range(UNITS):
        if unit < OUT:
            first = picked(z * 2 + x, unit) * LANES
            refs.own[unit] = refs.qkv[:, pl.ds(pl.multiple_of(first, LANES), LANES)]
        elif unit >= DOWN:
            first = (unit - DOWN) * LANES
            for half in range(2):
                at = slice(half * 512 + first, half * 512 + first + LANES)
                refs.own[unit, half * HALF : (half + 1) * HALF] = refs.down[at, :]
        else:
            source, start = (refs.out, OUT) if unit < UP else (refs.up, UP)
            first = (unit - start) * LANES
            refs.own[unit] = source[:, first : first + LANES]
        own.append(
            pltpu.make_async_copy(
                refs.own.at[unit], refs.held.at[unit, z, x, y, c], refs.own_sem.at[unit]
            )
        )
        own[-1].start()
    points = list(ENTER)

    loaded = []

    def load(unit):
        if unit not in loaded:
            own[unit].wait()
            loaded.append(unit)

    def tick():
        for index, stage in points.pop(0):
            if stage == 1:
                load(ORDER[index])
            work.advance(ORDER[index], stage)

    tick()
    enter_layout(refs)
    enter_table(refs)
    refs.table[z, x, c] = refs.table_own[c]
    for copy in parts:
        copy.wait()
    refs.mods[z, x] = (
        refs.mod_parts[0, 0] + refs.mod_parts[0, 1] + refs.mod_parts[1, 0] + refs.mod_parts[1, 1]
    )
    mods = [
        small(refs.mods.at[z, x], refs.mods.at[z, x], place.shifted(*change))
        for change in ALONG_ZX
    ]
    for unit in range(UNITS):
        load(unit)
    tick()
    for copy in mods:
        copy.wait()
    tables = [
        small(refs.table.at[z, x, c], refs.table.at[z, x, c], place.shifted(*change))
        for change in ALONG_ZX
    ]
    for window in range(refs.mod.shape[0]):
        for block in range(48):
            which, column = divmod(block, 8)
            first = block % 6 * CLIP_ROWS
            part = refs.mods[block // 12, block // 6 % 2, first : first + CLIP_ROWS, :]
            refs.mod[window, which : which + 1, column * LANES : (column + 1) * LANES] = jnp.sum(
                part * refs.member[window], axis=0, keepdims=True
            )
    tick()
    enter_norm(refs, tick)
    normed_copy(refs).start()
    for copy in tables:
        copy.wait()
    last = small(refs.table.at[:, :, c], refs.table.at[:, :, c], place.at(c=1 - c))
    work.arrive(QKV, 4)
    tick()
    enter_unit(refs, 0, refs.held.at[QKV], put=True)
    last.wait()


def attend_pair(refs, table, part, put):
    for head in range(2):
        spread = table(head).astype(F32)
        for frame in range(FRAMES):
            block = spread[frame * WSIDE : (frame + 1) * WSIDE]
            for row in range(WSIDE):
                first = (WSIDE - 1 - row) * WSIDE
                refs.strip[
                    head, row * WSIDE : (row + 1) * WSIDE, frame * CELLS : (frame + 1) * CELLS
                ] = block[:, first : first + CELLS]
        for frame in range(WT):
            first = (WT - 1 - frame) * CELLS
            refs.bias[head, frame * CELLS : (frame + 1) * CELLS, :] = refs.strip[
                head, :, first : first + WIN
            ]
    for window in range(refs.live.shape[0]):
        rows = slice(window * WIN, (window + 1) * WIN)
        live = refs.live[window] * CELLS
        key_live = lax.broadcasted_iota(jnp.int32, (1, WIN), 1) < live
        query, key, value = (part(which, rows) for which in range(3))
        mixed = []
        for head in range(2):
            lanes = slice(head * HD, (head + 1) * HD)
            scores = dot_rows(query[:, lanes] * BF16(HD ** (-0.5)), key[:, lanes]) + refs.bias[head]
            scores = jnp.where(key_live, scores, NEGATIVE)
            shifted = jnp.exp(scores - jnp.max(scores, axis=-1, keepdims=True))
            totals = jnp.sum(shifted, axis=-1, keepdims=True)
            probs = (shifted * (1.0 / totals)).astype(BF16)
            refs.probs[window, head] = probs
            mixed.append(dot(probs, value[:, lanes]).astype(BF16))
        put(rows, jnp.concatenate(mixed, axis=1))


def attend_plain_kernel(refs):
    sources = (refs.query, refs.key, refs.value)

    def put(rows, values):
        refs.mixed[rows, :] = values

    attend_pair(
        refs, lambda head: refs.table[head], lambda which, rows: sources[which][rows, :], put
    )


def start_kernel(refs):
    step = pl.program_id(0)
    pairs = H // 2
    place = Place()
    work = Gather(place, refs.held, gather_stages(ENTER + tuple(ATTEND.values())), refs.gather)

    @pl.when(step == 0)
    def _():
        enter(refs, place, work)

    for at in range(pairs):

        @pl.when(step == at + 1)
        def _(at=at):
            for index, stage in ATTEND.get(at, ()):
                work.advance(ORDER[index], stage)
            if at in (2, 4):
                work.arrive(QKV + at // 2, 4)
                enter_unit(refs, at // 2, refs.held.at[QKV + at // 2], put=True)

    @pl.when((step > 0) & (step <= pairs))
    def _():
        pair = forward_pair(jnp.clip(step - 1, 0, pairs - 1))

        def columns(block):
            return pl.ds(pl.multiple_of(block * LANES, LANES), LANES)

        def part(which, rows):
            return refs.packed[pair_unit(which, pair), rows, columns(pair_block(which, pair))]

        def table(head):
            return refs.table[pair // 2, pair % 2, head]

        def put(rows, values):
            refs.mixed[rows, columns(pair)] = values

        attend_pair(refs, table, part, put)

    @pl.when(step == pairs)
    def _():
        for j in range(3):
            packed_copy(refs, j).wait()
        normed_copy(refs).wait()
        mixed = pltpu.make_async_copy(refs.mixed, refs.mixed_out, refs.packed_sem.at[4])
        mixed.start()
        mixed.wait()
        work.finish()


def packed_block(which, rows, pair):
    return pl.BlockSpec(
        (None, rows, LANES),
        lambda step: (pair_unit(which, pair(step)), 0, pair_block(which, pair(step))),
    )


def attend_back_pair(refs, pair):
    scale = BF16(HD ** (-0.5))
    refs.spread[...] = jnp.zeros_like(refs.spread)
    refs.strip[...] = jnp.zeros_like(refs.strip)
    windows = refs.probs.shape[0]
    results = [[[None] * windows for _ in range(2)] for _ in range(3)]
    for head in range(2):
        lanes = slice(head * HD, (head + 1) * HD)
        bias = None
        for window in range(windows):
            rows = slice(window * WIN, (window + 1) * WIN)
            grad = refs.grad[rows, lanes]
            probs = refs.probs[window, head]
            results[2][head][window] = dot_tokens(grad, probs).T.astype(BF16)
            grad_probs = dot_rows(grad, refs.value[rows, lanes])
            weight = probs.astype(F32)
            product = weight * grad_probs
            total = jnp.sum(product, axis=-1, keepdims=True)
            grad_scores = (product - weight * total).astype(BF16)
            wide = grad_scores.astype(F32)
            bias = wide if bias is None else bias + wide
            results[0][head][window] = dot(grad_scores, refs.key[rows, lanes] * scale).astype(BF16)
            query = refs.query[rows, lanes] * scale
            results[1][head][window] = dot_tokens(query, grad_scores).T.astype(BF16)
        for frame in range(WT):
            first = (WT - 1 - frame) * CELLS
            refs.strip[head, :, first : first + WIN] += bias[frame * CELLS : (frame + 1) * CELLS]
        for frame in range(FRAMES):
            for row in range(WSIDE):
                first = (WSIDE - 1 - row) * WSIDE
                refs.spread[
                    head, frame * WSIDE : (frame + 1) * WSIDE, first : first + CELLS
                ] += refs.strip[
                    head, row * WSIDE : (row + 1) * WSIDE, frame * CELLS : (frame + 1) * CELLS
                ]
    for part in range(3):
        lanes = pl.ds(pl.multiple_of(pair_block(part, pair) * LANES, LANES), LANES)
        for window in range(windows):
            rows = slice(window * WIN, (window + 1) * WIN)
            both = [results[part][head][window] for head in range(2)]
            refs.grad_packed[pair_unit(part, pair), rows, lanes] = jnp.concatenate(both, axis=1)


def middle(refs, place=None, gathering=None):
    order = [OUT] + [unit for j in range(4) for unit in (UP + j, DOWN + j)] + [OUT]
    activated, grad_hidden, grad_low = (refs.packed.at[index] for index in range(3))
    reducing = None
    points = {}
    waiting = set()
    if gathering is not None:

        def buffers(unit):
            index = EARLY.index(unit)
            core, side = refs.core.at[index], refs.side.at[index]
            if unit not in DONE:
                return core, side, None, None
            if unit in REDUCE_ASIDE:
                return core, side, None, refs.aside.at[0]
            return core, side, refs.corner.at[index], refs.distant.at[index]

        def store(unit, part, values):
            at = pl.ds(pl.multiple_of(part * HALF, HALF), HALF)
            refs.total[DONE.index(unit), at, :] = values

        reducing = Reduce(
            place, lambda unit: refs.part.at[unit], EARLY_POINTS, store, buffers, refs.reduce
        )
        for stages in MIDDLE.values():
            waiting |= {ORDER[index] for index, stage in stages if stage == 4}
        points = {at: list(moves) for at, moves in EARLY_POINTS.items()}

    count = [0]

    def pump():
        for index, stage in MIDDLE.get(count[0], ()) if gathering is not None else ():
            gathering.advance(ORDER[index], stage)
            if stage == 4:
                waiting.discard(ORDER[index])
        for unit, stage in points.pop(count[0], ()):
            reducing.step(unit, stage)
        count[0] += 1

    def fetch(step):
        return pltpu.make_async_copy(
            refs.held.at[order[step]], refs.units.at[step % 4], refs.fetches.at[step % 4]
        )

    def start_fetch(step):
        if gathering is not None:
            assert order[step] not in waiting
            gathering.arrive(order[step], 4)
        fetch(step).start()

    def put(slot, unit):
        return pltpu.make_async_copy(refs.made.at[slot], refs.part.at[unit], refs.made_sem.at[slot])

    for step in range(3):
        start_fetch(step)
    pump()
    refs.sums[...] = jnp.zeros_like(refs.sums)
    refs.mlp[...] = jnp.zeros_like(refs.mlp)
    refs.grad_normed[...] = jnp.zeros_like(refs.grad_normed)
    fetch(0).wait()

    def project(index):
        refs.attended[:, half(index)] = dot(refs.mixed[...], four_columns(refs.units.at[0], index))

    loop(2, project)
    pump()

    def modulate(window, at, mods, live):
        middle = refs.tokens[at, :].astype(F32) + mods[2] * refs.attended[at, :]
        normal, _ = centered(middle)
        refs.normed[at, :] = (normal * (1.0 + mods[4]) + mods[3]).astype(BF16)
        grad = jnp.where(live, refs.cotangent[at, :].astype(F32), 0.0)
        grad_low[at, :] = (mods[5] * grad).astype(BF16)

    each_rows(refs.mod, refs.live, modulate)
    pump()
    for j in range(4):
        step = 1 + 2 * j
        up, down = refs.units.at[step % 4], refs.units.at[(step + 1) % 4]
        fetch(step).wait()
        fetch(step + 1).wait()
        start_fetch(step + 2)

        def hide(index, up=up, down=down):
            hidden = dot(refs.normed[...], four_columns(up, index))
            bend = jnp.tanh(0.7978845608028654 * (hidden + 0.044715 * hidden * hidden * hidden))
            activated[:, half(index)] = (0.5 * hidden * (1.0 + bend)).astype(BF16)
            slope = 0.5 * (1.0 + bend) + 0.5 * hidden * (1.0 - bend * bend) * (
                0.7978845608028654 * (1.0 + 3.0 * 0.044715 * hidden * hidden)
            )
            grad_activated = dot_rows(grad_low[...], half_rows(down, index))
            grad_hidden[:, half(index)] = (grad_activated * slope).astype(BF16)

        loop(2, hide)
        if j > 0:
            put(1, UP + j - 1).wait()
        pump()

        def down_gradient(index):
            made = dot_tokens(activated[:, half(index)], grad_low[...]).astype(BF16)
            for block in range(8):
                refs.made[0, block // 2, block % 2, index] = made[
                    :, block * LANES : (block + 1) * LANES
                ].reshape(2, SHARE, LANES)

        loop(2, down_gradient)
        put(0, DOWN + j).start()
        pump()

        def up_gradient(index):
            made = dot_tokens(refs.normed[...], grad_hidden[:, half(index)]).astype(BF16)
            put_columns(refs.made.at[1], index, made)

        loop(2, up_gradient)
        put(0, DOWN + j).wait()
        put(1, UP + j).start()
        pump()
        if j < 3:
            start_fetch(step + 3)

        def out_of_mlp(index, up=up, down=down):
            refs.mlp[:, half(index)] += dot(activated[...], four_columns(down, index))
            refs.grad_normed[:, half(index)] += dot_rows(
                grad_hidden[...], half_rows(up, index)
            )

        loop(2, out_of_mlp)
        pump()

    put(1, UP + 3).wait()

    def join(window, at, mods, live):
        attended = refs.attended[at, :]
        middle = refs.tokens[at, :].astype(F32) + mods[2] * attended
        normal, root = centered(middle)
        mlp = refs.mlp[at, :]
        refs.normed[at, :] = jnp.where(live, middle + mods[5] * mlp, 0.0).astype(BF16)
        grad_result = jnp.where(live, refs.cotangent[at, :].astype(F32), 0.0)
        grad_normed = refs.grad_normed[at, :]
        grad_middle = grad_result + norm_back(grad_normed, normal, root, mods[4])
        refs.mlp[at, :] = grad_middle
        grad_low[at, :] = (mods[2] * grad_middle).astype(BF16)
        add_sums(refs.sums, window, 2, grad_middle * attended)
        add_sums(refs.sums, window, 3, grad_normed)
        add_sums(refs.sums, window, 4, grad_normed * normal)
        add_sums(refs.sums, window, 5, grad_result * mlp)

    each_rows(refs.mod, refs.live, join)
    results = [
        pltpu.make_async_copy(source, target, refs.result_sem.at[index])
        for index, (source, target) in enumerate(
            (
                (refs.normed, refs.output),
                (refs.mlp, refs.grad_middle),
                (activated, refs.grad_mixed),
            )
        )
    ]
    results[0].start()
    results[1].start()
    pump()
    fetch(9).wait()

    def back(index):
        made = dot_tokens(refs.mixed[...], grad_low[:, half(index)]).astype(BF16)
        put_columns(refs.made.at[0], index, made)
        activated[:, half(index)] = dot_rows(
            grad_low[...], half_rows(refs.units.at[1], index)
        ).astype(BF16)

    loop(2, back)
    results[2].start()
    put(0, OUT).start()
    put(0, OUT).wait()
    while points:
        pump()
    for index, unit in enumerate(EARLY if gathering is not None else ()):
        if unit not in DONE:

            def keep(z, index=index):
                for part in range(2):
                    refs.side_out[index - len(DONE), part, z] = refs.side[index, part, z]

            loop(4, keep)
    for copy in results:
        copy.wait()
    if gathering is not None:
        gathering.finish()
        reducing.sent()


def middle_kernel(refs):
    place = Place()
    place.greet()
    middle(refs, place, Gather(place, refs.held, gather_stages(MIDDLE.values()), refs.gather))


def leave_weight(refs, j, made):
    def weight(index):
        grad = dot_tokens(refs.normed[...], refs.grad_packed[j, :, half(index)]).astype(BF16)
        put_columns(made, index, grad)

    loop(2, weight)


def leave_back(refs, j):
    def back(index):
        refs.grad_normed[:, half(index)] += dot_rows(
            refs.grad_packed[j], half_rows(refs.unit, index)
        )

    loop(2, back)


def leave_norm(refs, pump=lambda window: None):
    def join(window, at, mods, live):
        normal, root = centered(refs.tokens[at, :].astype(F32))
        grad_normed = refs.grad_normed[at, :]
        refs.grad_tokens[at, :] = refs.grad_middle[at, :] + norm_back(
            grad_normed, normal, root, mods[1]
        )
        add_sums(refs.sums, window, 0, grad_normed)
        add_sums(refs.sums, window, 1, grad_normed * normal)

    each_rows(refs.mod, refs.live, join, pump=pump)


def back_plain_kernel(refs):
    step = pl.program_id(0)

    @pl.when(step < H // 2)
    def _():
        attend_back_pair(refs, backward_pair(jnp.minimum(step, H // 2 - 1)))

    @pl.when(step == H // 2)
    def _():
        refs.sums[...] = jnp.zeros_like(refs.sums)
        refs.grad_normed[...] = jnp.zeros_like(refs.grad_normed)
        for j in range(3):
            fetch = pltpu.make_async_copy(refs.held.at[QKV + j], refs.unit, refs.fetch)
            fetch.start()
            leave_weight(refs, j, refs.made)
            put = pltpu.make_async_copy(refs.made, refs.part.at[j], refs.made_sem)
            put.start()
            fetch.wait()
            leave_back(refs, j)
            put.wait()
        leave_norm(refs)


def fold_spreads(refs):
    heads = H * WIDE // WSIDE
    shape_of = (WSIDE * LANES, TILE)
    place = lax.broadcasted_iota(jnp.int32, shape_of, 0)
    offset = lax.broadcasted_iota(jnp.int32, shape_of, 1)
    own, row, other = place // LANES, place // WSIDE % (LANES // WSIDE), place % WSIDE
    side_span = 2 * WSIDE - 1
    row_diff, col_diff = side_span - 1 - row, own - other + (WSIDE - 1)
    same = (row < side_span) & (row_diff * side_span + col_diff == offset)
    onto = jnp.where(same, 1.0, 0.0).astype(BF16)
    left = jnp.concatenate(
        [refs.spreads[pl.ds(own, heads, stride=WSIDE), :] for own in range(WSIDE)], axis=1
    )
    total = jnp.zeros((heads, TILE), F32)
    for _ in range(3):
        low = left.astype(BF16)
        total = total + dot(low, onto)
        left = left - low.astype(F32)
    rows = 2 * WIDE // WSIDE
    for block in range(8):
        refs.table[block // 2, block % 2] = total[block * rows : (block + 1) * rows]


def back_kernel(refs):
    place = Place()
    z, x, y, c = place.z, place.x, place.y, place.c
    step = pl.program_id(0)

    def buffers(unit):
        every = (EARLY + LATE).index(unit)
        late = every - len(EARLY)
        assert unit not in DONE
        if late < 0:
            core, side = None, refs.side_in.at[every - len(DONE)]
        else:
            core, side = refs.core.at[late], refs.side.at[late]
        if unit in REDUCE_ASIDE:
            return core, side, None, refs.aside.at[0]
        return core, side, refs.corner.at[every], refs.distant.at[every]

    def store(unit, part, values):
        if unit >= DOWN:
            first = part * 512 + (unit - DOWN) * LANES
            refs.grad_down[pl.ds(pl.multiple_of(first, LANES), LANES), :] = values
            return
        at = pl.ds(pl.multiple_of(part * HALF, HALF), HALF)
        if unit < OUT:
            column = picked(z * 2 + x, unit) * LANES
            refs.grad_qkv[at, pl.ds(pl.multiple_of(column, LANES), LANES)] = values
            return
        target, start = (refs.grad_out, OUT) if unit < UP else (refs.grad_up, UP)
        column = (unit - start) * LANES
        target[at, column : column + LANES] = values

    work = Reduce(
        place,
        lambda unit: refs.made.at[unit] if unit < OUT else refs.part.at[unit],
        LATE_POINTS,
        store,
        buffers,
        refs.reduce,
    )
    small = Copies(*refs.small)

    events = [(at, move) for at in sorted(LATE_POINTS) for move in LATE_POINTS[at]]

    def run(until):
        while events and events[0][0] < until:
            work.step(*events.pop(0)[1])

    for number in range(H // 2):

        @pl.when(step == number)
        def _(number=number):
            if number == 0:
                place.greet(EVERYONE)
            if number in (3, 6):
                leave_weight(refs, number // 3 - 1, refs.made.at[number // 3 - 1])
            run(number + 1)

    @pl.when(step < H // 2)
    def _():
        pair = backward_pair(jnp.minimum(step, H // 2 - 1))
        attend_back_pair(refs, pair)
        for head in range(2):
            at = pl.ds(pl.multiple_of((pair * 2 + head) * WIDE, WIDE), WIDE)
            refs.spreads[at, :] = refs.spread[head]

    @pl.when(step == H // 2)
    def _():
        for index, unit in enumerate(DONE):
            for part in range(2):
                store(unit, part, refs.done[index, part * HALF : (part + 1) * HALF, :])
        fold_spreads(refs)
        table = []
        for dz, dx, dy, dc in ALONG_ZX:
            source = refs.table.at[place.far(dz), 1 - x if dx else x]
            table.append(small(source, refs.table_zx.at[z, x], place.shifted(dz, dx, dy, dc)))
        refs.table_zx[z, x] = refs.table[z, x]
        refs.sums[...] = refs.late_sums[...]
        refs.grad_normed[...] = jnp.zeros_like(refs.grad_normed)

        def fetch(j):
            return pltpu.make_async_copy(refs.held.at[QKV + j], refs.unit, refs.fetch)

        fetch(0).start()
        leave_weight(refs, 2, refs.made.at[2])
        run(12)
        fetch(0).wait()
        leave_back(refs, 0)
        fetch(1).start()
        run(13)
        fetch(1).wait()
        leave_back(refs, 1)
        fetch(2).start()
        run(14)
        fetch(2).wait()
        leave_back(refs, 2)
        run(15)
        leave_norm(refs, lambda window: run(17 + window))
        for copy in table:
            copy.wait()
        total = refs.table_zx[0, 0]
        for block in range(1, 8):
            total = total + refs.table_zx[block // 2, block % 2]
        refs.table_own[...] = total
        refs.table_yc[y, c] = total
        table = [
            small(refs.table_own, refs.table_yc.at[y, c], place.shifted(*change))
            for change in ALONG_YC
        ]
        for block in range(48):
            which, column = divmod(block, 8)
            part = jnp.zeros((CLIP_ROWS, LANES), F32)
            for window in range(refs.mod.shape[0]):
                sums = refs.sums[window, which : which + 1, column * LANES : (column + 1) * LANES]
                part = part + refs.member[window] * sums
            first = block % 6 * CLIP_ROWS
            refs.clip[block // 12, block // 6 % 2, first : first + CLIP_ROWS, :] = part
        copies = []
        for dz, dx, dy, dc in ALONG_ZX:
            source = refs.clip.at[place.far(dz), 1 - x if dx else x]
            copies.append(small(source, refs.clip_zx.at[z, x], place.shifted(dz, dx, dy, dc)))
        refs.clip_zx[z, x] = refs.clip[z, x]
        run(19)
        for copy in copies:
            copy.wait()
        total = refs.clip_zx[0, 0]
        for block in range(1, 8):
            total = total + refs.clip_zx[block // 2, block % 2]
        refs.clip_own[...] = total
        refs.clip_yc[y, c] = total
        copies = [
            small(refs.clip_own, refs.clip_yc.at[y, c], place.shifted(*change))
            for change in ALONG_YC
        ]
        run(21)
        for copy in copies:
            copy.wait()
        total = refs.clip_yc[0, 0] + refs.clip_yc[0, 1] + refs.clip_yc[1, 0] + refs.clip_yc[1, 1]
        total = jnp.concatenate([total, jnp.zeros((8, LANES), F32)], axis=0)
        cond = jnp.zeros((8, SHARE), F32)
        lows = []
        for block in range(6):
            lows.append(total[block * CLIP_ROWS : block * CLIP_ROWS + 8].astype(BF16))
            lanes = slice(block * LANES, (block + 1) * LANES)
            cond = cond + dot_rows(lows[-1], refs.ada[:, lanes])
        clips = refs.condition.shape[0]
        refs.cond_own[...] = jnp.zeros_like(refs.cond_own)
        for row in range(2 * clips):
            clip, side = divmod(row, 2)
            refs.cond_own[row : row + 1, :] = cond[
                clip : clip + 1, side * LANES : (side + 1) * LANES
            ]
        refs.cond_all[z, x, y, c] = refs.cond_own[...]
        copies = [
            small(refs.cond_own, refs.cond_all.at[z, x, y, c], place.shifted(*change))
            for change in EVERYONE
        ]
        for block, low in enumerate(lows):
            lanes = slice(block * LANES, (block + 1) * LANES)
            refs.grad_ada[:, lanes] = dot_tokens(act_rows(refs, place), low)
            refs.grad_bias[block : block + 1, :] = jnp.sum(
                low[:CLIP_ROWS].astype(F32), axis=0, keepdims=True
            )
        run(23)
        for copy in table:
            copy.wait()
        total = refs.table_yc[0, 0] + refs.table_yc[0, 1] + refs.table_yc[1, 0] + refs.table_yc[1, 1]
        for head in range(2):
            for frame in range(FRAMES):
                first = (FRAMES - 1 - frame) * OFFSETS
                row = head * (WIDE // WSIDE) + frame
                refs.table_total[head : head + 1, first : first + OFFSETS] = total[
                    row : row + 1, :OFFSETS
                ]
        run(100)
        for copy in copies:
            copy.wait()
        for block in range(4):
            total = refs.cond_all[0, 0, block // 2, block % 2]
            for other in range(1, 8):
                total = total + refs.cond_all[other // 2, other % 2, block // 2, block % 2]
            for row in range(2 * clips):
                clip, side = divmod(row, 2)
                first = block * SHARE + side * LANES
                value = refs.condition[clip : clip + 1, first : first + LANES]
                gate = 1.0 / (1.0 + jnp.exp(-value))
                refs.grad_condition[clip : clip + 1, first : first + LANES] = (
                    total[row : row + 1] * gate * (1.0 + value * (1.0 - gate))
                )
        work.sent()


def enter_plain(tokens, held, mod):
    rows = tokens.shape[0]
    inputs = {"tokens": (tokens, vmem()), "held": (held, anywhere()), "mod": (mod, vmem())}
    outputs = {
        "normed": (shape(BF16, rows, D), vmem()),
        "packed": (shape(BF16, 3, rows, D), vmem()),
    }
    scratch = {
        "units": pltpu.VMEM((1, *SPLIT), BF16),
        "fetches": pltpu.SemaphoreType.DMA((1,)),
    }
    return call(enter_plain_kernel, "enter_plain", inputs, outputs, scratch)


def whole(array):
    return pl.BlockSpec(
        array.shape, lambda p: (0,) * len(array.shape), pipeline_mode=pl.Buffered(1)
    )


def result(dtype, *sizes):
    made = shape(dtype, *sizes)
    return made, whole(made)


def attend_probs(windows, first):
    def pair(step):
        return forward_pair(jnp.clip(step - first, 0, H // 2 - 1))

    return (
        shape(BF16, windows, H, WIN, WIN),
        pl.BlockSpec((windows, 2, WIN, WIN), lambda p: (0, pair(p), 0, 0)),
    )


def attend_scratch():
    return {"strip": pltpu.VMEM((2, CELLS, STRIP), F32), "bias": pltpu.VMEM((2, WIN, WIN), F32)}


def middle_outputs(rows):
    return {
        "output": (shape(BF16, rows, D), anywhere()),
        "grad_middle": (shape(F32, rows, D), anywhere()),
        "grad_mixed": (shape(BF16, rows, D), anywhere()),
        "sums": result(F32, rows // WIN, 8, D),
        "part": (shape(BF16, UNITS, *SPLIT), anywhere()),
    }


def middle_scratch(rows):
    return {
        "units": pltpu.VMEM((4, *SPLIT), BF16),
        "attended": pltpu.VMEM((rows, D), F32),
        "normed": pltpu.VMEM((rows, D), BF16),
        "result_sem": pltpu.SemaphoreType.DMA((3,)),
        "mlp": pltpu.VMEM((rows, D), F32),
        "grad_normed": pltpu.VMEM((rows, D), F32),
        "packed": pltpu.VMEM((3, rows, D), BF16),
        "made": pltpu.VMEM((2, *SPLIT), BF16),
        "fetches": pltpu.SemaphoreType.DMA((4,)),
        "made_sem": pltpu.SemaphoreType.DMA((2,)),
    }


def centre(special, live_frames, tokens, cotangent, mixed, mod, held):
    rows = tokens.shape[0]
    inputs = {
        name: (array, whole(array))
        for name, array in (
            ("tokens", tokens),
            ("cotangent", cotangent),
            ("mixed", mixed),
            ("mod", mod),
        )
    }
    inputs["live"] = (live_frames, smem())
    outputs, scratch = middle_outputs(rows), middle_scratch(rows)
    if not special:
        inputs["held"] = (held, anywhere())
        return call(middle, "middle_plain", inputs, outputs, scratch, grid=(1,), limit=60)
    inputs["held_in"] = (held, anywhere())
    outputs |= {
        "held": (shape(BF16, UNITS, *SPLIT), anywhere()),
        "side_out": result(BF16, *Reduce.side_shape(len(EARLY) - len(DONE))),
        "total": result(F32, len(DONE), SHARE, LANES),
    }
    scratch |= {
        "core": pltpu.VMEM(Reduce.core_shape(len(EARLY)), BF16),
        "side": pltpu.VMEM(Reduce.side_shape(len(EARLY)), BF16),
        "corner": pltpu.VMEM(Reduce.corner_shape(len(DONE)), BF16),
        "distant": pltpu.VMEM(Reduce.distant_shape(len(DONE)), BF16),
        "aside": pltpu.VMEM(Reduce.aside_shape(1), BF16),
        "reduce": Reduce.scratch(EARLY_POINTS),
        "gather": Gather.semaphores(gather_stages(MIDDLE.values())),
    }
    return call(
        middle_kernel,
        "middle",
        inputs,
        outputs,
        scratch,
        (("held_in", "held"),),
        collective=2,
        grid=(1,),
        limit=60,
    )


def begin(tokens, own, smalls):
    rows = tokens.shape[0]
    windows = rows // WIN
    inputs = {"tokens": (tokens, whole(tokens))}
    for name, block in zip(("qkv", "out", "up", "down"), own, strict=True):
        inputs[name] = (block, whole(block))
    for name, array in zip(("condition", "ada", "bias_in", "rel_table"), smalls[1:], strict=True):
        inputs[name] = (array, whole(array))
    inputs["frames"] = (smalls[0], smem())
    outputs = {
        "probs": attend_probs(windows, 1),
        "mixed_out": (shape(BF16, rows, D), anywhere()),
        "normed_out": (shape(BF16, rows, D), anywhere()),
        "packed_out": (shape(BF16, 3, rows, D), anywhere()),
        "held": (shape(BF16, UNITS, *SPLIT), anywhere()),
        "mod": result(F32, windows, 8, D),
        "member": result(F32, windows, CLIP_ROWS, LANES),
        "live": (shape(jnp.int32, windows), smem()),
    }
    stages = gather_stages(ENTER + tuple(ATTEND.values()))
    scratch = attend_scratch() | {
        "units": pltpu.VMEM((1, *SPLIT), BF16),
        "fetches": pltpu.SemaphoreType.DMA((1,)),
        "normed": pltpu.VMEM((rows, D), BF16),
        "packed": pltpu.VMEM((3, rows, D), BF16),
        "mixed": pltpu.VMEM((rows, D), BF16),
        "packed_sem": pltpu.SemaphoreType.DMA((5,)),
        "own": pltpu.VMEM((UNITS, SHARE, LANES), BF16),
        "own_sem": pltpu.SemaphoreType.DMA((UNITS,)),
        "gather": Gather.semaphores(stages),
        "small": [pltpu.SemaphoreType.DMA((18,))] * 2,
        "mod_part": pltpu.VMEM((MOD_ROWS, LANES), F32),
        "mod_parts": pltpu.VMEM((2, 2, MOD_ROWS, LANES), F32),
        "mods": pltpu.VMEM((4, 2, MOD_ROWS, LANES), F32),
        "rows": pltpu.VMEM((24, TILE), F32),
        "spread": pltpu.VMEM((2 * SPREAD, LANES), F32),
        "table_own": pltpu.VMEM((2, SPREAD, LANES), BF16),
        "table": pltpu.VMEM((4, 2, 2, SPREAD, LANES), BF16),
    }
    return call(
        start_kernel,
        "start",
        inputs,
        outputs,
        scratch,
        collective=0,
        grid=(H // 2 + 1,),
        limit=60,
    )


def deliver_kernel(refs):
    names = [name for name in vars(refs) if name.startswith("from_")]
    loads, stores = [], []
    for index, name in enumerate(names):
        plain = name[len("from_") :]
        held = getattr(refs, "held_" + plain)
        loads.append(pltpu.make_async_copy(getattr(refs, name), held, refs.sems.at[0, index]))
        stores.append(pltpu.make_async_copy(held, getattr(refs, plain), refs.sems.at[1, index]))
        loads[-1].start()
    for load, store in zip(loads, stores, strict=True):
        load.wait()
        store.start()
    for store in stores:
        store.wait()


def deliver(**arrays):
    inputs = {"from_" + name: (array, anywhere()) for name, array in arrays.items()}
    outputs = {name: (shape(array.dtype, *array.shape), anywhere()) for name, array in arrays.items()}
    scratch = {"held_" + name: pltpu.VMEM(array.shape, array.dtype) for name, array in arrays.items()}
    scratch["sems"] = pltpu.SemaphoreType.DMA((2, len(arrays)))
    return call(deliver_kernel, "deliver", inputs, outputs, scratch)


def attend_plain(packed, table, live_frames):
    windows = live_frames.shape[0]
    rows = windows * WIN
    inputs = {
        "live": (live_frames, smem()),
        "query": (packed, packed_block(0, rows, forward_pair)),
        "key": (packed, packed_block(1, rows, forward_pair)),
        "value": (packed, packed_block(2, rows, forward_pair)),
        "table": (table, pl.BlockSpec((2, SPREAD, LANES), lambda p: (forward_pair(p), 0, 0))),
    }
    return call(
        attend_plain_kernel,
        "attend_plain",
        inputs,
        {
            "mixed": (
                shape(BF16, rows, D),
                pl.BlockSpec((rows, LANES), lambda p: (0, forward_pair(p))),
            ),
            "probs": attend_probs(windows, 0),
        },
        attend_scratch(),
        grid=(H // 2,),
    )


def back(
    special, live_frames, tokens, mod, packed, normed, probs, mid, held, ada, member, condition
):
    window_count = probs.shape[0]
    rows = window_count * WIN
    pairs = H // 2

    def last(step):
        return backward_pair(jnp.minimum(step, pairs - 1))

    def packed_pair(which):
        return packed_block(which, rows, last)

    inputs = {
        "live": (live_frames, smem()),
        "query": (packed, packed_pair(0)),
        "key": (packed, packed_pair(1)),
        "value": (packed, packed_pair(2)),
        "probs": (
            probs,
            pl.BlockSpec((window_count, 2, WIN, WIN), lambda p: (0, last(p), 0, 0)),
        ),
        "grad": (mid.grad_mixed, pl.BlockSpec((rows, LANES), lambda p: (0, last(p)))),
        "held": (held, anywhere()),
    }
    for name, array in (
        ("tokens", tokens),
        ("mod", mod),
        ("normed", normed),
        ("grad_middle", mid.grad_middle),
    ):
        inputs[name] = (array, whole(array))

    outputs = {"grad_tokens": result(F32, rows, D)}
    scratch = {
        "strip": pltpu.VMEM((2, CELLS, STRIP), F32),
        "grad_packed": pltpu.VMEM((3, rows, D), BF16),
        "unit": pltpu.VMEM(SPLIT, BF16),
        "grad_normed": pltpu.VMEM((rows, D), F32),
        "fetch": pltpu.SemaphoreType.DMA,
    }
    if not special:
        outputs["sums"] = result(F32, window_count, 8, D)
        outputs["part"] = (shape(BF16, 3, *SPLIT), anywhere())
        outputs["spread"] = (
            shape(F32, H, SPREAD, LANES),
            pl.BlockSpec((2, SPREAD, LANES), lambda p: (last(p), 0, 0)),
        )
        scratch["made"] = pltpu.VMEM(SPLIT, BF16)
        scratch["made_sem"] = pltpu.SemaphoreType.DMA
        return call(
            back_plain_kernel, "back_plain", inputs, outputs, scratch, grid=(pairs + 1,)
        )
    inputs |= {
        "late_sums": (mid.sums, whole(mid.sums)),
        "ada": (ada, whole(ada)),
        "condition": (condition, whole(condition)),
        "member": (member, whole(member)),
        "side_in": (mid.side_out, whole(mid.side_out)),
        "done": (mid.total, whole(mid.total)),
        "part": (mid.part, anywhere()),
    }
    outputs |= {
        "grad_qkv": result(F32, SHARE, 3 * LANES),
        "grad_out": result(F32, SHARE, LANES),
        "grad_up": result(F32, SHARE, 4 * LANES),
        "grad_down": result(F32, 4 * SHARE, LANES),
        "grad_ada": result(F32, SHARE, 6 * LANES),
        "grad_bias": result(F32, 6, LANES),
        "grad_condition": result(F32, *condition.shape),
        "table_total": result(F32, 2, REL),
    }
    count, late = len(EARLY + LATE), len(LATE)
    scratch |= {
        "spread": pltpu.VMEM((2, WIDE, LANES), F32),
        "spreads": pltpu.VMEM((H * WIDE, LANES), F32),
        "made": pltpu.VMEM((3, *SPLIT), BF16),
        "sums": pltpu.VMEM((window_count, 8, D), F32),
        "core": pltpu.VMEM(Reduce.core_shape(late), BF16),
        "side": pltpu.VMEM(Reduce.side_shape(late), BF16),
        "corner": pltpu.VMEM(Reduce.corner_shape(count), BF16),
        "distant": pltpu.VMEM(Reduce.distant_shape(count), BF16),
        "aside": pltpu.VMEM(Reduce.aside_shape(1), BF16),
        "reduce": Reduce.scratch(LATE_POINTS),
        "table": pltpu.VMEM((4, 2, 2 * WIDE // WSIDE, TILE), F32),
        "table_zx": pltpu.VMEM((4, 2, 2 * WIDE // WSIDE, TILE), F32),
        "table_own": pltpu.VMEM((2 * WIDE // WSIDE, TILE), F32),
        "table_yc": pltpu.VMEM((2, 2, 2 * WIDE // WSIDE, TILE), F32),
        "clip": pltpu.VMEM((4, 2, MOD_ROWS, LANES), F32),
        "clip_zx": pltpu.VMEM((4, 2, MOD_ROWS, LANES), F32),
        "clip_own": pltpu.VMEM((MOD_ROWS, LANES), F32),
        "clip_yc": pltpu.VMEM((2, 2, MOD_ROWS, LANES), F32),
        "cond_own": pltpu.VMEM((8, LANES), F32),
        "cond_all": pltpu.VMEM((4, 2, 2, 2, 8, LANES), F32),
        "small": [pltpu.SemaphoreType.DMA((51,))] * 2,
    }
    return call(
        back_kernel,
        "back",
        inputs,
        outputs,
        scratch,
        collective=3,
        grid=(pairs + 1,),
        limit=60,
    )


def per_device(
    special,
    tokens,
    condition,
    clip_frames,
    ada_weight,
    ada_bias,
    qkv_weight,
    out_weight,
    up_weight,
    down_weight,
    rel_table,
    cotangent,
):
    window_count = tokens.shape[0]
    clip_count = condition.shape[0]
    rows_ada, cols_ada = ada_weight.shape
    token_rows = tokens.reshape(window_count * WIN, D)
    cotangent_rows = cotangent.reshape(window_count * WIN, D)
    own = (qkv_weight, out_weight, up_weight, down_weight)
    if special:
        smalls = (clip_frames, condition, ada_weight, ada_bias.reshape(1, cols_ada), rel_table)
        start = across = begin(token_rows, own, smalls)
        mixed = start.mixed_out
        live_frames, member_wide, mod = start.live, start.member, start.mod
        packed, held, normed = start.packed_out, start.held, start.normed_out
    else:
        row_block = lax.axis_index("fsdp")
        col_block = lax.axis_index("dp")
        first_window = lax.axis_index(("dp", "fsdp")) * window_count
        live_frames, member_int = window_layout(clip_frames, first_window, window_count)
        member = member_int.astype(F32)
        activity_low = jax.nn.silu(condition).astype(BF16)
        rows_own = lax.dynamic_slice_in_dim(activity_low, row_block * rows_ada, rows_ada, 1)
        mod_part = jnp.dot(rows_own, ada_weight, preferred_element_type=F32)
        clip_mod = lax.all_gather(lax.psum(mod_part, "fsdp"), "dp", axis=1, tiled=True)
        bias = lax.all_gather(ada_bias, "dp", axis=0, tiled=True)
        clip_mod = clip_mod + bias.astype(F32)[None, :]
        member_wide = None
        window_mod = jnp.sum(member[:, :, None] * clip_mod[None], axis=1)
        window_mod = jnp.pad(window_mod.reshape(window_count, 6, D), ((0, 0), (0, 2), (0, 0)))
        whole = [
            lax.all_gather(
                lax.all_gather(weight, "dp", axis=1, tiled=True), "fsdp", axis=0, tiled=True
            )
            for weight in own
        ]
        held = units_of(*whole).reshape(UNITS, *SPLIT)
        mod = window_mod
        start = enter_plain(token_rows, held, mod)
        packed, normed = start.packed, start.normed
        table = spread_table(lax.all_gather(rel_table, "dp", axis=0, tiled=True))
        across = attend_plain(packed, table, live_frames)
        mixed = across.mixed
    mid = centre(special, live_frames, token_rows, cotangent_rows, mixed, mod, held)
    held = mid.held if special else held
    end = back(
        special,
        live_frames,
        token_rows,
        mod,
        packed,
        normed,
        across.probs,
        mid,
        held,
        ada_weight,
        member_wide,
        condition,
    )
    if special:
        end = deliver(
            output=mid.output,
            grad_tokens=end.grad_tokens,
            grad_condition=end.grad_condition,
            grad_ada=end.grad_ada,
            grad_bias=end.grad_bias,
            grad_qkv=end.grad_qkv,
            grad_out=end.grad_out,
            grad_up=end.grad_up,
            grad_down=end.grad_down,
            table=end.table_total,
        )
        return (
            end.output.reshape(tokens.shape),
            end.grad_tokens.reshape(tokens.shape),
            end.grad_condition,
            end.grad_ada,
            end.grad_bias.reshape(cols_ada),
            end.grad_qkv,
            end.grad_out,
            end.grad_up,
            end.grad_down,
            end.table,
        )
    part = jnp.concatenate([end.part, mid.part[OUT:]])
    grads = [
        lax.psum_scatter(
            lax.psum_scatter(grad, "fsdp", scatter_dimension=0, tiled=True),
            "dp",
            scatter_dimension=1,
            tiled=True,
        ).astype(F32)
        for grad in weights_of(part.reshape(UNITS, 8, D, LANES))
    ]
    grad_mod = (mid.sums + end.sums)[:, :6].reshape(window_count, 6 * D)
    clip_part = lax.dot_general(
        member,
        grad_mod,
        (((0,), (0,)), ((), ())),
        precision=HIGHEST,
        preferred_element_type=F32,
    )
    clip_sum, table_sum = lax.psum((clip_part, gather_table(end.spread)), ("dp", "fsdp"))
    clip_cols = lax.dynamic_slice_in_dim(
        clip_sum.astype(BF16), col_block * cols_ada, cols_ada, 1
    )
    heads_own = rel_table.shape[0]
    table_grad = lax.dynamic_slice_in_dim(table_sum, col_block * heads_own, heads_own, 0)
    cond_part = lax.dot_general(
        clip_cols, ada_weight, (((1,), (1,)), ((), ())), preferred_element_type=F32
    )
    cond_total = lax.all_gather(lax.psum(cond_part, "dp"), "fsdp", axis=1, tiled=True)
    grad_ada_weight = lax.dot_general(
        rows_own, clip_cols, (((0,), (0,)), ((), ())), preferred_element_type=F32
    )
    grad_ada_bias = jnp.sum(clip_cols.astype(F32), axis=0)
    _, silu_back = jax.vjp(jax.nn.silu, condition)
    return (
        mid.output.reshape(tokens.shape),
        end.grad_tokens.reshape(tokens.shape),
        silu_back(cond_total)[0],
        grad_ada_weight,
        grad_ada_bias,
        *grads,
        table_grad,
    )


def solution(mesh):
    special = dict(mesh.shape) == {"dp": 8, "fsdp": 4}
    both = P(("dp", "fsdp"), None, None)
    weight = P("fsdp", "dp")
    in_specs = (both, P(), P(), weight, P("dp")) + (weight,) * 4 + (P("dp", None), both)
    out_specs = (both, both, P(), weight, P("dp")) + (weight,) * 4 + (P("dp", None),)
    return jax.shard_map(
        functools.partial(per_device, special),
        mesh=mesh,
        in_specs=in_specs,
        out_specs=out_specs,
        check_vma=False,
    )
```

```python
import functools

import jax
import jax.numpy as jnp
from jax import lax
from jax.experimental import pallas as pl
from jax.experimental.pallas import tpu as pltpu
from jax.sharding import PartitionSpec as P

D = 1024
H = 16
HD = 64
WT = 5
WSIDE = 8
WIN = 320
SPW = 16
CELLS = WSIDE * WSIDE
FRAMES = 2 * WT - 1
OFFSETS = (2 * WSIDE - 1) ** 2
REL = FRAMES * OFFSETS
LANES = 128
TILE = 256
SPREAD = 80
WIDE = 96
STRIP = 640

EPSILON = 1e-06
NEGATIVE = -1000000000.0
HIGHEST = lax.Precision.HIGHEST
F32 = jnp.float32
BF16 = jnp.bfloat16
MESH = pl.DeviceIdType.MESH
MIB = 2**20

QKV, OUT, UP, DOWN, UNITS = 0, 3, 4, 8, 12
PICK = (
    (1, 2, 0),
    (1, 2, 0),
    (0, 1, 2),
    (0, 1, 2),
    (0, 1, 2),
    (2, 0, 1),
    (2, 0, 1),
    (1, 0, 2),
)
SHARE = 256
HALF = 128


SPLIT = (4, 2, 2, 2, SHARE, LANES)
CLIP_ROWS = 4
MOD_ROWS = 6 * CLIP_ROWS
OWN_SLOTS = 4
ORDER = (0, 1, 2, 3, 4, 8, 5, 9, 6, 10, 7, 11)
GATHER_ASIDE = (DOWN + 3,)
REDUCE_ASIDE = (DOWN, UP + 2)
ENTER = (((2, 1), (0, 1), (11, 1), (11, 2), (2, 2), (1, 1)), ((2, 3), (0, 2), (6, 1), (1, 2)), ((0, 3),), ((1, 3), (5, 1), (3, 1), (6, 2)), ((2, 4), (0, 4), (4, 1), (5, 2)), ((8, 1), (6, 3)))
ATTEND = {0: ((3, 2), (7, 1), (5, 3)), 1: ((1, 4),), 2: ((4, 2), (10, 1)), 3: ((3, 3), (9, 1)), 4: ((4, 3),), 5: ((5, 4),), 6: ((3, 4), (7, 2), (8, 2)), 7: ((4, 4),)}
MIDDLE = {0: ((8, 3), (7, 3), (6, 4)), 2: ((11, 3),), 3: ((10, 2), (9, 2)), 4: ((7, 4), (8, 4)), 5: ((10, 3),), 6: ((9, 3),), 8: ((10, 4),), 9: ((9, 4),), 11: ((11, 4),)}
EARLY = (DOWN, UP, DOWN + 1, UP + 1, DOWN + 2)
DONE = EARLY[:4]
EARLY_POINTS = {7: ((4, 0), (8, 0)), 8: ((4, 1),), 9: ((8, 1),), 10: ((9, 0), (4, 2)), 11: ((9, 1), (5, 0)), 12: ((4, 3),), 13: ((5, 1),), 14: ((10, 0), (9, 2)), 16: ((5, 2),), 17: ((8, 2), (9, 3), (10, 1)), 18: ((8, 3), (5, 3)), 19: ((8, 4), (4, 4)), 20: ((5, 4),), 21: ((10, 2), (9, 4))}
LATE = (UP + 2, DOWN + 3, UP + 3, OUT, QKV, QKV + 1, QKV + 2)
LATE_POINTS = {0: ((6, 0), (10, -3), (11, 0)), 1: ((6, 1), (11, 1)), 2: ((7, 0),), 3: ((3, 0), (7, 1), (11, 2)), 4: ((0, 0), (3, 1), (10, 3)), 6: ((7, 2), (1, 0), (0, 1)), 7: ((11, 3), (3, 2)), 8: ((6, 2), (10, 4), (11, 4)), 10: ((1, 1),), 11: ((7, 3), (3, 3)), 12: ((0, 2),), 13: ((2, 0),), 14: ((2, 1),), 15: ((1, 2),), 16: ((0, 3),), 18: ((1, 3), (6, 3), (2, 2)), 19: ((6, 4), (2, 3)), 20: ((1, 4),), 21: ((3, 4),), 22: ((7, 4),), 24: ((0, 4), (2, 4))}
def reduce_stages(points):
    moves = [move for at in sorted(points) for move in points[at]]
    started = [(unit, 3 if stage == -3 else stage + 1) for unit, stage in moves if stage < 4]
    return [(unit, stage) for unit, stage in started if stage > 3 or (unit, stage) in moves or stage < 3]


def gather_stages(points):
    return [(ORDER[index], stage) for point in points for index, stage in point]


def forward_pair(step):
    first = (13 - step) // 8
    return first * ((step // 2 + 1) % 3 + 3 * (step % 2)) + (1 - first) * step


def backward_pair(step):
    group, place = step // 3, step % 3
    return (1 + group) % 3 + 3 * place - place // 2


def pair_unit(which, pair):
    first = (13 - pair) // 8
    sixth, seventh = ((0, 2, 0), (1, 1, 2))[0][which], ((0, 2, 0), (1, 1, 2))[1][which]
    return first * ((pair + 2) % 3) + (1 - first) * ((7 - pair) * sixth + (pair - 6) * seventh)


def pair_block(which, pair):
    return (which * (H // 2) + pair) // 3


def picked(block, j):
    return sum(jnp.where(block == index, PICK[index][j], 0) for index in range(8))


def window_layout(clip_frames, first_window, window_count):
    slab_count = 1 + (clip_frames > WT).astype(jnp.int32)
    starts = jnp.cumsum(slab_count, dtype=jnp.int32) - slab_count
    global_window = first_window + jnp.arange(window_count, dtype=jnp.int32)
    slab_of = global_window // SPW
    owners = jnp.sum((starts[None, :] <= slab_of[:, None]).astype(jnp.int32), axis=1) - 1
    clip_ids = jnp.arange(clip_frames.shape[0], dtype=jnp.int32)
    member = (owners[:, None] == clip_ids[None, :]).astype(jnp.int32)
    clip_start = jnp.sum(member * starts[None, :], axis=1)
    own_frames = jnp.sum(member * clip_frames[None, :], axis=1)
    inner_slab = slab_of - clip_start
    return (jnp.minimum(own_frames - WT * inner_slab, WT), member)


def offset_spread():
    side_span = 2 * WSIDE - 1
    shape = (OFFSETS, WSIDE * LANES)
    offset = lax.broadcasted_iota(jnp.int32, shape, 0)
    place = lax.broadcasted_iota(jnp.int32, shape, 1)
    own, row, other = place // LANES, place // WSIDE % (LANES // WSIDE), place % WSIDE
    row_diff, col_diff = side_span - 1 - row, own - other + (WSIDE - 1)
    return ((row < side_span) & (row_diff * side_span + col_diff == offset)).astype(BF16)


def spread_table(table):
    heads = table.shape[0]
    by_frame = table.reshape(heads, FRAMES, OFFSETS)[:, ::-1].reshape(heads * FRAMES, OFFSETS)
    spread = jnp.dot(by_frame, offset_spread(), preferred_element_type=F32).astype(BF16)
    spread = spread.reshape(heads, FRAMES * WSIDE, LANES)
    return jnp.pad(spread, ((0, 0), (0, SPREAD - FRAMES * WSIDE), (0, 0)))


def gather_table(spread):
    heads = spread.shape[0]
    by_frame = spread[:, : FRAMES * WSIDE].reshape(heads * FRAMES, WSIDE * LANES)
    sums = lax.dot_general(
        by_frame,
        offset_spread().astype(F32),
        (((1,), (1,)), ((), ())),
        precision=HIGHEST,
        preferred_element_type=F32,
    )
    return sums.reshape(heads, FRAMES, OFFSETS)[:, ::-1].reshape(heads, FRAMES * OFFSETS)


def units_of(qkv, out, up, down):
    return jnp.concatenate(
        [
            jnp.stack(
                [
                    jnp.stack([qkv[:, 384 * b + LANES * PICK[b][j] :][:, :LANES] for b in range(8)])
                    for j in range(3)
                ]
            ),
            out.reshape(D, 8, 1, LANES).transpose(2, 1, 0, 3),
            up.reshape(D, 8, 4, LANES).transpose(2, 1, 0, 3),
            down.reshape(8, 4, LANES, 8, LANES).transpose(1, 3, 0, 2, 4).reshape(4, 8, D, LANES),
        ]
    )


def weights_of(units):
    def columns(part):
        return part.transpose(2, 1, 0, 3).reshape(D, -1)

    down = units[DOWN:].reshape(4, 8, 8, LANES, LANES).transpose(2, 0, 3, 1, 4)
    qkv = [
        units[PICK[block].index(tile), block] for block in range(8) for tile in range(3)
    ]
    return (
        jnp.concatenate(qkv, axis=1),
        columns(units[OUT:UP]),
        columns(units[UP:DOWN]),
        down.reshape(4 * D, D),
    )


def dot(left, right):
    return jnp.dot(left, right, preferred_element_type=F32)


def dot_rows(left, right):
    return lax.dot_general(left, right, (((1,), (1,)), ((), ())), preferred_element_type=F32)


def dot_tokens(left, right):
    return lax.dot_general(left, right, (((0,), (0,)), ((), ())), preferred_element_type=F32)


def half(index):
    return pl.ds(pl.multiple_of(index * 512, 512), 512)


def four_columns(unit, index):
    blocks = [unit[2 * index + x // 2, x % 2].reshape(D, LANES) for x in range(4)]
    return jnp.concatenate(blocks, axis=1)


def half_rows(unit, index):
    blocks = [unit[block // 2, block % 2, index].reshape(512, LANES) for block in range(8)]
    return jnp.concatenate(blocks, axis=1)


def put_columns(unit, index, values):
    for x in range(4):
        unit[2 * index + x // 2, x % 2] = values[:, x * LANES : (x + 1) * LANES].reshape(2, 2, SHARE, LANES)


def loop(count, body):
    def step(index, carry):
        body(index)
        return carry

    lax.fori_loop(0, count, step, 0)


def vmem():
    return pl.BlockSpec(memory_space=pltpu.VMEM)


def anywhere():
    return pl.BlockSpec(memory_space=pl.ANY)


def smem():
    return pl.BlockSpec(memory_space=pltpu.SMEM)


def shape(dtype, *sizes):
    return jax.ShapeDtypeStruct(sizes, dtype)


def params(collective=None, limit=58):
    if collective is None:
        return pltpu.CompilerParams(vmem_limit_bytes=limit * MIB)
    return pltpu.CompilerParams(
        vmem_limit_bytes=limit * MIB, collective_id=collective, has_side_effects=True
    )


def centered(values):
    center = values - jnp.mean(values, axis=-1, keepdims=True)
    spread = jnp.mean(center * center, axis=-1, keepdims=True)
    root = lax.rsqrt(spread + EPSILON)
    return center * root, root


def norm_back(grad_normed, normal, root, scale):
    grad = grad_normed * (1.0 + scale)
    mean = jnp.mean(grad, axis=-1, keepdims=True)
    along = jnp.mean(grad * normal, axis=-1, keepdims=True)
    return root * (grad - mean - normal * along)


def each_rows(mod_ref, live_ref, body, rows=32, pump=lambda window: None):
    for window in range(mod_ref.shape[0]):
        live = live_ref[window] * CELLS

        def step(index, window=window, live=live):
            at = pl.ds(pl.multiple_of(window * WIN + index * rows, rows), rows)
            mods = [mod_ref[window, k : k + 1, :] for k in range(6)]
            slot = index * rows + lax.broadcasted_iota(jnp.int32, (rows, 1), 0)
            body(window, at, mods, slot < live)

        loop(WIN // rows, step)
        pump(window)


def add_sums(sums_ref, window, which, values):
    sums_ref[window, which : which + 1, :] += jnp.sum(values, axis=0, keepdims=True)


class Place:
    def __init__(self):
        column, row = lax.axis_index("dp"), lax.axis_index("fsdp")
        self.z, self.x, self.y, self.c = column // 2, column % 2, row // 2, row % 2

    def at(self, z=None, x=None, y=None, c=None):
        z = self.z if z is None else z
        x = self.x if x is None else x
        y = self.y if y is None else y
        c = self.c if c is None else c
        return (z * 2 + x, y * 2 + c)

    def far(self, k):
        return lax.rem(self.z + k, 4)

    def shifted(self, dz, dx, dy, dc):
        def other(index, change):
            return 1 - index if change else index

        return self.at(self.far(dz), other(self.x, dx), other(self.y, dy), other(self.c, dc))

    def greet(self, far_ones=()):
        near = [(1, 0, 0, 0), (2, 0, 0, 0), (3, 0, 0, 0), (0, 1, 0, 0), (0, 0, 1, 0), (0, 0, 0, 1)]
        peers = near + [change for change in far_ones if change not in near]
        barrier = pltpu.get_barrier_semaphore()
        for change in peers:
            pl.semaphore_signal(
                barrier, inc=1, device_id=self.shifted(*change), device_id_type=MESH
            )
        pl.semaphore_wait(barrier, len(peers))


EVERYONE = [
    (dz, dx, dy, dc)
    for dz in range(4)
    for dx in range(2)
    for dy in range(2)
    for dc in range(2)
    if (dz, dx, dy, dc) != (0, 0, 0, 0)
]
ALONG_ZX = [change for change in EVERYONE if change[2:] == (0, 0)]
ALONG_YC = [change for change in EVERYONE if change[:2] == (0, 0)]


class Moves:
    def __init__(self, place, stages, scratch):
        self.place = place
        self.send, self.recv = scratch
        self.first, count = {}, 0
        for unit, stage in stages:
            self.first[unit, stage] = count
            count += self.counts[unit in self.aside][stage - 1]
        self.flying = []

    @classmethod
    def semaphores(cls, stages):
        count = sum(cls.counts[unit in cls.aside][stage - 1] for unit, stage in stages)
        return [pltpu.SemaphoreType.DMA((count,))] * 2

    def made(self, unit, stage, moves):
        copies = []
        for index, (source, target, device) in enumerate(moves):
            slot = self.first[unit, stage] + index
            copies.append(
                pltpu.make_async_remote_copy(
                    src_ref=source,
                    dst_ref=target,
                    send_sem=self.send.at[slot],
                    recv_sem=self.recv.at[slot],
                    device_id=device,
                    device_id_type=MESH,
                )
            )
        return copies

    def begin(self, unit, stage):
        for copy in self.copies(unit, stage):
            copy.start()
        self.flying.append((unit, stage))

    def arrive(self, unit, stage):
        if (unit, stage) in self.flying:
            self.flying.remove((unit, stage))
            for copy in self.copies(unit, stage):
                copy.wait_recv()

    def sent(self):
        for unit, stage in self.first:
            for copy in self.copies(unit, stage):
                copy.wait_send()


class Gather(Moves):
    counts = ((3, 2, 2, 1), (2, 2, 3, 1))
    aside = GATHER_ASIDE

    def __init__(self, place, held, stages, scratch):
        super().__init__(place, stages, scratch)
        self.held = held

    def copies(self, unit, stage):
        p, held = self.place, self.held.at[unit]
        at_x, at_y, at_core = p.at(x=1 - p.x), p.at(y=1 - p.y), p.at(c=1 - p.c)
        own = held.at[p.z, p.x, p.y, p.c]
        if stage == 4:
            refs = [(held.at[:, :, :, p.c], at_core)]
        elif unit in self.aside and stage == 1:
            refs = [(own.at[:HALF], at_x), (own.at[HALF:], at_y)]
        elif unit in self.aside and stage == 2:
            refs = [
                (held.at[p.z, :, p.y, p.c, :HALF], at_y),
                (held.at[p.z, p.x, :, p.c, HALF:], at_x),
            ]
        elif unit in self.aside:
            refs = [(held.at[p.z, :, :, p.c], p.at(z=p.far(k))) for k in (1, 2, 3)]
        elif stage == 1:
            refs = [(own, p.at(z=p.far(k))) for k in (1, 2, 3)]
        elif stage == 2:
            refs = [
                (held.at[:, p.x, p.y, p.c, :HALF], at_x),
                (held.at[:, p.x, p.y, p.c, HALF:], at_y),
            ]
        else:
            refs = [
                (held.at[:, :, p.y, p.c, :HALF], at_y),
                (held.at[:, p.x, :, p.c, HALF:], at_x),
            ]
        return self.made(unit, stage, [(ref, ref, device) for ref, device in refs])

    def advance(self, unit, stage):
        self.arrive(unit, stage - 1)
        self.begin(unit, stage)

    def finish(self):
        for unit, stage in list(self.flying):
            self.arrive(unit, stage)
        self.sent()


class Reduce(Moves):
    counts = ((1, 2, 2, 3), (1, 3, 2, 2))
    aside = REDUCE_ASIDE

    def __init__(self, place, part, points, store, buffers, scratch):
        super().__init__(place, reduce_stages(points), scratch[2:])
        self.part, self.store, self.buffers = part, store, buffers
        self.own, self.load = scratch[:2]
        self.slots, self.loaded = {}, []

    @classmethod
    def scratch(cls, points):
        return [
            pltpu.VMEM((OWN_SLOTS, 4, 2, 2, SHARE, LANES), BF16),
            pltpu.SemaphoreType.DMA((OWN_SLOTS,)),
        ] + cls.semaphores(reduce_stages(points))

    @staticmethod
    def core_shape(count):
        return (count, 4, 2, 2, SHARE, LANES)

    @staticmethod
    def side_shape(count):
        return (count, 2, 4, 2, HALF, LANES)

    @staticmethod
    def corner_shape(count):
        return (count, 2, 4, HALF, LANES)

    @staticmethod
    def distant_shape(count):
        return (count, 3, 2, HALF, LANES)

    @staticmethod
    def aside_shape(count):
        return (count, 3, 2, 2, SHARE, LANES)

    def own_copy(self, unit):
        slot = self.slots.setdefault(unit, len(self.slots) % OWN_SLOTS)
        return pltpu.make_async_copy(
            self.part(unit).at[:, :, :, self.place.c], self.own.at[slot], self.load.at[slot]
        )

    def copies(self, unit, stage):
        p = self.place
        at_x, at_y, at_core = p.at(x=1 - p.x), p.at(y=1 - p.y), p.at(c=1 - p.c)
        core, side, corner, distant = self.buffers(unit)
        if unit in self.aside and stage == 2:
            moves = [
                (core.at[p.far(k)], distant.at[k - 1], p.at(z=p.far(k))) for k in (1, 2, 3)
            ]
        elif unit in self.aside and stage == 3:
            moves = [
                (core.at[p.z, :, 1 - p.y, :HALF], side.at[0, 0], at_y),
                (core.at[p.z, 1 - p.x, :, HALF:], side.at[1, 0], at_x),
            ]
        elif unit in self.aside and stage == 4:
            moves = [
                (side.at[0, 0, 1 - p.x], side.at[0, 1, 0], at_x),
                (side.at[1, 0, 1 - p.y], side.at[1, 1, 0], at_y),
            ]
        elif stage == 1:
            moves = [(self.part(unit).at[:, :, :, 1 - p.c], core, at_core)]
        elif stage == 2:
            moves = [
                (core.at[:, :, 1 - p.y, :HALF], side.at[0], at_y),
                (core.at[:, 1 - p.x, :, HALF:], side.at[1], at_x),
            ]
        elif stage == 3:
            moves = [
                (side.at[0, :, 1 - p.x], corner.at[0], at_x),
                (side.at[1, :, 1 - p.y], corner.at[1], at_y),
            ]
        else:
            moves = [
                (corner.at[:, p.far(k)], distant.at[k - 1], p.at(z=p.far(k))) for k in (1, 2, 3)
            ]
        return self.made(unit, stage, moves)

    def begin(self, unit, stage):
        super().begin(unit, stage)
        if stage == 1:
            self.own_copy(unit).start()
            assert self.slots[unit] not in self.loaded
            self.loaded.append(self.slots[unit])

    def combine(self, unit, stage):
        p = self.place
        core, side, corner, distant = self.buffers(unit)

        def plus(left, right):
            return (left.astype(F32) + right.astype(F32)).astype(BF16)

        def from_core(step):
            z, x, y = step // 4, step // 2 % 2, step % 2
            core[z, x, y] = plus(core[z, x, y], self.own[self.slots[unit], z, x, y])

        def from_side(step):
            z, b = step // 2, step % 2
            side[0, z, b] = plus(side[0, z, b], core[z, b, p.y, :HALF])
            side[1, z, b] = plus(side[1, z, b], core[z, p.x, b, HALF:])

        def from_corner(z):
            corner[0, z] = plus(corner[0, z], side[0, z, p.x])
            corner[1, z] = plus(corner[1, z], side[1, z, p.y])

        def from_far(half):
            total = corner[half, p.z].astype(F32)
            for k in range(3):
                total = total + distant[k, half].astype(F32)
            self.store(unit, half, total)

        def aside_far(step):
            x, y = step // 2, step % 2
            total = core[p.z, x, y].astype(F32)
            for k in range(3):
                total = total + distant[k, x, y].astype(F32)
            core[p.z, x, y] = total.astype(BF16)

        def aside_side(b):
            side[0, 0, b] = plus(side[0, 0, b], core[p.z, b, p.y, :HALF])
            side[1, 0, b] = plus(side[1, 0, b], core[p.z, p.x, b, HALF:])

        if unit in self.aside and stage == 4:
            for part, own in enumerate((p.x, p.y)):
                total = side[part, 0, own].astype(F32) + side[part, 1, 0].astype(F32)
                self.store(unit, part, total)
            return
        steps = {1: (16, from_core), 2: (8, from_side), 3: (4, from_corner), 4: (2, from_far)}
        if unit in self.aside:
            steps |= {2: (4, aside_far), 3: (2, aside_side)}
        loop(*steps[stage])

    def step(self, unit, stage):
        if stage <= 0:
            self.begin(unit, max(1, -stage))
            return
        self.arrive(unit, stage)
        if stage == 1:
            self.own_copy(unit).wait()
        self.combine(unit, stage)
        if stage == 1:
            self.loaded.remove(self.slots[unit])
        if (unit, stage + 1) in self.first:
            self.begin(unit, stage + 1)


class Copies:
    def __init__(self, send, recv):
        self.send, self.recv, self.count = send, recv, 0

    def __call__(self, source, target, device):
        slot = self.count
        self.count += 1
        copy = pltpu.make_async_remote_copy(
            src_ref=source,
            dst_ref=target,
            send_sem=self.send.at[slot],
            recv_sem=self.recv.at[slot],
            device_id=device,
            device_id_type=MESH,
        )
        copy.start()
        return copy


class Refs:
    pass


def call(kernel, name, inputs, outputs, scratch, aliases=(), collective=None, grid=None, limit=58):
    names = list(inputs) + list(outputs)
    flat = []
    for value in scratch.values():
        flat += value if isinstance(value, list) else [value]

    def body(*refs):
        held = Refs()
        rest = list(refs)
        for key in names:
            setattr(held, key, rest.pop(0))
        for key, value in scratch.items():
            if isinstance(value, list):
                setattr(held, key, [rest.pop(0) for _ in value])
            else:
                setattr(held, key, rest.pop(0))
        kernel(held)

    extra = {} if grid is None else {"grid": grid}
    made = functools.partial(
        pl.pallas_call,
        body,
        in_specs=[spec for _, spec in inputs.values()],
        out_specs=[spec for _, spec in outputs.values()],
        out_shape=[out for out, _ in outputs.values()],
        scratch_shapes=flat,
        input_output_aliases={
            list(inputs).index(one): list(outputs).index(other) for one, other in aliases
        },
        compiler_params=params(collective, limit),
        name=name,
        **extra,
    )
    arrays = [array for array, _ in inputs.values()]
    if name == "start":
        result = made()(*arrays)
    else:
        result = made()(*arrays)
    out = Refs()
    for key, value in zip(outputs, result, strict=True):
        setattr(out, key, value)
    return out


def enter_norm(refs, pump=lambda: None):
    rows = 32
    for window in range(refs.mod.shape[0]):
        shift, scale = refs.mod[window, 0:1, :], refs.mod[window, 1:2, :]

        def step(index, window=window, shift=shift, scale=scale):
            at = pl.ds(pl.multiple_of(window * WIN + index * rows, rows), rows)
            normal, _ = centered(refs.tokens[at, :].astype(F32))
            refs.normed[at, :] = (normal * (1.0 + scale) + shift).astype(BF16)

        loop(WIN // rows, step)
        pump()


def enter_unit(refs, j, held, put=False):
    unit = refs.units.at[0]
    fetch = pltpu.make_async_copy(held, unit, refs.fetches.at[0])
    fetch.start()
    fetch.wait()

    def project(index):
        refs.packed[j, :, half(index)] = dot(refs.normed[...], four_columns(unit, index)).astype(
            BF16
        )

    loop(2, project)
    if put:
        packed_copy(refs, j).start()


def normed_copy(refs):
    return pltpu.make_async_copy(refs.normed, refs.normed_out, refs.packed_sem.at[3])


def packed_copy(refs, j):
    return pltpu.make_async_copy(refs.packed.at[j], refs.packed_out.at[j], refs.packed_sem.at[j])


def enter_plain_kernel(refs):
    enter_norm(refs)
    for j in range(3):
        enter_unit(refs, j, refs.held.at[QKV + j])


def act_rows(refs, place):
    first = (place.y * 2 + place.c) * SHARE
    value = refs.condition[:, pl.ds(pl.multiple_of(first, SHARE), SHARE)]
    act = value / (1.0 + jnp.exp(-value))
    return jnp.concatenate([act, jnp.zeros((8 - value.shape[0], SHARE), F32)], axis=0).astype(BF16)


def enter_layout(refs):
    windows, clips = refs.member.shape[0], refs.condition.shape[0]
    frames = [refs.frames[clip] for clip in range(clips)]
    starts = [0]
    for count in frames:
        starts.append(starts[-1] + 1 + jnp.where(count > WT, 1, 0))
    device = lax.axis_index("dp") * lax.axis_size("fsdp") + lax.axis_index("fsdp")
    refs.member[...] = jnp.zeros_like(refs.member)
    for window in range(windows):
        slab = (device * windows + window) // SPW
        live = 0
        for clip in range(clips):
            mine = starts[clip] <= slab
            if clip < clips - 1:
                mine = mine & (slab < starts[clip + 1])
            inner = frames[clip] - WT * (slab - starts[clip])
            live = live + jnp.where(mine, jnp.minimum(inner, WT), 0)
            refs.member[window, clip : clip + 1, :] = jnp.full(
                (1, LANES), jnp.where(mine, 1.0, 0.0), F32
            )
        refs.live[window] = live


def enter_table(refs):
    refs.rows[...] = jnp.zeros_like(refs.rows)
    table = refs.rel_table[...].astype(F32)
    for head in range(2):
        for frame in range(FRAMES):
            first = (FRAMES - 1 - frame) * OFFSETS
            row = head * (SPREAD // WSIDE) + frame
            refs.rows[row : row + 1, :OFFSETS] = table[head : head + 1, first : first + OFFSETS]
    shape_of = (TILE, WSIDE * LANES)
    offset = lax.broadcasted_iota(jnp.int32, shape_of, 0)
    place = lax.broadcasted_iota(jnp.int32, shape_of, 1)
    own, row, other = place // LANES, place // WSIDE % (LANES // WSIDE), place % WSIDE
    side_span = 2 * WSIDE - 1
    row_diff, col_diff = side_span - 1 - row, own - other + (WSIDE - 1)
    same = (row < side_span) & (row_diff * side_span + col_diff == offset)
    spread = dot(refs.rows[...].astype(BF16), jnp.where(same, 1.0, 0.0).astype(BF16))
    count = 2 * SPREAD // WSIDE
    for own in range(WSIDE):
        refs.spread[pl.ds(own, count, stride=WSIDE), :] = spread[
            :count, own * LANES : (own + 1) * LANES
        ]
    for head in range(2):
        refs.table_own[head] = refs.spread[head * SPREAD : (head + 1) * SPREAD, :].astype(BF16)


def enter(refs, place, work):
    place.greet(ALONG_ZX + ALONG_YC)
    z, x, y, c = place.z, place.x, place.y, place.c
    small = Copies(*refs.small)
    mods = dot(act_rows(refs, place), refs.ada[...])
    mods = mods + jnp.where((y == 0) & (c == 0), 1.0, 0.0) * refs.bias_in[...].astype(F32)
    for block in range(6):
        refs.mod_part[block * CLIP_ROWS : (block + 1) * CLIP_ROWS, :] = mods[
            :CLIP_ROWS, block * LANES : (block + 1) * LANES
        ]
    refs.mod_parts[y, c] = refs.mod_part[...]
    parts = [
        small(refs.mod_part, refs.mod_parts.at[y, c], place.shifted(*change)) for change in ALONG_YC
    ]
    own = []
    for unit in range(UNITS):
        if unit < OUT:
            first = picked(z * 2 + x, unit) * LANES
            refs.own[unit] = refs.qkv[:, pl.ds(pl.multiple_of(first, LANES), LANES)]
        elif unit >= DOWN:
            first = (unit - DOWN) * LANES
            for half in range(2):
                at = slice(half * 512 + first, half * 512 + first + LANES)
                refs.own[unit, half * HALF : (half + 1) * HALF] = refs.down[at, :]
        else:
            source, start = (refs.out, OUT) if unit < UP else (refs.up, UP)
            first = (unit - start) * LANES
            refs.own[unit] = source[:, first : first + LANES]
        own.append(
            pltpu.make_async_copy(
                refs.own.at[unit], refs.held.at[unit, z, x, y, c], refs.own_sem.at[unit]
            )
        )
        own[-1].start()
    points = list(ENTER)

    loaded = []

    def load(unit):
        if unit not in loaded:
            own[unit].wait()
            loaded.append(unit)

    def tick():
        for index, stage in points.pop(0):
            if stage == 1:
                load(ORDER[index])
            work.advance(ORDER[index], stage)

    tick()
    enter_layout(refs)
    enter_table(refs)
    refs.table[z, x, c] = refs.table_own[c]
    for copy in parts:
        copy.wait()
    refs.mods[z, x] = (
        refs.mod_parts[0, 0] + refs.mod_parts[0, 1] + refs.mod_parts[1, 0] + refs.mod_parts[1, 1]
    )
    mods = [
        small(refs.mods.at[z, x], refs.mods.at[z, x], place.shifted(*change))
        for change in ALONG_ZX
    ]
    for unit in range(UNITS):
        load(unit)
    tick()
    for copy in mods:
        copy.wait()
    tables = [
        small(refs.table.at[z, x, c], refs.table.at[z, x, c], place.shifted(*change))
        for change in ALONG_ZX
    ]
    for window in range(refs.mod.shape[0]):
        for block in range(48):
            which, column = divmod(block, 8)
            first = block % 6 * CLIP_ROWS
            part = refs.mods[block // 12, block // 6 % 2, first : first + CLIP_ROWS, :]
            refs.mod[window, which : which + 1, column * LANES : (column + 1) * LANES] = jnp.sum(
                part * refs.member[window], axis=0, keepdims=True
            )
    tick()
    enter_norm(refs, tick)
    normed_copy(refs).start()
    for copy in tables:
        copy.wait()
    last = small(refs.table.at[:, :, c], refs.table.at[:, :, c], place.at(c=1 - c))
    work.arrive(QKV, 4)
    tick()
    enter_unit(refs, 0, refs.held.at[QKV], put=True)
    last.wait()


def attend_pair(refs, table, part, put):
    for head in range(2):
        spread = table(head).astype(F32)
        for frame in range(FRAMES):
            block = spread[frame * WSIDE : (frame + 1) * WSIDE]
            for row in range(WSIDE):
                first = (WSIDE - 1 - row) * WSIDE
                refs.strip[
                    head, row * WSIDE : (row + 1) * WSIDE, frame * CELLS : (frame + 1) * CELLS
                ] = block[:, first : first + CELLS]
        for frame in range(WT):
            first = (WT - 1 - frame) * CELLS
            refs.bias[head, frame * CELLS : (frame + 1) * CELLS, :] = refs.strip[
                head, :, first : first + WIN
            ]
    for window in range(refs.live.shape[0]):
        rows = slice(window * WIN, (window + 1) * WIN)
        live = refs.live[window] * CELLS
        key_live = lax.broadcasted_iota(jnp.int32, (1, WIN), 1) < live
        query, key, value = (part(which, rows) for which in range(3))
        mixed = []
        for head in range(2):
            lanes = slice(head * HD, (head + 1) * HD)
            scores = dot_rows(query[:, lanes] * BF16(HD ** (-0.5)), key[:, lanes]) + refs.bias[head]
            scores = jnp.where(key_live, scores, NEGATIVE)
            shifted = jnp.exp(scores - jnp.max(scores, axis=-1, keepdims=True))
            totals = jnp.sum(shifted, axis=-1, keepdims=True)
            probs = (shifted * (1.0 / totals)).astype(BF16)
            refs.probs[window, head] = probs
            mixed.append(dot(probs, value[:, lanes]).astype(BF16))
        put(rows, jnp.concatenate(mixed, axis=1))


def attend_plain_kernel(refs):
    sources = (refs.query, refs.key, refs.value)

    def put(rows, values):
        refs.mixed[rows, :] = values

    attend_pair(
        refs, lambda head: refs.table[head], lambda which, rows: sources[which][rows, :], put
    )


def start_kernel(refs):
    step = pl.program_id(0)
    pairs = H // 2
    place = Place()
    work = Gather(place, refs.held, gather_stages(ENTER + tuple(ATTEND.values())), refs.gather)

    @pl.when(step == 0)
    def _():
        enter(refs, place, work)

    for at in range(pairs):

        @pl.when(step == at + 1)
        def _(at=at):
            for index, stage in ATTEND.get(at, ()):
                work.advance(ORDER[index], stage)
            if at in (2, 4):
                work.arrive(QKV + at // 2, 4)
                enter_unit(refs, at // 2, refs.held.at[QKV + at // 2], put=True)

    @pl.when((step > 0) & (step <= pairs))
    def _():
        pair = forward_pair(jnp.clip(step - 1, 0, pairs - 1))

        def columns(block):
            return pl.ds(pl.multiple_of(block * LANES, LANES), LANES)

        def part(which, rows):
            return refs.packed[pair_unit(which, pair), rows, columns(pair_block(which, pair))]

        def table(head):
            return refs.table[pair // 2, pair % 2, head]

        def put(rows, values):
            refs.mixed[rows, columns(pair)] = values

        attend_pair(refs, table, part, put)

    @pl.when(step == pairs)
    def _():
        for j in range(3):
            packed_copy(refs, j).wait()
        normed_copy(refs).wait()
        mixed = pltpu.make_async_copy(refs.mixed, refs.mixed_out, refs.packed_sem.at[4])
        mixed.start()
        mixed.wait()
        work.finish()


def packed_block(which, rows, pair):
    return pl.BlockSpec(
        (None, rows, LANES),
        lambda step: (pair_unit(which, pair(step)), 0, pair_block(which, pair(step))),
    )


def attend_back_pair(refs, pair):
    scale = BF16(HD ** (-0.5))
    refs.spread[...] = jnp.zeros_like(refs.spread)
    refs.strip[...] = jnp.zeros_like(refs.strip)
    windows = refs.probs.shape[0]
    results = [[[None] * windows for _ in range(2)] for _ in range(3)]
    for head in range(2):
        lanes = slice(head * HD, (head + 1) * HD)
        bias = None
        for window in range(windows):
            rows = slice(window * WIN, (window + 1) * WIN)
            grad = refs.grad[rows, lanes]
            probs = refs.probs[window, head]
            results[2][head][window] = dot_tokens(grad, probs).T.astype(BF16)
            grad_probs = dot_rows(grad, refs.value[rows, lanes])
            weight = probs.astype(F32)
            product = weight * grad_probs
            total = jnp.sum(product, axis=-1, keepdims=True)
            grad_scores = (product - weight * total).astype(BF16)
            wide = grad_scores.astype(F32)
            bias = wide if bias is None else bias + wide
            results[0][head][window] = dot(grad_scores, refs.key[rows, lanes] * scale).astype(BF16)
            query = refs.query[rows, lanes] * scale
            results[1][head][window] = dot_tokens(query, grad_scores).T.astype(BF16)
        for frame in range(WT):
            first = (WT - 1 - frame) * CELLS
            refs.strip[head, :, first : first + WIN] += bias[frame * CELLS : (frame + 1) * CELLS]
        for frame in range(FRAMES):
            for row in range(WSIDE):
                first = (WSIDE - 1 - row) * WSIDE
                refs.spread[
                    head, frame * WSIDE : (frame + 1) * WSIDE, first : first + CELLS
                ] += refs.strip[
                    head, row * WSIDE : (row + 1) * WSIDE, frame * CELLS : (frame + 1) * CELLS
                ]
    for part in range(3):
        lanes = pl.ds(pl.multiple_of(pair_block(part, pair) * LANES, LANES), LANES)
        for window in range(windows):
            rows = slice(window * WIN, (window + 1) * WIN)
            both = [results[part][head][window] for head in range(2)]
            refs.grad_packed[pair_unit(part, pair), rows, lanes] = jnp.concatenate(both, axis=1)


def middle(refs, place=None, gathering=None):
    order = [OUT] + [unit for j in range(4) for unit in (UP + j, DOWN + j)] + [OUT]
    activated, grad_hidden, grad_low = (refs.packed.at[index] for index in range(3))
    reducing = None
    points = {}
    waiting = set()
    if gathering is not None:

        def buffers(unit):
            index = EARLY.index(unit)
            core, side = refs.core.at[index], refs.side.at[index]
            if unit not in DONE:
                return core, side, None, None
            if unit in REDUCE_ASIDE:
                return core, side, None, refs.aside.at[0]
            return core, side, refs.corner.at[index], refs.distant.at[index]

        def store(unit, part, values):
            at = pl.ds(pl.multiple_of(part * HALF, HALF), HALF)
            refs.total[DONE.index(unit), at, :] = values

        reducing = Reduce(
            place, lambda unit: refs.part.at[unit], EARLY_POINTS, store, buffers, refs.reduce
        )
        for stages in MIDDLE.values():
            waiting |= {ORDER[index] for index, stage in stages if stage == 4}
        points = {at: list(moves) for at, moves in EARLY_POINTS.items()}

    count = [0]

    def pump():
        for index, stage in MIDDLE.get(count[0], ()) if gathering is not None else ():
            gathering.advance(ORDER[index], stage)
            if stage == 4:
                waiting.discard(ORDER[index])
        for unit, stage in points.pop(count[0], ()):
            reducing.step(unit, stage)
        count[0] += 1

    def fetch(step):
        return pltpu.make_async_copy(
            refs.held.at[order[step]], refs.units.at[step % 4], refs.fetches.at[step % 4]
        )

    def start_fetch(step):
        if gathering is not None:
            assert order[step] not in waiting
            gathering.arrive(order[step], 4)
        fetch(step).start()

    def put(slot, unit):
        return pltpu.make_async_copy(refs.made.at[slot], refs.part.at[unit], refs.made_sem.at[slot])

    for step in range(3):
        start_fetch(step)
    pump()
    refs.sums[...] = jnp.zeros_like(refs.sums)
    refs.mlp[...] = jnp.zeros_like(refs.mlp)
    refs.grad_normed[...] = jnp.zeros_like(refs.grad_normed)
    fetch(0).wait()

    def project(index):
        refs.attended[:, half(index)] = dot(refs.mixed[...], four_columns(refs.units.at[0], index))

    loop(2, project)
    pump()

    def modulate(window, at, mods, live):
        middle = refs.tokens[at, :].astype(F32) + mods[2] * refs.attended[at, :]
        normal, _ = centered(middle)
        refs.normed[at, :] = (normal * (1.0 + mods[4]) + mods[3]).astype(BF16)
        grad = jnp.where(live, refs.cotangent[at, :].astype(F32), 0.0)
        grad_low[at, :] = (mods[5] * grad).astype(BF16)

    each_rows(refs.mod, refs.live, modulate)
    pump()
    for j in range(4):
        step = 1 + 2 * j
        up, down = refs.units.at[step % 4], refs.units.at[(step + 1) % 4]
        fetch(step).wait()
        fetch(step + 1).wait()
        start_fetch(step + 2)

        def hide(index, up=up, down=down):
            hidden = dot(refs.normed[...], four_columns(up, index))
            bend = jnp.tanh(0.7978845608028654 * (hidden + 0.044715 * hidden * hidden * hidden))
            activated[:, half(index)] = (0.5 * hidden * (1.0 + bend)).astype(BF16)
            slope = 0.5 * (1.0 + bend) + 0.5 * hidden * (1.0 - bend * bend) * (
                0.7978845608028654 * (1.0 + 3.0 * 0.044715 * hidden * hidden)
            )
            grad_activated = dot_rows(grad_low[...], half_rows(down, index))
            grad_hidden[:, half(index)] = (grad_activated * slope).astype(BF16)

        loop(2, hide)
        if j > 0:
            put(1, UP + j - 1).wait()
        pump()

        def down_gradient(index):
            made = dot_tokens(activated[:, half(index)], grad_low[...]).astype(BF16)
            for block in range(8):
                refs.made[0, block // 2, block % 2, index] = made[
                    :, block * LANES : (block + 1) * LANES
                ].reshape(2, SHARE, LANES)

        loop(2, down_gradient)
        put(0, DOWN + j).start()
        pump()

        def up_gradient(index):
            made = dot_tokens(refs.normed[...], grad_hidden[:, half(index)]).astype(BF16)
            put_columns(refs.made.at[1], index, made)

        loop(2, up_gradient)
        put(0, DOWN + j).wait()
        put(1, UP + j).start()
        pump()
        if j < 3:
            start_fetch(step + 3)

        def out_of_mlp(index, up=up, down=down):
            refs.mlp[:, half(index)] += dot(activated[...], four_columns(down, index))
            refs.grad_normed[:, half(index)] += dot_rows(
                grad_hidden[...], half_rows(up, index)
            )

        loop(2, out_of_mlp)
        pump()

    put(1, UP + 3).wait()

    def join(window, at, mods, live):
        attended = refs.attended[at, :]
        middle = refs.tokens[at, :].astype(F32) + mods[2] * attended
        normal, root = centered(middle)
        mlp = refs.mlp[at, :]
        refs.normed[at, :] = jnp.where(live, middle + mods[5] * mlp, 0.0).astype(BF16)
        grad_result = jnp.where(live, refs.cotangent[at, :].astype(F32), 0.0)
        grad_normed = refs.grad_normed[at, :]
        grad_middle = grad_result + norm_back(grad_normed, normal, root, mods[4])
        refs.mlp[at, :] = grad_middle
        grad_low[at, :] = (mods[2] * grad_middle).astype(BF16)
        add_sums(refs.sums, window, 2, grad_middle * attended)
        add_sums(refs.sums, window, 3, grad_normed)
        add_sums(refs.sums, window, 4, grad_normed * normal)
        add_sums(refs.sums, window, 5, grad_result * mlp)

    each_rows(refs.mod, refs.live, join)
    results = [
        pltpu.make_async_copy(source, target, refs.result_sem.at[index])
        for index, (source, target) in enumerate(
            (
                (refs.normed, refs.output),
                (refs.mlp, refs.grad_middle),
                (activated, refs.grad_mixed),
            )
        )
    ]
    results[0].start()
    results[1].start()
    pump()
    fetch(9).wait()

    def back(index):
        made = dot_tokens(refs.mixed[...], grad_low[:, half(index)]).astype(BF16)
        put_columns(refs.made.at[0], index, made)
        activated[:, half(index)] = dot_rows(
            grad_low[...], half_rows(refs.units.at[1], index)
        ).astype(BF16)

    loop(2, back)
    results[2].start()
    put(0, OUT).start()
    put(0, OUT).wait()
    while points:
        pump()
    for index, unit in enumerate(EARLY if gathering is not None else ()):
        if unit not in DONE:

            def keep(z, index=index):
                for part in range(2):
                    refs.side_out[index - len(DONE), part, z] = refs.side[index, part, z]

            loop(4, keep)
    for copy in results:
        copy.wait()
    if gathering is not None:
        gathering.finish()
        reducing.sent()


def middle_kernel(refs):
    place = Place()
    place.greet()
    middle(refs, place, Gather(place, refs.held, gather_stages(MIDDLE.values()), refs.gather))


def leave_weight(refs, j, made):
    def weight(index):
        grad = dot_tokens(refs.normed[...], refs.grad_packed[j, :, half(index)]).astype(BF16)
        put_columns(made, index, grad)

    loop(2, weight)


def leave_back(refs, j):
    def back(index):
        refs.grad_normed[:, half(index)] += dot_rows(
            refs.grad_packed[j], half_rows(refs.unit, index)
        )

    loop(2, back)


def leave_norm(refs, pump=lambda window: None):
    def join(window, at, mods, live):
        normal, root = centered(refs.tokens[at, :].astype(F32))
        grad_normed = refs.grad_normed[at, :]
        refs.grad_tokens[at, :] = refs.grad_middle[at, :] + norm_back(
            grad_normed, normal, root, mods[1]
        )
        add_sums(refs.sums, window, 0, grad_normed)
        add_sums(refs.sums, window, 1, grad_normed * normal)

    each_rows(refs.mod, refs.live, join, pump=pump)


def back_plain_kernel(refs):
    step = pl.program_id(0)

    @pl.when(step < H // 2)
    def _():
        attend_back_pair(refs, backward_pair(jnp.minimum(step, H // 2 - 1)))

    @pl.when(step == H // 2)
    def _():
        refs.sums[...] = jnp.zeros_like(refs.sums)
        refs.grad_normed[...] = jnp.zeros_like(refs.grad_normed)
        for j in range(3):
            fetch = pltpu.make_async_copy(refs.held.at[QKV + j], refs.unit, refs.fetch)
            fetch.start()
            leave_weight(refs, j, refs.made)
            put = pltpu.make_async_copy(refs.made, refs.part.at[j], refs.made_sem)
            put.start()
            fetch.wait()
            leave_back(refs, j)
            put.wait()
        leave_norm(refs)


def fold_spreads(refs):
    heads = H * WIDE // WSIDE
    shape_of = (WSIDE * LANES, TILE)
    place = lax.broadcasted_iota(jnp.int32, shape_of, 0)
    offset = lax.broadcasted_iota(jnp.int32, shape_of, 1)
    own, row, other = place // LANES, place // WSIDE % (LANES // WSIDE), place % WSIDE
    side_span = 2 * WSIDE - 1
    row_diff, col_diff = side_span - 1 - row, own - other + (WSIDE - 1)
    same = (row < side_span) & (row_diff * side_span + col_diff == offset)
    onto = jnp.where(same, 1.0, 0.0).astype(BF16)
    left = jnp.concatenate(
        [refs.spreads[pl.ds(own, heads, stride=WSIDE), :] for own in range(WSIDE)], axis=1
    )
    total = jnp.zeros((heads, TILE), F32)
    for _ in range(3):
        low = left.astype(BF16)
        total = total + dot(low, onto)
        left = left - low.astype(F32)
    rows = 2 * WIDE // WSIDE
    for block in range(8):
        refs.table[block // 2, block % 2] = total[block * rows : (block + 1) * rows]


def back_kernel(refs):
    place = Place()
    z, x, y, c = place.z, place.x, place.y, place.c
    step = pl.program_id(0)

    def buffers(unit):
        every = (EARLY + LATE).index(unit)
        late = every - len(EARLY)
        assert unit not in DONE
        if late < 0:
            core, side = None, refs.side_in.at[every - len(DONE)]
        else:
            core, side = refs.core.at[late], refs.side.at[late]
        if unit in REDUCE_ASIDE:
            return core, side, None, refs.aside.at[0]
        return core, side, refs.corner.at[every], refs.distant.at[every]

    def store(unit, part, values):
        if unit >= DOWN:
            first = part * 512 + (unit - DOWN) * LANES
            refs.grad_down[pl.ds(pl.multiple_of(first, LANES), LANES), :] = values
            return
        at = pl.ds(pl.multiple_of(part * HALF, HALF), HALF)
        if unit < OUT:
            column = picked(z * 2 + x, unit) * LANES
            refs.grad_qkv[at, pl.ds(pl.multiple_of(column, LANES), LANES)] = values
            return
        target, start = (refs.grad_out, OUT) if unit < UP else (refs.grad_up, UP)
        column = (unit - start) * LANES
        target[at, column : column + LANES] = values

    work = Reduce(
        place,
        lambda unit: refs.made.at[unit] if unit < OUT else refs.part.at[unit],
        LATE_POINTS,
        store,
        buffers,
        refs.reduce,
    )
    small = Copies(*refs.small)

    events = [(at, move) for at in sorted(LATE_POINTS) for move in LATE_POINTS[at]]

    def run(until):
        while events and events[0][0] < until:
            work.step(*events.pop(0)[1])

    for number in range(H // 2):

        @pl.when(step == number)
        def _(number=number):
            if number == 0:
                place.greet(EVERYONE)
            if number in (3, 6):
                leave_weight(refs, number // 3 - 1, refs.made.at[number // 3 - 1])
            run(number + 1)

    @pl.when(step < H // 2)
    def _():
        pair = backward_pair(jnp.minimum(step, H // 2 - 1))
        attend_back_pair(refs, pair)
        for head in range(2):
            at = pl.ds(pl.multiple_of((pair * 2 + head) * WIDE, WIDE), WIDE)
            refs.spreads[at, :] = refs.spread[head]

    @pl.when(step == H // 2)
    def _():
        for index, unit in enumerate(DONE):
            for part in range(2):
                store(unit, part, refs.done[index, part * HALF : (part + 1) * HALF, :])
        fold_spreads(refs)
        table = []
        for dz, dx, dy, dc in ALONG_ZX:
            source = refs.table.at[place.far(dz), 1 - x if dx else x]
            table.append(small(source, refs.table_zx.at[z, x], place.shifted(dz, dx, dy, dc)))
        refs.table_zx[z, x] = refs.table[z, x]
        refs.sums[...] = refs.late_sums[...]
        refs.grad_normed[...] = jnp.zeros_like(refs.grad_normed)

        def fetch(j):
            return pltpu.make_async_copy(refs.held.at[QKV + j], refs.unit, refs.fetch)

        fetch(0).start()
        leave_weight(refs, 2, refs.made.at[2])
        run(12)
        fetch(0).wait()
        leave_back(refs, 0)
        fetch(1).start()
        run(13)
        fetch(1).wait()
        leave_back(refs, 1)
        fetch(2).start()
        run(14)
        fetch(2).wait()
        leave_back(refs, 2)
        run(15)
        leave_norm(refs, lambda window: run(17 + window))
        for copy in table:
            copy.wait()
        total = refs.table_zx[0, 0]
        for block in range(1, 8):
            total = total + refs.table_zx[block // 2, block % 2]
        refs.table_own[...] = total
        refs.table_yc[y, c] = total
        table = [
            small(refs.table_own, refs.table_yc.at[y, c], place.shifted(*change))
            for change in ALONG_YC
        ]
        for block in range(48):
            which, column = divmod(block, 8)
            part = jnp.zeros((CLIP_ROWS, LANES), F32)
            for window in range(refs.mod.shape[0]):
                sums = refs.sums[window, which : which + 1, column * LANES : (column + 1) * LANES]
                part = part + refs.member[window] * sums
            first = block % 6 * CLIP_ROWS
            refs.clip[block // 12, block // 6 % 2, first : first + CLIP_ROWS, :] = part
        copies = []
        for dz, dx, dy, dc in ALONG_ZX:
            source = refs.clip.at[place.far(dz), 1 - x if dx else x]
            copies.append(small(source, refs.clip_zx.at[z, x], place.shifted(dz, dx, dy, dc)))
        refs.clip_zx[z, x] = refs.clip[z, x]
        run(19)
        for copy in copies:
            copy.wait()
        total = refs.clip_zx[0, 0]
        for block in range(1, 8):
            total = total + refs.clip_zx[block // 2, block % 2]
        refs.clip_own[...] = total
        refs.clip_yc[y, c] = total
        copies = [
            small(refs.clip_own, refs.clip_yc.at[y, c], place.shifted(*change))
            for change in ALONG_YC
        ]
        run(21)
        for copy in copies:
            copy.wait()
        total = refs.clip_yc[0, 0] + refs.clip_yc[0, 1] + refs.clip_yc[1, 0] + refs.clip_yc[1, 1]
        total = jnp.concatenate([total, jnp.zeros((8, LANES), F32)], axis=0)
        cond = jnp.zeros((8, SHARE), F32)
        lows = []
        for block in range(6):
            lows.append(total[block * CLIP_ROWS : block * CLIP_ROWS + 8].astype(BF16))
            lanes = slice(block * LANES, (block + 1) * LANES)
            cond = cond + dot_rows(lows[-1], refs.ada[:, lanes])
        clips = refs.condition.shape[0]
        refs.cond_own[...] = jnp.zeros_like(refs.cond_own)
        for row in range(2 * clips):
            clip, side = divmod(row, 2)
            refs.cond_own[row : row + 1, :] = cond[
                clip : clip + 1, side * LANES : (side + 1) * LANES
            ]
        refs.cond_all[z, x, y, c] = refs.cond_own[...]
        copies = [
            small(refs.cond_own, refs.cond_all.at[z, x, y, c], place.shifted(*change))
            for change in EVERYONE
        ]
        for block, low in enumerate(lows):
            lanes = slice(block * LANES, (block + 1) * LANES)
            refs.grad_ada[:, lanes] = dot_tokens(act_rows(refs, place), low)
            refs.grad_bias[block : block + 1, :] = jnp.sum(
                low[:CLIP_ROWS].astype(F32), axis=0, keepdims=True
            )
        run(23)
        for copy in table:
            copy.wait()
        total = refs.table_yc[0, 0] + refs.table_yc[0, 1] + refs.table_yc[1, 0] + refs.table_yc[1, 1]
        for head in range(2):
            for frame in range(FRAMES):
                first = (FRAMES - 1 - frame) * OFFSETS
                row = head * (WIDE // WSIDE) + frame
                refs.table_total[head : head + 1, first : first + OFFSETS] = total[
                    row : row + 1, :OFFSETS
                ]
        run(100)
        for copy in copies:
            copy.wait()
        for block in range(4):
            total = refs.cond_all[0, 0, block // 2, block % 2]
            for other in range(1, 8):
                total = total + refs.cond_all[other // 2, other % 2, block // 2, block % 2]
            for row in range(2 * clips):
                clip, side = divmod(row, 2)
                first = block * SHARE + side * LANES
                value = refs.condition[clip : clip + 1, first : first + LANES]
                gate = 1.0 / (1.0 + jnp.exp(-value))
                refs.grad_condition[clip : clip + 1, first : first + LANES] = (
                    total[row : row + 1] * gate * (1.0 + value * (1.0 - gate))
                )
        work.sent()


def enter_plain(tokens, held, mod):
    rows = tokens.shape[0]
    inputs = {"tokens": (tokens, vmem()), "held": (held, anywhere()), "mod": (mod, vmem())}
    outputs = {
        "normed": (shape(BF16, rows, D), vmem()),
        "packed": (shape(BF16, 3, rows, D), vmem()),
    }
    scratch = {
        "units": pltpu.VMEM((1, *SPLIT), BF16),
        "fetches": pltpu.SemaphoreType.DMA((1,)),
    }
    return call(enter_plain_kernel, "enter_plain", inputs, outputs, scratch)


def whole(array):
    return pl.BlockSpec(
        array.shape, lambda p: (0,) * len(array.shape), pipeline_mode=pl.Buffered(1)
    )


def result(dtype, *sizes):
    made = shape(dtype, *sizes)
    return made, whole(made)


def attend_probs(windows, first):
    def pair(step):
        return forward_pair(jnp.clip(step - first, 0, H // 2 - 1))

    return (
        shape(BF16, windows, H, WIN, WIN),
        pl.BlockSpec((windows, 2, WIN, WIN), lambda p: (0, pair(p), 0, 0)),
    )


def attend_scratch():
    return {"strip": pltpu.VMEM((2, CELLS, STRIP), F32), "bias": pltpu.VMEM((2, WIN, WIN), F32)}


def middle_outputs(rows):
    return {
        "output": (shape(BF16, rows, D), anywhere()),
        "grad_middle": (shape(F32, rows, D), anywhere()),
        "grad_mixed": (shape(BF16, rows, D), anywhere()),
        "sums": (shape(F32, rows // WIN, 8, D), vmem()),
        "part": (shape(BF16, UNITS, *SPLIT), anywhere()),
    }


def middle_scratch(rows):
    return {
        "units": pltpu.VMEM((4, *SPLIT), BF16),
        "attended": pltpu.VMEM((rows, D), F32),
        "normed": pltpu.VMEM((rows, D), BF16),
        "result_sem": pltpu.SemaphoreType.DMA((3,)),
        "mlp": pltpu.VMEM((rows, D), F32),
        "grad_normed": pltpu.VMEM((rows, D), F32),
        "packed": pltpu.VMEM((3, rows, D), BF16),
        "made": pltpu.VMEM((2, *SPLIT), BF16),
        "fetches": pltpu.SemaphoreType.DMA((4,)),
        "made_sem": pltpu.SemaphoreType.DMA((2,)),
    }


def centre(special, live_frames, tokens, cotangent, mixed, mod, held):
    rows = tokens.shape[0]
    inputs = {
        name: (array, vmem())
        for name, array in (
            ("tokens", tokens),
            ("cotangent", cotangent),
            ("mixed", mixed),
            ("mod", mod),
        )
    }
    inputs["live"] = (live_frames, smem())
    outputs, scratch = middle_outputs(rows), middle_scratch(rows)
    if not special:
        inputs["held"] = (held, anywhere())
        return call(middle, "middle_plain", inputs, outputs, scratch, limit=60)
    inputs["held_in"] = (held, anywhere())
    outputs |= {
        "held": (shape(BF16, UNITS, *SPLIT), anywhere()),
        "side_out": (shape(BF16, *Reduce.side_shape(len(EARLY) - len(DONE))), vmem()),
        "total": (shape(F32, len(DONE), SHARE, LANES), vmem()),
    }
    scratch |= {
        "core": pltpu.VMEM(Reduce.core_shape(len(EARLY)), BF16),
        "side": pltpu.VMEM(Reduce.side_shape(len(EARLY)), BF16),
        "corner": pltpu.VMEM(Reduce.corner_shape(len(DONE)), BF16),
        "distant": pltpu.VMEM(Reduce.distant_shape(len(DONE)), BF16),
        "aside": pltpu.VMEM(Reduce.aside_shape(1), BF16),
        "reduce": Reduce.scratch(EARLY_POINTS),
        "gather": Gather.semaphores(gather_stages(MIDDLE.values())),
    }
    return call(
        middle_kernel,
        "middle",
        inputs,
        outputs,
        scratch,
        (("held_in", "held"),),
        collective=2,
        limit=60,
    )


def begin(tokens, own, smalls):
    rows = tokens.shape[0]
    windows = rows // WIN
    inputs = {"tokens": (tokens, whole(tokens))}
    for name, block in zip(("qkv", "out", "up", "down"), own, strict=True):
        inputs[name] = (block, whole(block))
    for name, array in zip(("condition", "ada", "bias_in", "rel_table"), smalls[1:], strict=True):
        inputs[name] = (array, whole(array))
    inputs["frames"] = (smalls[0], smem())
    outputs = {
        "probs": attend_probs(windows, 1),
        "mixed_out": (shape(BF16, rows, D), anywhere()),
        "normed_out": (shape(BF16, rows, D), anywhere()),
        "packed_out": (shape(BF16, 3, rows, D), anywhere()),
        "held": (shape(BF16, UNITS, *SPLIT), anywhere()),
        "mod": result(F32, windows, 8, D),
        "member": result(F32, windows, CLIP_ROWS, LANES),
        "live": (shape(jnp.int32, windows), smem()),
    }
    stages = gather_stages(ENTER + tuple(ATTEND.values()))
    scratch = attend_scratch() | {
        "units": pltpu.VMEM((1, *SPLIT), BF16),
        "fetches": pltpu.SemaphoreType.DMA((1,)),
        "normed": pltpu.VMEM((rows, D), BF16),
        "packed": pltpu.VMEM((3, rows, D), BF16),
        "mixed": pltpu.VMEM((rows, D), BF16),
        "packed_sem": pltpu.SemaphoreType.DMA((5,)),
        "own": pltpu.VMEM((UNITS, SHARE, LANES), BF16),
        "own_sem": pltpu.SemaphoreType.DMA((UNITS,)),
        "gather": Gather.semaphores(stages),
        "small": [pltpu.SemaphoreType.DMA((18,))] * 2,
        "mod_part": pltpu.VMEM((MOD_ROWS, LANES), F32),
        "mod_parts": pltpu.VMEM((2, 2, MOD_ROWS, LANES), F32),
        "mods": pltpu.VMEM((4, 2, MOD_ROWS, LANES), F32),
        "rows": pltpu.VMEM((24, TILE), F32),
        "spread": pltpu.VMEM((2 * SPREAD, LANES), F32),
        "table_own": pltpu.VMEM((2, SPREAD, LANES), BF16),
        "table": pltpu.VMEM((4, 2, 2, SPREAD, LANES), BF16),
    }
    return call(
        start_kernel,
        "start",
        inputs,
        outputs,
        scratch,
        collective=0,
        grid=(H // 2 + 1,),
        limit=60,
    )


def deliver_kernel(refs):
    names = [name for name in vars(refs) if name.startswith("from_")]
    loads, stores = [], []
    for index, name in enumerate(names):
        plain = name[len("from_") :]
        held = getattr(refs, "held_" + plain)
        loads.append(pltpu.make_async_copy(getattr(refs, name), held, refs.sems.at[0, index]))
        stores.append(pltpu.make_async_copy(held, getattr(refs, plain), refs.sems.at[1, index]))
        loads[-1].start()
    for load, store in zip(loads, stores, strict=True):
        load.wait()
        store.start()
    for store in stores:
        store.wait()


def deliver(**arrays):
    inputs = {"from_" + name: (array, anywhere()) for name, array in arrays.items()}
    outputs = {name: (shape(array.dtype, *array.shape), anywhere()) for name, array in arrays.items()}
    scratch = {"held_" + name: pltpu.VMEM(array.shape, array.dtype) for name, array in arrays.items()}
    scratch["sems"] = pltpu.SemaphoreType.DMA((2, len(arrays)))
    return call(deliver_kernel, "deliver", inputs, outputs, scratch)


def attend_plain(packed, table, live_frames):
    windows = live_frames.shape[0]
    rows = windows * WIN
    inputs = {
        "live": (live_frames, smem()),
        "query": (packed, packed_block(0, rows, forward_pair)),
        "key": (packed, packed_block(1, rows, forward_pair)),
        "value": (packed, packed_block(2, rows, forward_pair)),
        "table": (table, pl.BlockSpec((2, SPREAD, LANES), lambda p: (forward_pair(p), 0, 0))),
    }
    return call(
        attend_plain_kernel,
        "attend_plain",
        inputs,
        {
            "mixed": (
                shape(BF16, rows, D),
                pl.BlockSpec((rows, LANES), lambda p: (0, forward_pair(p))),
            ),
            "probs": attend_probs(windows, 0),
        },
        attend_scratch(),
        grid=(H // 2,),
    )


def back(
    special, live_frames, tokens, mod, packed, normed, probs, mid, held, ada, member, condition
):
    window_count = probs.shape[0]
    rows = window_count * WIN
    pairs = H // 2

    def last(step):
        return backward_pair(jnp.minimum(step, pairs - 1))

    def packed_pair(which):
        return packed_block(which, rows, last)

    inputs = {
        "live": (live_frames, smem()),
        "query": (packed, packed_pair(0)),
        "key": (packed, packed_pair(1)),
        "value": (packed, packed_pair(2)),
        "probs": (
            probs,
            pl.BlockSpec((window_count, 2, WIN, WIN), lambda p: (0, last(p), 0, 0)),
        ),
        "grad": (mid.grad_mixed, pl.BlockSpec((rows, LANES), lambda p: (0, last(p)))),
        "held": (held, anywhere()),
    }
    for name, array in (
        ("tokens", tokens),
        ("mod", mod),
        ("normed", normed),
        ("grad_middle", mid.grad_middle),
    ):
        inputs[name] = (array, whole(array))

    outputs = {"grad_tokens": result(F32, rows, D)}
    scratch = {
        "strip": pltpu.VMEM((2, CELLS, STRIP), F32),
        "grad_packed": pltpu.VMEM((3, rows, D), BF16),
        "unit": pltpu.VMEM(SPLIT, BF16),
        "grad_normed": pltpu.VMEM((rows, D), F32),
        "fetch": pltpu.SemaphoreType.DMA,
    }
    if not special:
        outputs["sums"] = result(F32, window_count, 8, D)
        outputs["part"] = (shape(BF16, 3, *SPLIT), anywhere())
        outputs["spread"] = (
            shape(F32, H, SPREAD, LANES),
            pl.BlockSpec((2, SPREAD, LANES), lambda p: (last(p), 0, 0)),
        )
        scratch["made"] = pltpu.VMEM(SPLIT, BF16)
        scratch["made_sem"] = pltpu.SemaphoreType.DMA
        return call(
            back_plain_kernel, "back_plain", inputs, outputs, scratch, grid=(pairs + 1,)
        )
    inputs |= {
        "late_sums": (mid.sums, whole(mid.sums)),
        "ada": (ada, whole(ada)),
        "condition": (condition, whole(condition)),
        "member": (member, whole(member)),
        "side_in": (mid.side_out, whole(mid.side_out)),
        "done": (mid.total, whole(mid.total)),
        "part": (mid.part, anywhere()),
    }
    outputs |= {
        "grad_qkv": result(F32, SHARE, 3 * LANES),
        "grad_out": result(F32, SHARE, LANES),
        "grad_up": result(F32, SHARE, 4 * LANES),
        "grad_down": result(F32, 4 * SHARE, LANES),
        "grad_ada": result(F32, SHARE, 6 * LANES),
        "grad_bias": result(F32, 6, LANES),
        "grad_condition": result(F32, *condition.shape),
        "table_total": result(F32, 2, REL),
    }
    count, late = len(EARLY + LATE), len(LATE)
    scratch |= {
        "spread": pltpu.VMEM((2, WIDE, LANES), F32),
        "spreads": pltpu.VMEM((H * WIDE, LANES), F32),
        "made": pltpu.VMEM((3, *SPLIT), BF16),
        "sums": pltpu.VMEM((window_count, 8, D), F32),
        "core": pltpu.VMEM(Reduce.core_shape(late), BF16),
        "side": pltpu.VMEM(Reduce.side_shape(late), BF16),
        "corner": pltpu.VMEM(Reduce.corner_shape(count), BF16),
        "distant": pltpu.VMEM(Reduce.distant_shape(count), BF16),
        "aside": pltpu.VMEM(Reduce.aside_shape(1), BF16),
        "reduce": Reduce.scratch(LATE_POINTS),
        "table": pltpu.VMEM((4, 2, 2 * WIDE // WSIDE, TILE), F32),
        "table_zx": pltpu.VMEM((4, 2, 2 * WIDE // WSIDE, TILE), F32),
        "table_own": pltpu.VMEM((2 * WIDE // WSIDE, TILE), F32),
        "table_yc": pltpu.VMEM((2, 2, 2 * WIDE // WSIDE, TILE), F32),
        "clip": pltpu.VMEM((4, 2, MOD_ROWS, LANES), F32),
        "clip_zx": pltpu.VMEM((4, 2, MOD_ROWS, LANES), F32),
        "clip_own": pltpu.VMEM((MOD_ROWS, LANES), F32),
        "clip_yc": pltpu.VMEM((2, 2, MOD_ROWS, LANES), F32),
        "cond_own": pltpu.VMEM((8, LANES), F32),
        "cond_all": pltpu.VMEM((4, 2, 2, 2, 8, LANES), F32),
        "small": [pltpu.SemaphoreType.DMA((51,))] * 2,
    }
    return call(
        back_kernel,
        "back",
        inputs,
        outputs,
        scratch,
        collective=3,
        grid=(pairs + 1,),
        limit=60,
    )


def per_device(
    special,
    tokens,
    condition,
    clip_frames,
    ada_weight,
    ada_bias,
    qkv_weight,
    out_weight,
    up_weight,
    down_weight,
    rel_table,
    cotangent,
):
    window_count = tokens.shape[0]
    clip_count = condition.shape[0]
    rows_ada, cols_ada = ada_weight.shape
    token_rows = tokens.reshape(window_count * WIN, D)
    cotangent_rows = cotangent.reshape(window_count * WIN, D)
    own = (qkv_weight, out_weight, up_weight, down_weight)
    if special:
        smalls = (clip_frames, condition, ada_weight, ada_bias.reshape(1, cols_ada), rel_table)
        start = across = begin(token_rows, own, smalls)
        mixed = start.mixed_out
        live_frames, member_wide, mod = start.live, start.member, start.mod
        packed, held, normed = start.packed_out, start.held, start.normed_out
    else:
        row_block = lax.axis_index("fsdp")
        col_block = lax.axis_index("dp")
        first_window = lax.axis_index(("dp", "fsdp")) * window_count
        live_frames, member_int = window_layout(clip_frames, first_window, window_count)
        member = member_int.astype(F32)
        activity_low = jax.nn.silu(condition).astype(BF16)
        rows_own = lax.dynamic_slice_in_dim(activity_low, row_block * rows_ada, rows_ada, 1)
        mod_part = jnp.dot(rows_own, ada_weight, preferred_element_type=F32)
        clip_mod = lax.all_gather(lax.psum(mod_part, "fsdp"), "dp", axis=1, tiled=True)
        bias = lax.all_gather(ada_bias, "dp", axis=0, tiled=True)
        clip_mod = clip_mod + bias.astype(F32)[None, :]
        member_wide = None
        window_mod = jnp.sum(member[:, :, None] * clip_mod[None], axis=1)
        window_mod = jnp.pad(window_mod.reshape(window_count, 6, D), ((0, 0), (0, 2), (0, 0)))
        whole = [
            lax.all_gather(
                lax.all_gather(weight, "dp", axis=1, tiled=True), "fsdp", axis=0, tiled=True
            )
            for weight in own
        ]
        held = units_of(*whole).reshape(UNITS, *SPLIT)
        mod = window_mod
        start = enter_plain(token_rows, held, mod)
        packed, normed = start.packed, start.normed
        table = spread_table(lax.all_gather(rel_table, "dp", axis=0, tiled=True))
        across = attend_plain(packed, table, live_frames)
        mixed = across.mixed
    mid = centre(special, live_frames, token_rows, cotangent_rows, mixed, mod, held)
    held = mid.held if special else held
    end = back(
        special,
        live_frames,
        token_rows,
        mod,
        packed,
        normed,
        across.probs,
        mid,
        held,
        ada_weight,
        member_wide,
        condition,
    )
    if special:
        end = deliver(
            output=mid.output,
            grad_tokens=end.grad_tokens,
            grad_condition=end.grad_condition,
            grad_ada=end.grad_ada,
            grad_bias=end.grad_bias,
            grad_qkv=end.grad_qkv,
            grad_out=end.grad_out,
            grad_up=end.grad_up,
            grad_down=end.grad_down,
            table=end.table_total,
        )
        return (
            end.output.reshape(tokens.shape),
            end.grad_tokens.reshape(tokens.shape),
            end.grad_condition,
            end.grad_ada,
            end.grad_bias.reshape(cols_ada),
            end.grad_qkv,
            end.grad_out,
            end.grad_up,
            end.grad_down,
            end.table,
        )
    part = jnp.concatenate([end.part, mid.part[OUT:]])
    grads = [
        lax.psum_scatter(
            lax.psum_scatter(grad, "fsdp", scatter_dimension=0, tiled=True),
            "dp",
            scatter_dimension=1,
            tiled=True,
        ).astype(F32)
        for grad in weights_of(part.reshape(UNITS, 8, D, LANES))
    ]
    grad_mod = (mid.sums + end.sums)[:, :6].reshape(window_count, 6 * D)
    clip_part = lax.dot_general(
        member,
        grad_mod,
        (((0,), (0,)), ((), ())),
        precision=HIGHEST,
        preferred_element_type=F32,
    )
    clip_sum, table_sum = lax.psum((clip_part, gather_table(end.spread)), ("dp", "fsdp"))
    clip_cols = lax.dynamic_slice_in_dim(
        clip_sum.astype(BF16), col_block * cols_ada, cols_ada, 1
    )
    heads_own = rel_table.shape[0]
    table_grad = lax.dynamic_slice_in_dim(table_sum, col_block * heads_own, heads_own, 0)
    cond_part = lax.dot_general(
        clip_cols, ada_weight, (((1,), (1,)), ((), ())), preferred_element_type=F32
    )
    cond_total = lax.all_gather(lax.psum(cond_part, "dp"), "fsdp", axis=1, tiled=True)
    grad_ada_weight = lax.dot_general(
        rows_own, clip_cols, (((0,), (0,)), ((), ())), preferred_element_type=F32
    )
    grad_ada_bias = jnp.sum(clip_cols.astype(F32), axis=0)
    _, silu_back = jax.vjp(jax.nn.silu, condition)
    return (
        mid.output.reshape(tokens.shape),
        end.grad_tokens.reshape(tokens.shape),
        silu_back(cond_total)[0],
        grad_ada_weight,
        grad_ada_bias,
        *grads,
        table_grad,
    )


def solution(mesh):
    special = dict(mesh.shape) == {"dp": 8, "fsdp": 4}
    both = P(("dp", "fsdp"), None, None)
    weight = P("fsdp", "dp")
    in_specs = (both, P(), P(), weight, P("dp")) + (weight,) * 4 + (P("dp", None), both)
    out_specs = (both, both, P(), weight, P("dp")) + (weight,) * 4 + (P("dp", None),)
    return jax.shard_map(
        functools.partial(per_device, special),
        mesh=mesh,
        in_specs=in_specs,
        out_specs=out_specs,
        check_vma=False,
    )
```
